32 devices in a mesh: tm: 4 (over x, core), tile: 8 (over z, y).
Axes of the slice: x: 2, y: 2, z: 4, core: 2. Of those that a mesh axis runs over, the one named last changes fastest.
Arguments:
- recording: bfloat16 [65536, 512], P('tile', 'tm'), may hold values from -300 to 300
- footprints: bfloat16 [65536, 256], P('tile'), may hold values from -0.375 to 0.375
- pattern: int32 [256, 4], P('tile'), may hold values from 0 to 35, as said below
- decay: float32 [16384], P('tile'), may hold values from 0.96 to 1
- frame_gain: float32 [512], P('tm'), may hold values from 0.6 to 1
- spikes: float32 [16384, 512], P('tile', 'tm'), may hold values from 0 to 0.15
Outputs:
- spikes_out: float32 [16384, 512], P('tile', 'tm')
- traces_last: float32 [16384, 512], P('tile', 'tm')
The draws below stay inside these ranges and needn't reach their ends.
Inputs may be any that keep to these rules, and one draw needn't show every extreme that they name: `pattern`: with p = q % 32, row q holds 4 different values between p and p + 4, always including p, p + 2 and p + 4, in some order; value v names the stripe's own neuron block v - 2, so values under 2 or over 2048 // 64 + 1 name edge blocks of the adjacent stripes.
All inputs are finite; a program needn't handle non-finite values.
Results may differ from the reference program's by a relative error of at most 0.00073.
Values may be sent and summed in bfloat16 or wider, within the bound.
No kernel may reach another device: no remote copies, remote signals or barrier semaphores. Data moves between devices by JAX's collectives and lax.ppermute only.
A program may use at most 128 MiB of HBM per device.

```python
import math
import jax
import jax.numpy as jnp
from jax import lax

NEU_BLOCK = 64
PIX_BLOCK = 256
K = 4
HB = 2
ITERS = 2
NEU_DEV = 2048
NEURONS = 16384
PIXELS = 65536
FRAMES = 512
N_TILE = 8


def draw_recording(key, part):
    key_rows, key_cols, key_base = jax.random.split(key, 3)
    row_scale = jnp.exp(jax.random.uniform(key_rows, (PIXELS, 1), jnp.float32, math.log(0.3), math.log(3.0)))
    col_scale = jnp.exp(jax.random.uniform(key_cols, (1, FRAMES), jnp.float32, math.log(0.3), math.log(3.0)))
    pixel_pos = jnp.arange(PIXELS, dtype=jnp.float32)[:, None] / PIXELS - 0.5
    frame_pos = jnp.arange(FRAMES, dtype=jnp.float32)[None, :] / FRAMES - 0.5
    rising = jnp.exp(math.log(3.0) * (pixel_pos + frame_pos))
    values = jax.random.normal(key_base, (PIXELS, FRAMES), jnp.float32) * row_scale * col_scale * rising
    return values.astype(jnp.bfloat16)


def draw_pattern(key, part):
    stripe_blocks = NEU_DEV // NEU_BLOCK
    block_rows = PIXELS // PIX_BLOCK
    local_block = (jnp.arange(block_rows, dtype=jnp.int32) % stripe_blocks).astype(jnp.int32)
    inner = jnp.array([offset for offset in range(1 - HB, HB) if offset != 0], jnp.int32)
    anchors = jnp.array([-HB, 0, HB], jnp.int32)
    row_keys = jax.random.split(key, block_rows)

    def one_row(row_key):
        key_pick, key_order = jax.random.split(row_key)
        extra = jax.random.permutation(key_pick, inner)[:K - 3]
        offsets = jnp.concatenate([anchors, extra])
        return jax.random.permutation(key_order, offsets)
    offsets = jax.vmap(one_row)(row_keys)
    return (local_block[:, None] + HB + offsets).astype(jnp.int32)


def draw_decay(key, part):
    key_kind, key_fast, key_slow = jax.random.split(key, 3)
    share = 0.5
    quick = jax.random.uniform(key_kind, (NEURONS,), jnp.float32) < share
    tau_fast = jnp.exp(jax.random.uniform(key_fast, (NEURONS,), jnp.float32, math.log(30.0), math.log(50.0)))
    tau_slow = jnp.exp(jax.random.uniform(key_slow, (NEURONS,), jnp.float32, math.log(2.0 * FRAMES), math.log(8.0 * FRAMES)))
    tau_all = jnp.where(quick, tau_fast, tau_slow)
    return jnp.exp(-1.0 / tau_all).astype(jnp.float32)


def draw_frame_gain(key, part):
    key_spot, key_level = jax.random.split(key)
    spots = jax.random.choice(key_spot, FRAMES, (3,), replace=False)
    levels = jax.random.uniform(key_level, (3,), jnp.float32, 0.6, 0.8)
    return jnp.ones((FRAMES,), jnp.float32).at[spots].set(levels)


def shard_levels(key, dims, cuts, smallest, largest):
    level = 1.0
    for axis_at, shards_of in cuts:
        draws = jax.random.uniform(jax.random.fold_in(jax.random.fold_in(key, 6), axis_at), (shards_of,), jnp.float32, smallest / len(cuts), largest / len(cuts))
        level = level * jnp.repeat(jnp.exp(draws), dims[axis_at] // shards_of).reshape((-1,) + (1,) * (len(dims) - 1 - axis_at))
    return level


def noise(own_key, dims, scale, reach, cuts=(), kind=jnp.bfloat16):
    entries = scale * jax.random.normal(own_key, dims, jnp.float32)
    if cuts:
        entries = entries * shard_levels(own_key, dims, cuts, -0.22, 0.18)
    return jnp.clip(entries, -reach, reach).astype(kind)


def setup_inputs(seed: int = 0) -> dict:
    streams_of = jax.random.split(jax.random.key(seed), 7)
    return {
        "recording": draw_recording(jax.random.fold_in(streams_of[6], 71), 0),
        "footprints": noise(streams_of[1], (PIXELS, K * NEU_BLOCK), (K * NEU_BLOCK) ** -0.5, 0.375, ((0, 8),)),
        "pattern": draw_pattern(jax.random.fold_in(streams_of[6], 71), 0),
        "decay": draw_decay(jax.random.fold_in(streams_of[6], 71), 0),
        "frame_gain": draw_frame_gain(jax.random.fold_in(streams_of[6], 71), 0),
        "spikes": jnp.clip(0.15 * jax.random.uniform(streams_of[5], (NEURONS, FRAMES), jnp.float32) ** shard_levels(streams_of[5], (NEURONS, FRAMES), ((0, 8), (1, 4)), -0.2, 0.2), 0.0, 0.15),
    }


def forward_filter(drive, decay, frame_gain):

    def advance(state, column):
        source, factor = column
        state = decay * factor * state + source
        return (state, state)
    _, rows_out = lax.scan(advance, jnp.zeros(decay.shape, jnp.float32), (drive.T, frame_gain))
    return rows_out.T

def backward_filter(source, decay, frame_gain):
    next_gain = jnp.concatenate([frame_gain[1:], jnp.zeros((1,), jnp.float32)])

    def retreat(state, column):
        values, factor = column
        state = values + decay * factor * state
        return (state, state)
    _, rows_out = lax.scan(retreat, jnp.zeros(decay.shape, jnp.float32), (source.T, next_gain), reverse=True)
    return rows_out.T

def footprint_apply(values, footprints, pattern):
    stripe_blocks = NEU_DEV // NEU_BLOCK
    total_blocks = NEURONS // NEU_BLOCK
    padded = jnp.pad(values.reshape(total_blocks, NEU_BLOCK, FRAMES), ((HB, HB), (0, 0), (0, 0)))
    stripes = footprints.reshape(N_TILE, stripe_blocks, PIX_BLOCK, K * NEU_BLOCK)
    patterns = pattern.reshape(N_TILE, stripe_blocks, K)

    def one_stripe(items):
        stripe, feet, rows_idx = items
        picked = padded[stripe * stripe_blocks + rows_idx]
        picked = picked.reshape(stripe_blocks, K * NEU_BLOCK, FRAMES).astype(jnp.float32)
        return jnp.einsum('paj,pjf->paf', feet.astype(jnp.float32), picked, precision=lax.Precision.HIGHEST)
    fitted = lax.map(one_stripe, (jnp.arange(N_TILE, dtype=jnp.int32), stripes, patterns))
    return fitted.reshape(PIXELS, FRAMES)

def footprint_adjoint(residual, footprints, pattern):
    stripe_blocks = NEU_DEV // NEU_BLOCK
    total_blocks = NEURONS // NEU_BLOCK
    stripes = footprints.reshape(N_TILE, stripe_blocks, PIX_BLOCK, K * NEU_BLOCK)
    resid_stripes = residual.reshape(N_TILE, stripe_blocks, PIX_BLOCK, FRAMES)
    patterns = pattern.reshape(N_TILE, stripe_blocks, K)

    def one_stripe(totals, items):
        stripe, feet, resid, rows_idx = items
        contrib = jnp.einsum('paj,paf->pjf', feet.astype(jnp.float32), resid.astype(jnp.float32), precision=lax.Precision.HIGHEST)
        contrib = contrib.reshape(stripe_blocks * K, NEU_BLOCK, FRAMES)
        targets = (stripe * stripe_blocks + rows_idx).reshape(-1).astype(jnp.int32)
        return (totals.at[targets].add(contrib), None)
    start = jnp.zeros((total_blocks + 2 * HB, NEU_BLOCK, FRAMES), jnp.float32)
    totals, _ = lax.scan(one_stripe, start, (jnp.arange(N_TILE, dtype=jnp.int32), stripes, resid_stripes, patterns))
    return totals[HB:HB + total_blocks].reshape(NEURONS, FRAMES)

def reference(recording, footprints, pattern, decay, frame_gain, spikes):
    gain = jnp.sqrt(1.0 - decay * decay)[:, None]
    record = recording.astype(jnp.float32)
    current = spikes
    traces = spikes
    for iteration in range(ITERS):
        traces = forward_filter(gain * current, decay, frame_gain)
        fitted = footprint_apply(traces.astype(jnp.bfloat16), footprints, pattern)
        residual = (fitted - record).astype(jnp.bfloat16)
        gradient = gain * backward_filter(footprint_adjoint(residual, footprints, pattern), decay, frame_gain)
        direction = forward_filter(gain * gradient, decay, frame_gain).astype(jnp.bfloat16)
        projected = footprint_apply(direction, footprints, pattern)
        step_size = jnp.sum(gradient * gradient) / (jnp.sum(projected * projected) + 1e-06)
        current = jnp.maximum(current - step_size * gradient, 0.0)
    return (current, traces)
```

```python
import jax
import jax.numpy as jnp
from jax import lax
from jax.sharding import PartitionSpec as P

NEU_BLOCK = 64
PIX_BLOCK = 256
K = 4
HB = 2
ITERS = 2


def entering(array, axis, combine, identity, reverse):
    length, place = (lax.axis_size(axis), lax.axis_index(axis))
    everything = jax.tree.map(lambda part: lax.all_gather(part, axis), array)
    start = jax.tree.map(
        lambda part, zero: jnp.broadcast_to(jnp.asarray(zero, part.dtype), part.shape),
        array,
        identity,
    )

    def turn(k, before):
        at = length - 1 - k if reverse else k
        reached = at > place if reverse else at < place
        new = combine(before, jax.tree.map(lambda part: part[at], everything))
        return jax.tree.map(lambda a, b: jnp.where(reached, a, b), new, before)

    return lax.fori_loop(0, length, turn, start)


def padded(array, sides, width):
    for axis, dim in sides:
        size, length = (lax.axis_size(axis), array.shape[dim])
        up = [(i, (i + 1) % size) for i in range(size - 1)]
        down = [(j, i) for i, j in up]
        last = lax.slice_in_dim(array, length - width, length, axis=dim)
        initial = lax.slice_in_dim(array, 0, width, axis=dim)
        before = lax.ppermute(last, axis, up)
        after = lax.ppermute(initial, axis, down)
        array = jnp.concatenate([before, array, after], axis=dim)
    return array


def shifted(array, axis, by):
    length = lax.axis_size(axis)
    pairs = [(i, i + by) for i in range(length) if 0 <= i + by < length]
    return lax.ppermute(array, axis, pairs)


def chain_affine(earlier, latter):
    return (earlier[0] * latter[0], latter[0] * earlier[1] + latter[1])


def tri_matmul(values, table):
    return jnp.dot(
        values, table, precision=lax.Precision.HIGHEST, preferred_element_type=jnp.float32
    )


def incoming_forward(summary):
    result = entering(
        summary, "tm", chain_affine, (jnp.ones_like(summary[0]), jnp.zeros_like(summary[1])), False
    )
    return result[1]


def incoming_backward(summary):
    result = entering(
        summary, "tm", chain_affine, (jnp.ones_like(summary[0]), jnp.zeros_like(summary[1])), True
    )
    return result[1]


def per_device(recording, footprints, pattern, decay, frame_gain, spikes):
    neurons, frames = spikes.shape
    blocks = neurons // NEU_BLOCK
    rim_rows = HB * NEU_BLOCK
    drive_gain = jnp.sqrt(1.0 - decay * decay)[:, None]
    decay_rate = decay[:, None] * frame_gain[None, :]
    back_rate = jnp.concatenate(
        [decay[:, None] * frame_gain[None, 1:], jnp.ones((neurons, 1), jnp.float32)], axis=1
    )
    foot_blocks = footprints.reshape(blocks, PIX_BLOCK, K * NEU_BLOCK)
    record = recording.astype(jnp.float32)
    row_pos = lax.broadcasted_iota(jnp.int32, (frames, frames), 0)
    col_pos = lax.broadcasted_iota(jnp.int32, (frames, frames), 1)
    upper_incl = (row_pos <= col_pos).astype(jnp.float32)
    upper_strict = (row_pos < col_pos).astype(jnp.float32)
    lower_incl = (row_pos >= col_pos).astype(jnp.float32)
    fwd_total = jnp.exp(tri_matmul(jnp.log(decay_rate), upper_incl))
    back_log = tri_matmul(jnp.log(back_rate), upper_strict)
    back_prefix = jnp.exp(back_log)
    back_total = jnp.exp(back_log[:, -1:] - back_log)
    wide_onehot = (
        pattern.reshape(1, -1) == jnp.arange(blocks + 2 * HB, dtype=jnp.int32)[:, None]
    ).astype(jnp.float32)

    def forward_pass(drive):
        local_part = fwd_total * tri_matmul(drive / fwd_total, upper_incl)
        carry_in = incoming_forward((fwd_total[:, -1], local_part[:, -1]))
        return local_part + fwd_total * carry_in[:, None]

    def footprint_apply(values):
        extended = padded(values, (("tile", 0),), rim_rows)
        picked = extended.reshape(blocks + 2 * HB, NEU_BLOCK, frames)[pattern]
        picked = picked.reshape(blocks, K * NEU_BLOCK, frames)
        fitted = jnp.einsum("paj,pjf->paf", foot_blocks, picked, preferred_element_type=jnp.float32)
        return fitted.reshape(blocks * PIX_BLOCK, frames)

    current = spikes
    traces = spikes
    for iteration in range(ITERS):
        traces = forward_pass(drive_gain * current)
        fitted = footprint_apply(traces.astype(jnp.bfloat16))
        residual = (fitted - record).astype(jnp.bfloat16)
        contrib = jnp.einsum(
            "paj,paf->pjf",
            foot_blocks,
            residual.reshape(blocks, PIX_BLOCK, frames),
            preferred_element_type=jnp.float32,
        )
        contrib = contrib.reshape(blocks * K, NEU_BLOCK * frames)
        summed = jnp.dot(
            wide_onehot,
            contrib,
            precision=lax.Precision.HIGHEST,
            preferred_element_type=jnp.float32,
        )
        summed = summed.reshape(neurons + 2 * rim_rows, frames)
        from_above = shifted(summed[:rim_rows], "tile", -1)
        from_below = shifted(summed[rim_rows + neurons :], "tile", 1)
        own_sums = summed[rim_rows : rim_rows + neurons]
        own_sums = own_sums.at[:rim_rows].add(from_below)
        backward_local_part = (
            tri_matmul(own_sums.at[neurons - rim_rows :].add(from_above) * back_prefix, lower_incl)
            / back_prefix
        )
        head = decay_rate[:, 0]
        backward_carry_in = incoming_backward(
            (head * back_total[:, 0], head * backward_local_part[:, 0])
        )
        gradient = drive_gain * (backward_local_part + back_total * backward_carry_in[:, None])
        direction = forward_pass(drive_gain * gradient).astype(jnp.bfloat16)
        projected = footprint_apply(direction)
        sums = jnp.stack([jnp.sum(gradient * gradient), jnp.sum(projected * projected)])
        if iteration == 0:
            sums = jnp.sum(lax.all_gather(sums, ("tile", "tm")), axis=0)
        else:
            sums = jnp.sum(lax.all_gather(sums, "tm"), axis=0)
            sums = jnp.sum(lax.all_gather(sums, "tile"), axis=0)
        grad_sq, image_sq = sums[0], sums[1]
        step_size = grad_sq / (image_sq + 1e-06)
        current = jnp.maximum(current - step_size * gradient, 0.0)
    return (current, traces)


def solution(mesh):
    return jax.shard_map(
        per_device,
        mesh=mesh,
        in_specs=(
            P("tile", "tm"),
            P("tile", None),
            P("tile", None),
            P("tile"),
            P("tm"),
            P("tile", "tm"),
        ),
        out_specs=(P("tile", "tm"), P("tile", "tm")),
        check_vma=False,
    )
```

```python
import jax
import jax.numpy as jnp
from jax import lax
from jax.sharding import PartitionSpec as P

NEU_BLOCK = 64
PIX_BLOCK = 256
K = 4
HB = 2
ITERS = 2


def entering(array, axis, combine, identity, reverse):
    length, place = (lax.axis_size(axis), lax.axis_index(axis))
    gather = told_all if reverse else lax.all_gather
    everything = jax.tree.map(lambda part: gather(part, axis), array)
    start = jax.tree.map(
        lambda part, zero: jnp.broadcast_to(jnp.asarray(zero, part.dtype), part.shape),
        array,
        identity,
    )

    def turn(k, before):
        at = length - 1 - k if reverse else k
        reached = at > place if reverse else at < place
        new = combine(before, jax.tree.map(lambda part: part[at], everything))
        return jax.tree.map(lambda a, b: jnp.where(reached, a, b), new, before)

    return lax.fori_loop(0, length, turn, start)


def told_all(values, axis):
    copies = jnp.broadcast_to(values, (lax.axis_size(axis),) + values.shape)
    return lax.all_to_all(copies, axis, 0, 0)


def padded(array, sides, width):
    for axis, dim in sides:
        size, length = (lax.axis_size(axis), array.shape[dim])
        up = [(i, (i + 1) % size) for i in range(size - 1)]
        down = [(j, i) for i, j in up]
        last = lax.slice_in_dim(array, length - width, length, axis=dim)
        initial = lax.slice_in_dim(array, 0, width, axis=dim)
        before = lax.ppermute(last, axis, up)
        after = lax.ppermute(initial, axis, down)
        array = jnp.concatenate([before, array, after], axis=dim)
    return array


def shifted(array, axis, by):
    length = lax.axis_size(axis)
    pairs = [(i, i + by) for i in range(length) if 0 <= i + by < length]
    return lax.ppermute(array, axis, pairs)


def chain_affine(earlier, latter):
    return (earlier[0] * latter[0], latter[0] * earlier[1] + latter[1])


def tri_matmul(values, table):
    return jnp.dot(
        values, table, precision=lax.Precision.HIGHEST, preferred_element_type=jnp.float32
    )


def incoming_forward(summary):
    result = entering(
        summary, "tm", chain_affine, (jnp.ones_like(summary[0]), jnp.zeros_like(summary[1])), False
    )
    return result[1]


def incoming_backward(summary):
    result = entering(
        summary, "tm", chain_affine, (jnp.ones_like(summary[0]), jnp.zeros_like(summary[1])), True
    )
    return result[1]


def per_device(recording, footprints, pattern, decay, frame_gain, spikes):
    neurons, frames = spikes.shape
    blocks = neurons // NEU_BLOCK
    rim_rows = HB * NEU_BLOCK
    drive_gain = jnp.sqrt(1.0 - decay * decay)[:, None]
    decay_rate = decay[:, None] * frame_gain[None, :]
    back_rate = jnp.concatenate(
        [decay[:, None] * frame_gain[None, 1:], jnp.ones((neurons, 1), jnp.float32)], axis=1
    )
    foot_blocks = footprints.reshape(blocks, PIX_BLOCK, K * NEU_BLOCK)
    record = recording.astype(jnp.float32)
    row_pos = lax.broadcasted_iota(jnp.int32, (frames, frames), 0)
    col_pos = lax.broadcasted_iota(jnp.int32, (frames, frames), 1)
    upper_incl = (row_pos <= col_pos).astype(jnp.float32)
    upper_strict = (row_pos < col_pos).astype(jnp.float32)
    lower_incl = (row_pos >= col_pos).astype(jnp.float32)
    fwd_total = jnp.exp(tri_matmul(jnp.log(decay_rate), upper_incl))
    back_log = tri_matmul(jnp.log(back_rate), upper_strict)
    back_prefix = jnp.exp(back_log)
    back_total = jnp.exp(back_log[:, -1:] - back_log)
    wide_onehot = (
        pattern.reshape(1, -1) == jnp.arange(blocks + 2 * HB, dtype=jnp.int32)[:, None]
    ).astype(jnp.float32)

    def forward_pass(drive):
        local_part = fwd_total * tri_matmul(drive / fwd_total, upper_incl)
        carry_in = incoming_forward((fwd_total[:, -1], local_part[:, -1]))
        return local_part + fwd_total * carry_in[:, None]

    def footprint_apply(values):
        extended = padded(values, (("tile", 0),), rim_rows)
        picked = extended.reshape(blocks + 2 * HB, NEU_BLOCK, frames)[pattern]
        picked = picked.reshape(blocks, K * NEU_BLOCK, frames)
        fitted = jnp.einsum("paj,pjf->paf", foot_blocks, picked, preferred_element_type=jnp.float32)
        return fitted.reshape(blocks * PIX_BLOCK, frames)

    current = spikes
    traces = spikes
    for iteration in range(ITERS):
        traces = forward_pass(drive_gain * current)
        fitted = footprint_apply(traces.astype(jnp.bfloat16))
        residual = (fitted - record).astype(jnp.bfloat16)
        contrib = jnp.einsum(
            "paj,paf->pjf",
            foot_blocks,
            residual.reshape(blocks, PIX_BLOCK, frames),
            preferred_element_type=jnp.float32,
        )
        contrib = contrib.reshape(blocks * K, NEU_BLOCK * frames)
        summed = jnp.dot(
            wide_onehot,
            contrib,
            precision=lax.Precision.HIGHEST,
            preferred_element_type=jnp.float32,
        )
        summed = summed.reshape(neurons + 2 * rim_rows, frames)
        from_above = shifted(summed[:rim_rows], "tile", -1)
        from_below = shifted(summed[rim_rows + neurons :], "tile", 1)
        own_sums = summed[rim_rows : rim_rows + neurons]
        own_sums = own_sums.at[:rim_rows].add(from_below)
        backward_local_part = (
            tri_matmul(own_sums.at[neurons - rim_rows :].add(from_above) * back_prefix, lower_incl)
            / back_prefix
        )
        head = decay_rate[:, 0]
        backward_carry_in = incoming_backward(
            (head * back_total[:, 0], head * backward_local_part[:, 0])
        )
        gradient = drive_gain * (backward_local_part + back_total * backward_carry_in[:, None])
        direction = forward_pass(drive_gain * gradient).astype(jnp.bfloat16)
        projected = footprint_apply(direction)
        sums = jnp.stack([jnp.sum(gradient * gradient), jnp.sum(projected * projected)])
        if iteration == 0:
            sums = jnp.sum(told_all(sums, ("tile", "tm")), axis=0)
        else:
            sums = jnp.sum(lax.all_gather(sums, "tm"), axis=0)
            sums = jnp.sum(told_all(sums, "tile"), axis=0)
        grad_sq, image_sq = sums[0], sums[1]
        step_size = grad_sq / (image_sq + 1e-06)
        current = jnp.maximum(current - step_size * gradient, 0.0)
    return (current, traces)


def solution(mesh):
    return jax.shard_map(
        per_device,
        mesh=mesh,
        in_specs=(
            P("tile", "tm"),
            P("tile", None),
            P("tile", None),
            P("tile"),
            P("tm"),
            P("tile", "tm"),
        ),
        out_specs=(P("tile", "tm"), P("tile", "tm")),
        check_vma=False,
    )
```

```python
import functools

import jax
import jax.numpy as jnp
from jax import lax
from jax.experimental import pallas as pl
from jax.experimental.pallas import tpu as pltpu
from jax.sharding import PartitionSpec as P

NEU_BLOCK = 64
PIX_BLOCK = 256
K = 4
HB = 2
ITERS = 2
LANES = 128
RIM = HB * NEU_BLOCK // LANES
FEET_PARTS = 4
F32 = jnp.float32
BF16 = jnp.bfloat16
VMEM = pl.BlockSpec(memory_space=pltpu.VMEM)
SMEM = pl.BlockSpec(memory_space=pltpu.SMEM)
ANY = pl.BlockSpec(memory_space=pl.ANY)


def padded8(rows):
    return -(-rows // 8) * 8


def table(frames, reverse):
    row = lax.broadcasted_iota(jnp.int32, (frames, 2 * frames), 0)
    col = lax.broadcasted_iota(jnp.int32, (frames, 2 * frames), 1)
    col = jnp.where(col >= frames, col - frames, col)
    keep = col >= row if reverse else col <= row
    return jnp.where(keep, 1.0, 0.0).astype(BF16)


def summed(sums_table, values):
    high = values.astype(BF16)
    low = (values - high.astype(F32)).astype(BF16)
    both = jnp.concatenate([high, low], axis=0)
    return jnp.dot(sums_table, both, preferred_element_type=F32)


def powers(log_decay, frames, mid, sign):
    groups = frames // 8
    coarse = (8 * lax.broadcasted_iota(jnp.int32, (groups, LANES), 0) - mid).astype(F32) * sign
    fine = lax.broadcasted_iota(jnp.int32, (8, LANES), 0).astype(F32) * sign
    coarse = jnp.exp(coarse * log_decay)
    fine = jnp.exp(fine * log_decay)
    return (coarse[:, None, :] * fine[None, :, :]).reshape(frames, LANES)


def prep_kernel(spikes, below, above, decay, gains, s3, p3, pinv3, z3, rows, pay):
    frames = spikes.shape[1]
    own = spikes.shape[0] // LANES
    chunks = own + 2 * RIM
    mid = frames // 2 - 1
    sums_table = table(frames, False)
    lane = lax.broadcasted_iota(jnp.int32, (8, frames), 1)
    prefix = jnp.broadcast_to(gains[...], (8, frames))
    step = 1
    while step < frames:
        prefix = prefix * jnp.where(lane >= step, pltpu.roll(prefix, step, 1), 1.0)
        step *= 2
    middle = jnp.broadcast_to(prefix[0:1, mid : mid + 1], (8, frames))
    prefix_col = jnp.broadcast_to((prefix / middle)[0:1], (LANES, frames)).T
    inverse_col = jnp.broadcast_to((middle / prefix)[0:1], (LANES, frames)).T
    rows[...] = jnp.ones_like(rows)
    pay[...] = jnp.zeros_like(pay)
    pay[0, chunks : chunks + 1, :] = gains[...]
    for c in range(chunks):
        if c < RIM:
            rate, field = below[LANES : LANES + 1, :], below[0:LANES, :]
        elif c >= RIM + own:
            rate, field = above[LANES : LANES + 1, :], above[0:LANES, :]
        else:
            i = c - RIM
            rate, field = decay[i : i + 1, :], spikes[i * LANES : (i + 1) * LANES, :]
        rate = jnp.where(rate > 0.0, rate, 1.0)
        log_rate = jnp.log(rate)
        gain = jnp.sqrt(1.0 - rate * rate)
        p = powers(log_rate, frames, mid, 1.0) * prefix_col
        pinv = powers(log_rate, frames, mid, -1.0) * inverse_col
        field = field.T
        z = summed(sums_table, field * gain * pinv)
        last = p[frames - 1 : frames, :]
        s3[c] = field
        p3[c] = p
        pinv3[c] = pinv
        z3[c] = z
        half = rate
        for _ in range(frames.bit_length() - 2):
            half = half * half
        rows[0, c : c + 1, :] = gain
        rows[1, c : c + 1, :] = half * middle[0:1, 0:1]
        rows[2, c : c + 1, :] = half * half
        pay[0, c : c + 1, :] = last * z[frames - 1 : frames, :]
        scale = last * gain
        pay[1, c : c + 1, :] = scale * scale * jnp.sum(pinv * pinv, axis=0, keepdims=True)


def block_totals(pays, chunks, rows):
    totals = []
    for m in range(pays.shape[0]):
        gain = jnp.broadcast_to(pays[m, 0, chunks : chunks + 1, :], (8, LANES))
        step = 1
        while step < LANES:
            gain = gain * pltpu.roll(gain, step, 1)
            step *= 2
        totals.append(rows[2] * gain[0:1])
    return totals


def step_size(stats):
    both = jnp.sum(stats[...], axis=0)
    both = jnp.broadcast_to(both, (8, LANES))
    other = pltpu.roll(both, LANES // 2, 1)
    first = lax.broadcasted_iota(jnp.int32, (8, LANES), 1) < LANES // 2
    grad_sq = jnp.where(first, both, other)
    image_sq = jnp.where(first, other, both)
    return (grad_sq / (image_sq + 1e-06))[0:1]


def update_kernel(s3, g3, stats, p3, pinv3, rows, new3, z3, pay):
    chunks, frames = s3.shape[0], s3.shape[1]
    sums_table = table(frames, False)
    size = step_size(stats)
    pay[...] = jnp.zeros_like(pay)
    for c in range(chunks):
        field = jnp.maximum(s3[c] - size * g3[c], 0.0)
        z = summed(sums_table, field * rows[0, c : c + 1, :] * pinv3[c])
        new3[c] = field
        z3[c] = z
        pay[c : c + 1, :] = p3[c, frames - 1 : frames, :] * z[frames - 1 : frames, :]


def final_kernel(s3, g3, stats, out):
    size = step_size(stats)
    for i in range(out.shape[0] // LANES):
        c = i + RIM
        out[i * LANES : (i + 1) * LANES, :] = jnp.maximum(s3[c] - size * g3[c], 0.0).T


def feet_copies(feet, feet_here, sems):
    size = feet.shape[0] // FEET_PARTS
    return [
        pltpu.make_async_copy(
            feet.at[pl.ds(i * size, size)], feet_here.at[pl.ds(i * size, size)], sems.at[i]
        )
        for i in range(FEET_PARTS)
    ]


def picked(ext, pattern, q):
    parts = [
        ext[pl.ds(pl.multiple_of(pattern[q, k] * NEU_BLOCK, NEU_BLOCK), NEU_BLOCK), :]
        for k in range(K)
    ]
    return jnp.concatenate(parts, axis=0)


def residual_kernel(
    last, pattern, z3, p3, rows, pay, pays, feet, record, *rest
):
    if last:
        mid3, below3, above3, traces = rest[:4]
        rest = rest[4:]
    else:
        mid3, below3, above3 = rest[:3]
        rest = rest[3:]
    feet_here, record_here, ext, contrib, place, sems = rest
    chunks, frames = z3.shape[0], z3.shape[1]
    own = chunks - 2 * RIM
    stripe = pattern.shape[0]
    copies = feet_copies(feet, feet_here, sems)
    size = record.shape[0] // FEET_PARTS
    others = [
        pltpu.make_async_copy(
            record.at[pl.ds(i * size, size)],
            record_here.at[pl.ds(i * size, size)],
            sems.at[FEET_PARTS + i],
        )
        for i in range(FEET_PARTS)
    ]
    for a, b in zip(copies, others):
        a.start()
        b.start()
    me = lax.axis_index("tm")
    totals = block_totals(pay, chunks, rows)
    carry = jnp.zeros_like(totals[0])
    for m in range(pays.shape[0]):
        carry = jnp.where(m < me, pays[m] + totals[m] * carry, carry)
    carry = carry * rows[1]
    for c in range(chunks):
        field = (p3[c] * (z3[c] + carry[c : c + 1, :])).T
        ext[c * LANES : (c + 1) * LANES, :] = field.astype(BF16)
        if last and RIM <= c < RIM + own:
            traces[(c - RIM) * LANES : (c - RIM + 1) * LANES, :] = field
    for q in range(stripe):
        for v in range(2 * HB + 1):
            place[q, v] = -1
        for k in range(K):
            place[q, pattern[q, k] - q] = k
    for part in range(FEET_PARTS):
        copies[part].wait()
        others[part].wait()
        for q in range(part * stripe // FEET_PARTS, (part + 1) * stripe // FEET_PARTS):
            at = pl.ds(q * PIX_BLOCK, PIX_BLOCK)
            foot = feet_here[at, :]
            fitted = jnp.dot(foot, picked(ext, pattern, q), preferred_element_type=F32)
            residual = (fitted - record_here[at, :].astype(F32)).astype(BF16)
            contrib[q * K * NEU_BLOCK : (q + 1) * K * NEU_BLOCK, :] = lax.dot_general(
                foot, residual, (((0,), (0,)), ((), ())), preferred_element_type=F32
            )
    per_chunk = LANES // NEU_BLOCK
    for c in range(chunks):
        halves = []
        for b in range(c * per_chunk, (c + 1) * per_chunk):
            total = jnp.zeros((NEU_BLOCK, frames), F32)
            for v in range(2 * HB + 1):
                q = b - v
                if 0 <= q < stripe:
                    k = place[q, v]
                    at = pl.multiple_of((q * K + jnp.maximum(k, 0)) * NEU_BLOCK, NEU_BLOCK)
                    value = contrib[pl.ds(at, NEU_BLOCK), :]
                    if v % 2:
                        value = jnp.where(k >= 0, value, 0.0)
                    total = total + value
            halves.append(total)
        whole = jnp.concatenate(halves, axis=0).T
        if c < 2 * RIM:
            below3[c] = whole
        elif c >= chunks - 2 * RIM:
            above3[c - (chunks - 2 * RIM)] = whole
        else:
            mid3[c - 2 * RIM] = whole


def adjoint_kernel(mid3, below3, above3, from_below, from_above, p3, pinv3, rows, r3, pay):
    chunks, frames = p3.shape[0], p3.shape[1]
    sums_table = table(frames, True)
    pay[...] = jnp.zeros_like(pay)
    for c in range(chunks):
        if c < 2 * RIM:
            field = below3[c] + from_below[c]
        elif c >= chunks - 2 * RIM:
            at = c - (chunks - 2 * RIM)
            field = above3[at] + from_above[at]
        else:
            field = mid3[c - 2 * RIM]
        p, pinv = p3[c], pinv3[c]
        r = summed(sums_table, field * p)
        r3[c] = r
        gain = rows[0, c : c + 1, :]
        pay[0, c : c + 1, :] = rows[1, c : c + 1, :] * r[0:1, :]
        pay[1, c : c + 1, :] = (
            p[frames - 1 : frames, :]
            * gain
            * gain
            * jnp.sum(pinv * pinv * r, axis=0, keepdims=True)
        )


def direction_kernel(
    pattern, r3, p3, pinv3, rows, pay, pays, feet, g3, stats, feet_here, ext, sems
):
    chunks, frames = r3.shape[0], r3.shape[1]
    own = chunks - 2 * RIM
    stripe = pattern.shape[0]
    copies = feet_copies(feet, feet_here, sems)
    for a in copies:
        a.start()
    me = lax.axis_index("tm")
    totals = block_totals(pay, chunks, rows)
    blocks = pays.shape[0]
    entering = [None] * blocks
    state = jnp.zeros_like(totals[0])
    for m in reversed(range(blocks)):
        entering[m] = state
        state = pays[m, 0] + totals[m] * state
    carry = jnp.zeros_like(totals[0])
    adjoint = jnp.zeros_like(totals[0])
    for m in range(blocks):
        end = pays[m, 1] + pay[m, 1] * entering[m]
        carry = jnp.where(m < me, end + totals[m] * carry, carry)
        adjoint = jnp.where(m == me, entering[m], adjoint)
    carry = carry * rows[1]
    sums_table = table(frames, False)
    grad_sq = jnp.zeros((8, LANES), F32)
    for c in range(chunks):
        p, pinv = p3[c], pinv3[c]
        gain = rows[0, c : c + 1, :]
        gradient = (
            gain * pinv * (r3[c] + p[frames - 1 : frames, :] * adjoint[c : c + 1, :])
        )
        g3[c] = gradient
        if RIM <= c < RIM + own:
            grad_sq += jnp.sum((gradient * gradient).reshape(frames // 8, 8, LANES), axis=0)
        z = summed(sums_table, gain * gradient * pinv)
        field = (p * (z + carry[c : c + 1, :])).T
        ext[c * LANES : (c + 1) * LANES, :] = field.astype(BF16)
    image_sq = jnp.zeros((8, frames), F32)
    for part in range(FEET_PARTS):
        copies[part].wait()
        for q in range(part * stripe // FEET_PARTS, (part + 1) * stripe // FEET_PARTS):
            foot = feet_here[pl.ds(q * PIX_BLOCK, PIX_BLOCK), :]
            image = jnp.dot(foot, picked(ext, pattern, q), preferred_element_type=F32)
            image_sq += jnp.sum((image * image).reshape(PIX_BLOCK // 8, 8, frames), axis=0)
    first = lax.broadcasted_iota(jnp.int32, (1, LANES), 1) < LANES // 2
    both = jnp.where(first, jnp.sum(grad_sq), jnp.sum(image_sq))
    stats[...] = jnp.broadcast_to(both[None], stats.shape)


def f32(*shape):
    return jax.ShapeDtypeStruct(shape, F32)


def call(kernel, name, outs, in_specs, scratch=()):
    return pl.pallas_call(
        kernel,
        name=name,
        out_shape=outs,
        in_specs=in_specs,
        out_specs=jax.tree.map(lambda _: VMEM, outs),
        scratch_shapes=scratch,
        compiler_params=pltpu.CompilerParams(vmem_limit_bytes=40 * 2**20),
    )


def neighbours(to_below, to_above):
    size = lax.axis_size("tile")
    up = [(i, i + 1) for i in range(size - 1)]
    down = [(i + 1, i) for i in range(size - 1)]
    return lax.ppermute(to_above, "tile", up), lax.ppermute(to_below, "tile", down)


def per_device(recording, footprints, pattern, decay, frame_gain, spikes):
    neurons, frames = spikes.shape
    pixels = recording.shape[0]
    stripe = pattern.shape[0]
    own = neurons // LANES
    chunks = own + 2 * RIM
    lines = padded8(chunks + 1)
    devices = lax.axis_size("tile") * lax.axis_size("tm")
    field = f32(chunks, frames, LANES)
    rates = decay.reshape(own, LANES)
    edge = HB * NEU_BLOCK
    from_below, from_above = neighbours(
        jnp.concatenate([spikes[:edge], rates[:RIM]], axis=0),
        jnp.concatenate([spikes[-edge:], rates[-RIM:]], axis=0),
    )
    s3, p3, pinv3, z3, rows, pay = call(
        prep_kernel,
        "prep",
        (field, field, field, field, f32(3, lines, LANES), f32(2, lines, LANES)),
        [VMEM] * 5,
    )(spikes, from_below, from_above, rates, frame_gain.reshape(1, frames))
    constants = lax.all_gather(pay, "tm")
    pays = constants[:, 0]
    for iteration in range(ITERS):
        last = iteration == ITERS - 1
        outs = (
            f32(chunks - 4 * RIM, frames, LANES),
            f32(2 * RIM, frames, LANES),
            f32(2 * RIM, frames, LANES),
        ) + ((f32(neurons, frames),) if last else ())
        mid3, below3, above3, *traces = call(
            functools.partial(residual_kernel, last),
            "residual",
            outs,
            [SMEM, VMEM, VMEM, VMEM, VMEM, VMEM, ANY, ANY],
            [
                pltpu.VMEM((pixels, K * NEU_BLOCK), BF16),
                pltpu.VMEM((pixels, frames), BF16),
                pltpu.VMEM((chunks * LANES, frames), BF16),
                pltpu.VMEM((stripe * K * NEU_BLOCK, frames), F32),
                pltpu.SMEM((stripe, 2 * HB + 1), jnp.int32),
                pltpu.SemaphoreType.DMA((2 * FEET_PARTS,)),
            ],
        )(pattern, z3, p3, rows, constants, pays, footprints, recording)
        from_below, from_above = neighbours(below3, above3)
        r3, pay = call(
            adjoint_kernel, "adjoint", (field, f32(2, lines, LANES)), [VMEM] * 8
        )(mid3, below3, above3, from_below, from_above, p3, pinv3, rows)
        pays = lax.all_gather(pay, "tm")
        g3, stats = call(
            direction_kernel,
            "direction",
            (field, f32(devices, 1, LANES)),
            [SMEM, VMEM, VMEM, VMEM, VMEM, VMEM, VMEM, ANY],
            [
                pltpu.VMEM((pixels, K * NEU_BLOCK), BF16),
                pltpu.VMEM((chunks * LANES, frames), BF16),
                pltpu.SemaphoreType.DMA((FEET_PARTS,)),
            ],
        )(pattern, r3, p3, pinv3, rows, constants, pays, footprints)
        stats = lax.all_to_all(stats, ("tile", "tm"), 0, 0)
        if last:
            out = call(final_kernel, "final", f32(neurons, frames), [VMEM] * 3)(s3, g3, stats)
            return out, traces[0]
        s3, z3, pay = call(
            update_kernel, "update", (field, field, f32(lines, LANES)), [VMEM] * 6
        )(s3, g3, stats, p3, pinv3, rows)
        pays = lax.all_gather(pay, "tm")


def solution(mesh):
    return jax.shard_map(
        per_device,
        mesh=mesh,
        in_specs=(
            P("tile", "tm"),
            P("tile", None),
            P("tile", None),
            P("tile"),
            P("tm"),
            P("tile", "tm"),
        ),
        out_specs=(P("tile", "tm"), P("tile", "tm")),
        check_vma=False,
    )
```

```python
import jax
import jax.numpy as jnp
from jax import lax
from jax.experimental import pallas as pl
from jax.experimental.pallas import tpu as pltpu
from jax.sharding import PartitionSpec as P

NEU_BLOCK = 64
PIX_BLOCK = 256
K = 4
HB = 2
ITERS = 2
LANES = 128
RIM = HB * NEU_BLOCK // LANES
F32 = jnp.float32
BF16 = jnp.bfloat16
VMEM = pl.BlockSpec(memory_space=pltpu.VMEM)
SMEM = pl.BlockSpec(memory_space=pltpu.SMEM)


def padded8(rows):
    return -(-rows // 8) * 8


def table(frames, reverse):
    row = lax.broadcasted_iota(jnp.int32, (frames, 2 * frames), 0)
    col = lax.broadcasted_iota(jnp.int32, (frames, 2 * frames), 1)
    col = jnp.where(col >= frames, col - frames, col)
    keep = col >= row if reverse else col <= row
    return jnp.where(keep, 1.0, 0.0).astype(BF16)


def summed(sums_table, values):
    high = values.astype(BF16)
    low = (values - high.astype(F32)).astype(BF16)
    both = jnp.concatenate([high, low], axis=0)
    return jnp.dot(sums_table, both, preferred_element_type=F32)


def powers(log_decay, frames, mid, sign):
    groups = frames // 8
    coarse = (8 * lax.broadcasted_iota(jnp.int32, (groups, LANES), 0) - mid).astype(F32) * sign
    fine = lax.broadcasted_iota(jnp.int32, (8, LANES), 0).astype(F32) * sign
    coarse = jnp.exp(coarse * log_decay)
    fine = jnp.exp(fine * log_decay)
    return (coarse[:, None, :] * fine[None, :, :]).reshape(frames, LANES)


def chunk(field, c):
    own, rim = field
    inner = own.shape[0]
    if c < RIM:
        return rim.at[c]
    if c >= RIM + inner:
        return rim.at[c - inner]
    return own.at[c - RIM]


def chunk_count(field):
    return field[0].shape[0] + field[1].shape[0]


def prep_chunk(c, rate, field, gains, s3, p3, pinv3, z3, rows, pay):
    frames = field.shape[1]
    middle, prefix_col, inverse_col, sums_table = gains
    mid = frames // 2 - 1
    rate = jnp.where(rate > 0.0, rate, 1.0)
    log_rate = jnp.log(rate)
    gain = jnp.sqrt(1.0 - rate * rate)
    p = powers(log_rate, frames, mid, 1.0) * prefix_col
    pinv = powers(log_rate, frames, mid, -1.0) * inverse_col
    field = field.T
    z = summed(sums_table, field * gain * pinv)
    last = p[frames - 1 : frames, :]
    s3[...] = field
    p3[...] = p
    pinv3[...] = pinv
    z3[...] = z
    half = rate
    for _ in range(frames.bit_length() - 2):
        half = half * half
    rows[0, c : c + 1, :] = gain
    rows[1, c : c + 1, :] = half * middle
    rows[2, c : c + 1, :] = half * half
    pay[0, c : c + 1, :] = last * z[frames - 1 : frames, :]
    scale = last * gain
    pay[1, c : c + 1, :] = scale * scale * jnp.sum(pinv * pinv, axis=0, keepdims=True)


def gain_columns(gains):
    frames = gains.shape[1]
    mid = frames // 2 - 1
    lane = lax.broadcasted_iota(jnp.int32, (8, frames), 1)
    prefix = jnp.broadcast_to(gains[...], (8, frames))
    step = 1
    while step < frames:
        prefix = prefix * jnp.where(lane >= step, pltpu.roll(prefix, step, 1), 1.0)
        step *= 2
    middle = jnp.broadcast_to(prefix[0:1, mid : mid + 1], (8, frames))
    prefix_col = jnp.broadcast_to((prefix / middle)[0:1], (LANES, frames)).T
    inverse_col = jnp.broadcast_to((middle / prefix)[0:1], (LANES, frames)).T
    return middle[0:1, 0:1], prefix_col, inverse_col, table(frames, False)


def prep_own_kernel(spikes, decay, gains, s3, p3, pinv3, z3, rows, pay):
    own = s3.shape[0]
    chunks = own + 2 * RIM
    columns = gain_columns(gains)
    rows[...] = jnp.ones_like(rows)
    pay[...] = jnp.zeros_like(pay)
    pay[0, chunks : chunks + 1, :] = gains[...]
    for i in range(own):
        field = spikes[i * LANES : (i + 1) * LANES, :]
        at = [ref.at[i] for ref in (s3, p3, pinv3, z3)]
        prep_chunk(i + RIM, decay[i : i + 1, :], field, columns, *at, rows, pay)


def sides(even, first, second):
    return jnp.where(even, second, first), jnp.where(even, first, second)


def prep_rim_kernel(first, second, gains, rows_own, pay_own, s3, p3, pinv3, z3, rows, pay):
    rims = s3.shape[0]
    own = rows_own.shape[1] - padded8(1)
    columns = gain_columns(gains)
    rows[...] = rows_own[...]
    pay[...] = pay_own[...]
    even = lax.axis_index("tile") % 2 == 0
    below, above = sides(even, first[...], second[...])
    for i in range(rims):
        message = below if i < RIM else above
        j = i % RIM
        c = i if i < RIM else own + i
        at = [ref.at[i] for ref in (s3, p3, pinv3, z3)]
        field = message[j * LANES : (j + 1) * LANES, :]
        rate = message[RIM * LANES + j : RIM * LANES + j + 1, :]
        prep_chunk(c, rate, field, columns, *at, rows, pay)


def block_totals(pays, chunks, rows):
    totals = []
    for m in range(pays.shape[0]):
        gain = jnp.broadcast_to(pays[m, 0, chunks : chunks + 1, :], (8, LANES))
        step = 1
        while step < LANES:
            gain = gain * pltpu.roll(gain, step, 1)
            step *= 2
        totals.append(rows[2] * gain[0:1])
    return totals


def step_size(stats):
    both = jnp.sum(stats[...], axis=0)
    both = jnp.broadcast_to(both, (8, LANES))
    other = pltpu.roll(both, LANES // 2, 1)
    first = lax.broadcasted_iota(jnp.int32, (8, LANES), 1) < LANES // 2
    grad_sq = jnp.where(first, both, other)
    image_sq = jnp.where(first, other, both)
    return (grad_sq / (image_sq + 1e-06))[0:1]


def update_kernel(s3, g3, stats, p3, pinv3, rows, new3, z3, pay):
    chunks = chunk_count(s3)
    frames = g3.shape[1]
    sums_table = table(frames, False)
    size = step_size(stats)
    pay[...] = jnp.zeros_like(pay)
    for c in range(chunks):
        field = jnp.maximum(chunk(s3, c)[...] - size * g3[c], 0.0)
        z = summed(sums_table, field * rows[0, c : c + 1, :] * chunk(pinv3, c)[...])
        chunk(new3, c)[...] = field
        chunk(z3, c)[...] = z
        last = chunk(p3, c)[frames - 1 : frames, :]
        pay[c : c + 1, :] = last * z[frames - 1 : frames, :]


def final_kernel(s3, g3, stats, out):
    size = step_size(stats)
    for i in range(out.shape[0] // LANES):
        field = jnp.maximum(s3[i] - size * g3[i + RIM], 0.0)
        out[i * LANES : (i + 1) * LANES, :] = field.T


def picked(ext, pattern, q):
    parts = [
        ext[pl.ds(pl.multiple_of(pattern[q, k] * NEU_BLOCK, NEU_BLOCK), NEU_BLOCK), :]
        for k in range(K)
    ]
    return jnp.concatenate(parts, axis=0)


def foot_of(feet, q):
    return feet[q * PIX_BLOCK : (q + 1) * PIX_BLOCK, :]


def pull_back(pattern, ext, feet, record, contrib, place, start, stop):
    for q in range(start, stop):
        for v in range(2 * HB + 1):
            place[q, v] = -1
        for k in range(K):
            place[q, pattern[q, k] - q] = k
    for q in range(start, stop):
        foot = foot_of(feet, q)
        fitted = jnp.dot(foot, picked(ext, pattern, q), preferred_element_type=F32)
        residual = (fitted - foot_of(record, q).astype(F32)).astype(BF16)
        contrib[q * K * NEU_BLOCK : (q + 1) * K * NEU_BLOCK, :] = lax.dot_general(
            foot, residual, (((0,), (0,)), ((), ())), preferred_element_type=F32
        )


def gathered(contrib, place, c, ranges):
    frames = contrib.shape[1]
    per_chunk = LANES // NEU_BLOCK
    halves = []
    for b in range(c * per_chunk, (c + 1) * per_chunk):
        total = jnp.zeros((NEU_BLOCK, frames), F32)
        for v in range(2 * HB + 1):
            q = b - v
            if any(start <= q < stop for start, stop in ranges):
                k = place[q, v]
                at = pl.multiple_of((q * K + jnp.maximum(k, 0)) * NEU_BLOCK, NEU_BLOCK)
                value = contrib[pl.ds(at, NEU_BLOCK), :]
                if v % 2:
                    value = jnp.where(k >= 0, value, 0.0)
                total = total + value
        halves.append(total)
    return jnp.concatenate(halves, axis=0).T


def edge_kernel(
    pattern, z3, p3, rows, pay, pays, feet, record, ext, zones, spill, send_a, send_b, state, *scratch
):
    contrib, place = scratch
    chunks = chunk_count(z3)
    stripe = pattern.shape[0]
    edge = 2 * HB
    me = lax.axis_index("tm")
    totals = block_totals(pay, chunks, rows)
    carry = jnp.zeros_like(totals[0])
    for m in range(pays.shape[0]):
        carry = jnp.where(m < me, pays[m] + totals[m] * carry, carry)
    carry = carry * rows[1]
    state[...] = carry
    for c in range(chunks):
        field = chunk(p3, c)[...] * (chunk(z3, c)[...] + carry[c : c + 1, :])
        ext[c * LANES : (c + 1) * LANES, :] = field.T.astype(BF16)
    ranges = ((0, edge), (stripe - edge, stripe))
    for start, stop in ranges:
        pull_back(pattern, ext, feet, record, contrib, place, start, stop)
    even = lax.axis_index("tile") % 2 == 0
    for i in range(2 * RIM):
        below = gathered(contrib, place, i, ranges)
        above = gathered(contrib, place, chunks - 2 * RIM + i, ranges)
        zones[i] = below
        zones[2 * RIM + i] = above
        send_a[i] = jnp.where(even, above, below).astype(BF16)
        send_b[i] = jnp.where(even, below, above).astype(BF16)
        spill[i] = gathered(contrib, place, 2 * RIM + i, ranges)
        spill[2 * RIM + i] = gathered(contrib, place, chunks - 4 * RIM + i, ranges)


def adjoint_chunk(sums_table, field, p, pinv, rows, c, r3, pay):
    frames = field.shape[0]
    r = summed(sums_table, field * p)
    r3[...] = r
    gain = rows[0, c : c + 1, :]
    pay[0, c : c + 1, :] = rows[1, c : c + 1, :] * r[0:1, :]
    ends = p[frames - 1 : frames, :] * gain * gain
    pay[1, c : c + 1, :] = ends * jnp.sum(pinv * pinv * r, axis=0, keepdims=True)


def inner_kernel(pattern, p3, pinv3, rows, ext, spill, feet, record, r3, pay, *scratch):
    contrib, place = scratch
    chunks = chunk_count(p3)
    frames = spill.shape[1]
    stripe = pattern.shape[0]
    edge = 2 * HB
    pull_back(pattern, ext, feet, record, contrib, place, edge, stripe - edge)
    sums_table = table(frames, True)
    pay[...] = jnp.zeros_like(pay)
    inner = chunks - 4 * RIM
    for i in range(inner):
        c = i + 2 * RIM
        field = gathered(contrib, place, c, ((edge, stripe - edge),))
        if i < 2 * RIM:
            field = field + spill[i]
        if i >= inner - 2 * RIM:
            field = field + spill[i - inner + 4 * RIM]
        p, pinv = chunk(p3, c)[...], chunk(pinv3, c)[...]
        adjoint_chunk(sums_table, field, p, pinv, rows, c, r3.at[i], pay)


def border_kernel(zones, got_a, got_b, p3, pinv3, rows, pay_inner, r3, pay):
    chunks = chunk_count(p3)
    frames = zones.shape[1]
    sums_table = table(frames, True)
    pay[...] = pay_inner[...]
    even = lax.axis_index("tile") % 2 == 0
    for i in range(2 * RIM):
        both = sides(even, got_a[i].astype(F32), got_b[i].astype(F32))
        for side, c in ((0, i), (1, chunks - 2 * RIM + i)):
            at = side * 2 * RIM + i
            field = zones[at] + both[side]
            p, pinv = chunk(p3, c)[...], chunk(pinv3, c)[...]
            adjoint_chunk(sums_table, field, p, pinv, rows, c, r3.at[at], pay)


def direction_kernel(
    pattern, r_inner, r_border, p3, pinv3, rows, pay, pays, feet, g3, stats, ext
):
    chunks, frames = g3.shape[0], g3.shape[1]
    own = chunks - 2 * RIM
    stripe = pattern.shape[0]
    me = lax.axis_index("tm")
    totals = block_totals(pay, chunks, rows)
    blocks = pays.shape[0]
    entering = [None] * blocks
    state = jnp.zeros_like(totals[0])
    for m in reversed(range(blocks)):
        entering[m] = state
        state = pays[m, 0] + totals[m] * state
    carry = jnp.zeros_like(totals[0])
    adjoint = jnp.zeros_like(totals[0])
    for m in range(blocks):
        end = pays[m, 1] + pay[m, 1] * entering[m]
        carry = jnp.where(m < me, end + totals[m] * carry, carry)
        adjoint = jnp.where(m == me, entering[m], adjoint)
    carry = carry * rows[1]
    sums_table = table(frames, False)
    grad_sq = jnp.zeros((8, LANES), F32)
    for c in range(chunks):
        p, pinv = chunk(p3, c)[...], chunk(pinv3, c)[...]
        if c < 2 * RIM:
            r = r_border[c]
        elif c >= chunks - 2 * RIM:
            r = r_border[c - chunks + 4 * RIM]
        else:
            r = r_inner[c - 2 * RIM]
        gain = rows[0, c : c + 1, :]
        gradient = gain * pinv * (r + p[frames - 1 : frames, :] * adjoint[c : c + 1, :])
        g3[c] = gradient
        if RIM <= c < RIM + own:
            grad_sq += jnp.sum((gradient * gradient).reshape(frames // 8, 8, LANES), axis=0)
        z = summed(sums_table, gain * gradient * pinv)
        field = (p * (z + carry[c : c + 1, :])).T
        ext[c * LANES : (c + 1) * LANES, :] = field.astype(BF16)
    image_sq = jnp.zeros((8, frames), F32)
    for q in range(stripe):
        image = jnp.dot(foot_of(feet, q), picked(ext, pattern, q), preferred_element_type=F32)
        image_sq += jnp.sum((image * image).reshape(PIX_BLOCK // 8, 8, frames), axis=0)
    first = lax.broadcasted_iota(jnp.int32, (1, LANES), 1) < LANES // 2
    both = jnp.where(first, jnp.sum(grad_sq), jnp.sum(image_sq))
    stats[...] = jnp.broadcast_to(both[None], stats.shape)


def traces_kernel(z3, p3, state, traces):
    for i in range(z3.shape[0]):
        c = i + RIM
        field = p3[i] * (z3[i] + state[c : c + 1, :])
        traces[i * LANES : (i + 1) * LANES, :] = field.T


def f32(*shape):
    return jax.ShapeDtypeStruct(shape, F32)


def bf16(*shape):
    return jax.ShapeDtypeStruct(shape, BF16)


def call(kernel, name, micros, outs, args, scratch=()):
    specs = [SMEM if arg.dtype == jnp.int32 else VMEM for arg in jax.tree.leaves(args)]
    in_specs = jax.tree.unflatten(jax.tree.structure(args), specs)
    return pl.pallas_call(
        kernel,
        name=name,
        out_shape=outs,
        in_specs=in_specs,
        out_specs=jax.tree.map(lambda _: VMEM, outs),
        scratch_shapes=scratch,
        compiler_params=pltpu.CompilerParams(vmem_limit_bytes=16 * 2**20),
        cost_estimate=pl.CostEstimate(
            flops=int(micros * 1e8), bytes_accessed=int(micros * 3e6), transcendentals=0
        ),
    )(*args)


def swapped(first, second):
    size = lax.axis_size("tile")

    def pairs(start):
        both = [(i, i + 1) for i in range(start, size - 1, 2)]
        return both + [(j, i) for i, j in both]

    return lax.ppermute(first, "tile", pairs(0)), lax.ppermute(second, "tile", pairs(1))


def per_device(recording, footprints, pattern, decay, frame_gain, spikes):
    neurons, frames = spikes.shape
    stripe = pattern.shape[0]
    own = neurons // LANES
    chunks = own + 2 * RIM
    lines = own + padded8(1)
    devices = lax.axis_size("tile") * lax.axis_size("tm")
    split = (f32(own, frames, LANES), f32(2 * RIM, frames, LANES))
    rates = decay.reshape(own, LANES)
    gains = frame_gain.reshape(1, frames)
    even = lax.axis_index("tile") % 2 == 0

    def rim_message(above):
        at = jnp.where(above, own - RIM, 0)
        return jnp.concatenate(
            [
                lax.dynamic_slice(spikes, (at * LANES, 0), (RIM * LANES, frames)),
                lax.dynamic_slice(rates, (at, 0), (RIM, LANES)),
            ],
            axis=0,
        )

    first, second = swapped(rim_message(even), rim_message(jnp.logical_not(even)))
    *owns, rows, pay = call(
        prep_own_kernel,
        "prep_own",
        1.6,
        (split[0],) * 4 + (f32(3, lines, LANES), f32(2, lines, LANES)),
        (spikes, rates, gains),
    )
    *rims, rows, pay = call(
        prep_rim_kernel,
        "prep_rim",
        0.3,
        (split[1],) * 4 + (f32(3, lines, LANES), f32(2, lines, LANES)),
        (first, second, gains, rows, pay),
    )
    s3, p3, pinv3, z3 = zip(owns, rims)
    constants = lax.all_gather(pay, "tm")
    pays = constants[:, 0]
    scratch = [
        pltpu.VMEM((stripe * K * NEU_BLOCK, frames), F32),
        pltpu.SMEM((stripe, 2 * HB + 1), jnp.int32),
    ]
    zone = (2 * RIM, frames, LANES)
    border = (4 * RIM, frames, LANES)
    for iteration in range(ITERS):
        ext, zones, spill, send_a, send_b, state = call(
            edge_kernel,
            "edge",
            2.5,
            (
                bf16(chunks * LANES, frames),
                f32(*border),
                f32(*border),
                bf16(*zone),
                bf16(*zone),
                f32(lines, LANES),
            ),
            (pattern, z3, p3, rows, constants, pays, footprints, recording),
            scratch,
        )
        got_a, got_b = swapped(send_a, send_b)
        r_inner, pay = call(
            inner_kernel,
            "inner",
            4.0,
            (f32(chunks - 4 * RIM, frames, LANES), f32(2, lines, LANES)),
            (pattern, p3, pinv3, rows, ext, spill, footprints, recording),
            scratch,
        )
        r_border, pay = call(
            border_kernel,
            "border",
            0.3,
            (f32(*border), f32(2, lines, LANES)),
            (zones, got_a, got_b, p3, pinv3, rows, pay),
        )
        pays = lax.all_gather(pay, "tm")
        g3, stats = call(
            direction_kernel,
            "direction",
            4.0,
            (f32(chunks, frames, LANES), f32(devices, 1, LANES)),
            (pattern, r_inner, r_border, p3, pinv3, rows, constants, pays, footprints),
            [pltpu.VMEM((chunks * LANES, frames), BF16)],
        )
        stats = lax.all_to_all(stats, ("tile", "tm"), 0, 0)
        if iteration == ITERS - 1:
            traces = call(
                traces_kernel, "traces", 1.4, f32(neurons, frames), (z3[0], p3[0], state)
            )
            out = call(final_kernel, "final", 1.4, f32(neurons, frames), (s3[0], g3, stats))
            return out, traces
        s3, z3, pay = call(
            update_kernel,
            "update",
            0.6,
            (split, split, f32(lines, LANES)),
            (s3, g3, stats, p3, pinv3, rows),
        )
        pays = lax.all_gather(pay, "tm")


def solution(mesh):
    return jax.shard_map(
        per_device,
        mesh=mesh,
        in_specs=(
            P("tile", "tm"),
            P("tile", None),
            P("tile", None),
            P("tile"),
            P("tm"),
            P("tile", "tm"),
        ),
        out_specs=(P("tile", "tm"), P("tile", "tm")),
        check_vma=False,
    )
```

```python
import jax
import jax.numpy as jnp
from jax import lax
from jax.experimental import pallas as pl
from jax.experimental.pallas import tpu as pltpu
from jax.sharding import PartitionSpec as P

NEU_BLOCK = 64
PIX_BLOCK = 256
PARTS = 4
K = 4
HB = 2
ITERS = 2
LANES = 128
RIM = HB * NEU_BLOCK // LANES
F32 = jnp.float32
BF16 = jnp.bfloat16
VMEM = pl.BlockSpec(memory_space=pltpu.VMEM)
HBM = pl.BlockSpec(memory_space=pltpu.HBM)
SMEM = pl.BlockSpec(memory_space=pltpu.SMEM)


def padded8(rows):
    return -(-rows // 8) * 8


def table(frames, reverse):
    row = lax.broadcasted_iota(jnp.int32, (frames, 2 * frames), 0)
    col = lax.broadcasted_iota(jnp.int32, (frames, 2 * frames), 1)
    col = jnp.where(col >= frames, col - frames, col)
    keep = col >= row if reverse else col <= row
    return jnp.where(keep, 1.0, 0.0).astype(BF16)


def summed(sums_table, values):
    high = values.astype(BF16)
    low = (values - high.astype(F32)).astype(BF16)
    both = jnp.concatenate([high, low], axis=0)
    return jnp.dot(sums_table, both, preferred_element_type=F32)


def powers(log_decay, frames, mid, sign):
    groups = frames // 8
    coarse = (8 * lax.broadcasted_iota(jnp.int32, (groups, LANES), 0) - mid).astype(F32) * sign
    fine = lax.broadcasted_iota(jnp.int32, (8, LANES), 0).astype(F32) * sign
    coarse = jnp.exp(coarse * log_decay)
    fine = jnp.exp(fine * log_decay)
    return (coarse[:, None, :] * fine[None, :, :]).reshape(frames, LANES)


def chunk(field, c):
    own, rim = field
    inner = own.shape[0]
    if c < RIM:
        return rim.at[c]
    if c >= RIM + inner:
        return rim.at[c - inner]
    return own.at[c - RIM]


def chunk_count(field):
    return field[0].shape[0] + field[1].shape[0]


def prep_chunk(c, rate, field, gains, s3, p3, pinv3, z3, rows, pay):
    frames = field.shape[1]
    middle, prefix_col, inverse_col, sums_table = gains
    mid = frames // 2 - 1
    rate = jnp.where(rate > 0.0, rate, 1.0)
    log_rate = jnp.log(rate)
    gain = jnp.sqrt(1.0 - rate * rate)
    p = powers(log_rate, frames, mid, 1.0) * prefix_col
    pinv = powers(log_rate, frames, mid, -1.0) * inverse_col
    field = field.T
    z = summed(sums_table, field * gain * pinv)
    last = p[frames - 1 : frames, :]
    s3[...] = field
    p3[...] = p
    pinv3[...] = pinv
    z3[...] = z
    half = rate
    for _ in range(frames.bit_length() - 2):
        half = half * half
    rows[0, c : c + 1, :] = gain
    rows[1, c : c + 1, :] = half * middle
    rows[2, c : c + 1, :] = half * half
    pay[0, c : c + 1, :] = last * z[frames - 1 : frames, :]
    scale = last * gain
    pay[1, c : c + 1, :] = scale * scale * jnp.sum(pinv * pinv, axis=0, keepdims=True)


def gain_columns(gains):
    frames = gains.shape[1]
    mid = frames // 2 - 1
    lane = lax.broadcasted_iota(jnp.int32, (8, frames), 1)
    prefix = jnp.broadcast_to(gains, (8, frames))
    step = 1
    while step < frames:
        prefix = prefix * jnp.where(lane >= step, pltpu.roll(prefix, step, 1), 1.0)
        step *= 2
    middle = jnp.broadcast_to(prefix[0:1, mid : mid + 1], (1, LANES))
    whole = jnp.broadcast_to(prefix[0:1, frames - 1 : frames], (1, LANES))
    prefix_col = jnp.broadcast_to(prefix[0:1] / middle, (LANES, frames)).T
    inverse_col = jnp.broadcast_to(middle / prefix[0:1], (LANES, frames)).T
    return middle, whole, prefix_col, inverse_col


def rims_kernel(spikes, decay, gains, first, second, rates_here, gains_here, sems):
    edge = RIM * LANES
    neurons = spikes.shape[0]
    own = decay.shape[0]
    even = lax.axis_index("tile") % 2 == 0
    top = jnp.where(even, neurons - edge, 0)
    bottom = jnp.where(even, 0, neurons - edge)
    copies = [
        pltpu.make_async_copy(decay, rates_here, sems.at[0]),
        pltpu.make_async_copy(gains, gains_here, sems.at[1]),
        pltpu.make_async_copy(
            spikes.at[pl.ds(pl.multiple_of(top, LANES), edge)], first.at[pl.ds(0, edge)], sems.at[2]
        ),
        pltpu.make_async_copy(
            spikes.at[pl.ds(pl.multiple_of(bottom, LANES), edge)],
            second.at[pl.ds(0, edge)],
            sems.at[3],
        ),
    ]
    for copy in copies:
        copy.start()
    first[edge:, :] = jnp.zeros_like(first[edge:, :])
    second[edge:, :] = jnp.zeros_like(second[edge:, :])
    copies[0].wait()
    lower, upper = rates_here[0:RIM, :], rates_here[own - RIM : own, :]
    first[edge : edge + RIM, :] = jnp.where(even, upper, lower)
    second[edge : edge + RIM, :] = jnp.where(even, lower, upper)
    for copy in copies[1:]:
        copy.wait()


def prep_own_kernel(
    spikes, decay, gains, s3, p3, pinv3, z3, rows, pay, columns, spikes_here, sems
):
    own = s3.shape[0]
    chunks = own + 2 * RIM
    size = spikes.shape[0] // PARTS
    copies = [
        pltpu.make_async_copy(
            spikes.at[pl.ds(i * size, size)], spikes_here.at[pl.ds(i * size, size)], sems.at[i]
        )
        for i in range(PARTS)
    ]
    for copy in copies:
        copy.start()
    middle, whole, prefix_col, inverse_col = gain_columns(gains[...])
    columns[0] = prefix_col
    columns[1] = inverse_col
    rows[...] = jnp.ones_like(rows)
    rows[0, chunks : chunks + 1, :] = middle
    pay[...] = jnp.zeros_like(pay)
    pay[0, chunks : chunks + 1, :] = whole
    shared = middle, prefix_col, inverse_col, table(spikes.shape[1], False)
    for i in range(own):
        if i % (own // PARTS) == 0:
            copies[i // (own // PARTS)].wait()
        field = spikes_here[i * LANES : (i + 1) * LANES, :]
        at = [ref.at[i] for ref in (s3, p3, pinv3, z3)]
        prep_chunk(i + RIM, decay[i : i + 1, :], field, shared, *at, rows, pay)


def sides(even, first, second):
    return jnp.where(even, second, first), jnp.where(even, first, second)


def prep_rim_kernel(first, second, columns, rows_own, pay_own, s3, p3, pinv3, z3, rows, pay):
    rims, frames = s3.shape[0], s3.shape[1]
    own = rows_own.shape[1] - padded8(1)
    chunks = own + 2 * RIM
    middle = rows_own[0, chunks : chunks + 1, :]
    shared = middle, columns[0], columns[1], table(frames, False)
    rows[...] = rows_own[...]
    pay[...] = pay_own[...]
    even = lax.axis_index("tile") % 2 == 0
    below, above = sides(even, first[...], second[...])
    for i in range(rims):
        message = below if i < RIM else above
        j = i % RIM
        c = i if i < RIM else own + i
        at = [ref.at[i] for ref in (s3, p3, pinv3, z3)]
        field = message[j * LANES : (j + 1) * LANES, :]
        rate = message[RIM * LANES + j : RIM * LANES + j + 1, :]
        prep_chunk(c, rate, field, shared, *at, rows, pay)


def block_totals(pays, chunks, rows):
    return [rows[2] * pays[m, 0, chunks : chunks + 1, :] for m in range(pays.shape[0])]


def step_size(stats):
    both = jnp.sum(jnp.sum(stats[...], axis=0), axis=1, keepdims=True)
    return jnp.broadcast_to(both[0:1] / (both[1:2] + 1e-06), (1, LANES))


def update_kernel(s3, g3, stats, p3, pinv3, rows, new3, z3, pay):
    chunks = chunk_count(s3)
    frames = g3.shape[1]
    sums_table = table(frames, False)
    size = step_size(stats)
    pay[...] = jnp.zeros_like(pay)
    for c in range(chunks):
        field = jnp.maximum(chunk(s3, c)[...] - size * g3[c], 0.0)
        z = summed(sums_table, field * rows[0, c : c + 1, :] * chunk(pinv3, c)[...])
        if len(new3) == 2:
            chunk(new3, c)[...] = field
        elif RIM <= c < chunks - RIM:
            new3[0][c - RIM] = field
        chunk(z3, c)[...] = z
        last = chunk(p3, c)[frames - 1 : frames, :]
        pay[c : c + 1, :] = last * z[frames - 1 : frames, :]


def final_kernel(s3, g3, stats, out, here, sems):
    size = step_size(stats)
    own = s3.shape[0]
    rows = out.shape[0] // PARTS
    copies = [
        pltpu.make_async_copy(
            here.at[pl.ds(i * rows, rows)], out.at[pl.ds(i * rows, rows)], sems.at[i]
        )
        for i in range(PARTS)
    ]
    for i in range(own):
        field = jnp.maximum(s3[i] - size * g3[i + RIM], 0.0)
        here[i * LANES : (i + 1) * LANES, :] = field.T
        if (i + 1) % (own // PARTS) == 0:
            copies[i // (own // PARTS)].start()
    for copy in copies:
        copy.wait()


def picked(ext, pattern, q):
    parts = [
        ext[pl.ds(pl.multiple_of(pattern[k, q] * NEU_BLOCK, NEU_BLOCK), NEU_BLOCK), :]
        for k in range(K)
    ]
    return jnp.concatenate(parts, axis=0)


def foot_of(feet, q):
    return feet[q * PIX_BLOCK : (q + 1) * PIX_BLOCK, :]


def pull_back(pattern, ext, feet, record, contrib, place, start, stop):
    for q in range(start, stop):
        for v in range(2 * HB + 1):
            place[q, v] = -1
        for k in range(K):
            place[q, pattern[k, q] - q] = k
    for q in range(start, stop):
        foot = foot_of(feet, q)
        fitted = jnp.dot(foot, picked(ext, pattern, q), preferred_element_type=F32)
        residual = (fitted - foot_of(record, q).astype(F32)).astype(BF16)
        contrib[q * K * NEU_BLOCK : (q + 1) * K * NEU_BLOCK, :] = lax.dot_general(
            foot, residual, (((0,), (0,)), ((), ())), preferred_element_type=F32
        )


def gathered(contrib, place, c, ranges):
    frames = contrib.shape[1]
    per_chunk = LANES // NEU_BLOCK
    halves = []
    for b in range(c * per_chunk, (c + 1) * per_chunk):
        total = jnp.zeros((NEU_BLOCK, frames), F32)
        for v in range(2 * HB + 1):
            q = b - v
            if any(start <= q < stop for start, stop in ranges):
                k = place[q, v]
                at = pl.multiple_of((q * K + jnp.maximum(k, 0)) * NEU_BLOCK, NEU_BLOCK)
                value = contrib[pl.ds(at, NEU_BLOCK), :]
                if v % 2:
                    value = jnp.where(k >= 0, value, 0.0)
                total = total + value
        halves.append(total)
    return jnp.concatenate(halves, axis=0).T


def edge_kernel(
    pattern, z3, p3, rows, pay, pays, feet, record, ext, zones, spill, send_a, send_b, state, *scratch
):
    contrib, place, *fetched = scratch
    chunks = chunk_count(z3)
    stripe = pattern.shape[1]
    edge = 2 * HB
    copies = []
    if fetched:
        feet_here, sems = fetched
        for i, start in enumerate((0, stripe - edge)):
            at = pl.ds(start * PIX_BLOCK, edge * PIX_BLOCK)
            copies.append(pltpu.make_async_copy(feet.at[at], feet_here.at[at], sems.at[i]))
            copies[-1].start()
        feet = feet_here
    me = lax.axis_index("tm")
    totals = block_totals(pay, chunks, rows)
    carry = jnp.zeros_like(totals[0])
    for m in range(pays.shape[0]):
        carry = jnp.where(m < me, pays[m] + totals[m] * carry, carry)
    carry = carry * rows[1]
    state[...] = carry
    for c in range(chunks):
        field = chunk(p3, c)[...] * (chunk(z3, c)[...] + carry[c : c + 1, :])
        ext[c * LANES : (c + 1) * LANES, :] = field.T.astype(BF16)
    ranges = ((0, edge), (stripe - edge, stripe))
    for i, (start, stop) in enumerate(ranges):
        if copies:
            copies[i].wait()
        pull_back(pattern, ext, feet, record, contrib, place, start, stop)
    even = lax.axis_index("tile") % 2 == 0
    for i in range(2 * RIM):
        below = gathered(contrib, place, i, ranges)
        above = gathered(contrib, place, chunks - 2 * RIM + i, ranges)
        zones[i] = below
        zones[2 * RIM + i] = above
        send_a[i] = jnp.where(even, above, below).astype(BF16)
        send_b[i] = jnp.where(even, below, above).astype(BF16)
        spill[i] = gathered(contrib, place, 2 * RIM + i, ranges)
        spill[2 * RIM + i] = gathered(contrib, place, chunks - 4 * RIM + i, ranges)


def adjoint_chunk(sums_table, field, p, pinv, rows, c, r3, pay):
    frames = field.shape[0]
    r = summed(sums_table, field * p)
    r3[...] = r
    gain = rows[0, c : c + 1, :]
    pay[0, c : c + 1, :] = rows[1, c : c + 1, :] * r[0:1, :]
    ends = p[frames - 1 : frames, :] * gain * gain
    pay[1, c : c + 1, :] = ends * jnp.sum(pinv * pinv * r, axis=0, keepdims=True)


def inner_kernel(pattern, p3, pinv3, rows, ext, spill, feet, record, r3, pay, *scratch):
    contrib, place = scratch
    chunks = chunk_count(p3)
    frames = spill.shape[1]
    stripe = pattern.shape[1]
    edge = 2 * HB
    pull_back(pattern, ext, feet, record, contrib, place, edge, stripe - edge)
    sums_table = table(frames, True)
    pay[...] = jnp.zeros_like(pay)
    inner = chunks - 4 * RIM
    for i in range(inner):
        c = i + 2 * RIM
        field = gathered(contrib, place, c, ((edge, stripe - edge),))
        if i < 2 * RIM:
            field = field + spill[i]
        if i >= inner - 2 * RIM:
            field = field + spill[i - inner + 4 * RIM]
        p, pinv = chunk(p3, c)[...], chunk(pinv3, c)[...]
        adjoint_chunk(sums_table, field, p, pinv, rows, c, r3.at[i], pay)


def border_kernel(zones, got_a, got_b, p3, pinv3, rows, pay_inner, r3, pay):
    chunks = chunk_count(p3)
    frames = zones.shape[1]
    sums_table = table(frames, True)
    pay[...] = pay_inner[...]
    even = lax.axis_index("tile") % 2 == 0
    for i in range(2 * RIM):
        both = sides(even, got_a[i].astype(F32), got_b[i].astype(F32))
        for side, c in ((0, i), (1, chunks - 2 * RIM + i)):
            at = side * 2 * RIM + i
            field = zones[at] + both[side]
            p, pinv = chunk(p3, c)[...], chunk(pinv3, c)[...]
            adjoint_chunk(sums_table, field, p, pinv, rows, c, r3.at[at], pay)


def direction_kernel(
    pattern, r_inner, r_border, p3, pinv3, rows, pay, pays, feet, g3, stats, ext
):
    chunks, frames = g3.shape[0], g3.shape[1]
    own = chunks - 2 * RIM
    stripe = pattern.shape[1]
    me = lax.axis_index("tm")
    totals = block_totals(pay, chunks, rows)
    blocks = pays.shape[0]
    entering = [None] * blocks
    state = jnp.zeros_like(totals[0])
    for m in reversed(range(blocks)):
        entering[m] = state
        state = pays[m, 0] + totals[m] * state
    carry = jnp.zeros_like(totals[0])
    adjoint = jnp.zeros_like(totals[0])
    for m in range(blocks):
        end = pays[m, 1] + pay[m, 1] * entering[m]
        carry = jnp.where(m < me, end + totals[m] * carry, carry)
        adjoint = jnp.where(m == me, entering[m], adjoint)
    carry = carry * rows[1]
    sums_table = table(frames, False)
    grad_sq = jnp.zeros((8, LANES), F32)
    for c in range(chunks):
        p, pinv = chunk(p3, c)[...], chunk(pinv3, c)[...]
        if c < 2 * RIM:
            r = r_border[c]
        elif c >= chunks - 2 * RIM:
            r = r_border[c - chunks + 4 * RIM]
        else:
            r = r_inner[c - 2 * RIM]
        gain = rows[0, c : c + 1, :]
        gradient = gain * pinv * (r + p[frames - 1 : frames, :] * adjoint[c : c + 1, :])
        g3[c] = gradient
        if RIM <= c < RIM + own:
            grad_sq += jnp.sum((gradient * gradient).reshape(frames // 8, 8, LANES), axis=0)
        z = summed(sums_table, gain * gradient * pinv)
        field = (p * (z + carry[c : c + 1, :])).T
        ext[c * LANES : (c + 1) * LANES, :] = field.astype(BF16)
    image_sq = jnp.zeros((8, frames), F32)
    for q in range(stripe):
        image = jnp.dot(foot_of(feet, q), picked(ext, pattern, q), preferred_element_type=F32)
        image_sq += jnp.sum((image * image).reshape(PIX_BLOCK // 8, 8, frames), axis=0)
    both = jnp.concatenate(
        [
            jnp.sum(grad_sq, axis=0, keepdims=True),
            jnp.sum(image_sq, axis=0, keepdims=True),
        ],
        axis=0,
    )
    stats[...] = jnp.broadcast_to(both[None], stats.shape)


def traces_kernel(z3, p3, state, traces):
    for i in range(z3.shape[0]):
        c = i + RIM
        field = p3[i] * (z3[i] + state[c : c + 1, :])
        traces[i * LANES : (i + 1) * LANES, :] = field.T


def f32(*shape):
    return jax.ShapeDtypeStruct(shape, F32)


def bf16(*shape):
    return jax.ShapeDtypeStruct(shape, BF16)


def call(kernel, name, micros, outs, args, scratch=(), far=(), far_out=False, keep=()):
    def spec(place, arg):
        if place in far:
            return HBM
        return SMEM if arg.dtype == jnp.int32 else VMEM

    in_specs = [jax.tree.map(lambda x: spec(i, x), arg) for i, arg in enumerate(args)]
    in_specs.append(jax.tree.map(lambda _: VMEM, keep))

    def body(*refs):
        kernel(*refs[: len(args)], *refs[len(args) + 1 :])

    return pl.pallas_call(
        body,
        name=name,
        out_shape=outs,
        in_specs=in_specs,
        out_specs=jax.tree.map(lambda _: HBM if far_out else VMEM, outs),
        scratch_shapes=scratch,
        compiler_params=pltpu.CompilerParams(vmem_limit_bytes=16 * 2**20),
        cost_estimate=pl.CostEstimate(
            flops=int(micros * 1e8), bytes_accessed=int(micros * 3e6), transcendentals=0
        ),
    )(*args, keep)


def swapped(first, second):
    size = lax.axis_size("tile")

    def pairs(start):
        both = [(i, i + 1) for i in range(start, size - 1, 2)]
        return both + [(j, i) for i, j in both]

    return lax.ppermute(first, "tile", pairs(0)), lax.ppermute(second, "tile", pairs(1))


def per_device(recording, footprints, pattern, decay, frame_gain, spikes):
    neurons, frames = spikes.shape
    pixels = recording.shape[0]
    stripe = pattern.shape[0]
    pattern = pattern.T
    own = neurons // LANES
    chunks = own + 2 * RIM
    lines = own + padded8(1)
    devices = lax.axis_size("tile") * lax.axis_size("tm")
    split = (f32(own, frames, LANES), f32(2 * RIM, frames, LANES))
    message = f32(RIM * LANES + padded8(RIM), frames)
    first, second, rates, gains = call(
        rims_kernel,
        "rims",
        1.0,
        (message, message, f32(own, LANES), f32(1, frames)),
        (spikes, decay.reshape(own, LANES), frame_gain.reshape(1, frames)),
        [pltpu.SemaphoreType.DMA((4,))],
        far=(0, 1, 2),
    )
    first, second = swapped(first, second)
    *owns, rows, pay, columns = call(
        prep_own_kernel,
        "prep_own",
        1.6,
        (split[0],) * 4
        + (f32(3, lines, LANES), f32(2, lines, LANES), f32(2, frames, LANES)),
        (spikes, rates, gains),
        [pltpu.VMEM((neurons, frames), F32), pltpu.SemaphoreType.DMA((PARTS,))],
        far=(0,),
    )
    *rims, rows, pay = call(
        prep_rim_kernel,
        "prep_rim",
        0.3,
        (split[1],) * 4 + (f32(3, lines, LANES), f32(2, lines, LANES)),
        (first, second, columns, rows, pay),
    )
    s3, p3, pinv3, z3 = zip(owns, rims)
    constants = lax.all_gather(pay, "tm")
    pays = constants[:, 0]
    scratch = [
        pltpu.VMEM((stripe * K * NEU_BLOCK, frames), F32),
        pltpu.SMEM((stripe, 2 * HB + 1), jnp.int32),
    ]
    fetched = [pltpu.VMEM((pixels, K * NEU_BLOCK), BF16), pltpu.SemaphoreType.DMA((2,))]
    zone = (2 * RIM, frames, LANES)
    border = (4 * RIM, frames, LANES)
    for iteration in range(ITERS):
        begins, ends = iteration == 0, iteration == ITERS - 1
        ext, zones, spill, send_a, send_b, state = call(
            edge_kernel,
            "edge",
            2.5,
            (
                bf16(chunks * LANES, frames),
                f32(*border),
                f32(*border),
                bf16(*zone),
                bf16(*zone),
                f32(lines, LANES),
            ),
            (pattern, z3, p3, rows, constants, pays, footprints, recording),
            scratch + (fetched if begins else []),
            far=(6,) if begins else (),
            keep=(s3[0],) if ends else (),
        )
        got_a, got_b = swapped(send_a, send_b)
        held = (s3[0], z3[0], state) if ends else ()
        r_inner, pay = call(
            inner_kernel,
            "inner",
            4.0,
            (f32(chunks - 4 * RIM, frames, LANES), f32(2, lines, LANES)),
            (pattern, p3, pinv3, rows, ext, spill, footprints, recording),
            scratch,
            keep=held,
        )
        r_border, pay = call(
            border_kernel,
            "border",
            0.3,
            (f32(*border), f32(2, lines, LANES)),
            (zones, got_a, got_b, p3, pinv3, rows, pay),
            keep=held,
        )
        pays = lax.all_gather(pay, "tm")
        g3, stats = call(
            direction_kernel,
            "direction",
            4.0,
            (f32(chunks, frames, LANES), f32(devices, 2, LANES)),
            (pattern, r_inner, r_border, p3, pinv3, rows, constants, pays, footprints),
            [pltpu.VMEM((chunks * LANES, frames), BF16)],
            keep=held,
        )
        stats = lax.all_to_all(stats, ("tile", "tm"), 0, 0)
        if ends:
            traces = call(
                traces_kernel,
                "traces",
                1.4,
                f32(neurons, frames),
                (z3[0], p3[0], state),
                keep=(s3[0],),
            )
            out = call(
                final_kernel,
                "final",
                1.4,
                f32(neurons, frames),
                (s3[0], g3, stats),
                [pltpu.VMEM((neurons, frames), F32), pltpu.SemaphoreType.DMA((PARTS,))],
                far_out=True,
            )
            return out, traces
        s3, z3, pay = call(
            update_kernel,
            "update",
            0.6,
            (split if iteration < ITERS - 2 else split[:1], split, f32(lines, LANES)),
            (s3, g3, stats, p3, pinv3, rows),
        )
        pays = lax.all_gather(pay, "tm")


def solution(mesh):
    return jax.shard_map(
        per_device,
        mesh=mesh,
        in_specs=(
            P("tile", "tm"),
            P("tile", None),
            P("tile", None),
            P("tile"),
            P("tm"),
            P("tile", "tm"),
        ),
        out_specs=(P("tile", "tm"), P("tile", "tm")),
        check_vma=False,
    )
```

```python
import jax
import jax.numpy as jnp
from jax import lax
from jax.experimental import pallas as pl
from jax.experimental.pallas import tpu as pltpu
from jax.sharding import PartitionSpec as P

NEU_BLOCK = 64
PIX_BLOCK = 256
PARTS = 4
K = 4
HB = 2
ITERS = 2
LANES = 128
RIM = HB * NEU_BLOCK // LANES
F32 = jnp.float32
BF16 = jnp.bfloat16
VMEM = pl.BlockSpec(memory_space=pltpu.VMEM)
HBM = pl.BlockSpec(memory_space=pltpu.HBM)
SMEM = pl.BlockSpec(memory_space=pltpu.SMEM)


def padded8(rows):
    return -(-rows // 8) * 8


def table(frames, reverse):
    row = lax.broadcasted_iota(jnp.int32, (frames, 2 * frames), 0)
    col = lax.broadcasted_iota(jnp.int32, (frames, 2 * frames), 1)
    col = jnp.where(col >= frames, col - frames, col)
    keep = col >= row if reverse else col <= row
    return jnp.where(keep, 1.0, 0.0).astype(BF16)


def summed(sums_table, values):
    high = values.astype(BF16)
    low = (values - high.astype(F32)).astype(BF16)
    both = jnp.concatenate([high, low], axis=0)
    return jnp.dot(sums_table, both, preferred_element_type=F32)


def powers(log_decay, frames, mid, sign):
    groups = frames // 8
    coarse = (8 * lax.broadcasted_iota(jnp.int32, (groups, LANES), 0) - mid).astype(F32) * sign
    fine = lax.broadcasted_iota(jnp.int32, (8, LANES), 0).astype(F32) * sign
    coarse = jnp.exp(coarse * log_decay)
    fine = jnp.exp(fine * log_decay)
    return (coarse[:, None, :] * fine[None, :, :]).reshape(frames, LANES)


def chunk(field, c):
    own, rim = field
    inner = own.shape[0]
    if c < RIM:
        return rim.at[c]
    if c >= RIM + inner:
        return rim.at[c - inner]
    return own.at[c - RIM]


def chunk_count(field):
    return field[0].shape[0] + field[1].shape[0]


def prep_chunk(c, rate, field, gains, s3, p3, pinv3, z3, rows, pay):
    frames = field.shape[1]
    middle, prefix_col, inverse_col, sums_table = gains
    mid = frames // 2 - 1
    rate = jnp.where(rate > 0.0, rate, 1.0)
    log_rate = jnp.log(rate)
    gain = jnp.sqrt(1.0 - rate * rate)
    p = powers(log_rate, frames, mid, 1.0) * prefix_col
    pinv = powers(log_rate, frames, mid, -1.0) * inverse_col
    field = field.T
    z = summed(sums_table, field * gain * pinv)
    last = p[frames - 1 : frames, :]
    s3[...] = field
    p3[...] = p
    pinv3[...] = pinv
    z3[...] = z
    half = rate
    for _ in range(frames.bit_length() - 2):
        half = half * half
    rows[0, c : c + 1, :] = gain
    rows[1, c : c + 1, :] = half * middle
    rows[2, c : c + 1, :] = half * half
    pay[0, c : c + 1, :] = last * z[frames - 1 : frames, :]
    scale = last * gain
    pay[1, c : c + 1, :] = scale * scale * jnp.sum(pinv * pinv, axis=0, keepdims=True)


def gain_columns(gains):
    frames = gains.shape[1]
    mid = frames // 2 - 1
    lane = lax.broadcasted_iota(jnp.int32, (8, frames), 1)
    prefix = jnp.broadcast_to(gains, (8, frames))
    step = 1
    while step < frames:
        prefix = prefix * jnp.where(lane >= step, pltpu.roll(prefix, step, 1), 1.0)
        step *= 2
    middle = jnp.broadcast_to(prefix[0:1, mid : mid + 1], (1, LANES))
    whole = jnp.broadcast_to(prefix[0:1, frames - 1 : frames], (1, LANES))
    prefix_col = jnp.broadcast_to(prefix[0:1] / middle, (LANES, frames)).T
    inverse_col = jnp.broadcast_to(middle / prefix[0:1], (LANES, frames)).T
    return middle, whole, prefix_col, inverse_col


def rims_kernel(spikes, decay, gains, first, second, rates_here, gains_here, sems):
    edge = RIM * LANES
    neurons = spikes.shape[0]
    own = decay.shape[0]
    even = lax.axis_index("tile") % 2 == 0
    top = jnp.where(even, neurons - edge, 0)
    bottom = jnp.where(even, 0, neurons - edge)
    copies = [
        pltpu.make_async_copy(decay, rates_here, sems.at[0]),
        pltpu.make_async_copy(gains, gains_here, sems.at[1]),
        pltpu.make_async_copy(
            spikes.at[pl.ds(pl.multiple_of(top, LANES), edge)], first.at[pl.ds(0, edge)], sems.at[2]
        ),
        pltpu.make_async_copy(
            spikes.at[pl.ds(pl.multiple_of(bottom, LANES), edge)],
            second.at[pl.ds(0, edge)],
            sems.at[3],
        ),
    ]
    for copy in copies:
        copy.start()
    first[edge:, :] = jnp.zeros_like(first[edge:, :])
    second[edge:, :] = jnp.zeros_like(second[edge:, :])
    copies[0].wait()
    lower, upper = rates_here[0:RIM, :], rates_here[own - RIM : own, :]
    first[edge : edge + RIM, :] = jnp.where(even, upper, lower)
    second[edge : edge + RIM, :] = jnp.where(even, lower, upper)
    for copy in copies[1:]:
        copy.wait()


def prep_own_kernel(
    spikes, decay, gains, feet, s3, p3, pinv3, z3, rows, pay, columns, feet_here, spikes_here, sems
):
    own = s3.shape[0]
    chunks = own + 2 * RIM
    size = spikes.shape[0] // PARTS
    copies = [
        pltpu.make_async_copy(
            spikes.at[pl.ds(i * size, size)], spikes_here.at[pl.ds(i * size, size)], sems.at[i]
        )
        for i in range(PARTS)
    ]
    for copy in copies:
        copy.start()
    fetch = pltpu.make_async_copy(feet, feet_here, sems.at[PARTS])
    fetch.start()
    middle, whole, prefix_col, inverse_col = gain_columns(gains[...])
    columns[0] = prefix_col
    columns[1] = inverse_col
    rows[...] = jnp.ones_like(rows)
    rows[0, chunks : chunks + 1, :] = middle
    pay[...] = jnp.zeros_like(pay)
    pay[0, chunks : chunks + 1, :] = whole
    shared = middle, prefix_col, inverse_col, table(spikes.shape[1], False)
    for i in range(own):
        if i % (own // PARTS) == 0:
            copies[i // (own // PARTS)].wait()
        field = spikes_here[i * LANES : (i + 1) * LANES, :]
        at = [ref.at[i] for ref in (s3, p3, pinv3, z3)]
        prep_chunk(i + RIM, decay[i : i + 1, :], field, shared, *at, rows, pay)
    fetch.wait()


def sides(even, first, second):
    return jnp.where(even, second, first), jnp.where(even, first, second)


def prep_rim_kernel(first, second, columns, rows_own, pay_own, s3, p3, pinv3, z3, rows, pay):
    rims, frames = s3.shape[0], s3.shape[1]
    own = rows_own.shape[1] - padded8(1)
    chunks = own + 2 * RIM
    middle = rows_own[0, chunks : chunks + 1, :]
    shared = middle, columns[0], columns[1], table(frames, False)
    rows[...] = rows_own[...]
    pay[...] = pay_own[...]
    even = lax.axis_index("tile") % 2 == 0
    below, above = sides(even, first[...], second[...])
    for i in range(rims):
        message = below if i < RIM else above
        j = i % RIM
        c = i if i < RIM else own + i
        at = [ref.at[i] for ref in (s3, p3, pinv3, z3)]
        field = message[j * LANES : (j + 1) * LANES, :]
        rate = message[RIM * LANES + j : RIM * LANES + j + 1, :]
        prep_chunk(c, rate, field, shared, *at, rows, pay)


def block_totals(pays, chunks, rows):
    return [rows[2] * pays[m, 0, chunks : chunks + 1, :] for m in range(pays.shape[0])]


def step_size(stats):
    both = jnp.sum(jnp.sum(stats[...], axis=0), axis=1, keepdims=True)
    return jnp.broadcast_to(both[0:1] / (both[1:2] + 1e-06), (1, LANES))


def update_kernel(s3, g3, stats, p3, pinv3, rows, new3, z3, pay):
    chunks = chunk_count(s3)
    frames = g3.shape[1]
    sums_table = table(frames, False)
    size = step_size(stats)
    pay[...] = jnp.zeros_like(pay)
    for c in range(chunks):
        field = jnp.maximum(chunk(s3, c)[...] - size * g3[c], 0.0)
        z = summed(sums_table, field * rows[0, c : c + 1, :] * chunk(pinv3, c)[...])
        if len(new3) == 2:
            chunk(new3, c)[...] = field
        elif RIM <= c < chunks - RIM:
            new3[0][c - RIM] = field
        chunk(z3, c)[...] = z
        last = chunk(p3, c)[frames - 1 : frames, :]
        pay[c : c + 1, :] = last * z[frames - 1 : frames, :]


def final_kernel(s3, g3, stats, out, here, sems):
    size = step_size(stats)
    own = s3.shape[0]
    rows = out.shape[0] // PARTS
    copies = [
        pltpu.make_async_copy(
            here.at[pl.ds(i * rows, rows)], out.at[pl.ds(i * rows, rows)], sems.at[i]
        )
        for i in range(PARTS)
    ]
    for i in range(own):
        field = jnp.maximum(s3[i] - size * g3[i + RIM], 0.0)
        here[i * LANES : (i + 1) * LANES, :] = field.T
        if (i + 1) % (own // PARTS) == 0:
            copies[i // (own // PARTS)].start()
    for copy in copies:
        copy.wait()


def picked(ext, pattern, q):
    parts = [
        ext[pl.ds(pl.multiple_of(pattern[k, q] * NEU_BLOCK, NEU_BLOCK), NEU_BLOCK), :]
        for k in range(K)
    ]
    return jnp.concatenate(parts, axis=0)


def foot_of(feet, q):
    return feet[q * PIX_BLOCK : (q + 1) * PIX_BLOCK, :]


def pull_back(pattern, ext, feet, record, contrib, place, start, stop):
    for q in range(start, stop):
        for v in range(2 * HB + 1):
            place[q, v] = -1
        for k in range(K):
            place[q, pattern[k, q] - q] = k
    for q in range(start, stop):
        foot = foot_of(feet, q)
        fitted = jnp.dot(foot, picked(ext, pattern, q), preferred_element_type=F32)
        residual = (fitted - foot_of(record, q).astype(F32)).astype(BF16)
        contrib[q * K * NEU_BLOCK : (q + 1) * K * NEU_BLOCK, :] = lax.dot_general(
            foot, residual, (((0,), (0,)), ((), ())), preferred_element_type=F32
        )


def gathered(contrib, place, c, ranges):
    frames = contrib.shape[1]
    per_chunk = LANES // NEU_BLOCK
    halves = []
    for b in range(c * per_chunk, (c + 1) * per_chunk):
        total = jnp.zeros((NEU_BLOCK, frames), F32)
        for v in range(2 * HB + 1):
            q = b - v
            if any(start <= q < stop for start, stop in ranges):
                k = place[q, v]
                at = pl.multiple_of((q * K + jnp.maximum(k, 0)) * NEU_BLOCK, NEU_BLOCK)
                value = contrib[pl.ds(at, NEU_BLOCK), :]
                if v % 2:
                    value = jnp.where(k >= 0, value, 0.0)
                total = total + value
        halves.append(total)
    return jnp.concatenate(halves, axis=0).T


def edge_kernel(
    pattern, z3, p3, rows, pay, pays, feet, record, ext, zones, spill, send_a, send_b, state, *scratch
):
    contrib, place = scratch
    chunks = chunk_count(z3)
    stripe = pattern.shape[1]
    edge = 2 * HB
    me = lax.axis_index("tm")
    totals = block_totals(pay, chunks, rows)
    carry = jnp.zeros_like(totals[0])
    for m in range(pays.shape[0]):
        carry = jnp.where(m < me, pays[m] + totals[m] * carry, carry)
    carry = carry * rows[1]
    state[...] = carry
    for c in range(chunks):
        field = chunk(p3, c)[...] * (chunk(z3, c)[...] + carry[c : c + 1, :])
        ext[c * LANES : (c + 1) * LANES, :] = field.T.astype(BF16)
    ranges = ((0, edge), (stripe - edge, stripe))
    for start, stop in ranges:
        pull_back(pattern, ext, feet, record, contrib, place, start, stop)
    even = lax.axis_index("tile") % 2 == 0
    for i in range(2 * RIM):
        below = gathered(contrib, place, i, ranges)
        above = gathered(contrib, place, chunks - 2 * RIM + i, ranges)
        zones[i] = below
        zones[2 * RIM + i] = above
        send_a[i] = jnp.where(even, above, below).astype(BF16)
        send_b[i] = jnp.where(even, below, above).astype(BF16)
        spill[i] = gathered(contrib, place, 2 * RIM + i, ranges)
        spill[2 * RIM + i] = gathered(contrib, place, chunks - 4 * RIM + i, ranges)


def adjoint_chunk(sums_table, field, p, pinv, rows, c, r3, pay):
    frames = field.shape[0]
    r = summed(sums_table, field * p)
    r3[...] = r
    gain = rows[0, c : c + 1, :]
    pay[0, c : c + 1, :] = rows[1, c : c + 1, :] * r[0:1, :]
    ends = p[frames - 1 : frames, :] * gain * gain
    pay[1, c : c + 1, :] = ends * jnp.sum(pinv * pinv * r, axis=0, keepdims=True)


def inner_kernel(pattern, p3, pinv3, rows, ext, spill, feet, record, r3, pay, *scratch):
    contrib, place = scratch
    chunks = chunk_count(p3)
    frames = spill.shape[1]
    stripe = pattern.shape[1]
    edge = 2 * HB
    pull_back(pattern, ext, feet, record, contrib, place, edge, stripe - edge)
    sums_table = table(frames, True)
    pay[...] = jnp.zeros_like(pay)
    inner = chunks - 4 * RIM
    for i in range(inner):
        c = i + 2 * RIM
        field = gathered(contrib, place, c, ((edge, stripe - edge),))
        if i < 2 * RIM:
            field = field + spill[i]
        if i >= inner - 2 * RIM:
            field = field + spill[i - inner + 4 * RIM]
        p, pinv = chunk(p3, c)[...], chunk(pinv3, c)[...]
        adjoint_chunk(sums_table, field, p, pinv, rows, c, r3.at[i], pay)


def border_kernel(zones, got_a, got_b, p3, pinv3, rows, pay_inner, r3, pay):
    chunks = chunk_count(p3)
    frames = zones.shape[1]
    sums_table = table(frames, True)
    pay[...] = pay_inner[...]
    even = lax.axis_index("tile") % 2 == 0
    for i in range(2 * RIM):
        both = sides(even, got_a[i].astype(F32), got_b[i].astype(F32))
        for side, c in ((0, i), (1, chunks - 2 * RIM + i)):
            at = side * 2 * RIM + i
            field = zones[at] + both[side]
            p, pinv = chunk(p3, c)[...], chunk(pinv3, c)[...]
            adjoint_chunk(sums_table, field, p, pinv, rows, c, r3.at[at], pay)


def direction_kernel(
    pattern, r_inner, r_border, p3, pinv3, rows, pay, pays, feet, g3, stats, ext
):
    chunks, frames = g3.shape[0], g3.shape[1]
    own = chunks - 2 * RIM
    stripe = pattern.shape[1]
    me = lax.axis_index("tm")
    totals = block_totals(pay, chunks, rows)
    blocks = pays.shape[0]
    entering = [None] * blocks
    state = jnp.zeros_like(totals[0])
    for m in reversed(range(blocks)):
        entering[m] = state
        state = pays[m, 0] + totals[m] * state
    carry = jnp.zeros_like(totals[0])
    adjoint = jnp.zeros_like(totals[0])
    for m in range(blocks):
        end = pays[m, 1] + pay[m, 1] * entering[m]
        carry = jnp.where(m < me, end + totals[m] * carry, carry)
        adjoint = jnp.where(m == me, entering[m], adjoint)
    carry = carry * rows[1]
    sums_table = table(frames, False)
    grad_sq = jnp.zeros((8, LANES), F32)
    for c in range(chunks):
        p, pinv = chunk(p3, c)[...], chunk(pinv3, c)[...]
        if c < 2 * RIM:
            r = r_border[c]
        elif c >= chunks - 2 * RIM:
            r = r_border[c - chunks + 4 * RIM]
        else:
            r = r_inner[c - 2 * RIM]
        gain = rows[0, c : c + 1, :]
        gradient = gain * pinv * (r + p[frames - 1 : frames, :] * adjoint[c : c + 1, :])
        g3[c] = gradient
        if RIM <= c < RIM + own:
            grad_sq += jnp.sum((gradient * gradient).reshape(frames // 8, 8, LANES), axis=0)
        z = summed(sums_table, gain * gradient * pinv)
        field = (p * (z + carry[c : c + 1, :])).T
        ext[c * LANES : (c + 1) * LANES, :] = field.astype(BF16)
    image_sq = jnp.zeros((8, frames), F32)
    for q in range(stripe):
        image = jnp.dot(foot_of(feet, q), picked(ext, pattern, q), preferred_element_type=F32)
        image_sq += jnp.sum((image * image).reshape(PIX_BLOCK // 8, 8, frames), axis=0)
    both = jnp.concatenate(
        [
            jnp.sum(grad_sq, axis=0, keepdims=True),
            jnp.sum(image_sq, axis=0, keepdims=True),
        ],
        axis=0,
    )
    stats[...] = jnp.broadcast_to(both[None], stats.shape)


def traces_kernel(z3, p3, state, traces):
    for i in range(z3.shape[0]):
        c = i + RIM
        field = p3[i] * (z3[i] + state[c : c + 1, :])
        traces[i * LANES : (i + 1) * LANES, :] = field.T


def f32(*shape):
    return jax.ShapeDtypeStruct(shape, F32)


def bf16(*shape):
    return jax.ShapeDtypeStruct(shape, BF16)


def call(
    kernel, name, micros, outs, args, scratch=(), far=(), far_out=False, keep=(), limit=16
):
    def spec(place, arg):
        if place in far:
            return HBM
        return SMEM if arg.dtype == jnp.int32 else VMEM

    in_specs = [jax.tree.map(lambda x: spec(i, x), arg) for i, arg in enumerate(args)]
    in_specs.append(jax.tree.map(lambda _: VMEM, keep))

    def body(*refs):
        kernel(*refs[: len(args)], *refs[len(args) + 1 :])

    return pl.pallas_call(
        body,
        name=name,
        out_shape=outs,
        in_specs=in_specs,
        out_specs=jax.tree.map(lambda _: HBM if far_out else VMEM, outs),
        scratch_shapes=scratch,
        compiler_params=pltpu.CompilerParams(vmem_limit_bytes=int(limit * 2**20)),
        cost_estimate=pl.CostEstimate(
            flops=int(micros * 1e8), bytes_accessed=int(micros * 3e6), transcendentals=0
        ),
    )(*args, keep)


def swapped(first, second):
    size = lax.axis_size("tile")

    def pairs(start):
        both = [(i, i + 1) for i in range(start, size - 1, 2)]
        return both + [(j, i) for i, j in both]

    return lax.ppermute(first, "tile", pairs(0)), lax.ppermute(second, "tile", pairs(1))


def per_device(recording, footprints, pattern, decay, frame_gain, spikes):
    neurons, frames = spikes.shape
    stripe = pattern.shape[0]
    pattern = pattern.T
    own = neurons // LANES
    chunks = own + 2 * RIM
    lines = own + padded8(1)
    devices = lax.axis_size("tile") * lax.axis_size("tm")
    split = (f32(own, frames, LANES), f32(2 * RIM, frames, LANES))
    message = f32(RIM * LANES + padded8(RIM), frames)
    first, second, rates, gains = call(
        rims_kernel,
        "rims",
        1.0,
        (message, message, f32(own, LANES), f32(1, frames)),
        (spikes, decay.reshape(own, LANES), frame_gain.reshape(1, frames)),
        [pltpu.SemaphoreType.DMA((4,))],
        far=(0, 1, 2),
        limit=52,
    )
    first, second = swapped(first, second)
    *owns, rows, pay, columns, footprints = call(
        prep_own_kernel,
        "prep_own",
        1.6,
        (split[0],) * 4
        + (f32(3, lines, LANES), f32(2, lines, LANES), f32(2, frames, LANES))
        + (bf16(*footprints.shape),),
        (spikes, rates, gains, footprints),
        [pltpu.VMEM((neurons, frames), F32), pltpu.SemaphoreType.DMA((PARTS + 1,))],
        far=(0, 3),
        limit=44,
    )
    *rims, rows, pay = call(
        prep_rim_kernel,
        "prep_rim",
        0.3,
        (split[1],) * 4 + (f32(3, lines, LANES), f32(2, lines, LANES)),
        (first, second, columns, rows, pay),
    )
    s3, p3, pinv3, z3 = zip(owns, rims)
    constants = lax.all_gather(pay, "tm")
    pays = constants[:, 0]
    scratch = [
        pltpu.VMEM((stripe * K * NEU_BLOCK, frames), F32),
        pltpu.SMEM((stripe, 2 * HB + 1), jnp.int32),
    ]
    zone = (2 * RIM, frames, LANES)
    border = (4 * RIM, frames, LANES)
    for iteration in range(ITERS):
        ends = iteration == ITERS - 1
        ext, zones, spill, send_a, send_b, state = call(
            edge_kernel,
            "edge",
            2.5,
            (
                bf16(chunks * LANES, frames),
                f32(*border),
                f32(*border),
                bf16(*zone),
                bf16(*zone),
                f32(lines, LANES),
            ),
            (pattern, z3, p3, rows, constants, pays, footprints, recording),
            scratch,
            keep=(s3[0],) if ends else (),
        )
        got_a, got_b = swapped(send_a, send_b)
        held = (s3[0], z3[0], state) if ends else ()
        r_inner, pay = call(
            inner_kernel,
            "inner",
            4.0,
            (f32(chunks - 4 * RIM, frames, LANES), f32(2, lines, LANES)),
            (pattern, p3, pinv3, rows, ext, spill, footprints, recording),
            scratch,
            keep=held,
        )
        r_border, pay = call(
            border_kernel,
            "border",
            0.3,
            (f32(*border), f32(2, lines, LANES)),
            (zones, got_a, got_b, p3, pinv3, rows, pay),
            keep=held,
        )
        pays = lax.all_gather(pay, "tm")
        g3, stats = call(
            direction_kernel,
            "direction",
            4.0,
            (f32(chunks, frames, LANES), f32(devices, 2, LANES)),
            (pattern, r_inner, r_border, p3, pinv3, rows, constants, pays, footprints),
            [pltpu.VMEM((chunks * LANES, frames), BF16)],
            keep=held,
        )
        stats = lax.all_to_all(stats, ("tile", "tm"), 0, 0)
        if ends:
            traces = call(
                traces_kernel,
                "traces",
                1.4,
                f32(neurons, frames),
                (z3[0], p3[0], state),
                keep=(s3[0], g3),
            )
            out = call(
                final_kernel,
                "final",
                1.4,
                f32(neurons, frames),
                (s3[0], g3, stats),
                [pltpu.VMEM((neurons, frames), F32), pltpu.SemaphoreType.DMA((PARTS,))],
                far_out=True,
            )
            return out, traces
        s3, z3, pay = call(
            update_kernel,
            "update",
            0.6,
            (split if iteration < ITERS - 2 else split[:1], split, f32(lines, LANES)),
            (s3, g3, stats, p3, pinv3, rows),
        )
        pays = lax.all_gather(pay, "tm")


def solution(mesh):
    return jax.shard_map(
        per_device,
        mesh=mesh,
        in_specs=(
            P("tile", "tm"),
            P("tile", None),
            P("tile", None),
            P("tile"),
            P("tm"),
            P("tile", "tm"),
        ),
        out_specs=(P("tile", "tm"), P("tile", "tm")),
        check_vma=False,
    )
```

```python
import jax
import jax.numpy as jnp
from jax import lax
from jax.experimental import pallas as pl
from jax.experimental.pallas import tpu as pltpu
from jax.sharding import PartitionSpec as P

NEU_BLOCK = 64
PIX_BLOCK = 256
PARTS = 4
K = 4
HB = 2
ITERS = 2
LANES = 128
RIM = HB * NEU_BLOCK // LANES
F32 = jnp.float32
BF16 = jnp.bfloat16
VMEM = pl.BlockSpec(memory_space=pltpu.VMEM)
HBM = pl.BlockSpec(memory_space=pltpu.HBM)
SMEM = pl.BlockSpec(memory_space=pltpu.SMEM)


def padded8(rows):
    return -(-rows // 8) * 8


def table(frames, reverse):
    row = lax.broadcasted_iota(jnp.int32, (frames, 2 * frames), 0)
    col = lax.broadcasted_iota(jnp.int32, (frames, 2 * frames), 1)
    col = jnp.where(col >= frames, col - frames, col)
    keep = col >= row if reverse else col <= row
    return jnp.where(keep, 1.0, 0.0).astype(BF16)


def summed(sums_table, values):
    high = values.astype(BF16)
    low = (values - high.astype(F32)).astype(BF16)
    both = jnp.concatenate([high, low], axis=0)
    return jnp.dot(sums_table, both, preferred_element_type=F32)


def powers(log_decay, frames, mid, sign):
    groups = frames // 8
    coarse = (8 * lax.broadcasted_iota(jnp.int32, (groups, LANES), 0) - mid).astype(F32) * sign
    fine = lax.broadcasted_iota(jnp.int32, (8, LANES), 0).astype(F32) * sign
    coarse = jnp.exp(coarse * log_decay)
    fine = jnp.exp(fine * log_decay)
    return (coarse[:, None, :] * fine[None, :, :]).reshape(frames, LANES)


def chunk(field, c):
    own, rim = field
    inner = own.shape[0]
    if c < RIM:
        return rim.at[c]
    if c >= RIM + inner:
        return rim.at[c - inner]
    return own.at[c - RIM]


def chunk_count(field):
    return field[0].shape[0] + field[1].shape[0]


def prep_chunk(c, rate, field, gains, s3, p3, pinv3, z3, rows, pay):
    frames = field.shape[1]
    middle, prefix_col, inverse_col, sums_table = gains
    mid = frames // 2 - 1
    rate = jnp.where(rate > 0.0, rate, 1.0)
    log_rate = jnp.log(rate)
    gain = jnp.sqrt(1.0 - rate * rate)
    p = powers(log_rate, frames, mid, 1.0) * prefix_col
    pinv = powers(log_rate, frames, mid, -1.0) * inverse_col
    field = field.T
    z = summed(sums_table, field * gain * pinv)
    last = p[frames - 1 : frames, :]
    s3[...] = field
    p3[...] = p
    pinv3[...] = pinv
    z3[...] = z
    half = rate
    for _ in range(frames.bit_length() - 2):
        half = half * half
    rows[0, c : c + 1, :] = gain
    rows[1, c : c + 1, :] = half * middle
    rows[2, c : c + 1, :] = half * half
    pay[0, c : c + 1, :] = last * z[frames - 1 : frames, :]
    scale = last * gain
    pay[1, c : c + 1, :] = scale * scale * jnp.sum(pinv * pinv, axis=0, keepdims=True)


def gain_columns(gains):
    frames = gains.shape[1]
    mid = frames // 2 - 1
    lane = lax.broadcasted_iota(jnp.int32, (8, frames), 1)
    prefix = jnp.broadcast_to(gains, (8, frames))
    step = 1
    while step < frames:
        prefix = prefix * jnp.where(lane >= step, pltpu.roll(prefix, step, 1), 1.0)
        step *= 2
    middle = jnp.broadcast_to(prefix[0:1, mid : mid + 1], (1, LANES))
    whole = jnp.broadcast_to(prefix[0:1, frames - 1 : frames], (1, LANES))
    prefix_col = jnp.broadcast_to(prefix[0:1] / middle, (LANES, frames)).T
    inverse_col = jnp.broadcast_to(middle / prefix[0:1], (LANES, frames)).T
    return middle, whole, prefix_col, inverse_col


def rims_kernel(spikes, decay, first, second, rates_here, spikes_here, sems):
    edge = RIM * LANES
    neurons = spikes.shape[0]
    own = decay.shape[0]
    even = lax.axis_index("tile") % 2 == 0
    top = jnp.where(even, neurons - edge, 0)
    bottom = jnp.where(even, 0, neurons - edge)
    copies = [
        pltpu.make_async_copy(decay, rates_here, sems.at[0]),
        pltpu.make_async_copy(
            spikes.at[pl.ds(pl.multiple_of(top, LANES), edge)], first.at[pl.ds(0, edge)], sems.at[1]
        ),
        pltpu.make_async_copy(
            spikes.at[pl.ds(pl.multiple_of(bottom, LANES), edge)],
            second.at[pl.ds(0, edge)],
            sems.at[2],
        ),
        pltpu.make_async_copy(spikes, spikes_here, sems.at[3]),
    ]
    for copy in copies:
        copy.start()
    first[edge:, :] = jnp.zeros_like(first[edge:, :])
    second[edge:, :] = jnp.zeros_like(second[edge:, :])
    copies[0].wait()
    lower, upper = rates_here[0:RIM, :], rates_here[own - RIM : own, :]
    first[edge : edge + RIM, :] = jnp.where(even, upper, lower)
    second[edge : edge + RIM, :] = jnp.where(even, lower, upper)
    for copy in copies[1:]:
        copy.wait()


def prep_own_kernel(
    spikes, decay, gains, feet, s3, p3, pinv3, z3, rows, pay, columns, feet_here, sem
):
    own = s3.shape[0]
    chunks = own + 2 * RIM
    fetch = pltpu.make_async_copy(feet, feet_here, sem)
    fetch.start()
    middle, whole, prefix_col, inverse_col = gain_columns(gains[...])
    columns[0] = prefix_col
    columns[1] = inverse_col
    rows[...] = jnp.ones_like(rows)
    rows[0, chunks : chunks + 1, :] = middle
    pay[...] = jnp.zeros_like(pay)
    pay[0, chunks : chunks + 1, :] = whole
    shared = middle, prefix_col, inverse_col, table(spikes.shape[1], False)
    for i in range(own):
        field = spikes[i * LANES : (i + 1) * LANES, :]
        at = [ref.at[i] for ref in (s3, p3, pinv3, z3)]
        prep_chunk(i + RIM, decay[i : i + 1, :], field, shared, *at, rows, pay)
    fetch.wait()


def sides(even, first, second):
    return jnp.where(even, second, first), jnp.where(even, first, second)


def prep_rim_kernel(first, second, columns, rows_own, pay_own, s3, p3, pinv3, z3, rows, pay):
    rims, frames = s3.shape[0], s3.shape[1]
    own = rows_own.shape[1] - padded8(1)
    chunks = own + 2 * RIM
    middle = rows_own[0, chunks : chunks + 1, :]
    shared = middle, columns[0], columns[1], table(frames, False)
    rows[...] = rows_own[...]
    pay[...] = pay_own[...]
    even = lax.axis_index("tile") % 2 == 0
    below, above = sides(even, first[...], second[...])
    for i in range(rims):
        message = below if i < RIM else above
        j = i % RIM
        c = i if i < RIM else own + i
        at = [ref.at[i] for ref in (s3, p3, pinv3, z3)]
        field = message[j * LANES : (j + 1) * LANES, :]
        rate = message[RIM * LANES + j : RIM * LANES + j + 1, :]
        prep_chunk(c, rate, field, shared, *at, rows, pay)


def block_totals(pays, chunks, rows):
    return [rows[2] * pays[m, 0, chunks : chunks + 1, :] for m in range(pays.shape[0])]


def step_size(stats):
    both = jnp.sum(jnp.sum(stats[...], axis=0), axis=1, keepdims=True)
    return jnp.broadcast_to(both[0:1] / (both[1:2] + 1e-06), (1, LANES))


def update_kernel(s3, g3, stats, p3, pinv3, rows, new3, z3, pay):
    chunks = chunk_count(s3)
    frames = g3.shape[1]
    sums_table = table(frames, False)
    size = step_size(stats)
    pay[...] = jnp.zeros_like(pay)
    for c in range(chunks):
        field = jnp.maximum(chunk(s3, c)[...] - size * g3[c], 0.0)
        z = summed(sums_table, field * rows[0, c : c + 1, :] * chunk(pinv3, c)[...])
        if len(new3) == 2:
            chunk(new3, c)[...] = field
        elif RIM <= c < chunks - RIM:
            new3[0][c - RIM] = field
        chunk(z3, c)[...] = z
        last = chunk(p3, c)[frames - 1 : frames, :]
        pay[c : c + 1, :] = last * z[frames - 1 : frames, :]


def final_kernel(s3, g3, stats, out, here, sems):
    size = step_size(stats)
    own = s3.shape[0]
    rows = out.shape[0] // PARTS
    copies = [
        pltpu.make_async_copy(
            here.at[pl.ds(i * rows, rows)], out.at[pl.ds(i * rows, rows)], sems.at[i]
        )
        for i in range(PARTS)
    ]
    for i in range(own):
        field = jnp.maximum(s3[i] - size * g3[i + RIM], 0.0)
        here[i * LANES : (i + 1) * LANES, :] = field.T
        if (i + 1) % (own // PARTS) == 0:
            copies[i // (own // PARTS)].start()
    for copy in copies:
        copy.wait()


def picked(ext, pattern, q):
    parts = [
        ext[pl.ds(pl.multiple_of(pattern[k, q] * NEU_BLOCK, NEU_BLOCK), NEU_BLOCK), :]
        for k in range(K)
    ]
    return jnp.concatenate(parts, axis=0)


def foot_of(feet, q):
    return feet[q * PIX_BLOCK : (q + 1) * PIX_BLOCK, :]


def pull_back(pattern, ext, feet, record, contrib, place, start, stop):
    for q in range(start, stop):
        for v in range(2 * HB + 1):
            place[q, v] = -1
        for k in range(K):
            place[q, pattern[k, q] - q] = k
    for q in range(start, stop):
        foot = foot_of(feet, q)
        fitted = jnp.dot(foot, picked(ext, pattern, q), preferred_element_type=F32)
        residual = (fitted - foot_of(record, q).astype(F32)).astype(BF16)
        contrib[q * K * NEU_BLOCK : (q + 1) * K * NEU_BLOCK, :] = lax.dot_general(
            foot, residual, (((0,), (0,)), ((), ())), preferred_element_type=F32
        )


def gathered(contrib, place, c, ranges):
    frames = contrib.shape[1]
    per_chunk = LANES // NEU_BLOCK
    halves = []
    for b in range(c * per_chunk, (c + 1) * per_chunk):
        total = jnp.zeros((NEU_BLOCK, frames), F32)
        for v in range(2 * HB + 1):
            q = b - v
            if any(start <= q < stop for start, stop in ranges):
                k = place[q, v]
                at = pl.multiple_of((q * K + jnp.maximum(k, 0)) * NEU_BLOCK, NEU_BLOCK)
                value = contrib[pl.ds(at, NEU_BLOCK), :]
                if v % 2:
                    value = jnp.where(k >= 0, value, 0.0)
                total = total + value
        halves.append(total)
    return jnp.concatenate(halves, axis=0).T


def edge_kernel(
    pattern, z3, p3, rows, pay, pays, feet, record, ext, zones, spill, send_a, send_b, *rest
):
    if len(rest) > 2:
        traces, contrib, place, traces_here, sems = rest
    else:
        contrib, place = rest
        traces = None
    copies = []
    chunks = chunk_count(z3)
    stripe = pattern.shape[1]
    edge = 2 * HB
    me = lax.axis_index("tm")
    totals = block_totals(pay, chunks, rows)
    carry = jnp.zeros_like(totals[0])
    for m in range(pays.shape[0]):
        carry = jnp.where(m < me, pays[m] + totals[m] * carry, carry)
    carry = carry * rows[1]
    for c in range(chunks):
        field = (chunk(p3, c)[...] * (chunk(z3, c)[...] + carry[c : c + 1, :])).T
        ext[c * LANES : (c + 1) * LANES, :] = field.astype(BF16)
        if traces is not None and RIM <= c < chunks - RIM:
            part = (chunks - 2 * RIM) // PARTS
            i = c - RIM
            traces_here[i * LANES : (i + 1) * LANES, :] = field
            if (i + 1) % part == 0:
                at = pl.ds((i + 1 - part) * LANES, part * LANES)
                copies.append(
                    pltpu.make_async_copy(traces_here.at[at], traces.at[at], sems.at[i // part])
                )
                copies[-1].start()
    ranges = ((0, edge), (stripe - edge, stripe))
    for start, stop in ranges:
        pull_back(pattern, ext, feet, record, contrib, place, start, stop)
    even = lax.axis_index("tile") % 2 == 0
    for i in range(2 * RIM):
        below = gathered(contrib, place, i, ranges)
        above = gathered(contrib, place, chunks - 2 * RIM + i, ranges)
        zones[i] = below
        zones[2 * RIM + i] = above
        send_a[i] = jnp.where(even, above, below).astype(BF16)
        send_b[i] = jnp.where(even, below, above).astype(BF16)
        spill[i] = gathered(contrib, place, 2 * RIM + i, ranges)
        spill[2 * RIM + i] = gathered(contrib, place, chunks - 4 * RIM + i, ranges)
    for copy in copies:
        copy.wait()


def adjoint_chunk(sums_table, field, p, pinv, rows, c, r3, pay):
    frames = field.shape[0]
    r = summed(sums_table, field * p)
    r3[...] = r
    gain = rows[0, c : c + 1, :]
    pay[0, c : c + 1, :] = rows[1, c : c + 1, :] * r[0:1, :]
    ends = p[frames - 1 : frames, :] * gain * gain
    pay[1, c : c + 1, :] = ends * jnp.sum(pinv * pinv * r, axis=0, keepdims=True)


def inner_kernel(pattern, p3, pinv3, rows, ext, spill, feet, record, r3, pay, *scratch):
    contrib, place = scratch
    chunks = chunk_count(p3)
    frames = spill.shape[1]
    stripe = pattern.shape[1]
    edge = 2 * HB
    pull_back(pattern, ext, feet, record, contrib, place, edge, stripe - edge)
    sums_table = table(frames, True)
    pay[...] = jnp.zeros_like(pay)
    inner = chunks - 4 * RIM
    for i in range(inner):
        c = i + 2 * RIM
        field = gathered(contrib, place, c, ((edge, stripe - edge),))
        if i < 2 * RIM:
            field = field + spill[i]
        if i >= inner - 2 * RIM:
            field = field + spill[i - inner + 4 * RIM]
        p, pinv = chunk(p3, c)[...], chunk(pinv3, c)[...]
        adjoint_chunk(sums_table, field, p, pinv, rows, c, r3.at[i], pay)


def border_kernel(zones, got_a, got_b, p3, pinv3, rows, pay_inner, r3, pay):
    chunks = chunk_count(p3)
    frames = zones.shape[1]
    sums_table = table(frames, True)
    pay[...] = pay_inner[...]
    even = lax.axis_index("tile") % 2 == 0
    for i in range(2 * RIM):
        both = sides(even, got_a[i].astype(F32), got_b[i].astype(F32))
        for side, c in ((0, i), (1, chunks - 2 * RIM + i)):
            at = side * 2 * RIM + i
            field = zones[at] + both[side]
            p, pinv = chunk(p3, c)[...], chunk(pinv3, c)[...]
            adjoint_chunk(sums_table, field, p, pinv, rows, c, r3.at[at], pay)


def direction_kernel(
    pattern, r_inner, r_border, p3, pinv3, rows, pay, pays, feet, g3, stats, ext
):
    chunks, frames = g3.shape[0], g3.shape[1]
    own = chunks - 2 * RIM
    stripe = pattern.shape[1]
    me = lax.axis_index("tm")
    totals = block_totals(pay, chunks, rows)
    blocks = pays.shape[0]
    entering = [None] * blocks
    state = jnp.zeros_like(totals[0])
    for m in reversed(range(blocks)):
        entering[m] = state
        state = pays[m, 0] + totals[m] * state
    carry = jnp.zeros_like(totals[0])
    adjoint = jnp.zeros_like(totals[0])
    for m in range(blocks):
        end = pays[m, 1] + pay[m, 1] * entering[m]
        carry = jnp.where(m < me, end + totals[m] * carry, carry)
        adjoint = jnp.where(m == me, entering[m], adjoint)
    carry = carry * rows[1]
    sums_table = table(frames, False)
    grad_sq = jnp.zeros((8, LANES), F32)
    for c in range(chunks):
        p, pinv = chunk(p3, c)[...], chunk(pinv3, c)[...]
        if c < 2 * RIM:
            r = r_border[c]
        elif c >= chunks - 2 * RIM:
            r = r_border[c - chunks + 4 * RIM]
        else:
            r = r_inner[c - 2 * RIM]
        gain = rows[0, c : c + 1, :]
        gradient = gain * pinv * (r + p[frames - 1 : frames, :] * adjoint[c : c + 1, :])
        g3[c] = gradient
        if RIM <= c < RIM + own:
            grad_sq += jnp.sum((gradient * gradient).reshape(frames // 8, 8, LANES), axis=0)
        z = summed(sums_table, gain * gradient * pinv)
        field = (p * (z + carry[c : c + 1, :])).T
        ext[c * LANES : (c + 1) * LANES, :] = field.astype(BF16)
    image_sq = jnp.zeros((8, frames), F32)
    for q in range(stripe):
        image = jnp.dot(foot_of(feet, q), picked(ext, pattern, q), preferred_element_type=F32)
        image_sq += jnp.sum((image * image).reshape(PIX_BLOCK // 8, 8, frames), axis=0)
    both = jnp.concatenate(
        [
            jnp.sum(grad_sq, axis=0, keepdims=True),
            jnp.sum(image_sq, axis=0, keepdims=True),
        ],
        axis=0,
    )
    stats[...] = jnp.broadcast_to(both[None], stats.shape)


def f32(*shape):
    return jax.ShapeDtypeStruct(shape, F32)


def bf16(*shape):
    return jax.ShapeDtypeStruct(shape, BF16)


def call(
    kernel, name, micros, outs, args, scratch=(), far=(), far_out=(), keep=(), limit=16
):
    def spec(place, arg):
        if place in far:
            return HBM
        return SMEM if arg.dtype == jnp.int32 else VMEM

    in_specs = [jax.tree.map(lambda x: spec(i, x), arg) for i, arg in enumerate(args)]
    in_specs.append(jax.tree.map(lambda _: VMEM, keep))

    def body(*refs):
        kernel(*refs[: len(args)], *refs[len(args) + 1 :])

    return pl.pallas_call(
        body,
        name=name,
        out_shape=outs,
        in_specs=in_specs,
        out_specs=tuple(
            jax.tree.map(lambda _: HBM if place in far_out else VMEM, out)
            for place, out in enumerate(outs)
        ),
        scratch_shapes=scratch,
        compiler_params=pltpu.CompilerParams(vmem_limit_bytes=int(limit * 2**20)),
        cost_estimate=pl.CostEstimate(
            flops=int(micros * 1e8), bytes_accessed=int(micros * 3e6), transcendentals=0
        ),
    )(*args, keep)


def swapped(first, second):
    size = lax.axis_size("tile")

    def pairs(start):
        both = [(i, i + 1) for i in range(start, size - 1, 2)]
        return both + [(j, i) for i, j in both]

    return lax.ppermute(first, "tile", pairs(0)), lax.ppermute(second, "tile", pairs(1))


def per_device(recording, footprints, pattern, decay, frame_gain, spikes):
    neurons, frames = spikes.shape
    stripe = pattern.shape[0]
    pattern = pattern.T
    own = neurons // LANES
    chunks = own + 2 * RIM
    lines = own + padded8(1)
    devices = lax.axis_size("tile") * lax.axis_size("tm")
    split = (f32(own, frames, LANES), f32(2 * RIM, frames, LANES))
    message = f32(RIM * LANES + padded8(RIM), frames)
    gains = frame_gain.reshape(1, frames)
    first, second, rates, spikes = call(
        rims_kernel,
        "rims",
        1.0,
        (message, message, f32(own, LANES), f32(neurons, frames)),
        (spikes, decay.reshape(own, LANES)),
        [pltpu.SemaphoreType.DMA((4,))],
        far=(0, 1),
        limit=52,
    )
    first, second = swapped(first, second)
    *owns, rows, pay, columns, footprints = call(
        prep_own_kernel,
        "prep_own",
        1.6,
        (split[0],) * 4
        + (f32(3, lines, LANES), f32(2, lines, LANES), f32(2, frames, LANES))
        + (bf16(*footprints.shape),),
        (spikes, rates, gains, footprints),
        [pltpu.SemaphoreType.DMA],
        far=(3,),
        limit=44,
    )
    *rims, rows, pay = call(
        prep_rim_kernel,
        "prep_rim",
        0.3,
        (split[1],) * 4 + (f32(3, lines, LANES), f32(2, lines, LANES)),
        (first, second, columns, rows, pay),
    )
    s3, p3, pinv3, z3 = zip(owns, rims)
    constants = lax.all_gather(pay, "tm")
    pays = constants[:, 0]
    scratch = [
        pltpu.VMEM((stripe * K * NEU_BLOCK, frames), F32),
        pltpu.SMEM((stripe, 2 * HB + 1), jnp.int32),
    ]
    staged = [pltpu.VMEM((neurons, frames), F32), pltpu.SemaphoreType.DMA((PARTS,))]
    zone = (2 * RIM, frames, LANES)
    border = (4 * RIM, frames, LANES)
    for iteration in range(ITERS):
        ends = iteration == ITERS - 1
        ext, zones, spill, send_a, send_b, *traces = call(
            edge_kernel,
            "edge",
            2.5,
            (
                bf16(chunks * LANES, frames),
                f32(*border),
                f32(*border),
                bf16(*zone),
                bf16(*zone),
            )
            + ((f32(neurons, frames),) if ends else ()),
            (pattern, z3, p3, rows, constants, pays, footprints, recording),
            scratch + (staged if ends else []),
            far_out=(5,),
            keep=(s3[0],) if ends else (),
        )
        got_a, got_b = swapped(send_a, send_b)
        held = (s3[0],) if ends else ()
        r_inner, pay = call(
            inner_kernel,
            "inner",
            4.0,
            (f32(chunks - 4 * RIM, frames, LANES), f32(2, lines, LANES)),
            (pattern, p3, pinv3, rows, ext, spill, footprints, recording),
            scratch,
            keep=held,
        )
        r_border, pay = call(
            border_kernel,
            "border",
            0.3,
            (f32(*border), f32(2, lines, LANES)),
            (zones, got_a, got_b, p3, pinv3, rows, pay),
            keep=held,
        )
        pays = lax.all_gather(pay, "tm")
        g3, stats = call(
            direction_kernel,
            "direction",
            4.0,
            (f32(chunks, frames, LANES), f32(devices, 2, LANES)),
            (pattern, r_inner, r_border, p3, pinv3, rows, constants, pays, footprints),
            [pltpu.VMEM((chunks * LANES, frames), BF16)],
            keep=held,
        )
        stats = lax.all_to_all(stats, ("tile", "tm"), 0, 0)
        if ends:
            (out,) = call(
                final_kernel,
                "final",
                1.4,
                (f32(neurons, frames),),
                (s3[0], g3, stats),
                staged,
                far_out=(0,),
            )
            return out, traces[0]
        s3, z3, pay = call(
            update_kernel,
            "update",
            0.6,
            (split if iteration < ITERS - 2 else split[:1], split, f32(lines, LANES)),
            (s3, g3, stats, p3, pinv3, rows),
        )
        pays = lax.all_gather(pay, "tm")


def solution(mesh):
    return jax.shard_map(
        per_device,
        mesh=mesh,
        in_specs=(
            P("tile", "tm"),
            P("tile", None),
            P("tile", None),
            P("tile"),
            P("tm"),
            P("tile", "tm"),
        ),
        out_specs=(P("tile", "tm"), P("tile", "tm")),
        check_vma=False,
    )
```

```python
import jax
import jax.numpy as jnp
from jax import lax
from jax.experimental import pallas as pl
from jax.experimental.pallas import tpu as pltpu
from jax.sharding import PartitionSpec as P

NEU_BLOCK = 64
PIX_BLOCK = 256
PARTS = 4
K = 4
HB = 2
ITERS = 2
LANES = 128
RIM = HB * NEU_BLOCK // LANES
F32 = jnp.float32
BF16 = jnp.bfloat16
VMEM = pl.BlockSpec(memory_space=pltpu.VMEM)
HBM = pl.BlockSpec(memory_space=pltpu.HBM)
SMEM = pl.BlockSpec(memory_space=pltpu.SMEM)


def padded8(rows):
    return -(-rows // 8) * 8


def table(frames, reverse):
    row = lax.broadcasted_iota(jnp.int32, (frames, 2 * frames), 0)
    col = lax.broadcasted_iota(jnp.int32, (frames, 2 * frames), 1)
    col = jnp.where(col >= frames, col - frames, col)
    keep = col >= row if reverse else col <= row
    return jnp.where(keep, 1.0, 0.0).astype(BF16)


def summed(sums_table, values):
    high = values.astype(BF16)
    low = (values - high.astype(F32)).astype(BF16)
    both = jnp.concatenate([high, low], axis=0)
    return jnp.dot(sums_table, both, preferred_element_type=F32)


def powers(log_decay, frames, mid, sign):
    groups = frames // 8
    coarse = (8 * lax.broadcasted_iota(jnp.int32, (groups, LANES), 0) - mid).astype(F32) * sign
    fine = lax.broadcasted_iota(jnp.int32, (8, LANES), 0).astype(F32) * sign
    coarse = jnp.exp(coarse * log_decay)
    fine = jnp.exp(fine * log_decay)
    return (coarse[:, None, :] * fine[None, :, :]).reshape(frames, LANES)


def chunk(field, c):
    own, rim = field
    inner = own.shape[0]
    if c < RIM:
        return rim.at[c]
    if c >= RIM + inner:
        return rim.at[c - inner]
    return own.at[c - RIM]


def chunk_count(field):
    return field[0].shape[0] + field[1].shape[0]


def prep_chunk(c, rate, field, gains, s3, p3, pinv3, z3, rows, pay):
    frames = field.shape[1]
    middle, prefix_col, inverse_col, sums_table = gains
    mid = frames // 2 - 1
    rate = jnp.where(rate > 0.0, rate, 1.0)
    log_rate = jnp.log(rate)
    gain = jnp.sqrt(1.0 - rate * rate)
    p = powers(log_rate, frames, mid, 1.0) * prefix_col
    pinv = powers(log_rate, frames, mid, -1.0) * inverse_col
    field = field.T
    z = summed(sums_table, field * gain * pinv)
    last = p[frames - 1 : frames, :]
    s3[...] = field
    p3[...] = p
    pinv3[...] = pinv
    z3[...] = z
    half = rate
    for _ in range(frames.bit_length() - 2):
        half = half * half
    rows[0, c : c + 1, :] = gain
    rows[1, c : c + 1, :] = half * middle
    rows[2, c : c + 1, :] = half * half
    pay[0, c : c + 1, :] = last * z[frames - 1 : frames, :]
    scale = last * gain
    pay[1, c : c + 1, :] = scale * scale * jnp.sum(pinv * pinv, axis=0, keepdims=True)


def gain_columns(gains):
    frames = gains.shape[1]
    mid = frames // 2 - 1
    lane = lax.broadcasted_iota(jnp.int32, (8, frames), 1)
    prefix = jnp.broadcast_to(gains, (8, frames))
    step = 1
    while step < frames:
        prefix = prefix * jnp.where(lane >= step, pltpu.roll(prefix, step, 1), 1.0)
        step *= 2
    middle = jnp.broadcast_to(prefix[0:1, mid : mid + 1], (1, LANES))
    whole = jnp.broadcast_to(prefix[0:1, frames - 1 : frames], (1, LANES))
    prefix_col = jnp.broadcast_to(prefix[0:1] / middle, (LANES, frames)).T
    inverse_col = jnp.broadcast_to(middle / prefix[0:1], (LANES, frames)).T
    return middle, whole, prefix_col, inverse_col


def rims_kernel(spikes, decay, first, second, rates_here, spikes_here, sems):
    edge = RIM * LANES
    neurons = spikes.shape[0]
    own = decay.shape[0]
    even = lax.axis_index("tile") % 2 == 0
    top = jnp.where(even, neurons - edge, 0)
    bottom = jnp.where(even, 0, neurons - edge)
    copies = [
        pltpu.make_async_copy(decay, rates_here, sems.at[0]),
        pltpu.make_async_copy(
            spikes.at[pl.ds(pl.multiple_of(top, LANES), edge)], first.at[pl.ds(0, edge)], sems.at[1]
        ),
        pltpu.make_async_copy(
            spikes.at[pl.ds(pl.multiple_of(bottom, LANES), edge)],
            second.at[pl.ds(0, edge)],
            sems.at[2],
        ),
        pltpu.make_async_copy(spikes, spikes_here, sems.at[3]),
    ]
    for copy in copies:
        copy.start()
    first[edge:, :] = jnp.zeros_like(first[edge:, :])
    second[edge:, :] = jnp.zeros_like(second[edge:, :])
    copies[0].wait()
    lower, upper = rates_here[0:RIM, :], rates_here[own - RIM : own, :]
    first[edge : edge + RIM, :] = jnp.where(even, upper, lower)
    second[edge : edge + RIM, :] = jnp.where(even, lower, upper)
    for copy in copies[1:]:
        copy.wait()


def prep_own_kernel(
    spikes, decay, gains, feet, s3, p3, pinv3, z3, rows, pay, columns, feet_here, sem
):
    own = s3.shape[0]
    chunks = own + 2 * RIM
    fetch = pltpu.make_async_copy(feet, feet_here, sem)
    fetch.start()
    middle, whole, prefix_col, inverse_col = gain_columns(gains[...])
    columns[0] = prefix_col
    columns[1] = inverse_col
    rows[...] = jnp.ones_like(rows)
    rows[0, chunks : chunks + 1, :] = middle
    pay[...] = jnp.zeros_like(pay)
    pay[0, chunks : chunks + 1, :] = whole
    shared = middle, prefix_col, inverse_col, table(spikes.shape[1], False)
    for i in range(own):
        field = spikes[i * LANES : (i + 1) * LANES, :]
        at = [ref.at[i] for ref in (s3, p3, pinv3, z3)]
        prep_chunk(i + RIM, decay[i : i + 1, :], field, shared, *at, rows, pay)
    fetch.wait()


def sides(even, first, second):
    return jnp.where(even, second, first), jnp.where(even, first, second)


def prep_rim_kernel(first, second, columns, rows_own, pay_own, s3, p3, pinv3, z3, rows, pay):
    rims, frames = s3.shape[0], s3.shape[1]
    own = rows_own.shape[1] - padded8(1)
    chunks = own + 2 * RIM
    middle = rows_own[0, chunks : chunks + 1, :]
    shared = middle, columns[0], columns[1], table(frames, False)
    rows[...] = rows_own[...]
    pay[...] = pay_own[...]
    even = lax.axis_index("tile") % 2 == 0
    below, above = sides(even, first[...], second[...])
    for i in range(rims):
        message = below if i < RIM else above
        j = i % RIM
        c = i if i < RIM else own + i
        at = [ref.at[i] for ref in (s3, p3, pinv3, z3)]
        field = message[j * LANES : (j + 1) * LANES, :]
        rate = message[RIM * LANES + j : RIM * LANES + j + 1, :]
        prep_chunk(c, rate, field, shared, *at, rows, pay)


def block_totals(pays, chunks, rows):
    return [rows[2] * pays[m, 0, chunks : chunks + 1, :] for m in range(pays.shape[0])]


def step_size(stats):
    both = jnp.sum(jnp.sum(stats[...], axis=0), axis=1, keepdims=True)
    return jnp.broadcast_to(both[0:1] / (both[1:2] + 1e-06), (1, LANES))


def update_kernel(s3, g3, stats, p3, pinv3, rows, new3, z3, pay):
    chunks = chunk_count(s3)
    frames = g3.shape[1]
    sums_table = table(frames, False)
    size = step_size(stats)
    pay[...] = jnp.zeros_like(pay)
    for c in range(chunks):
        field = jnp.maximum(chunk(s3, c)[...] - size * g3[c], 0.0)
        z = summed(sums_table, field * rows[0, c : c + 1, :] * chunk(pinv3, c)[...])
        if len(new3) == 2:
            chunk(new3, c)[...] = field
        elif RIM <= c < chunks - RIM:
            new3[0][c - RIM] = field
        chunk(z3, c)[...] = z
        last = chunk(p3, c)[frames - 1 : frames, :]
        pay[c : c + 1, :] = last * z[frames - 1 : frames, :]


def final_kernel(s3, g3, stats, out, here, sems):
    size = step_size(stats)
    own = s3.shape[0]
    rows = out.shape[0] // PARTS
    copies = [
        pltpu.make_async_copy(
            here.at[pl.ds(i * rows, rows)], out.at[pl.ds(i * rows, rows)], sems.at[i]
        )
        for i in range(PARTS)
    ]
    for i in range(own):
        field = jnp.maximum(s3[i] - size * g3[i + RIM], 0.0)
        here[i * LANES : (i + 1) * LANES, :] = field.T
        if (i + 1) % (own // PARTS) == 0:
            copies[i // (own // PARTS)].start()
    for copy in copies:
        copy.wait()


def picked(ext, pattern, q):
    parts = [
        ext[pl.ds(pl.multiple_of(pattern[k, q] * NEU_BLOCK, NEU_BLOCK), NEU_BLOCK), :]
        for k in range(K)
    ]
    return jnp.concatenate(parts, axis=0)


def foot_of(feet, q):
    return feet[q * PIX_BLOCK : (q + 1) * PIX_BLOCK, :]


def note_places(pattern, place, start, stop):
    for q in range(start, stop):
        for v in range(2 * HB + 1):
            place[q, v] = -1
        for k in range(K):
            place[q, pattern[k, q] - q] = k


def pull_back(pattern, ext, feet, record, contrib, q):
    foot = foot_of(feet, q)
    fitted = jnp.dot(foot, picked(ext, pattern, q), preferred_element_type=F32)
    residual = (fitted - foot_of(record, q).astype(F32)).astype(BF16)
    contrib[q * K * NEU_BLOCK : (q + 1) * K * NEU_BLOCK, :] = lax.dot_general(
        foot, residual, (((0,), (0,)), ((), ())), preferred_element_type=F32
    )


def gathered(contrib, place, c, ranges):
    frames = contrib.shape[1]
    per_chunk = LANES // NEU_BLOCK
    halves = []
    for b in range(c * per_chunk, (c + 1) * per_chunk):
        total = jnp.zeros((NEU_BLOCK, frames), F32)
        for v in range(2 * HB + 1):
            q = b - v
            if any(start <= q < stop for start, stop in ranges):
                k = place[q, v]
                at = pl.multiple_of((q * K + jnp.maximum(k, 0)) * NEU_BLOCK, NEU_BLOCK)
                value = contrib[pl.ds(at, NEU_BLOCK), :]
                if v % 2:
                    value = jnp.where(k >= 0, value, 0.0)
                total = total + value
        halves.append(total)
    return jnp.concatenate(halves, axis=0).T


def edge_kernel(
    pattern, z3, p3, rows, pay, pays, feet, record, ext, zones, spill, send_a, send_b, *rest
):
    *traces, contrib, place = rest
    chunks = chunk_count(z3)
    stripe = pattern.shape[1]
    edge = 2 * HB
    me = lax.axis_index("tm")
    totals = block_totals(pay, chunks, rows)
    carry = jnp.zeros_like(totals[0])
    for m in range(pays.shape[0]):
        carry = jnp.where(m < me, pays[m] + totals[m] * carry, carry)
    carry = carry * rows[1]
    ranges = ((0, edge), (stripe - edge, stripe))
    for start, stop in ranges:
        note_places(pattern, place, start, stop)

    def trace(c):
        field = (chunk(p3, c)[...] * (chunk(z3, c)[...] + carry[c : c + 1, :])).T
        ext[c * LANES : (c + 1) * LANES, :] = field.astype(BF16)
        if traces and RIM <= c < chunks - RIM:
            traces[0][(c - RIM) * LANES : (c - RIM + 1) * LANES, :] = field

    near = 4 * RIM
    for c in [*range(near), *range(chunks - near, chunks)]:
        trace(c)
    for start, stop in ranges:
        for q in range(start, stop):
            pull_back(pattern, ext, feet, record, contrib, q)
    for c in range(near, chunks - near):
        trace(c)
    even = lax.axis_index("tile") % 2 == 0
    for i in range(2 * RIM):
        below = gathered(contrib, place, i, ranges)
        above = gathered(contrib, place, chunks - 2 * RIM + i, ranges)
        zones[i] = below
        zones[2 * RIM + i] = above
        send_a[i] = jnp.where(even, above, below).astype(BF16)
        send_b[i] = jnp.where(even, below, above).astype(BF16)
        spill[i] = gathered(contrib, place, 2 * RIM + i, ranges)
        spill[2 * RIM + i] = gathered(contrib, place, chunks - 4 * RIM + i, ranges)


def adjoint_chunk(sums_table, field, p, pinv, rows, c, r3, pay):
    frames = field.shape[0]
    r = summed(sums_table, field * p)
    r3[...] = r
    gain = rows[0, c : c + 1, :]
    pay[0, c : c + 1, :] = rows[1, c : c + 1, :] * r[0:1, :]
    ends = p[frames - 1 : frames, :] * gain * gain
    pay[1, c : c + 1, :] = ends * jnp.sum(pinv * pinv * r, axis=0, keepdims=True)


def inner_kernel(pattern, p3, pinv3, rows, ext, spill, feet, record, traces, r3, pay, *rest):
    if traces:
        out, contrib, place, sem = rest
        copy = pltpu.make_async_copy(traces[0], out, sem)
        copy.start()
    else:
        contrib, place = rest
    chunks = chunk_count(p3)
    frames = spill.shape[1]
    stripe = pattern.shape[1]
    edge = 2 * HB
    per_chunk = LANES // NEU_BLOCK
    note_places(pattern, place, edge, stripe - edge)
    sums_table = table(frames, True)
    pay[...] = jnp.zeros_like(pay)
    inner = chunks - 4 * RIM
    q = edge
    for i in range(inner):
        c = i + 2 * RIM
        while q < min((c + 1) * per_chunk, stripe - edge):
            pull_back(pattern, ext, feet, record, contrib, q)
            q += 1
        field = gathered(contrib, place, c, ((edge, stripe - edge),))
        if i < 2 * RIM:
            field = field + spill[i]
        if i >= inner - 2 * RIM:
            field = field + spill[i - inner + 4 * RIM]
        p, pinv = chunk(p3, c)[...], chunk(pinv3, c)[...]
        adjoint_chunk(sums_table, field, p, pinv, rows, c, r3.at[i], pay)
    if traces:
        copy.wait()


def border_kernel(zones, got_a, got_b, p3, pinv3, rows, pay_inner, r3, pay):
    chunks = chunk_count(p3)
    frames = zones.shape[1]
    sums_table = table(frames, True)
    pay[...] = pay_inner[...]
    even = lax.axis_index("tile") % 2 == 0
    for i in range(2 * RIM):
        both = sides(even, got_a[i].astype(F32), got_b[i].astype(F32))
        for side, c in ((0, i), (1, chunks - 2 * RIM + i)):
            at = side * 2 * RIM + i
            field = zones[at] + both[side]
            p, pinv = chunk(p3, c)[...], chunk(pinv3, c)[...]
            adjoint_chunk(sums_table, field, p, pinv, rows, c, r3.at[at], pay)


def direction_kernel(
    pattern, r_inner, r_border, p3, pinv3, rows, pay, pays, feet, g3, stats, ext
):
    chunks, frames = g3.shape[0], g3.shape[1]
    own = chunks - 2 * RIM
    stripe = pattern.shape[1]
    me = lax.axis_index("tm")
    totals = block_totals(pay, chunks, rows)
    blocks = pays.shape[0]
    entering = [None] * blocks
    state = jnp.zeros_like(totals[0])
    for m in reversed(range(blocks)):
        entering[m] = state
        state = pays[m, 0] + totals[m] * state
    carry = jnp.zeros_like(totals[0])
    adjoint = jnp.zeros_like(totals[0])
    for m in range(blocks):
        end = pays[m, 1] + pay[m, 1] * entering[m]
        carry = jnp.where(m < me, end + totals[m] * carry, carry)
        adjoint = jnp.where(m == me, entering[m], adjoint)
    carry = carry * rows[1]
    sums_table = table(frames, False)
    grad_sq = jnp.zeros((8, LANES), F32)
    image_sq = jnp.zeros((8, frames), F32)
    per_chunk = LANES // NEU_BLOCK
    q = 0
    for c in range(chunks):
        p, pinv = chunk(p3, c)[...], chunk(pinv3, c)[...]
        if c < 2 * RIM:
            r = r_border[c]
        elif c >= chunks - 2 * RIM:
            r = r_border[c - chunks + 4 * RIM]
        else:
            r = r_inner[c - 2 * RIM]
        gain = rows[0, c : c + 1, :]
        gradient = gain * pinv * (r + p[frames - 1 : frames, :] * adjoint[c : c + 1, :])
        g3[c] = gradient
        if RIM <= c < RIM + own:
            grad_sq += jnp.sum((gradient * gradient).reshape(frames // 8, 8, LANES), axis=0)
        z = summed(sums_table, gain * gradient * pinv)
        field = (p * (z + carry[c : c + 1, :])).T
        ext[c * LANES : (c + 1) * LANES, :] = field.astype(BF16)
        while q < stripe and q + 2 * HB < (c + 1) * per_chunk:
            image = jnp.dot(foot_of(feet, q), picked(ext, pattern, q), preferred_element_type=F32)
            image_sq += jnp.sum((image * image).reshape(PIX_BLOCK // 8, 8, frames), axis=0)
            q += 1
    both = jnp.concatenate(
        [
            jnp.sum(grad_sq, axis=0, keepdims=True),
            jnp.sum(image_sq, axis=0, keepdims=True),
        ],
        axis=0,
    )
    stats[...] = jnp.broadcast_to(both[None], stats.shape)


def f32(*shape):
    return jax.ShapeDtypeStruct(shape, F32)


def bf16(*shape):
    return jax.ShapeDtypeStruct(shape, BF16)


def call(
    kernel, name, micros, outs, args, scratch=(), far=(), far_out=(), keep=(), limit=16
):
    def spec(place, arg):
        if place in far:
            return HBM
        return SMEM if arg.dtype == jnp.int32 else VMEM

    in_specs = [jax.tree.map(lambda x: spec(i, x), arg) for i, arg in enumerate(args)]
    in_specs.append(jax.tree.map(lambda _: VMEM, keep))

    def body(*refs):
        kernel(*refs[: len(args)], *refs[len(args) + 1 :])

    return pl.pallas_call(
        body,
        name=name,
        out_shape=outs,
        in_specs=in_specs,
        out_specs=tuple(
            jax.tree.map(lambda _: HBM if place in far_out else VMEM, out)
            for place, out in enumerate(outs)
        ),
        scratch_shapes=scratch,
        compiler_params=pltpu.CompilerParams(vmem_limit_bytes=int(limit * 2**20)),
        cost_estimate=pl.CostEstimate(
            flops=int(micros * 1e8), bytes_accessed=int(micros * 3e6), transcendentals=0
        ),
    )(*args, keep)


def swapped(first, second):
    size = lax.axis_size("tile")

    def pairs(start):
        both = [(i, i + 1) for i in range(start, size - 1, 2)]
        return both + [(j, i) for i, j in both]

    return lax.ppermute(first, "tile", pairs(0)), lax.ppermute(second, "tile", pairs(1))


def per_device(recording, footprints, pattern, decay, frame_gain, spikes):
    neurons, frames = spikes.shape
    stripe = pattern.shape[0]
    pattern = pattern.T
    own = neurons // LANES
    chunks = own + 2 * RIM
    lines = own + padded8(1)
    devices = lax.axis_size("tile") * lax.axis_size("tm")
    split = (f32(own, frames, LANES), f32(2 * RIM, frames, LANES))
    message = f32(RIM * LANES + padded8(RIM), frames)
    gains = frame_gain.reshape(1, frames)
    first, second, rates, spikes = call(
        rims_kernel,
        "rims",
        1.0,
        (message, message, f32(own, LANES), f32(neurons, frames)),
        (spikes, decay.reshape(own, LANES)),
        [pltpu.SemaphoreType.DMA((4,))],
        far=(0, 1),
        limit=52,
    )
    first, second = swapped(first, second)
    *owns, rows, pay, columns, footprints = call(
        prep_own_kernel,
        "prep_own",
        1.6,
        (split[0],) * 4
        + (f32(3, lines, LANES), f32(2, lines, LANES), f32(2, frames, LANES))
        + (bf16(*footprints.shape),),
        (spikes, rates, gains, footprints),
        [pltpu.SemaphoreType.DMA],
        far=(3,),
        limit=44,
    )
    *rims, rows, pay = call(
        prep_rim_kernel,
        "prep_rim",
        0.3,
        (split[1],) * 4 + (f32(3, lines, LANES), f32(2, lines, LANES)),
        (first, second, columns, rows, pay),
    )
    s3, p3, pinv3, z3 = zip(owns, rims)
    constants = lax.all_gather(pay, "tm")
    pays = constants[:, 0]
    scratch = [
        pltpu.VMEM((stripe * K * NEU_BLOCK, frames), F32),
        pltpu.SMEM((stripe, 2 * HB + 1), jnp.int32),
    ]
    staged = [pltpu.VMEM((neurons, frames), F32), pltpu.SemaphoreType.DMA((PARTS,))]
    zone = (2 * RIM, frames, LANES)
    border = (4 * RIM, frames, LANES)
    for iteration in range(ITERS):
        ends = iteration == ITERS - 1
        ext, zones, spill, send_a, send_b, *traces = call(
            edge_kernel,
            "edge",
            2.5,
            (
                bf16(chunks * LANES, frames),
                f32(*border),
                f32(*border),
                bf16(*zone),
                bf16(*zone),
            )
            + ((f32(neurons, frames),) if ends else ()),
            (pattern, z3, p3, rows, constants, pays, footprints, recording),
            scratch,
            keep=(s3[0],) if ends else (),
        )
        got_a, got_b = swapped(send_a, send_b)
        held = (s3[0],) if ends else ()
        r_inner, pay, *traces = call(
            inner_kernel,
            "inner",
            4.0,
            (f32(chunks - 4 * RIM, frames, LANES), f32(2, lines, LANES))
            + ((f32(neurons, frames),) if ends else ()),
            (pattern, p3, pinv3, rows, ext, spill, footprints, recording, traces),
            scratch + ([pltpu.SemaphoreType.DMA] if ends else []),
            far_out=(2,),
            keep=held,
        )
        r_border, pay = call(
            border_kernel,
            "border",
            0.3,
            (f32(*border), f32(2, lines, LANES)),
            (zones, got_a, got_b, p3, pinv3, rows, pay),
            keep=held,
        )
        pays = lax.all_gather(pay, "tm")
        g3, stats = call(
            direction_kernel,
            "direction",
            4.0,
            (f32(chunks, frames, LANES), f32(devices, 2, LANES)),
            (pattern, r_inner, r_border, p3, pinv3, rows, constants, pays, footprints),
            [pltpu.VMEM((chunks * LANES, frames), BF16)],
            keep=held,
        )
        stats = lax.all_to_all(stats, ("tile", "tm"), 0, 0)
        if ends:
            (out,) = call(
                final_kernel,
                "final",
                1.4,
                (f32(neurons, frames),),
                (s3[0], g3, stats),
                staged,
                far_out=(0,),
            )
            return out, traces[0]
        s3, z3, pay = call(
            update_kernel,
            "update",
            0.6,
            (split if iteration < ITERS - 2 else split[:1], split, f32(lines, LANES)),
            (s3, g3, stats, p3, pinv3, rows),
        )
        pays = lax.all_gather(pay, "tm")


def solution(mesh):
    return jax.shard_map(
        per_device,
        mesh=mesh,
        in_specs=(
            P("tile", "tm"),
            P("tile", None),
            P("tile", None),
            P("tile"),
            P("tm"),
            P("tile", "tm"),
        ),
        out_specs=(P("tile", "tm"), P("tile", "tm")),
        check_vma=False,
    )
```

```python
import jax
import jax.numpy as jnp
from jax import lax
from jax.experimental import pallas as pl
from jax.experimental.pallas import tpu as pltpu
from jax.sharding import PartitionSpec as P

NEU_BLOCK = 64
PIX_BLOCK = 256
PARTS = 4
K = 4
HB = 2
ITERS = 2
LANES = 128
RIM = HB * NEU_BLOCK // LANES
F32 = jnp.float32
BF16 = jnp.bfloat16
VMEM = pl.BlockSpec(memory_space=pltpu.VMEM)
HBM = pl.BlockSpec(memory_space=pltpu.HBM)
SMEM = pl.BlockSpec(memory_space=pltpu.SMEM)


def padded8(rows):
    return -(-rows // 8) * 8


def table(frames, reverse):
    row = lax.broadcasted_iota(jnp.int32, (frames, 2 * frames), 0)
    col = lax.broadcasted_iota(jnp.int32, (frames, 2 * frames), 1)
    col = jnp.where(col >= frames, col - frames, col)
    keep = col >= row if reverse else col <= row
    return jnp.where(keep, 1.0, 0.0).astype(BF16)


def summed(sums_table, values):
    high = values.astype(BF16)
    low = (values - high.astype(F32)).astype(BF16)
    both = jnp.concatenate([high, low], axis=0)
    return jnp.dot(sums_table, both, preferred_element_type=F32)


def powers(log_decay, frames, mid, sign):
    groups = frames // 8
    coarse = (8 * lax.broadcasted_iota(jnp.int32, (groups, LANES), 0) - mid).astype(F32) * sign
    fine = lax.broadcasted_iota(jnp.int32, (8, LANES), 0).astype(F32) * sign
    coarse = jnp.exp(coarse * log_decay)
    fine = jnp.exp(fine * log_decay)
    return (coarse[:, None, :] * fine[None, :, :]).reshape(frames, LANES)


def chunk(field, c):
    own, rim = field
    inner = own.shape[0]
    if c < RIM:
        return rim.at[c]
    if c >= RIM + inner:
        return rim.at[c - inner]
    return own.at[c - RIM]


def chunk_count(field):
    return field[0].shape[0] + field[1].shape[0]


def prep_chunk(c, rate, field, gains, s3, p3, pinv3, z3, rows, pay):
    frames = field.shape[1]
    middle, prefix_col, inverse_col, sums_table = gains
    mid = frames // 2 - 1
    rate = jnp.where(rate > 0.0, rate, 1.0)
    log_rate = jnp.log(rate)
    gain = jnp.sqrt(1.0 - rate * rate)
    p = powers(log_rate, frames, mid, 1.0) * prefix_col
    pinv = powers(log_rate, frames, mid, -1.0) * inverse_col
    field = field.T
    z = summed(sums_table, field * gain * pinv)
    last = p[frames - 1 : frames, :]
    s3[...] = field
    p3[...] = p
    pinv3[...] = pinv
    z3[...] = z
    half = rate
    for _ in range(frames.bit_length() - 2):
        half = half * half
    rows[0, c : c + 1, :] = gain
    rows[1, c : c + 1, :] = half * middle
    rows[2, c : c + 1, :] = half * half
    pay[0, c : c + 1, :] = last * z[frames - 1 : frames, :]
    scale = last * gain
    pay[1, c : c + 1, :] = scale * scale * jnp.sum(pinv * pinv, axis=0, keepdims=True)


def gain_columns(gains):
    frames = gains.shape[1]
    mid = frames // 2 - 1
    lane = lax.broadcasted_iota(jnp.int32, (8, frames), 1)
    prefix = jnp.broadcast_to(gains, (8, frames))
    step = 1
    while step < frames:
        prefix = prefix * jnp.where(lane >= step, pltpu.roll(prefix, step, 1), 1.0)
        step *= 2
    middle = jnp.broadcast_to(prefix[0:1, mid : mid + 1], (1, LANES))
    whole = jnp.broadcast_to(prefix[0:1, frames - 1 : frames], (1, LANES))
    prefix_col = jnp.broadcast_to(prefix[0:1] / middle, (LANES, frames)).T
    inverse_col = jnp.broadcast_to(middle / prefix[0:1], (LANES, frames)).T
    return middle, whole, prefix_col, inverse_col


def rims_kernel(spikes, decay, first, second, rates_here, spikes_here, sems):
    edge = RIM * LANES
    neurons = spikes.shape[0]
    own = decay.shape[0]
    even = lax.axis_index("tile") % 2 == 0
    top = jnp.where(even, neurons - edge, 0)
    bottom = jnp.where(even, 0, neurons - edge)
    copies = [
        pltpu.make_async_copy(decay, rates_here, sems.at[0]),
        pltpu.make_async_copy(
            spikes.at[pl.ds(pl.multiple_of(top, LANES), edge)], first.at[pl.ds(0, edge)], sems.at[1]
        ),
        pltpu.make_async_copy(
            spikes.at[pl.ds(pl.multiple_of(bottom, LANES), edge)],
            second.at[pl.ds(0, edge)],
            sems.at[2],
        ),
        pltpu.make_async_copy(spikes, spikes_here, sems.at[3]),
    ]
    for copy in copies:
        copy.start()
    first[edge:, :] = jnp.zeros_like(first[edge:, :])
    second[edge:, :] = jnp.zeros_like(second[edge:, :])
    copies[0].wait()
    lower, upper = rates_here[0:RIM, :], rates_here[own - RIM : own, :]
    first[edge : edge + RIM, :] = jnp.where(even, upper, lower)
    second[edge : edge + RIM, :] = jnp.where(even, lower, upper)
    for copy in copies[1:]:
        copy.wait()


def prep_own_kernel(
    spikes, decay, gains, feet, s3, p3, pinv3, z3, rows, pay, columns, feet_ends, sems
):
    own = s3.shape[0]
    chunks = own + 2 * RIM
    size = feet_ends.shape[0] // 2
    fetches = [
        pltpu.make_async_copy(
            feet.at[pl.ds(start, size)], feet_ends.at[pl.ds(i * size, size)], sems.at[i]
        )
        for i, start in enumerate((0, feet.shape[0] - size))
    ]
    for fetch in fetches:
        fetch.start()
    middle, whole, prefix_col, inverse_col = gain_columns(gains[...])
    columns[0] = prefix_col
    columns[1] = inverse_col
    rows[...] = jnp.ones_like(rows)
    rows[0, chunks : chunks + 1, :] = middle
    pay[...] = jnp.zeros_like(pay)
    pay[0, chunks : chunks + 1, :] = whole
    shared = middle, prefix_col, inverse_col, table(spikes.shape[1], False)
    for i in range(own):
        field = spikes[i * LANES : (i + 1) * LANES, :]
        at = [ref.at[i] for ref in (s3, p3, pinv3, z3)]
        prep_chunk(i + RIM, decay[i : i + 1, :], field, shared, *at, rows, pay)
    for fetch in fetches:
        fetch.wait()


def sides(even, first, second):
    return jnp.where(even, second, first), jnp.where(even, first, second)


def prep_rim_kernel(first, second, columns, rows_own, pay_own, s3, p3, pinv3, z3, rows, pay):
    rims, frames = s3.shape[0], s3.shape[1]
    own = rows_own.shape[1] - padded8(1)
    chunks = own + 2 * RIM
    middle = rows_own[0, chunks : chunks + 1, :]
    shared = middle, columns[0], columns[1], table(frames, False)
    rows[...] = rows_own[...]
    pay[...] = pay_own[...]
    even = lax.axis_index("tile") % 2 == 0
    below, above = sides(even, first[...], second[...])
    for i in range(rims):
        message = below if i < RIM else above
        j = i % RIM
        c = i if i < RIM else own + i
        at = [ref.at[i] for ref in (s3, p3, pinv3, z3)]
        field = message[j * LANES : (j + 1) * LANES, :]
        rate = message[RIM * LANES + j : RIM * LANES + j + 1, :]
        prep_chunk(c, rate, field, shared, *at, rows, pay)


def block_totals(pays, chunks, rows):
    return [rows[2] * pays[m, 0, chunks : chunks + 1, :] for m in range(pays.shape[0])]


def step_size(stats):
    both = jnp.sum(jnp.sum(stats[...], axis=0), axis=1, keepdims=True)
    return jnp.broadcast_to(both[0:1] / (both[1:2] + 1e-06), (1, LANES))


def update_kernel(s3, g3, stats, p3, pinv3, rows, new3, z3, pay):
    chunks = chunk_count(s3)
    frames = g3.shape[1]
    sums_table = table(frames, False)
    size = step_size(stats)
    pay[...] = jnp.zeros_like(pay)
    for c in range(chunks):
        field = jnp.maximum(chunk(s3, c)[...] - size * g3[c], 0.0)
        z = summed(sums_table, field * rows[0, c : c + 1, :] * chunk(pinv3, c)[...])
        if len(new3) == 2:
            chunk(new3, c)[...] = field
        elif RIM <= c < chunks - RIM:
            new3[0][c - RIM] = field
        chunk(z3, c)[...] = z
        last = chunk(p3, c)[frames - 1 : frames, :]
        pay[c : c + 1, :] = last * z[frames - 1 : frames, :]


def final_kernel(s3, g3, stats, out, here, sems):
    size = step_size(stats)
    own = s3.shape[0]
    rows = out.shape[0] // PARTS
    copies = [
        pltpu.make_async_copy(
            here.at[pl.ds(i * rows, rows)], out.at[pl.ds(i * rows, rows)], sems.at[i]
        )
        for i in range(PARTS)
    ]
    for i in range(own):
        field = jnp.maximum(s3[i] - size * g3[i + RIM], 0.0)
        here[i * LANES : (i + 1) * LANES, :] = field.T
        if (i + 1) % (own // PARTS) == 0:
            copies[i // (own // PARTS)].start()
    for copy in copies:
        copy.wait()


def picked(ext, pattern, q):
    parts = [
        ext[pl.ds(pl.multiple_of(pattern[k, q] * NEU_BLOCK, NEU_BLOCK), NEU_BLOCK), :]
        for k in range(K)
    ]
    return jnp.concatenate(parts, axis=0)


def block_of(field, q):
    return field[q * PIX_BLOCK : (q + 1) * PIX_BLOCK, :]


def foot_of(feet, q):
    ends, inner = feet
    near = ends.shape[0] // PIX_BLOCK // 2
    count = inner.shape[0] // PIX_BLOCK
    if q < near:
        return block_of(ends, q)
    if q >= near + count:
        return block_of(ends, q - count)
    return block_of(inner, q - near)


def note_places(pattern, place, start, stop):
    for q in range(start, stop):
        for v in range(2 * HB + 1):
            place[q, v] = -1
        for k in range(K):
            place[q, pattern[k, q] - q] = k


def pull_back(pattern, ext, feet, record, contrib, q):
    foot = foot_of(feet, q)
    fitted = jnp.dot(foot, picked(ext, pattern, q), preferred_element_type=F32)
    residual = (fitted - block_of(record, q).astype(F32)).astype(BF16)
    contrib[q * K * NEU_BLOCK : (q + 1) * K * NEU_BLOCK, :] = lax.dot_general(
        foot, residual, (((0,), (0,)), ((), ())), preferred_element_type=F32
    )


def gathered(contrib, place, c, ranges):
    frames = contrib.shape[1]
    per_chunk = LANES // NEU_BLOCK
    halves = []
    for b in range(c * per_chunk, (c + 1) * per_chunk):
        total = jnp.zeros((NEU_BLOCK, frames), F32)
        for v in range(2 * HB + 1):
            q = b - v
            if any(start <= q < stop for start, stop in ranges):
                k = place[q, v]
                at = pl.multiple_of((q * K + jnp.maximum(k, 0)) * NEU_BLOCK, NEU_BLOCK)
                value = contrib[pl.ds(at, NEU_BLOCK), :]
                if v % 2:
                    value = jnp.where(k >= 0, value, 0.0)
                total = total + value
        halves.append(total)
    return jnp.concatenate(halves, axis=0).T


def edge_kernel(
    pattern, z3, p3, rows, pay, pays, feet, record, ext, zones, spill, send_a, send_b, *rest
):
    if len(rest) == 4:
        feet_inner, contrib, place, sem = rest
        traces = ()
        size = feet[0].shape[0] // 2
        fetch = pltpu.make_async_copy(
            feet[1].at[pl.ds(size, feet_inner.shape[0])], feet_inner, sem
        )
        fetch.start()
        feet = (feet[0], feet_inner)
    else:
        *traces, contrib, place = rest
        fetch = None
    chunks = chunk_count(z3)
    stripe = pattern.shape[1]
    edge = 2 * HB
    me = lax.axis_index("tm")
    totals = block_totals(pay, chunks, rows)
    carry = jnp.zeros_like(totals[0])
    for m in range(pays.shape[0]):
        carry = jnp.where(m < me, pays[m] + totals[m] * carry, carry)
    carry = carry * rows[1]
    ranges = ((0, edge), (stripe - edge, stripe))
    for start, stop in ranges:
        note_places(pattern, place, start, stop)

    def trace(c):
        field = (chunk(p3, c)[...] * (chunk(z3, c)[...] + carry[c : c + 1, :])).T
        ext[c * LANES : (c + 1) * LANES, :] = field.astype(BF16)
        if traces and RIM <= c < chunks - RIM:
            traces[0][(c - RIM) * LANES : (c - RIM + 1) * LANES, :] = field

    near = 4 * RIM
    for c in [*range(near), *range(chunks - near, chunks)]:
        trace(c)
    for start, stop in ranges:
        for q in range(start, stop):
            pull_back(pattern, ext, feet, record, contrib, q)
    for c in range(near, chunks - near):
        trace(c)
    even = lax.axis_index("tile") % 2 == 0
    for i in range(2 * RIM):
        below = gathered(contrib, place, i, ranges)
        above = gathered(contrib, place, chunks - 2 * RIM + i, ranges)
        zones[i] = below
        zones[2 * RIM + i] = above
        send_a[i] = jnp.where(even, above, below).astype(BF16)
        send_b[i] = jnp.where(even, below, above).astype(BF16)
        spill[i] = gathered(contrib, place, 2 * RIM + i, ranges)
        spill[2 * RIM + i] = gathered(contrib, place, chunks - 4 * RIM + i, ranges)
    if fetch is not None:
        fetch.wait()


def adjoint_chunk(sums_table, field, p, pinv, rows, c, r3, pay):
    frames = field.shape[0]
    r = summed(sums_table, field * p)
    r3[...] = r
    gain = rows[0, c : c + 1, :]
    pay[0, c : c + 1, :] = rows[1, c : c + 1, :] * r[0:1, :]
    ends = p[frames - 1 : frames, :] * gain * gain
    pay[1, c : c + 1, :] = ends * jnp.sum(pinv * pinv * r, axis=0, keepdims=True)


def inner_kernel(pattern, p3, pinv3, rows, ext, spill, feet, record, traces, r3, pay, *rest):
    if traces:
        out, contrib, place, sem = rest
        copy = pltpu.make_async_copy(traces[0], out, sem)
        copy.start()
    else:
        contrib, place = rest
    chunks = chunk_count(p3)
    frames = spill.shape[1]
    stripe = pattern.shape[1]
    edge = 2 * HB
    note_places(pattern, place, edge, stripe - edge)
    sums_table = table(frames, True)
    pay[...] = jnp.zeros_like(pay)
    inner = chunks - 4 * RIM
    for q in range(edge, stripe - edge):
        pull_back(pattern, ext, feet, record, contrib, q)
    for i in range(inner):
        c = i + 2 * RIM
        field = gathered(contrib, place, c, ((edge, stripe - edge),))
        if i < 2 * RIM:
            field = field + spill[i]
        if i >= inner - 2 * RIM:
            field = field + spill[i - inner + 4 * RIM]
        p, pinv = chunk(p3, c)[...], chunk(pinv3, c)[...]
        adjoint_chunk(sums_table, field, p, pinv, rows, c, r3.at[i], pay)
    if traces:
        copy.wait()


def border_kernel(zones, got_a, got_b, p3, pinv3, rows, pay_inner, r3, pay):
    chunks = chunk_count(p3)
    frames = zones.shape[1]
    sums_table = table(frames, True)
    pay[...] = pay_inner[...]
    even = lax.axis_index("tile") % 2 == 0
    for i in range(2 * RIM):
        both = sides(even, got_a[i].astype(F32), got_b[i].astype(F32))
        for side, c in ((0, i), (1, chunks - 2 * RIM + i)):
            at = side * 2 * RIM + i
            field = zones[at] + both[side]
            p, pinv = chunk(p3, c)[...], chunk(pinv3, c)[...]
            adjoint_chunk(sums_table, field, p, pinv, rows, c, r3.at[at], pay)


def direction_kernel(
    pattern, r_inner, r_border, p3, pinv3, rows, pay, pays, feet, g3, stats, ext
):
    chunks, frames = g3.shape[0], g3.shape[1]
    own = chunks - 2 * RIM
    stripe = pattern.shape[1]
    me = lax.axis_index("tm")
    totals = block_totals(pay, chunks, rows)
    blocks = pays.shape[0]
    entering = [None] * blocks
    state = jnp.zeros_like(totals[0])
    for m in reversed(range(blocks)):
        entering[m] = state
        state = pays[m, 0] + totals[m] * state
    carry = jnp.zeros_like(totals[0])
    adjoint = jnp.zeros_like(totals[0])
    for m in range(blocks):
        end = pays[m, 1] + pay[m, 1] * entering[m]
        carry = jnp.where(m < me, end + totals[m] * carry, carry)
        adjoint = jnp.where(m == me, entering[m], adjoint)
    carry = carry * rows[1]
    sums_table = table(frames, False)
    grad_sq = jnp.zeros((8, LANES), F32)
    for c in range(chunks):
        p, pinv = chunk(p3, c)[...], chunk(pinv3, c)[...]
        if c < 2 * RIM:
            r = r_border[c]
        elif c >= chunks - 2 * RIM:
            r = r_border[c - chunks + 4 * RIM]
        else:
            r = r_inner[c - 2 * RIM]
        gain = rows[0, c : c + 1, :]
        gradient = gain * pinv * (r + p[frames - 1 : frames, :] * adjoint[c : c + 1, :])
        g3[c] = gradient
        if RIM <= c < RIM + own:
            grad_sq += jnp.sum((gradient * gradient).reshape(frames // 8, 8, LANES), axis=0)
        z = summed(sums_table, gain * gradient * pinv)
        field = (p * (z + carry[c : c + 1, :])).T
        ext[c * LANES : (c + 1) * LANES, :] = field.astype(BF16)
    image_sq = jnp.zeros((8, frames), F32)
    for q in range(stripe):
        image = jnp.dot(foot_of(feet, q), picked(ext, pattern, q), preferred_element_type=F32)
        image_sq += jnp.sum((image * image).reshape(PIX_BLOCK // 8, 8, frames), axis=0)
    both = jnp.concatenate(
        [
            jnp.sum(grad_sq, axis=0, keepdims=True),
            jnp.sum(image_sq, axis=0, keepdims=True),
        ],
        axis=0,
    )
    if len(stats.shape) == 3:
        stats[...] = jnp.broadcast_to(both[None], stats.shape)
    else:
        stats[...] = jnp.concatenate([both, jnp.zeros((stats.shape[0] - 2, LANES), F32)], axis=0)


def f32(*shape):
    return jax.ShapeDtypeStruct(shape, F32)


def bf16(*shape):
    return jax.ShapeDtypeStruct(shape, BF16)


def call(
    kernel, name, micros, outs, args, scratch=(), far=(), far_out=(), keep=(), limit=16
):
    def spec(arg):
        if any(arg is other for other in far):
            return HBM
        return SMEM if arg.dtype == jnp.int32 else VMEM

    in_specs = [jax.tree.map(spec, arg) for arg in args]
    in_specs.append(jax.tree.map(lambda _: VMEM, keep))

    def body(*refs):
        kernel(*refs[: len(args)], *refs[len(args) + 1 :])

    return pl.pallas_call(
        body,
        name=name,
        out_shape=outs,
        in_specs=in_specs,
        out_specs=tuple(
            jax.tree.map(lambda _: HBM if place in far_out else VMEM, out)
            for place, out in enumerate(outs)
        ),
        scratch_shapes=scratch,
        compiler_params=pltpu.CompilerParams(vmem_limit_bytes=int(limit * 2**20)),
        cost_estimate=pl.CostEstimate(
            flops=int(micros * 1e8), bytes_accessed=int(micros * 3e6), transcendentals=0
        ),
    )(*args, keep)


def swapped(first, second):
    size = lax.axis_size("tile")

    def pairs(start):
        both = [(i, i + 1) for i in range(start, size - 1, 2)]
        return both + [(j, i) for i, j in both]

    return lax.ppermute(first, "tile", pairs(0)), lax.ppermute(second, "tile", pairs(1))


def per_device(recording, footprints, pattern, decay, frame_gain, spikes):
    neurons, frames = spikes.shape
    stripe = pattern.shape[0]
    pattern = pattern.T
    own = neurons // LANES
    chunks = own + 2 * RIM
    lines = own + padded8(1)
    devices = lax.axis_size("tile") * lax.axis_size("tm")
    split = (f32(own, frames, LANES), f32(2 * RIM, frames, LANES))
    message = f32(RIM * LANES + padded8(RIM), frames)
    gains = frame_gain.reshape(1, frames)
    rates = decay.reshape(own, LANES)
    first, second, rates, spikes = call(
        rims_kernel,
        "rims",
        1.0,
        (message, message, f32(own, LANES), f32(neurons, frames)),
        (spikes, rates),
        [pltpu.SemaphoreType.DMA((4,))],
        far=(spikes, rates),
        limit=52,
    )
    first, second = swapped(first, second)
    ends_size = 4 * HB * PIX_BLOCK
    *owns, rows, pay, columns, feet_ends = call(
        prep_own_kernel,
        "prep_own",
        1.6,
        (split[0],) * 4
        + (f32(3, lines, LANES), f32(2, lines, LANES), f32(2, frames, LANES))
        + (bf16(ends_size, K * NEU_BLOCK),),
        (spikes, rates, gains, footprints),
        [pltpu.SemaphoreType.DMA((2,))],
        far=(footprints,),
        limit=44,
    )
    *rims, rows, pay = call(
        prep_rim_kernel,
        "prep_rim",
        0.3,
        (split[1],) * 4 + (f32(3, lines, LANES), f32(2, lines, LANES)),
        (first, second, columns, rows, pay),
    )
    s3, p3, pinv3, z3 = zip(owns, rims)
    constants = lax.all_gather(pay, "tm")
    pays = constants[:, 0]
    scratch = [
        pltpu.VMEM((stripe * K * NEU_BLOCK, frames), F32),
        pltpu.SMEM((stripe, 2 * HB + 1), jnp.int32),
    ]
    staged = [pltpu.VMEM((neurons, frames), F32), pltpu.SemaphoreType.DMA((PARTS,))]
    zone = (2 * RIM, frames, LANES)
    border = (4 * RIM, frames, LANES)
    feet = (feet_ends, footprints)
    for iteration in range(ITERS):
        ends = iteration == ITERS - 1
        begins = iteration == 0
        ext, zones, spill, send_a, send_b, *more = call(
            edge_kernel,
            "edge",
            2.5,
            (
                bf16(chunks * LANES, frames),
                f32(*border),
                f32(*border),
                bf16(*zone),
                bf16(*zone),
            )
            + ((bf16(footprints.shape[0] - ends_size, K * NEU_BLOCK),) if begins else ())
            + ((f32(neurons, frames),) if ends else ()),
            (pattern, z3, p3, rows, constants, pays, feet, recording),
            scratch + ([pltpu.SemaphoreType.DMA] if begins else []),
            keep=(s3[0],) if ends else (),
            far=(footprints,),
            limit=42 if begins else 16,
        )
        if begins:
            feet = (feet_ends, more[0])
        traces = more[-1:] if ends else []
        got_a, got_b = swapped(send_a, send_b)
        held = (s3[0],) if ends else ()
        r_inner, pay, *traces = call(
            inner_kernel,
            "inner",
            4.0,
            (f32(chunks - 4 * RIM, frames, LANES), f32(2, lines, LANES))
            + ((f32(neurons, frames),) if ends else ()),
            (pattern, p3, pinv3, rows, ext, spill, feet, recording, traces),
            scratch + ([pltpu.SemaphoreType.DMA] if ends else []),
            far_out=(2,),
            keep=held,
        )
        r_border, pay = call(
            border_kernel,
            "border",
            0.3,
            (f32(*border), f32(2, lines, LANES)),
            (zones, got_a, got_b, p3, pinv3, rows, pay),
            keep=held,
        )
        pays = lax.all_gather(pay, "tm")
        g3, stats = call(
            direction_kernel,
            "direction",
            4.0,
            (f32(chunks, frames, LANES), f32(devices, 2, LANES) if ends else f32(8, LANES)),
            (pattern, r_inner, r_border, p3, pinv3, rows, constants, pays, feet),
            [pltpu.VMEM((chunks * LANES, frames), BF16)],
            keep=held,
        )
        if ends:
            stats = lax.all_to_all(stats, ("tile", "tm"), 0, 0)
        else:
            stats = lax.all_gather(stats, ("tile", "tm"))
        if ends:
            (out,) = call(
                final_kernel,
                "final",
                1.4,
                (f32(neurons, frames),),
                (s3[0], g3, stats),
                staged,
                far_out=(0,),
            )
            return out, traces[0]
        s3, z3, pay = call(
            update_kernel,
            "update",
            0.6,
            (split if iteration < ITERS - 2 else split[:1], split, f32(lines, LANES)),
            (s3, g3, stats, p3, pinv3, rows),
        )
        pays = lax.all_gather(pay, "tm")


def solution(mesh):
    return jax.shard_map(
        per_device,
        mesh=mesh,
        in_specs=(
            P("tile", "tm"),
            P("tile", None),
            P("tile", None),
            P("tile"),
            P("tm"),
            P("tile", "tm"),
        ),
        out_specs=(P("tile", "tm"), P("tile", "tm")),
        check_vma=False,
    )
```

```python
import jax
import jax.numpy as jnp
from jax import lax
from jax.experimental import pallas as pl
from jax.experimental.pallas import tpu as pltpu
from jax.sharding import PartitionSpec as P

NEU_BLOCK = 64
PIX_BLOCK = 256
PARTS = 4
K = 4
HB = 2
ITERS = 2
LANES = 128
RIM = HB * NEU_BLOCK // LANES
F32 = jnp.float32
BF16 = jnp.bfloat16
VMEM = pl.BlockSpec(memory_space=pltpu.VMEM)
HBM = pl.BlockSpec(memory_space=pltpu.HBM)
SMEM = pl.BlockSpec(memory_space=pltpu.SMEM)


def padded8(rows):
    return -(-rows // 8) * 8


def table(frames, reverse):
    row = lax.broadcasted_iota(jnp.int32, (frames, 2 * frames), 0)
    col = lax.broadcasted_iota(jnp.int32, (frames, 2 * frames), 1)
    col = jnp.where(col >= frames, col - frames, col)
    keep = col >= row if reverse else col <= row
    return jnp.where(keep, 1.0, 0.0).astype(BF16)


def summed(sums_table, values):
    high = values.astype(BF16)
    low = (values - high.astype(F32)).astype(BF16)
    both = jnp.concatenate([high, low], axis=0)
    return jnp.dot(sums_table, both, preferred_element_type=F32)


def powers(log_decay, frames, mid, sign):
    groups = frames // 8
    coarse = (8 * lax.broadcasted_iota(jnp.int32, (groups, LANES), 0) - mid).astype(F32) * sign
    fine = lax.broadcasted_iota(jnp.int32, (8, LANES), 0).astype(F32) * sign
    coarse = jnp.exp(coarse * log_decay)
    fine = jnp.exp(fine * log_decay)
    return (coarse[:, None, :] * fine[None, :, :]).reshape(frames, LANES)


def chunk(field, c):
    own, rim = field
    inner = own.shape[0]
    if c < RIM:
        return rim.at[c]
    if c >= RIM + inner:
        return rim.at[c - inner]
    return own.at[c - RIM]


def chunk_count(field):
    return field[0].shape[0] + field[1].shape[0]


def prep_chunk(c, rate, field, gains, s3, p3, pinv3, z3, rows, pay):
    frames = field.shape[1]
    middle, prefix_col, inverse_col, sums_table = gains
    mid = frames // 2 - 1
    rate = jnp.where(rate > 0.0, rate, 1.0)
    log_rate = jnp.log(rate)
    gain = jnp.sqrt(1.0 - rate * rate)
    p = powers(log_rate, frames, mid, 1.0) * prefix_col
    pinv = powers(log_rate, frames, mid, -1.0) * inverse_col
    field = field.T
    z = summed(sums_table, field * gain * pinv)
    last = p[frames - 1 : frames, :]
    s3[...] = field
    p3[...] = p
    pinv3[...] = pinv
    z3[...] = z
    half = rate
    for _ in range(frames.bit_length() - 2):
        half = half * half
    rows[0, c : c + 1, :] = gain
    rows[1, c : c + 1, :] = half * middle
    rows[2, c : c + 1, :] = half * half
    pay[0, c : c + 1, :] = last * z[frames - 1 : frames, :]
    scale = last * gain
    pay[1, c : c + 1, :] = scale * scale * jnp.sum(pinv * pinv, axis=0, keepdims=True)


def gain_columns(gains):
    frames = gains.shape[1]
    mid = frames // 2 - 1
    lane = lax.broadcasted_iota(jnp.int32, (8, frames), 1)
    prefix = jnp.broadcast_to(gains, (8, frames))
    step = 1
    while step < frames:
        prefix = prefix * jnp.where(lane >= step, pltpu.roll(prefix, step, 1), 1.0)
        step *= 2
    middle = jnp.broadcast_to(prefix[0:1, mid : mid + 1], (1, LANES))
    whole = jnp.broadcast_to(prefix[0:1, frames - 1 : frames], (1, LANES))
    prefix_col = jnp.broadcast_to(prefix[0:1] / middle, (LANES, frames)).T
    inverse_col = jnp.broadcast_to(middle / prefix[0:1], (LANES, frames)).T
    return middle, whole, prefix_col, inverse_col


def rims_kernel(spikes, decay, first, second, rates_here, spikes_here, sems):
    edge = RIM * LANES
    neurons = spikes.shape[0]
    own = decay.shape[0]
    even = lax.axis_index("tile") % 2 == 0
    top = jnp.where(even, neurons - edge, 0)
    bottom = jnp.where(even, 0, neurons - edge)
    copies = [
        pltpu.make_async_copy(decay, rates_here, sems.at[0]),
        pltpu.make_async_copy(
            spikes.at[pl.ds(pl.multiple_of(top, LANES), edge)], first.at[pl.ds(0, edge)], sems.at[1]
        ),
        pltpu.make_async_copy(
            spikes.at[pl.ds(pl.multiple_of(bottom, LANES), edge)],
            second.at[pl.ds(0, edge)],
            sems.at[2],
        ),
        pltpu.make_async_copy(spikes, spikes_here, sems.at[3]),
    ]
    for copy in copies:
        copy.start()
    first[edge:, :] = jnp.zeros_like(first[edge:, :])
    second[edge:, :] = jnp.zeros_like(second[edge:, :])
    copies[0].wait()
    lower, upper = rates_here[0:RIM, :], rates_here[own - RIM : own, :]
    first[edge : edge + RIM, :] = jnp.where(even, upper, lower)
    second[edge : edge + RIM, :] = jnp.where(even, lower, upper)
    for copy in copies[1:]:
        copy.wait()


def prep_own_kernel(
    spikes, decay, gains, feet, s3, p3, pinv3, z3, rows, pay, columns, feet_ends, sems
):
    own = s3.shape[0]
    chunks = own + 2 * RIM
    size = feet_ends.shape[0] // 2
    fetches = [
        pltpu.make_async_copy(
            feet.at[pl.ds(start, size)], feet_ends.at[pl.ds(i * size, size)], sems.at[i]
        )
        for i, start in enumerate((0, feet.shape[0] - size))
    ]
    for fetch in fetches:
        fetch.start()
    middle, whole, prefix_col, inverse_col = gain_columns(gains[...])
    columns[0] = prefix_col
    columns[1] = inverse_col
    rows[...] = jnp.ones_like(rows)
    rows[0, chunks : chunks + 1, :] = middle
    pay[...] = jnp.zeros_like(pay)
    pay[0, chunks : chunks + 1, :] = whole
    shared = middle, prefix_col, inverse_col, table(spikes.shape[1], False)
    for i in range(own):
        field = spikes[i * LANES : (i + 1) * LANES, :]
        at = [ref.at[i] for ref in (s3, p3, pinv3, z3)]
        prep_chunk(i + RIM, decay[i : i + 1, :], field, shared, *at, rows, pay)
    for fetch in fetches:
        fetch.wait()


def sides(even, first, second):
    return jnp.where(even, second, first), jnp.where(even, first, second)


def prep_rim_kernel(first, second, columns, rows_own, pay_own, s3, p3, pinv3, z3, rows, pay):
    rims, frames = s3.shape[0], s3.shape[1]
    own = rows_own.shape[1] - padded8(1)
    chunks = own + 2 * RIM
    middle = rows_own[0, chunks : chunks + 1, :]
    shared = middle, columns[0], columns[1], table(frames, False)
    rows[...] = rows_own[...]
    pay[...] = pay_own[...]
    even = lax.axis_index("tile") % 2 == 0
    below, above = sides(even, first[...], second[...])
    for i in range(rims):
        message = below if i < RIM else above
        j = i % RIM
        c = i if i < RIM else own + i
        at = [ref.at[i] for ref in (s3, p3, pinv3, z3)]
        field = message[j * LANES : (j + 1) * LANES, :]
        rate = message[RIM * LANES + j : RIM * LANES + j + 1, :]
        prep_chunk(c, rate, field, shared, *at, rows, pay)


def block_totals(pays, chunks, rows):
    return [rows[2] * pays[m, 0, chunks : chunks + 1, :] for m in range(pays.shape[0])]


def step_size(stats):
    both = jnp.sum(jnp.sum(stats[...], axis=0), axis=1, keepdims=True)
    return jnp.broadcast_to(both[0:1] / (both[1:2] + 1e-06), (1, LANES))


def update_kernel(s3, g3, stats, p3, pinv3, rows, new3, z3, pay):
    chunks = chunk_count(s3)
    frames = g3.shape[1]
    sums_table = table(frames, False)
    size = step_size(stats)
    pay[...] = jnp.zeros_like(pay)
    for c in range(chunks):
        field = jnp.maximum(chunk(s3, c)[...] - size * g3[c], 0.0)
        z = summed(sums_table, field * rows[0, c : c + 1, :] * chunk(pinv3, c)[...])
        if len(new3) == 2:
            chunk(new3, c)[...] = field
        elif RIM <= c < chunks - RIM:
            new3[0][c - RIM] = field
        chunk(z3, c)[...] = z
        last = chunk(p3, c)[frames - 1 : frames, :]
        pay[c : c + 1, :] = last * z[frames - 1 : frames, :]


def final_kernel(s3, g3, stats, out, here, sems):
    size = step_size(stats)
    own = s3.shape[0]
    rows = out.shape[0] // PARTS
    copies = [
        pltpu.make_async_copy(
            here.at[pl.ds(i * rows, rows)], out.at[pl.ds(i * rows, rows)], sems.at[i]
        )
        for i in range(PARTS)
    ]
    for i in range(own):
        field = jnp.maximum(s3[i] - size * g3[i + RIM], 0.0)
        here[i * LANES : (i + 1) * LANES, :] = field.T
        if (i + 1) % (own // PARTS) == 0:
            copies[i // (own // PARTS)].start()
    for copy in copies:
        copy.wait()


def picked(ext, pattern, q, first=0):
    parts = [
        ext[pl.ds(pl.multiple_of((pattern[k, q] - first) * NEU_BLOCK, NEU_BLOCK), NEU_BLOCK), :]
        for k in range(K)
    ]
    return jnp.concatenate(parts, axis=0)


def block_of(field, q):
    return field[q * PIX_BLOCK : (q + 1) * PIX_BLOCK, :]


def foot_of(feet, q, stripe):
    count = feet.shape[0] // PIX_BLOCK
    return block_of(feet, q if q < count // 2 else q - stripe + count)


def note_places(pattern, place, start, stop):
    for q in range(start, stop):
        for v in range(2 * HB + 1):
            place[q, v] = -1
        for k in range(K):
            place[q, pattern[k, q] - q] = k


def pull_back(pattern, ext, feet, record, contrib, q):
    foot = foot_of(feet, q, pattern.shape[1])
    fitted = jnp.dot(foot, picked(ext, pattern, q), preferred_element_type=F32)
    residual = (fitted - block_of(record, q).astype(F32)).astype(BF16)
    contrib[q * K * NEU_BLOCK : (q + 1) * K * NEU_BLOCK, :] = lax.dot_general(
        foot, residual, (((0,), (0,)), ((), ())), preferred_element_type=F32
    )


def gathered(contrib, place, c, ranges):
    frames = contrib.shape[1]
    per_chunk = LANES // NEU_BLOCK
    halves = []
    for b in range(c * per_chunk, (c + 1) * per_chunk):
        total = jnp.zeros((NEU_BLOCK, frames), F32)
        for v in range(2 * HB + 1):
            q = b - v
            if any(start <= q < stop for start, stop in ranges):
                k = place[q, v]
                at = pl.multiple_of((q * K + jnp.maximum(k, 0)) * NEU_BLOCK, NEU_BLOCK)
                value = contrib[pl.ds(at, NEU_BLOCK), :]
                if v % 2:
                    value = jnp.where(k >= 0, value, 0.0)
                total = total + value
        halves.append(total)
    return jnp.concatenate(halves, axis=0).T


def edge_kernel(
    pattern, z3, p3, rows, pay, pays, feet, record, ext, zones, spill, send_a, send_b, *rest
):
    *traces, contrib, place = rest
    chunks = chunk_count(z3)
    stripe = pattern.shape[1]
    edge = 2 * HB
    me = lax.axis_index("tm")
    totals = block_totals(pay, chunks, rows)
    carry = jnp.zeros_like(totals[0])
    for m in range(pays.shape[0]):
        carry = jnp.where(m < me, pays[m] + totals[m] * carry, carry)
    carry = carry * rows[1]
    ranges = ((0, edge), (stripe - edge, stripe))
    for start, stop in ranges:
        note_places(pattern, place, start, stop)

    def trace(c):
        field = (chunk(p3, c)[...] * (chunk(z3, c)[...] + carry[c : c + 1, :])).T
        ext[c * LANES : (c + 1) * LANES, :] = field.astype(BF16)
        if traces and RIM <= c < chunks - RIM:
            traces[0][(c - RIM) * LANES : (c - RIM + 1) * LANES, :] = field

    near = 4 * RIM
    for c in [*range(near), *range(chunks - near, chunks)]:
        trace(c)
    for start, stop in ranges:
        for q in range(start, stop):
            pull_back(pattern, ext, feet, record, contrib, q)
    for c in range(near, chunks - near):
        trace(c)
    even = lax.axis_index("tile") % 2 == 0
    for i in range(2 * RIM):
        below = gathered(contrib, place, i, ranges)
        above = gathered(contrib, place, chunks - 2 * RIM + i, ranges)
        zones[i] = below
        zones[2 * RIM + i] = above
        send_a[i] = jnp.where(even, above, below).astype(BF16)
        send_b[i] = jnp.where(even, below, above).astype(BF16)
        spill[i] = gathered(contrib, place, 2 * RIM + i, ranges)
        spill[2 * RIM + i] = gathered(contrib, place, chunks - 4 * RIM + i, ranges)

def adjoint_chunk(sums_table, field, p, pinv, rows, c, r3, pay):
    frames = field.shape[0]
    r = summed(sums_table, field * p)
    r3[...] = r
    gain = rows[0, c : c + 1, :]
    pay[0, c : c + 1, :] = rows[1, c : c + 1, :] * r[0:1, :]
    ends = p[frames - 1 : frames, :] * gain * gain
    pay[1, c : c + 1, :] = ends * jnp.sum(pinv * pinv * r, axis=0, keepdims=True)


def inner_kernel(pattern, p3, pinv3, rows, ext, spill, feet, record, traces, r3, pay, *rest):
    if traces:
        out, contrib, place, sem = rest
        copy = pltpu.make_async_copy(traces[0], out, sem)
        copy.start()
    else:
        contrib, place = rest
    chunks = chunk_count(p3)
    frames = spill.shape[1]
    stripe = pattern.shape[1]
    edge = 2 * HB
    note_places(pattern, place, edge, stripe - edge)
    sums_table = table(frames, True)
    pay[...] = jnp.zeros_like(pay)
    inner = chunks - 4 * RIM
    for q in range(edge, stripe - edge):
        pull_back(pattern, ext, feet, record, contrib, q)
    for i in range(inner):
        c = i + 2 * RIM
        field = gathered(contrib, place, c, ((edge, stripe - edge),))
        if i < 2 * RIM:
            field = field + spill[i]
        if i >= inner - 2 * RIM:
            field = field + spill[i - inner + 4 * RIM]
        p, pinv = chunk(p3, c)[...], chunk(pinv3, c)[...]
        adjoint_chunk(sums_table, field, p, pinv, rows, c, r3.at[i], pay)
    if traces:
        copy.wait()


def border_kernel(zones, got_a, got_b, p3, pinv3, rows, pay_inner, r3, pay):
    chunks = chunk_count(p3)
    frames = zones.shape[1]
    sums_table = table(frames, True)
    pay[...] = pay_inner[...]
    even = lax.axis_index("tile") % 2 == 0
    for i in range(2 * RIM):
        both = sides(even, got_a[i].astype(F32), got_b[i].astype(F32))
        for side, c in ((0, i), (1, chunks - 2 * RIM + i)):
            at = side * 2 * RIM + i
            field = zones[at] + both[side]
            p, pinv = chunk(p3, c)[...], chunk(pinv3, c)[...]
            adjoint_chunk(sums_table, field, p, pinv, rows, c, r3.at[at], pay)


def direction_kernel(
    pattern, r_inner, r_border, p3, pinv3, rows, pay, pays, feet, g3, stats, low, high
):
    chunks, frames = g3.shape[0], g3.shape[1]
    own = chunks - 2 * RIM
    stripe = pattern.shape[1]
    me = lax.axis_index("tm")
    totals = block_totals(pay, chunks, rows)
    blocks = pays.shape[0]
    entering = [None] * blocks
    state = jnp.zeros_like(totals[0])
    for m in reversed(range(blocks)):
        entering[m] = state
        state = pays[m, 0] + totals[m] * state
    carry = jnp.zeros_like(totals[0])
    adjoint = jnp.zeros_like(totals[0])
    for m in range(blocks):
        end = pays[m, 1] + pay[m, 1] * entering[m]
        carry = jnp.where(m < me, end + totals[m] * carry, carry)
        adjoint = jnp.where(m == me, entering[m], adjoint)
    carry = carry * rows[1]
    sums_table = table(frames, False)
    grad_sq = jnp.zeros((8, LANES), F32)
    image_sq = jnp.zeros((8, frames), F32)
    per_chunk = LANES // NEU_BLOCK
    low_chunks = low.shape[0] // LANES
    first_high = chunks - high.shape[0] // LANES
    for c in range(chunks):
        p = chunk(p3, c)[...]
        if c < 2 * RIM:
            r = r_border[c]
        elif c >= chunks - 2 * RIM:
            r = r_border[c - chunks + 4 * RIM]
        else:
            r = r_inner[c - 2 * RIM]
        scale = rows[0, c : c + 1, :] * chunk(pinv3, c)[...]
        gradient = scale * (r + p[frames - 1 : frames, :] * adjoint[c : c + 1, :])
        g3[c] = gradient
        if RIM <= c < RIM + own:
            grad_sq += jnp.sum((gradient * gradient).reshape(frames // 8, 8, LANES), axis=0)
        z = summed(sums_table, scale * gradient)
        field = (p * (z + carry[c : c + 1, :])).astype(BF16).T
        if c < low_chunks:
            low[c * LANES : (c + 1) * LANES, :] = field
        if c >= first_high:
            high[(c - first_high) * LANES : (c - first_high + 1) * LANES, :] = field
    for q in range(stripe):
        if q + 2 * HB < low_chunks * per_chunk:
            named = picked(low, pattern, q, 0)
        else:
            named = picked(high, pattern, q, first_high * per_chunk)
        image = jnp.dot(foot_of(feet, q, stripe), named, preferred_element_type=F32)
        image_sq += jnp.sum((image * image).reshape(PIX_BLOCK // 8, 8, frames), axis=0)
    both = jnp.concatenate(
        [
            jnp.sum(grad_sq, axis=0, keepdims=True),
            jnp.sum(image_sq, axis=0, keepdims=True),
        ],
        axis=0,
    )
    stats[...] = jnp.broadcast_to(both[None], stats.shape)


def f32(*shape):
    return jax.ShapeDtypeStruct(shape, F32)


def bf16(*shape):
    return jax.ShapeDtypeStruct(shape, BF16)


def call(
    kernel, name, micros, outs, args, scratch=(), far=(), far_out=(), keep=(), limit=16
):
    def spec(arg):
        if any(arg is other for other in far):
            return HBM
        return SMEM if arg.dtype == jnp.int32 else VMEM

    in_specs = [jax.tree.map(spec, arg) for arg in args]
    in_specs.append(jax.tree.map(lambda _: VMEM, keep))

    def body(*refs):
        kernel(*refs[: len(args)], *refs[len(args) + 1 :])

    return pl.pallas_call(
        body,
        name=name,
        out_shape=outs,
        in_specs=in_specs,
        out_specs=tuple(
            jax.tree.map(lambda _: HBM if place in far_out else VMEM, out)
            for place, out in enumerate(outs)
        ),
        scratch_shapes=scratch,
        compiler_params=pltpu.CompilerParams(vmem_limit_bytes=int(limit * 2**20)),
        cost_estimate=pl.CostEstimate(
            flops=int(micros * 1e8), bytes_accessed=int(micros * 3e6), transcendentals=0
        ),
    )(*args, keep)


def swapped(first, second):
    size = lax.axis_size("tile")

    def pairs(start):
        both = [(i, i + 1) for i in range(start, size - 1, 2)]
        return both + [(j, i) for i, j in both]

    return lax.ppermute(first, "tile", pairs(0)), lax.ppermute(second, "tile", pairs(1))


def per_device(recording, footprints, pattern, decay, frame_gain, spikes):
    neurons, frames = spikes.shape
    stripe = pattern.shape[0]
    pattern = pattern.T
    own = neurons // LANES
    chunks = own + 2 * RIM
    lines = own + padded8(1)
    devices = lax.axis_size("tile") * lax.axis_size("tm")
    split = (f32(own, frames, LANES), f32(2 * RIM, frames, LANES))
    message = f32(RIM * LANES + padded8(RIM), frames)
    gains = frame_gain.reshape(1, frames)
    rates = decay.reshape(own, LANES)
    first, second, rates, spikes = call(
        rims_kernel,
        "rims",
        1.0,
        (message, message, f32(own, LANES), f32(neurons, frames)),
        (spikes, rates),
        [pltpu.SemaphoreType.DMA((4,))],
        far=(spikes, rates),
        limit=52,
    )
    first, second = swapped(first, second)
    ends_size = 4 * HB * PIX_BLOCK
    *owns, rows, pay, columns, feet_ends = call(
        prep_own_kernel,
        "prep_own",
        1.6,
        (split[0],) * 4
        + (f32(3, lines, LANES), f32(2, lines, LANES), f32(2, frames, LANES))
        + (bf16(ends_size, K * NEU_BLOCK),),
        (spikes, rates, gains, footprints),
        [pltpu.SemaphoreType.DMA((2,))],
        far=(footprints,),
        limit=44,
    )
    *rims, rows, pay = call(
        prep_rim_kernel,
        "prep_rim",
        0.3,
        (split[1],) * 4 + (f32(3, lines, LANES), f32(2, lines, LANES)),
        (first, second, columns, rows, pay),
    )
    s3, p3, pinv3, z3 = zip(owns, rims)
    constants = lax.all_gather(pay, "tm")
    pays = constants[:, 0]
    scratch = [
        pltpu.VMEM((stripe * K * NEU_BLOCK, frames), F32),
        pltpu.SMEM((stripe, 2 * HB + 1), jnp.int32),
    ]
    staged = [pltpu.VMEM((neurons, frames), F32), pltpu.SemaphoreType.DMA((PARTS,))]
    middle = stripe * NEU_BLOCK // LANES // 2
    halves = (middle + 2 * RIM, chunks - middle)
    zone = (2 * RIM, frames, LANES)
    border = (4 * RIM, frames, LANES)
    for iteration in range(ITERS):
        ends = iteration == ITERS - 1
        ext, zones, spill, send_a, send_b, *traces = call(
            edge_kernel,
            "edge",
            2.5,
            (
                bf16(chunks * LANES, frames),
                f32(*border),
                f32(*border),
                bf16(*zone),
                bf16(*zone),
            )
            + ((f32(neurons, frames),) if ends else ()),
            (pattern, z3, p3, rows, constants, pays, feet_ends, recording),
            scratch,
            keep=(s3[0],) if ends else (),
        )
        got_a, got_b = swapped(send_a, send_b)
        held = (s3[0],) if ends else ()
        r_inner, pay, *traces = call(
            inner_kernel,
            "inner",
            4.0,
            (f32(chunks - 4 * RIM, frames, LANES), f32(2, lines, LANES))
            + ((f32(neurons, frames),) if ends else ()),
            (pattern, p3, pinv3, rows, ext, spill, footprints, recording, traces),
            scratch + ([pltpu.SemaphoreType.DMA] if ends else []),
            far_out=(2,),
            keep=held,
        )
        r_border, pay = call(
            border_kernel,
            "border",
            0.3,
            (f32(*border), f32(2, lines, LANES)),
            (zones, got_a, got_b, p3, pinv3, rows, pay),
            keep=held,
        )
        pays = lax.all_gather(pay, "tm")
        g3, stats = call(
            direction_kernel,
            "direction",
            4.0,
            (f32(chunks, frames, LANES), f32(devices, 2, LANES)),
            (pattern, r_inner, r_border, p3, pinv3, rows, constants, pays, footprints),
            [
                pltpu.VMEM((halves[0] * LANES, frames), BF16),
                pltpu.VMEM((halves[1] * LANES, frames), BF16),
            ],
            keep=held,
        )
        stats = lax.all_to_all(stats, ("tile", "tm") if ends else ("tm", "tile"), 0, 0)
        if ends:
            (out,) = call(
                final_kernel,
                "final",
                1.4,
                (f32(neurons, frames),),
                (s3[0], g3, stats),
                staged,
                far_out=(0,),
            )
            return out, traces[0]
        s3, z3, pay = call(
            update_kernel,
            "update",
            0.6,
            (split if iteration < ITERS - 2 else split[:1], split, f32(lines, LANES)),
            (s3, g3, stats, p3, pinv3, rows),
        )
        pays = lax.all_gather(pay, "tm")


def solution(mesh):
    return jax.shard_map(
        per_device,
        mesh=mesh,
        in_specs=(
            P("tile", "tm"),
            P("tile", None),
            P("tile", None),
            P("tile"),
            P("tm"),
            P("tile", "tm"),
        ),
        out_specs=(P("tile", "tm"), P("tile", "tm")),
        check_vma=False,
    )
```

```python
import jax
import jax.numpy as jnp
from jax import lax
from jax.experimental import pallas as pl
from jax.experimental.pallas import tpu as pltpu
from jax.sharding import PartitionSpec as P

NEU_BLOCK = 64
PIX_BLOCK = 256
PARTS = 4
K = 4
HB = 2
ITERS = 2
LANES = 128
RIM = HB * NEU_BLOCK // LANES
F32 = jnp.float32
BF16 = jnp.bfloat16
VMEM = pl.BlockSpec(memory_space=pltpu.VMEM)
HBM = pl.BlockSpec(memory_space=pltpu.HBM)
SMEM = pl.BlockSpec(memory_space=pltpu.SMEM)


def padded8(rows):
    return -(-rows // 8) * 8


def table(frames, reverse):
    row = lax.broadcasted_iota(jnp.int32, (frames, 2 * frames), 0)
    col = lax.broadcasted_iota(jnp.int32, (frames, 2 * frames), 1)
    col = jnp.where(col >= frames, col - frames, col)
    keep = col >= row if reverse else col <= row
    return jnp.where(keep, 1.0, 0.0).astype(BF16)


def summed(sums_table, values):
    high = values.astype(BF16)
    low = (values - high.astype(F32)).astype(BF16)
    both = jnp.concatenate([high, low], axis=0)
    return jnp.dot(sums_table, both, preferred_element_type=F32)


def powers(log_decay, frames, mid, sign):
    groups = frames // 8
    coarse = (8 * lax.broadcasted_iota(jnp.int32, (groups, LANES), 0) - mid).astype(F32) * sign
    fine = lax.broadcasted_iota(jnp.int32, (8, LANES), 0).astype(F32) * sign
    coarse = jnp.exp(coarse * log_decay)
    fine = jnp.exp(fine * log_decay)
    return (coarse[:, None, :] * fine[None, :, :]).reshape(frames, LANES)


def chunk(field, c):
    own, rim = field
    inner = own.shape[0]
    if c < RIM:
        return rim.at[c]
    if c >= RIM + inner:
        return rim.at[c - inner]
    return own.at[c - RIM]


def chunk_count(field):
    return field[0].shape[0] + field[1].shape[0]


def prep_chunk(c, rate, field, gains, s3, p3, pinv3, z3, rows, pay):
    frames = field.shape[1]
    middle, prefix_col, inverse_col, sums_table = gains
    mid = frames // 2 - 1
    rate = jnp.where(rate > 0.0, rate, 1.0)
    log_rate = jnp.log(rate)
    gain = jnp.sqrt(1.0 - rate * rate)
    p = powers(log_rate, frames, mid, 1.0) * prefix_col
    pinv = powers(log_rate, frames, mid, -1.0) * inverse_col
    field = field.T
    z = summed(sums_table, field * gain * pinv)
    last = p[frames - 1 : frames, :]
    s3[...] = field
    p3[...] = p
    pinv3[...] = pinv
    z3[...] = z
    half = rate
    for _ in range(frames.bit_length() - 2):
        half = half * half
    rows[0, c : c + 1, :] = gain
    rows[1, c : c + 1, :] = half * middle
    rows[2, c : c + 1, :] = half * half
    pay[0, c : c + 1, :] = last * z[frames - 1 : frames, :]
    scale = last * gain
    pay[1, c : c + 1, :] = scale * scale * jnp.sum(pinv * pinv, axis=0, keepdims=True)


def gain_columns(gains):
    frames = gains.shape[1]
    mid = frames // 2 - 1
    lane = lax.broadcasted_iota(jnp.int32, (8, frames), 1)
    prefix = jnp.broadcast_to(gains, (8, frames))
    step = 1
    while step < frames:
        prefix = prefix * jnp.where(lane >= step, pltpu.roll(prefix, step, 1), 1.0)
        step *= 2
    middle = jnp.broadcast_to(prefix[0:1, mid : mid + 1], (1, LANES))
    whole = jnp.broadcast_to(prefix[0:1, frames - 1 : frames], (1, LANES))
    prefix_col = jnp.broadcast_to(prefix[0:1] / middle, (LANES, frames)).T
    inverse_col = jnp.broadcast_to(middle / prefix[0:1], (LANES, frames)).T
    return middle, whole, prefix_col, inverse_col


def rims_kernel(spikes, decay, first, second, rates_here, spikes_here, sems):
    edge = RIM * LANES
    neurons = spikes.shape[0]
    own = decay.shape[0]
    even = lax.axis_index("tile") % 2 == 0
    top = jnp.where(even, neurons - edge, 0)
    bottom = jnp.where(even, 0, neurons - edge)
    copies = [
        pltpu.make_async_copy(decay, rates_here, sems.at[0]),
        pltpu.make_async_copy(
            spikes.at[pl.ds(pl.multiple_of(top, LANES), edge)], first.at[pl.ds(0, edge)], sems.at[1]
        ),
        pltpu.make_async_copy(
            spikes.at[pl.ds(pl.multiple_of(bottom, LANES), edge)],
            second.at[pl.ds(0, edge)],
            sems.at[2],
        ),
        pltpu.make_async_copy(spikes, spikes_here, sems.at[3]),
    ]
    for copy in copies:
        copy.start()
    first[edge:, :] = jnp.zeros_like(first[edge:, :])
    second[edge:, :] = jnp.zeros_like(second[edge:, :])
    copies[0].wait()
    lower, upper = rates_here[0:RIM, :], rates_here[own - RIM : own, :]
    first[edge : edge + RIM, :] = jnp.where(even, upper, lower)
    second[edge : edge + RIM, :] = jnp.where(even, lower, upper)
    for copy in copies[1:]:
        copy.wait()


def after_start(compute):
    pl.when(lax.axis_index("tm") >= 0)(compute)


def prep_own_kernel(
    spikes, decay, gains, feet, s3, p3, pinv3, z3, rows, pay, columns, feet_ends, sems
):
    own = s3.shape[0]
    chunks = own + 2 * RIM
    size = feet_ends.shape[0] // 2
    fetches = [
        pltpu.make_async_copy(
            feet.at[pl.ds(start, size)], feet_ends.at[pl.ds(i * size, size)], sems.at[i]
        )
        for i, start in enumerate((0, feet.shape[0] - size))
    ]
    for fetch in fetches:
        fetch.start()

    @after_start
    def _():
        middle, whole, prefix_col, inverse_col = gain_columns(gains[...])
        columns[0] = prefix_col
        columns[1] = inverse_col
        rows[...] = jnp.ones_like(rows)
        rows[0, chunks : chunks + 1, :] = middle
        pay[...] = jnp.zeros_like(pay)
        pay[0, chunks : chunks + 1, :] = whole
        shared = middle, prefix_col, inverse_col, table(spikes.shape[1], False)
        for i in range(own):
            field = spikes[i * LANES : (i + 1) * LANES, :]
            at = [ref.at[i] for ref in (s3, p3, pinv3, z3)]
            prep_chunk(i + RIM, decay[i : i + 1, :], field, shared, *at, rows, pay)

    for fetch in fetches:
        fetch.wait()


def sides(even, first, second):
    return jnp.where(even, second, first), jnp.where(even, first, second)


def prep_rim_kernel(first, second, columns, rows_own, pay_own, s3, p3, pinv3, z3, rows, pay):
    rims, frames = s3.shape[0], s3.shape[1]
    own = rows_own.shape[1] - padded8(1)
    chunks = own + 2 * RIM
    middle = rows_own[0, chunks : chunks + 1, :]
    shared = middle, columns[0], columns[1], table(frames, False)
    rows[...] = rows_own[...]
    pay[...] = pay_own[...]
    even = lax.axis_index("tile") % 2 == 0
    below, above = sides(even, first[...], second[...])
    for i in range(rims):
        message = below if i < RIM else above
        j = i % RIM
        c = i if i < RIM else own + i
        at = [ref.at[i] for ref in (s3, p3, pinv3, z3)]
        field = message[j * LANES : (j + 1) * LANES, :]
        rate = message[RIM * LANES + j : RIM * LANES + j + 1, :]
        prep_chunk(c, rate, field, shared, *at, rows, pay)


def block_totals(pays, chunks, rows):
    return [rows[2] * pays[m, 0, chunks : chunks + 1, :] for m in range(pays.shape[0])]


def step_size(stats):
    both = jnp.sum(jnp.sum(stats[...], axis=0), axis=1, keepdims=True)
    return jnp.broadcast_to(both[0:1] / (both[1:2] + 1e-06), (1, LANES))


def update_kernel(s3, g3, stats, p3, pinv3, rows, new3, z3, pay):
    chunks = chunk_count(s3)
    frames = g3.shape[1]
    sums_table = table(frames, False)
    size = step_size(stats)
    pay[...] = jnp.zeros_like(pay)
    for c in range(chunks):
        field = jnp.maximum(chunk(s3, c)[...] - size * g3[c], 0.0)
        z = summed(sums_table, field * rows[0, c : c + 1, :] * chunk(pinv3, c)[...])
        if len(new3) == 2:
            chunk(new3, c)[...] = field
        elif RIM <= c < chunks - RIM:
            new3[0][c - RIM] = field
        chunk(z3, c)[...] = z
        last = chunk(p3, c)[frames - 1 : frames, :]
        pay[c : c + 1, :] = last * z[frames - 1 : frames, :]


def final_kernel(s3, g3, stats, out, here, sems):
    size = step_size(stats)
    part = s3.shape[0] // PARTS

    def copy(i):
        at = pl.ds(pl.multiple_of(i * part * LANES, LANES), part * LANES)
        return pltpu.make_async_copy(here.at[at], out.at[at], sems.at[i])

    @pl.loop(0, PARTS)
    def _(i):
        for j in range(part):
            c = i * part + j
            field = jnp.maximum(s3[c] - size * g3[c + RIM], 0.0)
            here[pl.ds(pl.multiple_of(c * LANES, LANES), LANES), :] = field.T
        copy(i).start()

    for i in range(PARTS):
        copy(i).wait()


def picked(ext, pattern, q, first=0):
    parts = [
        ext[pl.ds(pl.multiple_of((pattern[k, q] - first) * NEU_BLOCK, NEU_BLOCK), NEU_BLOCK), :]
        for k in range(K)
    ]
    return jnp.concatenate(parts, axis=0)


def block_of(field, q):
    return field[q * PIX_BLOCK : (q + 1) * PIX_BLOCK, :]


def foot_of(feet, q, stripe):
    count = feet.shape[0] // PIX_BLOCK
    return block_of(feet, q if q < count // 2 else q - stripe + count)


def note_places(pattern, place, start, stop):
    for q in range(start, stop):
        for v in range(2 * HB + 1):
            place[q, v] = -1
        for k in range(K):
            place[q, pattern[k, q] - q] = k


def pull_back(pattern, ext, feet, record, contrib, q):
    foot = foot_of(feet, q, pattern.shape[1])
    fitted = jnp.dot(foot, picked(ext, pattern, q), preferred_element_type=F32)
    residual = (fitted - block_of(record, q).astype(F32)).astype(BF16)
    contrib[q * K * NEU_BLOCK : (q + 1) * K * NEU_BLOCK, :] = lax.dot_general(
        foot, residual, (((0,), (0,)), ((), ())), preferred_element_type=F32
    )


def gathered(contrib, place, c, ranges):
    frames = contrib.shape[1]
    per_chunk = LANES // NEU_BLOCK
    halves = []
    for b in range(c * per_chunk, (c + 1) * per_chunk):
        total = jnp.zeros((NEU_BLOCK, frames), F32)
        for v in range(2 * HB + 1):
            q = b - v
            if any(start <= q < stop for start, stop in ranges):
                k = place[q, v]
                at = pl.multiple_of((q * K + jnp.maximum(k, 0)) * NEU_BLOCK, NEU_BLOCK)
                value = contrib[pl.ds(at, NEU_BLOCK), :]
                if v % 2:
                    value = jnp.where(k >= 0, value, 0.0)
                total = total + value
        halves.append(total)
    return jnp.concatenate(halves, axis=0).T


def edge_kernel(
    pattern, z3, p3, rows, pay, pays, feet, record, ext, zones, spill, send_a, send_b, *rest
):
    *traces, contrib, place = rest
    chunks = chunk_count(z3)
    stripe = pattern.shape[1]
    edge = 2 * HB
    me = lax.axis_index("tm")
    totals = block_totals(pay, chunks, rows)
    carry = jnp.zeros_like(totals[0])
    for m in range(pays.shape[0]):
        carry = jnp.where(m < me, pays[m] + totals[m] * carry, carry)
    carry = carry * rows[1]
    ranges = ((0, edge), (stripe - edge, stripe))
    for start, stop in ranges:
        note_places(pattern, place, start, stop)

    def trace(c):
        field = chunk(p3, c)[...] * (chunk(z3, c)[...] + carry[c : c + 1, :])
        at = slice(c * LANES, (c + 1) * LANES)
        if traces and RIM <= c < chunks - RIM:
            field = field.T
            traces[0][(c - RIM) * LANES : (c - RIM + 1) * LANES, :] = field
            ext[at, :] = field.astype(BF16)
        else:
            ext[at, :] = field.astype(BF16).T

    near = 4 * RIM
    for c in [*range(near), *range(chunks - near, chunks)]:
        trace(c)
    for start, stop in ranges:
        for q in range(start, stop):
            pull_back(pattern, ext, feet, record, contrib, q)
    for c in range(near, chunks - near):
        trace(c)
    even = lax.axis_index("tile") % 2 == 0
    for i in range(2 * RIM):
        below = gathered(contrib, place, i, ranges)
        above = gathered(contrib, place, chunks - 2 * RIM + i, ranges)
        zones[i] = below
        zones[2 * RIM + i] = above
        send_a[i] = jnp.where(even, above, below).astype(BF16)
        send_b[i] = jnp.where(even, below, above).astype(BF16)
        spill[i] = gathered(contrib, place, 2 * RIM + i, ranges)
        spill[2 * RIM + i] = gathered(contrib, place, chunks - 4 * RIM + i, ranges)

def adjoint_chunk(sums_table, field, p, pinv, rows, c, r3, pay):
    frames = field.shape[0]
    r = summed(sums_table, field * p)
    r3[...] = r
    gain = rows[0, c : c + 1, :]
    pay[0, c : c + 1, :] = rows[1, c : c + 1, :] * r[0:1, :]
    ends = p[frames - 1 : frames, :] * gain * gain
    pay[1, c : c + 1, :] = ends * jnp.sum(pinv * pinv * r, axis=0, keepdims=True)


def inner_kernel(pattern, p3, pinv3, rows, ext, spill, feet, record, traces, r3, pay, *rest):
    if traces:
        out, contrib, place, sem = rest
        copy = pltpu.make_async_copy(traces[0], out, sem)
        copy.start()
    else:
        contrib, place = rest

    def compute():
        chunks = chunk_count(p3)
        frames = spill.shape[1]
        stripe = pattern.shape[1]
        edge = 2 * HB
        note_places(pattern, place, edge, stripe - edge)
        sums_table = table(frames, True)
        pay[...] = jnp.zeros_like(pay)
        inner = chunks - 4 * RIM
        for q in range(edge, stripe - edge):
            pull_back(pattern, ext, feet, record, contrib, q)
        for i in range(inner):
            c = i + 2 * RIM
            field = gathered(contrib, place, c, ((edge, stripe - edge),))
            if i < 2 * RIM:
                field = field + spill[i]
            if i >= inner - 2 * RIM:
                field = field + spill[i - inner + 4 * RIM]
            p, pinv = chunk(p3, c)[...], chunk(pinv3, c)[...]
            adjoint_chunk(sums_table, field, p, pinv, rows, c, r3.at[i], pay)

    if traces:
        after_start(compute)
        copy.wait()
    else:
        compute()


def border_kernel(zones, got_a, got_b, p3, pinv3, rows, pay_inner, r3, pay):
    chunks = chunk_count(p3)
    frames = zones.shape[1]
    sums_table = table(frames, True)
    pay[...] = pay_inner[...]
    even = lax.axis_index("tile") % 2 == 0
    for i in range(2 * RIM):
        both = sides(even, got_a[i].astype(F32), got_b[i].astype(F32))
        for side, c in ((0, i), (1, chunks - 2 * RIM + i)):
            at = side * 2 * RIM + i
            field = zones[at] + both[side]
            p, pinv = chunk(p3, c)[...], chunk(pinv3, c)[...]
            adjoint_chunk(sums_table, field, p, pinv, rows, c, r3.at[at], pay)


def direction_kernel(
    pattern, r_inner, r_border, p3, pinv3, rows, pay, pays, feet, g3, stats, low, high
):
    chunks, frames = g3.shape[0], g3.shape[1]
    own = chunks - 2 * RIM
    stripe = pattern.shape[1]
    me = lax.axis_index("tm")
    totals = block_totals(pay, chunks, rows)
    blocks = pays.shape[0]
    entering = [None] * blocks
    state = jnp.zeros_like(totals[0])
    for m in reversed(range(blocks)):
        entering[m] = state
        state = pays[m, 0] + totals[m] * state
    carry = jnp.zeros_like(totals[0])
    adjoint = jnp.zeros_like(totals[0])
    for m in range(blocks):
        end = pays[m, 1] + pay[m, 1] * entering[m]
        carry = jnp.where(m < me, end + totals[m] * carry, carry)
        adjoint = jnp.where(m == me, entering[m], adjoint)
    carry = carry * rows[1]
    sums_table = table(frames, False)
    grad_sq = jnp.zeros((8, LANES), F32)
    image_sq = jnp.zeros((8, frames), F32)
    per_chunk = LANES // NEU_BLOCK
    low_chunks = low.shape[0] // LANES
    first_high = chunks - high.shape[0] // LANES
    for c in range(chunks):
        p = chunk(p3, c)[...]
        if c < 2 * RIM:
            r = r_border[c]
        elif c >= chunks - 2 * RIM:
            r = r_border[c - chunks + 4 * RIM]
        else:
            r = r_inner[c - 2 * RIM]
        scale = rows[0, c : c + 1, :] * chunk(pinv3, c)[...]
        gradient = scale * (r + p[frames - 1 : frames, :] * adjoint[c : c + 1, :])
        g3[c] = gradient
        if RIM <= c < RIM + own:
            grad_sq += jnp.sum((gradient * gradient).reshape(frames // 8, 8, LANES), axis=0)
        z = summed(sums_table, scale * gradient)
        field = (p * (z + carry[c : c + 1, :])).astype(BF16).T
        if c < low_chunks:
            low[c * LANES : (c + 1) * LANES, :] = field
        if c >= first_high:
            high[(c - first_high) * LANES : (c - first_high + 1) * LANES, :] = field
    for q in range(stripe):
        if q + 2 * HB < low_chunks * per_chunk:
            named = picked(low, pattern, q, 0)
        else:
            named = picked(high, pattern, q, first_high * per_chunk)
        image = jnp.dot(foot_of(feet, q, stripe), named, preferred_element_type=F32)
        image_sq += jnp.sum((image * image).reshape(PIX_BLOCK // 8, 8, frames), axis=0)
    both = jnp.concatenate(
        [
            jnp.sum(grad_sq, axis=0, keepdims=True),
            jnp.sum(image_sq, axis=0, keepdims=True),
        ],
        axis=0,
    )
    stats[...] = jnp.broadcast_to(both[None], stats.shape)


def f32(*shape):
    return jax.ShapeDtypeStruct(shape, F32)


def bf16(*shape):
    return jax.ShapeDtypeStruct(shape, BF16)


def call(
    kernel, name, micros, outs, args, scratch=(), far=(), far_out=(), keep=(), limit=16
):
    def spec(arg):
        if any(arg is other for other in far):
            return HBM
        return SMEM if arg.dtype == jnp.int32 else VMEM

    in_specs = [jax.tree.map(spec, arg) for arg in args]
    in_specs.append(jax.tree.map(lambda _: VMEM, keep))

    def body(*refs):
        kernel(*refs[: len(args)], *refs[len(args) + 1 :])

    return pl.pallas_call(
        body,
        name=name,
        out_shape=outs,
        in_specs=in_specs,
        out_specs=tuple(
            jax.tree.map(lambda _: HBM if place in far_out else VMEM, out)
            for place, out in enumerate(outs)
        ),
        scratch_shapes=scratch,
        compiler_params=pltpu.CompilerParams(vmem_limit_bytes=int(limit * 2**20)),
        cost_estimate=pl.CostEstimate(
            flops=int(micros * 1e8), bytes_accessed=int(micros * 3e6), transcendentals=0
        ),
    )(*args, keep)


def swapped(first, second):
    size = lax.axis_size("tile")

    def pairs(start):
        both = [(i, i + 1) for i in range(start, size - 1, 2)]
        return both + [(j, i) for i, j in both]

    return lax.ppermute(first, "tile", pairs(0)), lax.ppermute(second, "tile", pairs(1))


def per_device(recording, footprints, pattern, decay, frame_gain, spikes):
    neurons, frames = spikes.shape
    stripe = pattern.shape[0]
    pattern = pattern.T
    own = neurons // LANES
    chunks = own + 2 * RIM
    lines = own + padded8(1)
    devices = lax.axis_size("tile") * lax.axis_size("tm")
    split = (f32(own, frames, LANES), f32(2 * RIM, frames, LANES))
    message = f32(RIM * LANES + padded8(RIM), frames)
    gains = frame_gain.reshape(1, frames)
    rates = decay.reshape(own, LANES)
    first, second, rates, spikes = call(
        rims_kernel,
        "rims",
        1.0,
        (message, message, f32(own, LANES), f32(neurons, frames)),
        (spikes, rates),
        [pltpu.SemaphoreType.DMA((4,))],
        far=(spikes, rates),
        limit=52,
    )
    first, second = swapped(first, second)
    ends_size = 4 * HB * PIX_BLOCK
    *owns, rows, pay, columns, feet_ends = call(
        prep_own_kernel,
        "prep_own",
        1.6,
        (split[0],) * 4
        + (f32(3, lines, LANES), f32(2, lines, LANES), f32(2, frames, LANES))
        + (bf16(ends_size, K * NEU_BLOCK),),
        (spikes, rates, gains, footprints),
        [pltpu.SemaphoreType.DMA((2,))],
        far=(footprints,),
        limit=44,
    )
    *rims, rows, pay = call(
        prep_rim_kernel,
        "prep_rim",
        0.3,
        (split[1],) * 4 + (f32(3, lines, LANES), f32(2, lines, LANES)),
        (first, second, columns, rows, pay),
    )
    s3, p3, pinv3, z3 = zip(owns, rims)
    constants = lax.all_gather(pay, "tm")
    pays = constants[:, 0]
    scratch = [
        pltpu.VMEM((stripe * K * NEU_BLOCK, frames), F32),
        pltpu.SMEM((stripe, 2 * HB + 1), jnp.int32),
    ]
    staged = [pltpu.VMEM((neurons, frames), F32), pltpu.SemaphoreType.DMA((PARTS,))]
    middle = stripe * NEU_BLOCK // LANES // 2
    halves = (middle + 2 * RIM, chunks - middle)
    zone = (2 * RIM, frames, LANES)
    border = (4 * RIM, frames, LANES)
    for iteration in range(ITERS):
        ends = iteration == ITERS - 1
        ext, zones, spill, send_a, send_b, *traces = call(
            edge_kernel,
            "edge",
            2.5,
            (
                bf16(chunks * LANES, frames),
                f32(*border),
                f32(*border),
                bf16(*zone),
                bf16(*zone),
            )
            + ((f32(neurons, frames),) if ends else ()),
            (pattern, z3, p3, rows, constants, pays, feet_ends, recording),
            scratch,
            keep=(s3[0],) if ends else (),
        )
        got_a, got_b = swapped(send_a, send_b)
        held = (s3[0],) if ends else ()
        r_inner, pay, *traces = call(
            inner_kernel,
            "inner",
            4.0,
            (f32(chunks - 4 * RIM, frames, LANES), f32(2, lines, LANES))
            + ((f32(neurons, frames),) if ends else ()),
            (pattern, p3, pinv3, rows, ext, spill, footprints, recording, traces),
            scratch + ([pltpu.SemaphoreType.DMA] if ends else []),
            far_out=(2,),
            keep=held,
        )
        r_border, pay = call(
            border_kernel,
            "border",
            0.3,
            (f32(*border), f32(2, lines, LANES)),
            (zones, got_a, got_b, p3, pinv3, rows, pay),
            keep=held,
        )
        pays = lax.all_gather(pay, "tm")
        g3, stats = call(
            direction_kernel,
            "direction",
            4.0,
            (f32(chunks, frames, LANES), f32(devices, 2, LANES)),
            (pattern, r_inner, r_border, p3, pinv3, rows, constants, pays, footprints),
            [
                pltpu.VMEM((halves[0] * LANES, frames), BF16),
                pltpu.VMEM((halves[1] * LANES, frames), BF16),
            ],
            keep=held,
        )
        stats = lax.all_to_all(stats, ("tile", "tm"), 0, 0)
        if ends:
            (out,) = call(
                final_kernel,
                "final",
                1.4,
                (f32(neurons, frames),),
                (s3[0], g3, stats),
                staged,
                far_out=(0,),
            )
            return out, traces[0]
        s3, z3, pay = call(
            update_kernel,
            "update",
            0.6,
            (split if iteration < ITERS - 2 else split[:1], split, f32(lines, LANES)),
            (s3, g3, stats, p3, pinv3, rows),
        )
        pays = lax.all_gather(pay, "tm")


def solution(mesh):
    return jax.shard_map(
        per_device,
        mesh=mesh,
        in_specs=(
            P("tile", "tm"),
            P("tile", None),
            P("tile", None),
            P("tile"),
            P("tm"),
            P("tile", "tm"),
        ),
        out_specs=(P("tile", "tm"), P("tile", "tm")),
        check_vma=False,
    )
```

```python
import jax
import jax.numpy as jnp
from jax import lax
from jax.experimental import pallas as pl
from jax.experimental.pallas import tpu as pltpu
from jax.sharding import PartitionSpec as P

NEU_BLOCK = 64
PIX_BLOCK = 256
PARTS = 8
K = 4
HB = 2
ITERS = 2
LANES = 128
RIM = HB * NEU_BLOCK // LANES
F32 = jnp.float32
BF16 = jnp.bfloat16
VMEM = pl.BlockSpec(memory_space=pltpu.VMEM)
HBM = pl.BlockSpec(memory_space=pltpu.HBM)
SMEM = pl.BlockSpec(memory_space=pltpu.SMEM)


def padded8(rows):
    return -(-rows // 8) * 8


def table(frames, reverse):
    row = lax.broadcasted_iota(jnp.int32, (frames, 2 * frames), 0)
    col = lax.broadcasted_iota(jnp.int32, (frames, 2 * frames), 1)
    col = jnp.where(col >= frames, col - frames, col)
    keep = col >= row if reverse else col <= row
    return jnp.where(keep, 1.0, 0.0).astype(BF16)


def summed(sums_table, values):
    high = values.astype(BF16)
    low = (values - high.astype(F32)).astype(BF16)
    both = jnp.concatenate([high, low], axis=0)
    return jnp.dot(sums_table, both, preferred_element_type=F32)


def powers(log_decay, frames, mid, sign):
    groups = frames // 8
    coarse = (8 * lax.broadcasted_iota(jnp.int32, (groups, LANES), 0) - mid).astype(F32) * sign
    fine = lax.broadcasted_iota(jnp.int32, (8, LANES), 0).astype(F32) * sign
    coarse = jnp.exp(coarse * log_decay)
    fine = jnp.exp(fine * log_decay)
    return (coarse[:, None, :] * fine[None, :, :]).reshape(frames, LANES)


def chunk(field, c):
    own, rim = field
    inner = own.shape[0]
    if c < RIM:
        return rim.at[c]
    if c >= RIM + inner:
        return rim.at[c - inner]
    return own.at[c - RIM]


def chunk_count(field):
    return field[0].shape[0] + field[1].shape[0]


def prep_chunk(c, rate, field, gains, s3, p3, pinv3, z3, rows, pay):
    frames = field.shape[1]
    middle, prefix_col, inverse_col, sums_table = gains
    mid = frames // 2 - 1
    rate = jnp.where(rate > 0.0, rate, 1.0)
    log_rate = jnp.log(rate)
    gain = jnp.sqrt(1.0 - rate * rate)
    p = powers(log_rate, frames, mid, 1.0) * prefix_col
    pinv = powers(log_rate, frames, mid, -1.0) * inverse_col
    field = field.T
    z = summed(sums_table, field * gain * pinv)
    last = p[frames - 1 : frames, :]
    s3[...] = field
    p3[...] = p
    pinv3[...] = pinv
    z3[...] = z
    half = rate
    for _ in range(frames.bit_length() - 2):
        half = half * half
    rows[0, c : c + 1, :] = gain
    rows[1, c : c + 1, :] = half * middle
    rows[2, c : c + 1, :] = half * half
    pay[0, c : c + 1, :] = last * z[frames - 1 : frames, :]
    scale = last * gain
    pay[1, c : c + 1, :] = scale * scale * jnp.sum(pinv * pinv, axis=0, keepdims=True)


def gain_columns(gains):
    frames = gains.shape[1]
    mid = frames // 2 - 1
    lane = lax.broadcasted_iota(jnp.int32, (8, frames), 1)
    prefix = jnp.broadcast_to(gains, (8, frames))
    step = 1
    while step < frames:
        prefix = prefix * jnp.where(lane >= step, pltpu.roll(prefix, step, 1), 1.0)
        step *= 2
    middle = jnp.broadcast_to(prefix[0:1, mid : mid + 1], (1, LANES))
    whole = jnp.broadcast_to(prefix[0:1, frames - 1 : frames], (1, LANES))
    prefix_col = jnp.broadcast_to(prefix[0:1] / middle, (LANES, frames)).T
    inverse_col = jnp.broadcast_to(middle / prefix[0:1], (LANES, frames)).T
    return middle, whole, prefix_col, inverse_col


def rims_kernel(spikes, decay, first, second, rates_here, sems):
    edge = RIM * LANES
    neurons = spikes.shape[0]
    own = decay.shape[0]
    even = lax.axis_index("tile") % 2 == 0
    top = jnp.where(even, neurons - edge, 0)
    bottom = jnp.where(even, 0, neurons - edge)
    copies = [
        pltpu.make_async_copy(decay, rates_here, sems.at[0]),
        pltpu.make_async_copy(
            spikes.at[pl.ds(pl.multiple_of(top, LANES), edge)], first.at[pl.ds(0, edge)], sems.at[1]
        ),
        pltpu.make_async_copy(
            spikes.at[pl.ds(pl.multiple_of(bottom, LANES), edge)],
            second.at[pl.ds(0, edge)],
            sems.at[2],
        ),
    ]
    for copy in copies:
        copy.start()
    first[edge:, :] = jnp.zeros_like(first[edge:, :])
    second[edge:, :] = jnp.zeros_like(second[edge:, :])
    copies[0].wait()
    lower, upper = rates_here[0:RIM, :], rates_here[own - RIM : own, :]
    first[edge : edge + RIM, :] = jnp.where(even, upper, lower)
    second[edge : edge + RIM, :] = jnp.where(even, lower, upper)
    for copy in copies[1:]:
        copy.wait()


def after_start(compute):
    pl.when(lax.axis_index("tm") >= 0)(compute)


def prep_own_kernel(
    spikes, decay, gains, feet, s3, p3, pinv3, z3, rows, pay, columns, feet_ends, sems
):
    own = s3.shape[0]
    chunks = own + 2 * RIM
    size = feet_ends.shape[0] // 2
    fetches = [
        pltpu.make_async_copy(
            feet.at[pl.ds(start, size)], feet_ends.at[pl.ds(i * size, size)], sems.at[i]
        )
        for i, start in enumerate((0, feet.shape[0] - size))
    ]
    for fetch in fetches:
        fetch.start()

    @after_start
    def _():
        middle, whole, prefix_col, inverse_col = gain_columns(gains[...])
        columns[0] = prefix_col
        columns[1] = inverse_col
        rows[...] = jnp.ones_like(rows)
        rows[0, chunks : chunks + 1, :] = middle
        pay[...] = jnp.zeros_like(pay)
        pay[0, chunks : chunks + 1, :] = whole
        shared = middle, prefix_col, inverse_col, table(spikes.shape[1], False)
        for i in range(own):
            field = spikes[i * LANES : (i + 1) * LANES, :]
            at = [ref.at[i] for ref in (s3, p3, pinv3, z3)]
            prep_chunk(i + RIM, decay[i : i + 1, :], field, shared, *at, rows, pay)

    for fetch in fetches:
        fetch.wait()


def sides(even, first, second):
    return jnp.where(even, second, first), jnp.where(even, first, second)


def prep_rim_kernel(first, second, columns, rows_own, pay_own, s3, p3, pinv3, z3, rows, pay):
    rims, frames = s3.shape[0], s3.shape[1]
    own = rows_own.shape[1] - padded8(1)
    chunks = own + 2 * RIM
    middle = rows_own[0, chunks : chunks + 1, :]
    shared = middle, columns[0], columns[1], table(frames, False)
    rows[...] = rows_own[...]
    pay[...] = pay_own[...]
    even = lax.axis_index("tile") % 2 == 0
    below, above = sides(even, first[...], second[...])
    for i in range(rims):
        message = below if i < RIM else above
        j = i % RIM
        c = i if i < RIM else own + i
        at = [ref.at[i] for ref in (s3, p3, pinv3, z3)]
        field = message[j * LANES : (j + 1) * LANES, :]
        rate = message[RIM * LANES + j : RIM * LANES + j + 1, :]
        prep_chunk(c, rate, field, shared, *at, rows, pay)


def block_totals(pays, chunks, rows):
    return [rows[2] * pays[m, 0, chunks : chunks + 1, :] for m in range(pays.shape[0])]


def step_size(stats):
    both = jnp.sum(jnp.sum(stats[...], axis=0), axis=1, keepdims=True)
    return jnp.broadcast_to(both[0:1] / (both[1:2] + 1e-06), (1, LANES))


def update_kernel(s3, g3, stats, p3, pinv3, rows, new3, z3, pay):
    chunks = chunk_count(s3)
    frames = g3.shape[1]
    sums_table = table(frames, False)
    size = step_size(stats)
    pay[...] = jnp.zeros_like(pay)
    for c in range(chunks):
        field = jnp.maximum(chunk(s3, c)[...] - size * g3[c], 0.0)
        z = summed(sums_table, field * rows[0, c : c + 1, :] * chunk(pinv3, c)[...])
        if len(new3) == 2:
            chunk(new3, c)[...] = field
        elif RIM <= c < chunks - RIM:
            new3[0][c - RIM] = field
        chunk(z3, c)[...] = z
        last = chunk(p3, c)[frames - 1 : frames, :]
        pay[c : c + 1, :] = last * z[frames - 1 : frames, :]


def final_kernel(s3, g3, stats, out, here, sems):
    size = step_size(stats)
    part = s3.shape[0] // PARTS
    copies = [
        pltpu.make_async_copy(
            here.at[pl.ds(i * part * LANES, part * LANES)],
            out.at[pl.ds(i * part * LANES, part * LANES)],
            sems.at[i],
        )
        for i in range(PARTS)
    ]
    for i in range(PARTS):

        @after_start
        def _():
            for c in range(i * part, (i + 1) * part):
                field = jnp.maximum(s3[c] - size * g3[c + RIM], 0.0)
                here[c * LANES : (c + 1) * LANES, :] = field.T
            copies[i].start()

    for copy in copies:
        copy.wait()


def picked(ext, pattern, q, first=0):
    parts = [
        ext[pl.ds(pl.multiple_of((pattern[k, q] - first) * NEU_BLOCK, NEU_BLOCK), NEU_BLOCK), :]
        for k in range(K)
    ]
    return jnp.concatenate(parts, axis=0)


def block_of(field, q):
    return field[q * PIX_BLOCK : (q + 1) * PIX_BLOCK, :]


def foot_of(feet, q, stripe):
    count = feet.shape[0] // PIX_BLOCK
    return block_of(feet, q if q < count // 2 else q - stripe + count)


def note_places(pattern, place, start, stop):
    for q in range(start, stop):
        for v in range(2 * HB + 1):
            place[q, v] = -1
        for k in range(K):
            place[q, pattern[k, q] - q] = k


def pull_back(pattern, ext, feet, record, contrib, q):
    foot = foot_of(feet, q, pattern.shape[1])
    fitted = jnp.dot(foot, picked(ext, pattern, q), preferred_element_type=F32)
    residual = (fitted - block_of(record, q).astype(F32)).astype(BF16)
    contrib[q * K * NEU_BLOCK : (q + 1) * K * NEU_BLOCK, :] = lax.dot_general(
        foot, residual, (((0,), (0,)), ((), ())), preferred_element_type=F32
    )


def gathered(contrib, place, c, ranges):
    frames = contrib.shape[1]
    per_chunk = LANES // NEU_BLOCK
    halves = []
    for b in range(c * per_chunk, (c + 1) * per_chunk):
        total = jnp.zeros((NEU_BLOCK, frames), F32)
        for v in range(2 * HB + 1):
            q = b - v
            if any(start <= q < stop for start, stop in ranges):
                k = place[q, v]
                at = pl.multiple_of((q * K + jnp.maximum(k, 0)) * NEU_BLOCK, NEU_BLOCK)
                value = contrib[pl.ds(at, NEU_BLOCK), :]
                if v % 2:
                    value = jnp.where(k >= 0, value, 0.0)
                total = total + value
        halves.append(total)
    return jnp.concatenate(halves, axis=0).T


def edge_kernel(
    pattern, z3, p3, rows, pay, pays, feet, record, ext, zones, spill, send_a, send_b, *rest
):
    *traces, contrib, place = rest
    chunks = chunk_count(z3)
    stripe = pattern.shape[1]
    edge = 2 * HB
    me = lax.axis_index("tm")
    totals = block_totals(pay, chunks, rows)
    carry = jnp.zeros_like(totals[0])
    for m in range(pays.shape[0]):
        carry = jnp.where(m < me, pays[m] + totals[m] * carry, carry)
    carry = carry * rows[1]
    ranges = ((0, edge), (stripe - edge, stripe))
    for start, stop in ranges:
        note_places(pattern, place, start, stop)

    def trace(c):
        field = chunk(p3, c)[...] * (chunk(z3, c)[...] + carry[c : c + 1, :])
        at = slice(c * LANES, (c + 1) * LANES)
        if traces and RIM <= c < chunks - RIM:
            field = field.T
            traces[0][(c - RIM) * LANES : (c - RIM + 1) * LANES, :] = field
            ext[at, :] = field.astype(BF16)
        else:
            ext[at, :] = field.astype(BF16).T

    near = 4 * RIM
    for c in [*range(near), *range(chunks - near, chunks)]:
        trace(c)
    for start, stop in ranges:
        for q in range(start, stop):
            pull_back(pattern, ext, feet, record, contrib, q)
    for c in range(near, chunks - near):
        trace(c)
    even = lax.axis_index("tile") % 2 == 0
    for i in range(2 * RIM):
        below = gathered(contrib, place, i, ranges)
        above = gathered(contrib, place, chunks - 2 * RIM + i, ranges)
        zones[i] = below
        zones[2 * RIM + i] = above
        send_a[i] = jnp.where(even, above, below).astype(BF16)
        send_b[i] = jnp.where(even, below, above).astype(BF16)
        spill[i] = gathered(contrib, place, 2 * RIM + i, ranges)
        spill[2 * RIM + i] = gathered(contrib, place, chunks - 4 * RIM + i, ranges)

def adjoint_chunk(sums_table, field, p, pinv, rows, c, r3, pay):
    frames = field.shape[0]
    r = summed(sums_table, field * p)
    r3[...] = r
    gain = rows[0, c : c + 1, :]
    pay[0, c : c + 1, :] = rows[1, c : c + 1, :] * r[0:1, :]
    ends = p[frames - 1 : frames, :] * gain * gain
    pay[1, c : c + 1, :] = ends * jnp.sum(pinv * pinv * r, axis=0, keepdims=True)


def inner_kernel(pattern, p3, pinv3, rows, ext, spill, feet, record, traces, r3, pay, *rest):
    if traces:
        out, contrib, place, sem = rest
        copy = pltpu.make_async_copy(traces[0], out, sem)
        copy.start()
    else:
        contrib, place = rest

    def compute():
        chunks = chunk_count(p3)
        frames = spill.shape[1]
        stripe = pattern.shape[1]
        edge = 2 * HB
        note_places(pattern, place, edge, stripe - edge)
        sums_table = table(frames, True)
        pay[...] = jnp.zeros_like(pay)
        inner = chunks - 4 * RIM
        for q in range(edge, stripe - edge):
            pull_back(pattern, ext, feet, record, contrib, q)
        for i in range(inner):
            c = i + 2 * RIM
            field = gathered(contrib, place, c, ((edge, stripe - edge),))
            if i < 2 * RIM:
                field = field + spill[i]
            if i >= inner - 2 * RIM:
                field = field + spill[i - inner + 4 * RIM]
            p, pinv = chunk(p3, c)[...], chunk(pinv3, c)[...]
            adjoint_chunk(sums_table, field, p, pinv, rows, c, r3.at[i], pay)

    if traces:
        after_start(compute)
        copy.wait()
    else:
        compute()


def border_kernel(zones, got_a, got_b, p3, pinv3, rows, pay_inner, r3, pay):
    chunks = chunk_count(p3)
    frames = zones.shape[1]
    sums_table = table(frames, True)
    pay[...] = pay_inner[...]
    even = lax.axis_index("tile") % 2 == 0
    for i in range(2 * RIM):
        both = sides(even, got_a[i].astype(F32), got_b[i].astype(F32))
        for side, c in ((0, i), (1, chunks - 2 * RIM + i)):
            at = side * 2 * RIM + i
            field = zones[at] + both[side]
            p, pinv = chunk(p3, c)[...], chunk(pinv3, c)[...]
            adjoint_chunk(sums_table, field, p, pinv, rows, c, r3.at[at], pay)


def direction_kernel(
    pattern, r_inner, r_border, p3, pinv3, rows, pay, pays, feet, g3, stats, low, high
):
    chunks, frames = g3.shape[0], g3.shape[1]
    own = chunks - 2 * RIM
    stripe = pattern.shape[1]
    me = lax.axis_index("tm")
    totals = block_totals(pay, chunks, rows)
    blocks = pays.shape[0]
    entering = [None] * blocks
    state = jnp.zeros_like(totals[0])
    for m in reversed(range(blocks)):
        entering[m] = state
        state = pays[m, 0] + totals[m] * state
    carry = jnp.zeros_like(totals[0])
    adjoint = jnp.zeros_like(totals[0])
    for m in range(blocks):
        end = pays[m, 1] + pay[m, 1] * entering[m]
        carry = jnp.where(m < me, end + totals[m] * carry, carry)
        adjoint = jnp.where(m == me, entering[m], adjoint)
    carry = carry * rows[1]
    sums_table = table(frames, False)
    grad_sq = jnp.zeros((8, LANES), F32)
    image_sq = jnp.zeros((8, frames), F32)
    per_chunk = LANES // NEU_BLOCK
    low_chunks = low.shape[0] // LANES
    first_high = chunks - high.shape[0] // LANES
    for c in range(chunks):
        p = chunk(p3, c)[...]
        if c < 2 * RIM:
            r = r_border[c]
        elif c >= chunks - 2 * RIM:
            r = r_border[c - chunks + 4 * RIM]
        else:
            r = r_inner[c - 2 * RIM]
        scale = rows[0, c : c + 1, :] * chunk(pinv3, c)[...]
        gradient = scale * (r + p[frames - 1 : frames, :] * adjoint[c : c + 1, :])
        g3[c] = gradient
        if RIM <= c < RIM + own:
            grad_sq += jnp.sum((gradient * gradient).reshape(frames // 8, 8, LANES), axis=0)
        z = summed(sums_table, scale * gradient)
        field = (p * (z + carry[c : c + 1, :])).astype(BF16).T
        if c < low_chunks:
            low[c * LANES : (c + 1) * LANES, :] = field
        if c >= first_high:
            high[(c - first_high) * LANES : (c - first_high + 1) * LANES, :] = field
    for q in range(stripe):
        if q + 2 * HB < low_chunks * per_chunk:
            named = picked(low, pattern, q, 0)
        else:
            named = picked(high, pattern, q, first_high * per_chunk)
        image = jnp.dot(foot_of(feet, q, stripe), named, preferred_element_type=F32)
        image_sq += jnp.sum((image * image).reshape(PIX_BLOCK // 8, 8, frames), axis=0)
    both = jnp.concatenate(
        [
            jnp.sum(grad_sq, axis=0, keepdims=True),
            jnp.sum(image_sq, axis=0, keepdims=True),
        ],
        axis=0,
    )
    stats[...] = jnp.broadcast_to(both[None], stats.shape)


def f32(*shape):
    return jax.ShapeDtypeStruct(shape, F32)


def bf16(*shape):
    return jax.ShapeDtypeStruct(shape, BF16)


def call(
    kernel, name, micros, outs, args, scratch=(), far=(), far_out=(), keep=(), limit=16
):
    def spec(arg):
        if any(arg is other for other in far):
            return HBM
        return SMEM if arg.dtype == jnp.int32 else VMEM

    in_specs = [jax.tree.map(spec, arg) for arg in args]
    in_specs.append(jax.tree.map(lambda _: VMEM, keep))

    def body(*refs):
        kernel(*refs[: len(args)], *refs[len(args) + 1 :])

    return pl.pallas_call(
        body,
        name=name,
        out_shape=outs,
        in_specs=in_specs,
        out_specs=tuple(
            jax.tree.map(lambda _: HBM if place in far_out else VMEM, out)
            for place, out in enumerate(outs)
        ),
        scratch_shapes=scratch,
        compiler_params=pltpu.CompilerParams(vmem_limit_bytes=int(limit * 2**20)),
        cost_estimate=pl.CostEstimate(
            flops=int(micros * 1e8), bytes_accessed=int(micros * 3e6), transcendentals=0
        ),
    )(*args, keep)


def swapped(first, second):
    size = lax.axis_size("tile")

    def pairs(start):
        both = [(i, i + 1) for i in range(start, size - 1, 2)]
        return both + [(j, i) for i, j in both]

    return lax.ppermute(first, "tile", pairs(0)), lax.ppermute(second, "tile", pairs(1))


def per_device(recording, footprints, pattern, decay, frame_gain, spikes):
    neurons, frames = spikes.shape
    stripe = pattern.shape[0]
    pattern = pattern.T
    own = neurons // LANES
    chunks = own + 2 * RIM
    lines = own + padded8(1)
    devices = lax.axis_size("tile") * lax.axis_size("tm")
    split = (f32(own, frames, LANES), f32(2 * RIM, frames, LANES))
    message = f32(RIM * LANES + padded8(RIM), frames)
    gains = frame_gain.reshape(1, frames)
    rates = decay.reshape(own, LANES)
    first, second, rates = call(
        rims_kernel,
        "rims",
        1.0,
        (message, message, f32(own, LANES)),
        (spikes, rates),
        [pltpu.SemaphoreType.DMA((3,))],
        far=(spikes, rates),
        limit=53,
    )
    first, second = swapped(first, second)
    ends_size = 4 * HB * PIX_BLOCK
    *owns, rows, pay, columns, feet_ends = call(
        prep_own_kernel,
        "prep_own",
        1.6,
        (split[0],) * 4
        + (f32(3, lines, LANES), f32(2, lines, LANES), f32(2, frames, LANES))
        + (bf16(ends_size, K * NEU_BLOCK),),
        (spikes, rates, gains, footprints),
        [pltpu.SemaphoreType.DMA((2,))],
        far=(footprints,),
        limit=44,
    )
    *rims, rows, pay = call(
        prep_rim_kernel,
        "prep_rim",
        0.3,
        (split[1],) * 4 + (f32(3, lines, LANES), f32(2, lines, LANES)),
        (first, second, columns, rows, pay),
    )
    s3, p3, pinv3, z3 = zip(owns, rims)
    constants = lax.all_gather(pay, "tm")
    pays = constants[:, 0]
    scratch = [
        pltpu.VMEM((stripe * K * NEU_BLOCK, frames), F32),
        pltpu.SMEM((stripe, 2 * HB + 1), jnp.int32),
    ]
    staged = [pltpu.VMEM((neurons, frames), F32), pltpu.SemaphoreType.DMA((PARTS,))]
    middle = stripe * NEU_BLOCK // LANES // 2
    halves = (middle + 2 * RIM, chunks - middle)
    zone = (2 * RIM, frames, LANES)
    border = (4 * RIM, frames, LANES)
    for iteration in range(ITERS):
        ends = iteration == ITERS - 1
        ext, zones, spill, send_a, send_b, *traces = call(
            edge_kernel,
            "edge",
            2.5,
            (
                bf16(chunks * LANES, frames),
                f32(*border),
                f32(*border),
                bf16(*zone),
                bf16(*zone),
            )
            + ((f32(neurons, frames),) if ends else ()),
            (pattern, z3, p3, rows, constants, pays, feet_ends, recording),
            scratch,
            keep=(s3[0],) if ends else (),
        )
        got_a, got_b = swapped(send_a, send_b)
        held = (s3[0],) if ends else ()
        r_inner, pay, *traces = call(
            inner_kernel,
            "inner",
            4.0,
            (f32(chunks - 4 * RIM, frames, LANES), f32(2, lines, LANES))
            + ((f32(neurons, frames),) if ends else ()),
            (pattern, p3, pinv3, rows, ext, spill, footprints, recording, traces),
            scratch + ([pltpu.SemaphoreType.DMA] if ends else []),
            far_out=(2,),
            keep=held,
        )
        r_border, pay = call(
            border_kernel,
            "border",
            0.3,
            (f32(*border), f32(2, lines, LANES)),
            (zones, got_a, got_b, p3, pinv3, rows, pay),
            keep=held,
        )
        pays = lax.all_gather(pay, "tm")
        g3, stats = call(
            direction_kernel,
            "direction",
            4.0,
            (f32(chunks, frames, LANES), f32(devices, 2, LANES)),
            (pattern, r_inner, r_border, p3, pinv3, rows, constants, pays, footprints),
            [
                pltpu.VMEM((halves[0] * LANES, frames), BF16),
                pltpu.VMEM((halves[1] * LANES, frames), BF16),
            ],
            keep=held,
        )
        stats = lax.all_to_all(stats, ("tile", "tm"), 0, 0)
        if ends:
            (out,) = call(
                final_kernel,
                "final",
                1.4,
                (f32(neurons, frames),),
                (s3[0], g3, stats),
                staged,
                far_out=(0,),
            )
            return out, traces[0]
        s3, z3, pay = call(
            update_kernel,
            "update",
            0.6,
            (split if iteration < ITERS - 2 else split[:1], split, f32(lines, LANES)),
            (s3, g3, stats, p3, pinv3, rows),
        )
        pays = lax.all_gather(pay, "tm")


def solution(mesh):
    return jax.shard_map(
        per_device,
        mesh=mesh,
        in_specs=(
            P("tile", "tm"),
            P("tile", None),
            P("tile", None),
            P("tile"),
            P("tm"),
            P("tile", "tm"),
        ),
        out_specs=(P("tile", "tm"), P("tile", "tm")),
        check_vma=False,
    )
```

```python
import jax
import jax.numpy as jnp
from jax import lax
from jax.experimental import pallas as pl
from jax.experimental.pallas import tpu as pltpu
from jax.sharding import PartitionSpec as P

NEU_BLOCK = 64
PIX_BLOCK = 256
PARTS = 8
K = 4
HB = 2
ITERS = 2
LANES = 128
RIM = HB * NEU_BLOCK // LANES
F32 = jnp.float32
BF16 = jnp.bfloat16
VMEM = pl.BlockSpec(memory_space=pltpu.VMEM)
HBM = pl.BlockSpec(memory_space=pltpu.HBM)
SMEM = pl.BlockSpec(memory_space=pltpu.SMEM)


def padded8(rows):
    return -(-rows // 8) * 8


def table(frames, reverse):
    row = lax.broadcasted_iota(jnp.int32, (frames, 2 * frames), 0)
    col = lax.broadcasted_iota(jnp.int32, (frames, 2 * frames), 1)
    col = jnp.where(col >= frames, col - frames, col)
    keep = col >= row if reverse else col <= row
    return jnp.where(keep, 1.0, 0.0).astype(BF16)


def summed(sums_table, values):
    high = values.astype(BF16)
    low = (values - high.astype(F32)).astype(BF16)
    both = jnp.concatenate([high, low], axis=0)
    return jnp.dot(sums_table, both, preferred_element_type=F32)


def powers(log_decay, frames, mid, sign):
    groups = frames // 8
    coarse = (8 * lax.broadcasted_iota(jnp.int32, (groups, LANES), 0) - mid).astype(F32) * sign
    fine = lax.broadcasted_iota(jnp.int32, (8, LANES), 0).astype(F32) * sign
    coarse = jnp.exp(coarse * log_decay)
    fine = jnp.exp(fine * log_decay)
    return (coarse[:, None, :] * fine[None, :, :]).reshape(frames, LANES)


def chunk(field, c):
    own, rim = field
    inner = own.shape[0]
    if c < RIM:
        return rim.at[c]
    if c >= RIM + inner:
        return rim.at[c - inner]
    return own.at[c - RIM]


def chunk_count(field):
    return field[0].shape[0] + field[1].shape[0]


def prep_chunk(c, rate, field, gains, s3, p3, pinv3, z3, rows, pay):
    frames = field.shape[1]
    middle, prefix_col, inverse_col, sums_table = gains
    mid = frames // 2 - 1
    rate = jnp.where(rate > 0.0, rate, 1.0)
    log_rate = jnp.log(rate)
    gain = jnp.sqrt(1.0 - rate * rate)
    p = powers(log_rate, frames, mid, 1.0) * prefix_col
    pinv = powers(log_rate, frames, mid, -1.0) * inverse_col
    field = field.T
    z = summed(sums_table, field * gain * pinv)
    last = p[frames - 1 : frames, :]
    s3[...] = field
    p3[...] = p
    pinv3[...] = pinv
    z3[...] = z
    half = rate
    for _ in range(frames.bit_length() - 2):
        half = half * half
    rows[0, c : c + 1, :] = gain
    rows[1, c : c + 1, :] = half * middle
    rows[2, c : c + 1, :] = half * half
    pay[0, c : c + 1, :] = last * z[frames - 1 : frames, :]
    scale = last * gain
    pay[1, c : c + 1, :] = scale * scale * jnp.sum(pinv * pinv, axis=0, keepdims=True)


def gain_columns(gains):
    frames = gains.shape[1]
    mid = frames // 2 - 1
    lane = lax.broadcasted_iota(jnp.int32, (8, frames), 1)
    prefix = jnp.broadcast_to(gains, (8, frames))
    step = 1
    while step < frames:
        prefix = prefix * jnp.where(lane >= step, pltpu.roll(prefix, step, 1), 1.0)
        step *= 2
    middle = jnp.broadcast_to(prefix[0:1, mid : mid + 1], (1, LANES))
    whole = jnp.broadcast_to(prefix[0:1, frames - 1 : frames], (1, LANES))
    prefix_col = jnp.broadcast_to(prefix[0:1] / middle, (LANES, frames)).T
    inverse_col = jnp.broadcast_to(middle / prefix[0:1], (LANES, frames)).T
    return middle, whole, prefix_col, inverse_col


def rims_kernel(spikes, decay, first, second, rates_here, sems):
    edge = RIM * LANES
    neurons = spikes.shape[0]
    own = decay.shape[0]
    even = lax.axis_index("tile") % 2 == 0
    top = jnp.where(even, neurons - edge, 0)
    bottom = jnp.where(even, 0, neurons - edge)
    copies = [
        pltpu.make_async_copy(decay, rates_here, sems.at[0]),
        pltpu.make_async_copy(
            spikes.at[pl.ds(pl.multiple_of(top, LANES), edge)], first.at[pl.ds(0, edge)], sems.at[1]
        ),
        pltpu.make_async_copy(
            spikes.at[pl.ds(pl.multiple_of(bottom, LANES), edge)],
            second.at[pl.ds(0, edge)],
            sems.at[2],
        ),
    ]
    for copy in copies:
        copy.start()
    first[edge:, :] = jnp.zeros_like(first[edge:, :])
    second[edge:, :] = jnp.zeros_like(second[edge:, :])
    copies[0].wait()
    lower, upper = rates_here[0:RIM, :], rates_here[own - RIM : own, :]
    first[edge : edge + RIM, :] = jnp.where(even, upper, lower)
    second[edge : edge + RIM, :] = jnp.where(even, lower, upper)
    for copy in copies[1:]:
        copy.wait()


def after_start(compute):
    pl.when(lax.axis_index("tm") >= 0)(compute)


def prep_own_kernel(
    spikes, decay, gains, feet, s3, p3, pinv3, z3, rows, pay, columns, feet_ends, sems
):
    own = s3.shape[0]
    chunks = own + 2 * RIM
    size = feet_ends.shape[0] // 2
    fetches = [
        pltpu.make_async_copy(
            feet.at[pl.ds(start, size)], feet_ends.at[pl.ds(i * size, size)], sems.at[i]
        )
        for i, start in enumerate((0, feet.shape[0] - size))
    ]
    for fetch in fetches:
        fetch.start()

    @after_start
    def _():
        middle, whole, prefix_col, inverse_col = gain_columns(gains[...])
        columns[0] = prefix_col
        columns[1] = inverse_col
        rows[...] = jnp.ones_like(rows)
        rows[0, chunks : chunks + 1, :] = middle
        pay[...] = jnp.zeros_like(pay)
        pay[0, chunks : chunks + 1, :] = whole
        shared = middle, prefix_col, inverse_col, table(spikes.shape[1], False)
        for i in range(own):
            field = spikes[i * LANES : (i + 1) * LANES, :]
            at = [ref.at[i] for ref in (s3, p3, pinv3, z3)]
            prep_chunk(i + RIM, decay[i : i + 1, :], field, shared, *at, rows, pay)

    for fetch in fetches:
        fetch.wait()


def sides(even, first, second):
    return jnp.where(even, second, first), jnp.where(even, first, second)


def prep_rim_kernel(first, second, columns, rows_own, pay_own, s3, p3, pinv3, z3, rows, pay):
    rims, frames = s3.shape[0], s3.shape[1]
    own = rows_own.shape[1] - padded8(1)
    chunks = own + 2 * RIM
    middle = rows_own[0, chunks : chunks + 1, :]
    shared = middle, columns[0], columns[1], table(frames, False)
    rows[...] = rows_own[...]
    pay[...] = pay_own[...]
    even = lax.axis_index("tile") % 2 == 0
    below, above = sides(even, first[...], second[...])
    for i in range(rims):
        message = below if i < RIM else above
        j = i % RIM
        c = i if i < RIM else own + i
        at = [ref.at[i] for ref in (s3, p3, pinv3, z3)]
        field = message[j * LANES : (j + 1) * LANES, :]
        rate = message[RIM * LANES + j : RIM * LANES + j + 1, :]
        prep_chunk(c, rate, field, shared, *at, rows, pay)


def by_block(parts, me, index):
    values = [part[index] for part in parts]
    ordered = []
    for m in range(len(values)):
        value = values[0]
        for j in range(1, len(values)):
            value = jnp.where(me == m ^ j, values[j], value)
        ordered.append(value)
    return ordered


def block_totals(pay, me, chunks, rows):
    return [rows[2] * whole for whole in by_block(pay, me, (0, slice(chunks, chunks + 1)))]


def step_size(stats):
    both = jnp.sum(jnp.sum(stats[...], axis=0), axis=1, keepdims=True)
    return jnp.broadcast_to(both[0:1] / (both[1:2] + 1e-06), (1, LANES))


def update_kernel(s3, g3, stats, p3, pinv3, rows, new3, z3, pay):
    chunks = chunk_count(s3)
    frames = g3.shape[1]
    sums_table = table(frames, False)
    size = step_size(stats)
    pay[...] = jnp.zeros_like(pay)
    for c in range(chunks):
        field = jnp.maximum(chunk(s3, c)[...] - size * g3[c], 0.0)
        z = summed(sums_table, field * rows[0, c : c + 1, :] * chunk(pinv3, c)[...])
        if len(new3) == 2:
            chunk(new3, c)[...] = field
        elif RIM <= c < chunks - RIM:
            new3[0][c - RIM] = field
        chunk(z3, c)[...] = z
        last = chunk(p3, c)[frames - 1 : frames, :]
        pay[0, c : c + 1, :] = last * z[frames - 1 : frames, :]


def final_kernel(s3, g3, stats, out, here, sems):
    size = step_size(stats)
    part = s3.shape[0] // PARTS
    copies = [
        pltpu.make_async_copy(
            here.at[pl.ds(i * part * LANES, part * LANES)],
            out.at[pl.ds(i * part * LANES, part * LANES)],
            sems.at[i],
        )
        for i in range(PARTS)
    ]
    for i in range(PARTS):

        @after_start
        def _():
            for c in range(i * part, (i + 1) * part):
                field = jnp.maximum(s3[c] - size * g3[c + RIM], 0.0)
                here[c * LANES : (c + 1) * LANES, :] = field.T
            copies[i].start()

    for copy in copies:
        copy.wait()


def picked(ext, pattern, q, first=0):
    parts = [
        ext[pl.ds(pl.multiple_of((pattern[k, q] - first) * NEU_BLOCK, NEU_BLOCK), NEU_BLOCK), :]
        for k in range(K)
    ]
    return jnp.concatenate(parts, axis=0)


def block_of(field, q):
    return field[q * PIX_BLOCK : (q + 1) * PIX_BLOCK, :]


def foot_of(feet, q, stripe):
    count = feet.shape[0] // PIX_BLOCK
    return block_of(feet, q if q < count // 2 else q - stripe + count)


def note_places(pattern, place, start, stop):
    for q in range(start, stop):
        for v in range(2 * HB + 1):
            place[q, v] = -1
        for k in range(K):
            place[q, pattern[k, q] - q] = k


def pull_back(pattern, ext, feet, record, contrib, q):
    foot = foot_of(feet, q, pattern.shape[1])
    fitted = jnp.dot(foot, picked(ext, pattern, q), preferred_element_type=F32)
    residual = (fitted - block_of(record, q).astype(F32)).astype(BF16)
    contrib[q * K * NEU_BLOCK : (q + 1) * K * NEU_BLOCK, :] = lax.dot_general(
        foot, residual, (((0,), (0,)), ((), ())), preferred_element_type=F32
    )


def gathered(contrib, place, c, ranges):
    frames = contrib.shape[1]
    per_chunk = LANES // NEU_BLOCK
    halves = []
    for b in range(c * per_chunk, (c + 1) * per_chunk):
        total = jnp.zeros((NEU_BLOCK, frames), F32)
        for v in range(2 * HB + 1):
            q = b - v
            if any(start <= q < stop for start, stop in ranges):
                k = place[q, v]
                at = pl.multiple_of((q * K + jnp.maximum(k, 0)) * NEU_BLOCK, NEU_BLOCK)
                value = contrib[pl.ds(at, NEU_BLOCK), :]
                if v % 2:
                    value = jnp.where(k >= 0, value, 0.0)
                total = total + value
        halves.append(total)
    return jnp.concatenate(halves, axis=0).T


def edge_kernel(
    pattern, z3, p3, rows, pay, pays, feet, record, ext, zones, spill, send_a, send_b, *rest
):
    *traces, contrib, place = rest
    chunks = chunk_count(z3)
    stripe = pattern.shape[1]
    edge = 2 * HB
    me = lax.axis_index("tm")
    totals = block_totals(pay, me, chunks, rows)
    ends = by_block(pays, me, 0)
    carry = jnp.zeros_like(totals[0])
    for m, end in enumerate(ends):
        carry = jnp.where(m < me, end + totals[m] * carry, carry)
    carry = carry * rows[1]
    ranges = ((0, edge), (stripe - edge, stripe))
    for start, stop in ranges:
        note_places(pattern, place, start, stop)

    def trace(c):
        field = chunk(p3, c)[...] * (chunk(z3, c)[...] + carry[c : c + 1, :])
        at = slice(c * LANES, (c + 1) * LANES)
        if traces and RIM <= c < chunks - RIM:
            field = field.T
            traces[0][(c - RIM) * LANES : (c - RIM + 1) * LANES, :] = field
            ext[at, :] = field.astype(BF16)
        else:
            ext[at, :] = field.astype(BF16).T

    near = 4 * RIM
    for c in [*range(near), *range(chunks - near, chunks)]:
        trace(c)
    for start, stop in ranges:
        for q in range(start, stop):
            pull_back(pattern, ext, feet, record, contrib, q)
    for c in range(near, chunks - near):
        trace(c)
    even = lax.axis_index("tile") % 2 == 0
    for i in range(2 * RIM):
        below = gathered(contrib, place, i, ranges)
        above = gathered(contrib, place, chunks - 2 * RIM + i, ranges)
        zones[i] = below
        zones[2 * RIM + i] = above
        send_a[i] = jnp.where(even, above, below).astype(BF16)
        send_b[i] = jnp.where(even, below, above).astype(BF16)
        spill[i] = gathered(contrib, place, 2 * RIM + i, ranges)
        spill[2 * RIM + i] = gathered(contrib, place, chunks - 4 * RIM + i, ranges)

def adjoint_chunk(sums_table, field, p, pinv, rows, c, r3, pay):
    frames = field.shape[0]
    r = summed(sums_table, field * p)
    r3[...] = r
    gain = rows[0, c : c + 1, :]
    pay[0, c : c + 1, :] = rows[1, c : c + 1, :] * r[0:1, :]
    ends = p[frames - 1 : frames, :] * gain * gain
    pay[1, c : c + 1, :] = ends * jnp.sum(pinv * pinv * r, axis=0, keepdims=True)


def inner_kernel(pattern, p3, pinv3, rows, ext, spill, feet, record, traces, r3, pay, *rest):
    if traces:
        out, contrib, place, sem = rest
        copy = pltpu.make_async_copy(traces[0], out, sem)
        copy.start()
    else:
        contrib, place = rest

    def compute():
        chunks = chunk_count(p3)
        frames = spill.shape[1]
        stripe = pattern.shape[1]
        edge = 2 * HB
        note_places(pattern, place, edge, stripe - edge)
        sums_table = table(frames, True)
        pay[...] = jnp.zeros_like(pay)
        inner = chunks - 4 * RIM
        for q in range(edge, stripe - edge):
            pull_back(pattern, ext, feet, record, contrib, q)
        for i in range(inner):
            c = i + 2 * RIM
            field = gathered(contrib, place, c, ((edge, stripe - edge),))
            if i < 2 * RIM:
                field = field + spill[i]
            if i >= inner - 2 * RIM:
                field = field + spill[i - inner + 4 * RIM]
            p, pinv = chunk(p3, c)[...], chunk(pinv3, c)[...]
            adjoint_chunk(sums_table, field, p, pinv, rows, c, r3.at[i], pay)

    if traces:
        after_start(compute)
        copy.wait()
    else:
        compute()


def border_kernel(zones, got_a, got_b, p3, pinv3, rows, pay_inner, r3, pay):
    chunks = chunk_count(p3)
    frames = zones.shape[1]
    sums_table = table(frames, True)
    pay[...] = pay_inner[...]
    even = lax.axis_index("tile") % 2 == 0
    for i in range(2 * RIM):
        both = sides(even, got_a[i].astype(F32), got_b[i].astype(F32))
        for side, c in ((0, i), (1, chunks - 2 * RIM + i)):
            at = side * 2 * RIM + i
            field = zones[at] + both[side]
            p, pinv = chunk(p3, c)[...], chunk(pinv3, c)[...]
            adjoint_chunk(sums_table, field, p, pinv, rows, c, r3.at[at], pay)


def direction_kernel(
    pattern, r_inner, r_border, p3, pinv3, rows, pay, pays, feet, g3, stats, low, high
):
    chunks, frames = g3.shape[0], g3.shape[1]
    own = chunks - 2 * RIM
    stripe = pattern.shape[1]
    me = lax.axis_index("tm")
    totals = block_totals(pay, me, chunks, rows)
    gains = by_block(pay, me, 1)
    starts = by_block(pays, me, 0)
    ends = by_block(pays, me, 1)
    blocks = len(pays)
    entering = [None] * blocks
    state = jnp.zeros_like(totals[0])
    for m in reversed(range(blocks)):
        entering[m] = state
        state = starts[m] + totals[m] * state
    carry = jnp.zeros_like(totals[0])
    adjoint = jnp.zeros_like(totals[0])
    for m in range(blocks):
        end = ends[m] + gains[m] * entering[m]
        carry = jnp.where(m < me, end + totals[m] * carry, carry)
        adjoint = jnp.where(m == me, entering[m], adjoint)
    carry = carry * rows[1]
    sums_table = table(frames, False)
    grad_sq = jnp.zeros((8, LANES), F32)
    image_sq = jnp.zeros((8, frames), F32)
    per_chunk = LANES // NEU_BLOCK
    low_chunks = low.shape[0] // LANES
    first_high = chunks - high.shape[0] // LANES
    for c in range(chunks):
        p = chunk(p3, c)[...]
        if c < 2 * RIM:
            r = r_border[c]
        elif c >= chunks - 2 * RIM:
            r = r_border[c - chunks + 4 * RIM]
        else:
            r = r_inner[c - 2 * RIM]
        scale = rows[0, c : c + 1, :] * chunk(pinv3, c)[...]
        gradient = scale * (r + p[frames - 1 : frames, :] * adjoint[c : c + 1, :])
        g3[c] = gradient
        if RIM <= c < RIM + own:
            grad_sq += jnp.sum((gradient * gradient).reshape(frames // 8, 8, LANES), axis=0)
        z = summed(sums_table, scale * gradient)
        field = (p * (z + carry[c : c + 1, :])).astype(BF16).T
        if c < low_chunks:
            low[c * LANES : (c + 1) * LANES, :] = field
        if c >= first_high:
            high[(c - first_high) * LANES : (c - first_high + 1) * LANES, :] = field
    for q in range(stripe):
        if q + 2 * HB < low_chunks * per_chunk:
            named = picked(low, pattern, q, 0)
        else:
            named = picked(high, pattern, q, first_high * per_chunk)
        image = jnp.dot(foot_of(feet, q, stripe), named, preferred_element_type=F32)
        image_sq += jnp.sum((image * image).reshape(PIX_BLOCK // 8, 8, frames), axis=0)
    both = jnp.concatenate(
        [
            jnp.sum(grad_sq, axis=0, keepdims=True),
            jnp.sum(image_sq, axis=0, keepdims=True),
        ],
        axis=0,
    )
    stats[...] = jnp.broadcast_to(both[None], stats.shape)


def f32(*shape):
    return jax.ShapeDtypeStruct(shape, F32)


def bf16(*shape):
    return jax.ShapeDtypeStruct(shape, BF16)


def call(
    kernel, name, micros, outs, args, scratch=(), far=(), far_out=(), keep=(), limit=16
):
    def spec(arg):
        if any(arg is other for other in far):
            return HBM
        return SMEM if arg.dtype == jnp.int32 else VMEM

    in_specs = [jax.tree.map(spec, arg) for arg in args]
    in_specs.append(jax.tree.map(lambda _: VMEM, keep))

    def body(*refs):
        kernel(*refs[: len(args)], *refs[len(args) + 1 :])

    return pl.pallas_call(
        body,
        name=name,
        out_shape=outs,
        in_specs=in_specs,
        out_specs=tuple(
            jax.tree.map(lambda _: HBM if place in far_out else VMEM, out)
            for place, out in enumerate(outs)
        ),
        scratch_shapes=scratch,
        compiler_params=pltpu.CompilerParams(vmem_limit_bytes=int(limit * 2**20)),
        cost_estimate=pl.CostEstimate(
            flops=int(micros * 1e8), bytes_accessed=int(micros * 3e6), transcendentals=0
        ),
    )(*args, keep)


def swapped(first, second):
    size = lax.axis_size("tile")

    def pairs(start):
        both = [(i, i + 1) for i in range(start, size - 1, 2)]
        return both + [(j, i) for i, j in both]

    return lax.ppermute(first, "tile", pairs(0)), lax.ppermute(second, "tile", pairs(1))


def shared_blocks(value):
    size = lax.axis_size("tm")
    known = [value]
    bit = 1
    while bit < size:
        known += [lax.ppermute(x, "tm", [(i, i ^ bit) for i in range(size)]) for x in known]
        bit *= 2
    return tuple(known)


def per_device(recording, footprints, pattern, decay, frame_gain, spikes):
    neurons, frames = spikes.shape
    stripe = pattern.shape[0]
    pattern = pattern.T
    own = neurons // LANES
    chunks = own + 2 * RIM
    lines = own + padded8(1)
    devices = lax.axis_size("tile") * lax.axis_size("tm")
    split = (f32(own, frames, LANES), f32(2 * RIM, frames, LANES))
    message = f32(RIM * LANES + padded8(RIM), frames)
    gains = frame_gain.reshape(1, frames)
    rates = decay.reshape(own, LANES)
    first, second, rates = call(
        rims_kernel,
        "rims",
        1.0,
        (message, message, f32(own, LANES)),
        (spikes, rates),
        [pltpu.SemaphoreType.DMA((3,))],
        far=(spikes, rates),
        limit=53,
    )
    first, second = swapped(first, second)
    ends_size = 4 * HB * PIX_BLOCK
    *owns, rows, pay, columns, feet_ends = call(
        prep_own_kernel,
        "prep_own",
        1.6,
        (split[0],) * 4
        + (f32(3, lines, LANES), f32(2, lines, LANES), f32(2, frames, LANES))
        + (bf16(ends_size, K * NEU_BLOCK),),
        (spikes, rates, gains, footprints),
        [pltpu.SemaphoreType.DMA((2,))],
        far=(footprints,),
        limit=44,
    )
    *rims, rows, pay = call(
        prep_rim_kernel,
        "prep_rim",
        0.3,
        (split[1],) * 4 + (f32(3, lines, LANES), f32(2, lines, LANES)),
        (first, second, columns, rows, pay),
    )
    s3, p3, pinv3, z3 = zip(owns, rims)
    constants = pays = shared_blocks(pay)
    scratch = [
        pltpu.VMEM((stripe * K * NEU_BLOCK, frames), F32),
        pltpu.SMEM((stripe, 2 * HB + 1), jnp.int32),
    ]
    staged = [pltpu.VMEM((neurons, frames), F32), pltpu.SemaphoreType.DMA((PARTS,))]
    middle = stripe * NEU_BLOCK // LANES // 2
    halves = (middle + 2 * RIM, chunks - middle)
    zone = (2 * RIM, frames, LANES)
    border = (4 * RIM, frames, LANES)
    for iteration in range(ITERS):
        ends = iteration == ITERS - 1
        ext, zones, spill, send_a, send_b, *traces = call(
            edge_kernel,
            "edge",
            2.5,
            (
                bf16(chunks * LANES, frames),
                f32(*border),
                f32(*border),
                bf16(*zone),
                bf16(*zone),
            )
            + ((f32(neurons, frames),) if ends else ()),
            (pattern, z3, p3, rows, constants, pays, feet_ends, recording),
            scratch,
            keep=(s3[0],) if ends else (),
        )
        got_a, got_b = swapped(send_a, send_b)
        held = (s3[0],) if ends else ()
        r_inner, pay, *traces = call(
            inner_kernel,
            "inner",
            4.0,
            (f32(chunks - 4 * RIM, frames, LANES), f32(2, lines, LANES))
            + ((f32(neurons, frames),) if ends else ()),
            (pattern, p3, pinv3, rows, ext, spill, footprints, recording, traces),
            scratch + ([pltpu.SemaphoreType.DMA] if ends else []),
            far_out=(2,),
            keep=held,
        )
        r_border, pay = call(
            border_kernel,
            "border",
            0.3,
            (f32(*border), f32(2, lines, LANES)),
            (zones, got_a, got_b, p3, pinv3, rows, pay),
            keep=held,
        )
        pays = shared_blocks(pay)
        g3, stats = call(
            direction_kernel,
            "direction",
            4.0,
            (f32(chunks, frames, LANES), f32(devices, 2, LANES)),
            (pattern, r_inner, r_border, p3, pinv3, rows, constants, pays, footprints),
            [
                pltpu.VMEM((halves[0] * LANES, frames), BF16),
                pltpu.VMEM((halves[1] * LANES, frames), BF16),
            ],
            keep=held,
        )
        stats = lax.all_to_all(stats, ("tile", "tm"), 0, 0)
        if ends:
            (out,) = call(
                final_kernel,
                "final",
                1.4,
                (f32(neurons, frames),),
                (s3[0], g3, stats),
                staged,
                far_out=(0,),
            )
            return out, traces[0]
        s3, z3, pay = call(
            update_kernel,
            "update",
            0.6,
            (split if iteration < ITERS - 2 else split[:1], split, f32(1, lines, LANES)),
            (s3, g3, stats, p3, pinv3, rows),
        )
        pays = shared_blocks(pay)


def solution(mesh):
    return jax.shard_map(
        per_device,
        mesh=mesh,
        in_specs=(
            P("tile", "tm"),
            P("tile", None),
            P("tile", None),
            P("tile"),
            P("tm"),
            P("tile", "tm"),
        ),
        out_specs=(P("tile", "tm"), P("tile", "tm")),
        check_vma=False,
    )
```

```python
import functools

import jax
import jax.numpy as jnp
from jax import lax
from jax.experimental import pallas as pl
from jax.experimental.pallas import tpu as pltpu
from jax.sharding import PartitionSpec as P

NEU_BLOCK = 64
PIX_BLOCK = 256
PARTS = 8
K = 4
HB = 2
ITERS = 2
LANES = 128
RIM = HB * NEU_BLOCK // LANES
F32 = jnp.float32
BF16 = jnp.bfloat16
VMEM = pl.BlockSpec(memory_space=pltpu.VMEM)
HBM = pl.BlockSpec(memory_space=pltpu.HBM)
SMEM = pl.BlockSpec(memory_space=pltpu.SMEM)


def padded8(rows):
    return -(-rows // 8) * 8


def table(frames, reverse):
    row = lax.broadcasted_iota(jnp.int32, (frames, 2 * frames), 0)
    col = lax.broadcasted_iota(jnp.int32, (frames, 2 * frames), 1)
    col = jnp.where(col >= frames, col - frames, col)
    keep = col >= row if reverse else col <= row
    return jnp.where(keep, 1.0, 0.0).astype(BF16)


def summed(sums_table, values):
    high = values.astype(BF16)
    low = (values - high.astype(F32)).astype(BF16)
    both = jnp.concatenate([high, low], axis=0)
    return jnp.dot(sums_table, both, preferred_element_type=F32)


def powers(log_decay, frames, mid, sign):
    groups = frames // 8
    coarse = (8 * lax.broadcasted_iota(jnp.int32, (groups, LANES), 0) - mid).astype(F32) * sign
    fine = lax.broadcasted_iota(jnp.int32, (8, LANES), 0).astype(F32) * sign
    coarse = jnp.exp(coarse * log_decay)
    fine = jnp.exp(fine * log_decay)
    return (coarse[:, None, :] * fine[None, :, :]).reshape(frames, LANES)


def chunk(field, c):
    own, rim = field
    inner = own.shape[0]
    if c < RIM:
        return rim.at[c]
    if c >= RIM + inner:
        return rim.at[c - inner]
    return own.at[c - RIM]


def chunk_count(field):
    return field[0].shape[0] + field[1].shape[0]


def prep_chunk(c, rate, field, gains, s3, p3, pinv3, z3, rows, pay):
    frames = field.shape[1]
    middle, prefix_col, inverse_col, sums_table = gains
    mid = frames // 2 - 1
    rate = jnp.where(rate > 0.0, rate, 1.0)
    log_rate = jnp.log(rate)
    gain = jnp.sqrt(1.0 - rate * rate)
    p = powers(log_rate, frames, mid, 1.0) * prefix_col
    pinv = powers(log_rate, frames, mid, -1.0) * inverse_col
    field = field.T
    z = summed(sums_table, field * gain * pinv)
    last = p[frames - 1 : frames, :]
    s3[...] = field
    p3[...] = p
    pinv3[...] = pinv
    z3[...] = z
    half = rate
    for _ in range(frames.bit_length() - 2):
        half = half * half
    rows[0, c : c + 1, :] = gain
    rows[1, c : c + 1, :] = half * middle
    rows[2, c : c + 1, :] = half * half
    pay[0, c : c + 1, :] = last * z[frames - 1 : frames, :]
    scale = last * gain
    pay[1, c : c + 1, :] = scale * scale * jnp.sum(pinv * pinv, axis=0, keepdims=True)


def gain_columns(gains):
    frames = gains.shape[1]
    mid = frames // 2 - 1
    lane = lax.broadcasted_iota(jnp.int32, (8, frames), 1)
    prefix = jnp.broadcast_to(gains, (8, frames))
    step = 1
    while step < frames:
        prefix = prefix * jnp.where(lane >= step, pltpu.roll(prefix, step, 1), 1.0)
        step *= 2
    middle = jnp.broadcast_to(prefix[0:1, mid : mid + 1], (1, LANES))
    whole = jnp.broadcast_to(prefix[0:1, frames - 1 : frames], (1, LANES))
    prefix_col = jnp.broadcast_to(prefix[0:1] / middle, (LANES, frames)).T
    inverse_col = jnp.broadcast_to(middle / prefix[0:1], (LANES, frames)).T
    return middle, whole, prefix_col, inverse_col


def rims_kernel(spikes, decay, first, second, rates_here, sems):
    edge = RIM * LANES
    neurons = spikes.shape[0]
    own = decay.shape[0]
    even = lax.axis_index("tile") % 2 == 0
    top = jnp.where(even, neurons - edge, 0)
    bottom = jnp.where(even, 0, neurons - edge)
    copies = [
        pltpu.make_async_copy(decay, rates_here, sems.at[0]),
        pltpu.make_async_copy(
            spikes.at[pl.ds(pl.multiple_of(top, LANES), edge)], first.at[pl.ds(0, edge)], sems.at[1]
        ),
        pltpu.make_async_copy(
            spikes.at[pl.ds(pl.multiple_of(bottom, LANES), edge)],
            second.at[pl.ds(0, edge)],
            sems.at[2],
        ),
    ]
    for copy in copies:
        copy.start()
    first[edge:, :] = jnp.zeros_like(first[edge:, :])
    second[edge:, :] = jnp.zeros_like(second[edge:, :])
    copies[0].wait()
    lower, upper = rates_here[0:RIM, :], rates_here[own - RIM : own, :]
    first[edge : edge + RIM, :] = jnp.where(even, upper, lower)
    second[edge : edge + RIM, :] = jnp.where(even, lower, upper)
    for copy in copies[1:]:
        copy.wait()


def after_start(compute):
    pl.when(lax.axis_index("tm") >= 0)(compute)


def prep_own_kernel(
    spikes, decay, gains, feet, s3, p3, pinv3, z3, rows, pay, columns, feet_ends, sems
):
    own = s3.shape[0]
    chunks = own + 2 * RIM
    size = feet_ends.shape[0] // 2
    fetches = [
        pltpu.make_async_copy(
            feet.at[pl.ds(start, size)], feet_ends.at[pl.ds(i * size, size)], sems.at[i]
        )
        for i, start in enumerate((0, feet.shape[0] - size))
    ]
    for fetch in fetches:
        fetch.start()

    @after_start
    def _():
        middle, whole, prefix_col, inverse_col = gain_columns(gains[...])
        columns[0] = prefix_col
        columns[1] = inverse_col
        rows[...] = jnp.ones_like(rows)
        rows[0, chunks : chunks + 1, :] = middle
        pay[...] = jnp.zeros_like(pay)
        pay[0, chunks : chunks + 1, :] = whole
        shared = middle, prefix_col, inverse_col, table(spikes.shape[1], False)
        for i in range(own):
            field = spikes[i * LANES : (i + 1) * LANES, :]
            at = [ref.at[i] for ref in (s3, p3, pinv3, z3)]
            prep_chunk(i + RIM, decay[i : i + 1, :], field, shared, *at, rows, pay)

    for fetch in fetches:
        fetch.wait()


def sides(even, first, second):
    return jnp.where(even, second, first), jnp.where(even, first, second)


def prep_rim_kernel(first, second, columns, rows_own, pay_own, s3, p3, pinv3, z3, rows, pay):
    rims, frames = s3.shape[0], s3.shape[1]
    own = rows_own.shape[1] - padded8(1)
    chunks = own + 2 * RIM
    middle = rows_own[0, chunks : chunks + 1, :]
    shared = middle, columns[0], columns[1], table(frames, False)
    rows[...] = rows_own[...]
    pay[...] = pay_own[...]
    even = lax.axis_index("tile") % 2 == 0
    below, above = sides(even, first[...], second[...])
    for i in range(rims):
        message = below if i < RIM else above
        j = i % RIM
        c = i if i < RIM else own + i
        at = [ref.at[i] for ref in (s3, p3, pinv3, z3)]
        field = message[j * LANES : (j + 1) * LANES, :]
        rate = message[RIM * LANES + j : RIM * LANES + j + 1, :]
        prep_chunk(c, rate, field, shared, *at, rows, pay)


def by_block(halves, width, me, index):
    values = [
        half[j * width + index[0], *index[1:]]
        for half in halves
        for j in range(half.shape[0] // width)
    ]
    ordered = []
    for m in range(len(values)):
        value = values[0]
        for j in range(1, len(values)):
            value = jnp.where(me == m ^ j, values[j], value)
        ordered.append(value)
    return ordered


def block_totals(pay, me, chunks, rows):
    return [rows[2] * whole for whole in by_block(pay, 2, me, (0, slice(chunks, chunks + 1)))]


def step_size(stats):
    both = jnp.sum(jnp.sum(stats[...], axis=0), axis=1, keepdims=True)
    return jnp.broadcast_to(both[0:1] / (both[1:2] + 1e-06), (1, LANES))


def update_kernel(s3, g3, stats, p3, pinv3, rows, new3, z3, pay):
    chunks = chunk_count(s3)
    frames = g3.shape[1]
    sums_table = table(frames, False)
    size = step_size(stats)
    pay[...] = jnp.zeros_like(pay)
    for c in range(chunks):
        field = jnp.maximum(chunk(s3, c)[...] - size * g3[c], 0.0)
        z = summed(sums_table, field * rows[0, c : c + 1, :] * chunk(pinv3, c)[...])
        if len(new3) == 2:
            chunk(new3, c)[...] = field
        elif RIM <= c < chunks - RIM:
            new3[0][c - RIM] = field
        chunk(z3, c)[...] = z
        last = chunk(p3, c)[frames - 1 : frames, :]
        pay[0, c : c + 1, :] = last * z[frames - 1 : frames, :]


def final_kernel(s3, g3, stats, out, here, sems):
    size = step_size(stats)
    part = s3.shape[0] // PARTS
    copies = [
        pltpu.make_async_copy(
            here.at[pl.ds(i * part * LANES, part * LANES)],
            out.at[pl.ds(i * part * LANES, part * LANES)],
            sems.at[i],
        )
        for i in range(PARTS)
    ]
    for i in range(PARTS):

        @after_start
        def _():
            for c in range(i * part, (i + 1) * part):
                field = jnp.maximum(s3[c] - size * g3[c + RIM], 0.0)
                here[c * LANES : (c + 1) * LANES, :] = field.T
            copies[i].start()

    for copy in copies:
        copy.wait()


def picked(ext, pattern, q, first=0):
    parts = [
        ext[pl.ds(pl.multiple_of((pattern[k, q] - first) * NEU_BLOCK, NEU_BLOCK), NEU_BLOCK), :]
        for k in range(K)
    ]
    return jnp.concatenate(parts, axis=0)


def block_of(field, q):
    return field[q * PIX_BLOCK : (q + 1) * PIX_BLOCK, :]


def foot_of(feet, q, stripe):
    count = feet.shape[0] // PIX_BLOCK
    return block_of(feet, q if q < count // 2 else q - stripe + count)


def note_places(pattern, place, start, stop):
    for q in range(start, stop):
        for v in range(2 * HB + 1):
            place[q, v] = -1
        for k in range(K):
            place[q, pattern[k, q] - q] = k


def pull_back(pattern, ext, feet, record, contrib, q):
    foot = foot_of(feet, q, pattern.shape[1])
    fitted = jnp.dot(foot, picked(ext, pattern, q), preferred_element_type=F32)
    residual = (fitted - block_of(record, q).astype(F32)).astype(BF16)
    contrib[q * K * NEU_BLOCK : (q + 1) * K * NEU_BLOCK, :] = lax.dot_general(
        foot, residual, (((0,), (0,)), ((), ())), preferred_element_type=F32
    )


def gathered(contrib, place, c, ranges):
    frames = contrib.shape[1]
    per_chunk = LANES // NEU_BLOCK
    halves = []
    for b in range(c * per_chunk, (c + 1) * per_chunk):
        total = jnp.zeros((NEU_BLOCK, frames), F32)
        for v in range(2 * HB + 1):
            q = b - v
            if any(start <= q < stop for start, stop in ranges):
                k = place[q, v]
                at = pl.multiple_of((q * K + jnp.maximum(k, 0)) * NEU_BLOCK, NEU_BLOCK)
                value = contrib[pl.ds(at, NEU_BLOCK), :]
                if v % 2:
                    value = jnp.where(k >= 0, value, 0.0)
                total = total + value
        halves.append(total)
    return jnp.concatenate(halves, axis=0).T


def traced(z3, p3, carry, c):
    return chunk(p3, c)[...] * (chunk(z3, c)[...] + carry[c : c + 1, :])


def edge_kernel(
    width,
    pattern,
    z3,
    p3,
    rows,
    pay,
    pays,
    feet,
    record,
    state,
    zones,
    spill,
    send_a,
    send_b,
    contrib,
    place,
    ext,
):
    chunks = chunk_count(z3)
    stripe = pattern.shape[1]
    edge = 2 * HB
    me = lax.axis_index("tm")
    totals = block_totals(pay, me, chunks, rows)
    ends = by_block(pays, width, me, (0,))
    carry = jnp.zeros_like(totals[0])
    for m, end in enumerate(ends):
        carry = jnp.where(m < me, end + totals[m] * carry, carry)
    carry = carry * rows[1]
    ranges = ((0, edge), (stripe - edge, stripe))
    for start, stop in ranges:
        note_places(pattern, place, start, stop)

    state[...] = carry
    near = 4 * RIM
    for c in [*range(near), *range(chunks - near, chunks)]:
        field = traced(z3, p3, carry, c).astype(BF16).T
        ext[c * LANES : (c + 1) * LANES, :] = field
    for start, stop in ranges:
        for q in range(start, stop):
            pull_back(pattern, ext, feet, record, contrib, q)
    even = lax.axis_index("tile") % 2 == 0
    for i in range(2 * RIM):
        below = gathered(contrib, place, i, ranges)
        above = gathered(contrib, place, chunks - 2 * RIM + i, ranges)
        zones[i] = below
        zones[2 * RIM + i] = above
        send_a[i] = jnp.where(even, above, below).astype(BF16)
        send_b[i] = jnp.where(even, below, above).astype(BF16)
        spill[i] = gathered(contrib, place, 2 * RIM + i, ranges)
        spill[2 * RIM + i] = gathered(contrib, place, chunks - 4 * RIM + i, ranges)

def adjoint_chunk(sums_table, field, p, pinv, rows, c, r3, pay):
    frames = field.shape[0]
    r = summed(sums_table, field * p)
    r3[...] = r
    gain = rows[0, c : c + 1, :]
    pay[0, c : c + 1, :] = rows[1, c : c + 1, :] * r[0:1, :]
    ends = p[frames - 1 : frames, :] * gain * gain
    pay[1, c : c + 1, :] = ends * jnp.sum(pinv * pinv * r, axis=0, keepdims=True)


def inner_kernel(
    pattern, z3, p3, pinv3, rows, state, spill, feet, record, r3, pay, *rest
):
    *out, contrib, place, ext = rest[:4] if len(rest) > 3 else rest
    chunks = chunk_count(p3)
    own = chunks - 2 * RIM
    frames = spill.shape[1]
    stripe = pattern.shape[1]
    edge = 2 * HB
    carry = state[...]
    if out:
        traces_here, sem = rest[4:]
        copy = pltpu.make_async_copy(traces_here, out[0], sem)
        for c in range(RIM, RIM + own):
            field = traced(z3, p3, carry, c).T
            traces_here[(c - RIM) * LANES : (c - RIM + 1) * LANES, :] = field
            ext[c * LANES : (c + 1) * LANES, :] = field.astype(BF16)
        after_start(copy.start)
    else:
        for c in range(2 * RIM, chunks - 2 * RIM):
            field = traced(z3, p3, carry, c).astype(BF16).T
            ext[c * LANES : (c + 1) * LANES, :] = field

    def compute():
        note_places(pattern, place, edge, stripe - edge)
        sums_table = table(frames, True)
        pay[...] = jnp.zeros_like(pay)
        inner = chunks - 4 * RIM
        for q in range(edge, stripe - edge):
            pull_back(pattern, ext, feet, record, contrib, q)
        for i in range(inner):
            c = i + 2 * RIM
            field = gathered(contrib, place, c, ((edge, stripe - edge),))
            if i < 2 * RIM:
                field = field + spill[i]
            if i >= inner - 2 * RIM:
                field = field + spill[i - inner + 4 * RIM]
            p, pinv = chunk(p3, c)[...], chunk(pinv3, c)[...]
            adjoint_chunk(sums_table, field, p, pinv, rows, c, r3.at[i], pay)

    if out:
        after_start(compute)
        copy.wait()
    else:
        compute()


def border_kernel(zones, got_a, got_b, p3, pinv3, rows, pay_inner, r3, pay):
    chunks = chunk_count(p3)
    frames = zones.shape[1]
    sums_table = table(frames, True)
    pay[...] = pay_inner[...]
    even = lax.axis_index("tile") % 2 == 0
    for i in range(2 * RIM):
        both = sides(even, got_a[i].astype(F32), got_b[i].astype(F32))
        for side, c in ((0, i), (1, chunks - 2 * RIM + i)):
            at = side * 2 * RIM + i
            field = zones[at] + both[side]
            p, pinv = chunk(p3, c)[...], chunk(pinv3, c)[...]
            adjoint_chunk(sums_table, field, p, pinv, rows, c, r3.at[at], pay)


def direction_kernel(
    pattern, r_inner, r_border, p3, pinv3, rows, pay, pays, feet, g3, stats, low, high
):
    chunks, frames = g3.shape[0], g3.shape[1]
    own = chunks - 2 * RIM
    stripe = pattern.shape[1]
    me = lax.axis_index("tm")
    totals = block_totals(pay, me, chunks, rows)
    gains = by_block(pay, 2, me, (1,))
    starts = by_block(pays, 2, me, (0,))
    ends = by_block(pays, 2, me, (1,))
    blocks = len(starts)
    entering = [None] * blocks
    state = jnp.zeros_like(totals[0])
    for m in reversed(range(blocks)):
        entering[m] = state
        state = starts[m] + totals[m] * state
    carry = jnp.zeros_like(totals[0])
    adjoint = jnp.zeros_like(totals[0])
    for m in range(blocks):
        end = ends[m] + gains[m] * entering[m]
        carry = jnp.where(m < me, end + totals[m] * carry, carry)
        adjoint = jnp.where(m == me, entering[m], adjoint)
    carry = carry * rows[1]
    sums_table = table(frames, False)
    grad_sq = jnp.zeros((8, LANES), F32)
    image_sq = jnp.zeros((8, frames), F32)
    per_chunk = LANES // NEU_BLOCK
    low_chunks = low.shape[0] // LANES
    first_high = chunks - high.shape[0] // LANES
    for c in range(chunks):
        p = chunk(p3, c)[...]
        if c < 2 * RIM:
            r = r_border[c]
        elif c >= chunks - 2 * RIM:
            r = r_border[c - chunks + 4 * RIM]
        else:
            r = r_inner[c - 2 * RIM]
        scale = rows[0, c : c + 1, :] * chunk(pinv3, c)[...]
        gradient = scale * (r + p[frames - 1 : frames, :] * adjoint[c : c + 1, :])
        g3[c] = gradient
        if RIM <= c < RIM + own:
            grad_sq += jnp.sum((gradient * gradient).reshape(frames // 8, 8, LANES), axis=0)
        z = summed(sums_table, scale * gradient)
        field = (p * (z + carry[c : c + 1, :])).astype(BF16).T
        if c < low_chunks:
            low[c * LANES : (c + 1) * LANES, :] = field
        if c >= first_high:
            high[(c - first_high) * LANES : (c - first_high + 1) * LANES, :] = field
    for q in range(stripe):
        if q + 2 * HB < low_chunks * per_chunk:
            named = picked(low, pattern, q, 0)
        else:
            named = picked(high, pattern, q, first_high * per_chunk)
        image = jnp.dot(foot_of(feet, q, stripe), named, preferred_element_type=F32)
        image_sq += jnp.sum((image * image).reshape(PIX_BLOCK // 8, 8, frames), axis=0)
    both = jnp.concatenate(
        [
            jnp.sum(grad_sq, axis=0, keepdims=True),
            jnp.sum(image_sq, axis=0, keepdims=True),
        ],
        axis=0,
    )
    stats[...] = jnp.broadcast_to(both[None], stats.shape)


def f32(*shape):
    return jax.ShapeDtypeStruct(shape, F32)


def bf16(*shape):
    return jax.ShapeDtypeStruct(shape, BF16)


def call(
    kernel, name, micros, outs, args, scratch=(), far=(), far_out=(), keep=(), limit=16
):
    def spec(arg):
        if any(arg is other for other in far):
            return HBM
        return SMEM if arg.dtype == jnp.int32 else VMEM

    in_specs = [jax.tree.map(spec, arg) for arg in args]
    in_specs.append(jax.tree.map(lambda _: VMEM, keep))

    def body(*refs):
        kernel(*refs[: len(args)], *refs[len(args) + 1 :])

    return pl.pallas_call(
        body,
        name=name,
        out_shape=outs,
        in_specs=in_specs,
        out_specs=tuple(
            jax.tree.map(lambda _: HBM if place in far_out else VMEM, out)
            for place, out in enumerate(outs)
        ),
        scratch_shapes=scratch,
        compiler_params=pltpu.CompilerParams(vmem_limit_bytes=int(limit * 2**20)),
        cost_estimate=pl.CostEstimate(
            flops=int(micros * 1e8), bytes_accessed=int(micros * 3e6), transcendentals=0
        ),
    )(*args, keep)


def swapped(first, second):
    size = lax.axis_size("tile")

    def pairs(start):
        both = [(i, i + 1) for i in range(start, size - 1, 2)]
        return both + [(j, i) for i, j in both]

    return lax.ppermute(first, "tile", pairs(0)), lax.ppermute(second, "tile", pairs(1))


def shared_blocks(value):
    size = lax.axis_size("tm")
    bit = 1
    while True:
        other = lax.ppermute(value, "tm", [(i, i ^ bit) for i in range(size)])
        bit *= 2
        if bit >= size:
            return value, other
        value = jnp.concatenate([value, other], axis=0)


def per_device(recording, footprints, pattern, decay, frame_gain, spikes):
    neurons, frames = spikes.shape
    stripe = pattern.shape[0]
    pattern = pattern.T
    own = neurons // LANES
    chunks = own + 2 * RIM
    lines = own + padded8(1)
    devices = lax.axis_size("tile") * lax.axis_size("tm")
    split = (f32(own, frames, LANES), f32(2 * RIM, frames, LANES))
    message = f32(RIM * LANES + padded8(RIM), frames)
    gains = frame_gain.reshape(1, frames)
    rates = decay.reshape(own, LANES)
    first, second, rates = call(
        rims_kernel,
        "rims",
        1.0,
        (message, message, f32(own, LANES)),
        (spikes, rates),
        [pltpu.SemaphoreType.DMA((3,))],
        far=(spikes, rates),
        limit=53,
    )
    first, second = swapped(first, second)
    ends_size = 4 * HB * PIX_BLOCK
    *owns, rows, pay, columns, feet_ends = call(
        prep_own_kernel,
        "prep_own",
        1.6,
        (split[0],) * 4
        + (f32(3, lines, LANES), f32(2, lines, LANES), f32(2, frames, LANES))
        + (bf16(ends_size, K * NEU_BLOCK),),
        (spikes, rates, gains, footprints),
        [pltpu.SemaphoreType.DMA((2,))],
        far=(footprints,),
        limit=44,
    )
    *rims, rows, pay = call(
        prep_rim_kernel,
        "prep_rim",
        0.3,
        (split[1],) * 4 + (f32(3, lines, LANES), f32(2, lines, LANES)),
        (first, second, columns, rows, pay),
    )
    s3, p3, pinv3, z3 = zip(owns, rims)
    constants = pays = shared_blocks(pay)
    scratch = [
        pltpu.VMEM((stripe * K * NEU_BLOCK, frames), F32),
        pltpu.SMEM((stripe, 2 * HB + 1), jnp.int32),
        pltpu.VMEM((chunks * LANES, frames), BF16),
    ]
    staged = [pltpu.VMEM((neurons, frames), F32), pltpu.SemaphoreType.DMA((PARTS,))]
    middle = stripe * NEU_BLOCK // LANES // 2
    halves = (middle + 2 * RIM, chunks - middle)
    zone = (2 * RIM, frames, LANES)
    border = (4 * RIM, frames, LANES)
    for iteration in range(ITERS):
        ends = iteration == ITERS - 1
        state, zones, spill, send_a, send_b = call(
            functools.partial(edge_kernel, pays[0].shape[0] // (lax.axis_size("tm") // 2)),
            "edge",
            2.5,
            (
                f32(lines, LANES),
                f32(*border),
                f32(*border),
                bf16(*zone),
                bf16(*zone),
            ),
            (pattern, z3, p3, rows, constants, pays, feet_ends, recording),
            scratch,
            keep=(s3[0],) if ends else (),
        )
        got_a, got_b = swapped(send_a, send_b)
        held = (s3[0],) if ends else ()
        r_inner, pay, *traces = call(
            inner_kernel,
            "inner",
            4.0,
            (f32(chunks - 4 * RIM, frames, LANES), f32(2, lines, LANES))
            + ((f32(neurons, frames),) if ends else ()),
            (pattern, z3, p3, pinv3, rows, state, spill, footprints, recording),
            scratch + ([staged[0], pltpu.SemaphoreType.DMA] if ends else []),
            far_out=(2,),
            keep=held,
        )
        r_border, pay = call(
            border_kernel,
            "border",
            0.3,
            (f32(*border), f32(2, lines, LANES)),
            (zones, got_a, got_b, p3, pinv3, rows, pay),
            keep=held,
        )
        pays = shared_blocks(pay)
        g3, stats = call(
            direction_kernel,
            "direction",
            4.0,
            (f32(chunks, frames, LANES), f32(devices, 2, LANES)),
            (pattern, r_inner, r_border, p3, pinv3, rows, constants, pays, footprints),
            [
                pltpu.VMEM((halves[0] * LANES, frames), BF16),
                pltpu.VMEM((halves[1] * LANES, frames), BF16),
            ],
            keep=held,
        )
        stats = lax.all_to_all(stats, ("tile", "tm"), 0, 0)
        if ends:
            (out,) = call(
                final_kernel,
                "final",
                1.4,
                (f32(neurons, frames),),
                (s3[0], g3, stats),
                staged,
                far_out=(0,),
            )
            return out, traces[0]
        s3, z3, pay = call(
            update_kernel,
            "update",
            0.6,
            (split if iteration < ITERS - 2 else split[:1], split, f32(1, lines, LANES)),
            (s3, g3, stats, p3, pinv3, rows),
        )
        pays = shared_blocks(pay)


def solution(mesh):
    return jax.shard_map(
        per_device,
        mesh=mesh,
        in_specs=(
            P("tile", "tm"),
            P("tile", None),
            P("tile", None),
            P("tile"),
            P("tm"),
            P("tile", "tm"),
        ),
        out_specs=(P("tile", "tm"), P("tile", "tm")),
        check_vma=False,
    )
```

```python
import jax
import jax.numpy as jnp
from jax import lax
from jax.experimental import pallas as pl
from jax.experimental.pallas import tpu as pltpu
from jax.sharding import PartitionSpec as P

NEU_BLOCK = 64
PIX_BLOCK = 256
PARTS = 8
K = 4
HB = 2
ITERS = 2
LANES = 128
RIM = HB * NEU_BLOCK // LANES
F32 = jnp.float32
BF16 = jnp.bfloat16
VMEM = pl.BlockSpec(memory_space=pltpu.VMEM)
HBM = pl.BlockSpec(memory_space=pltpu.HBM)


def padded8(rows):
    return -(-rows // 8) * 8


def table(frames, reverse):
    row = lax.broadcasted_iota(jnp.int32, (frames, 2 * frames), 0)
    col = lax.broadcasted_iota(jnp.int32, (frames, 2 * frames), 1)
    col = jnp.where(col >= frames, col - frames, col)
    keep = col >= row if reverse else col <= row
    return jnp.where(keep, 1.0, 0.0).astype(BF16)


def summed(sums_table, values):
    high = values.astype(BF16)
    low = (values - high.astype(F32)).astype(BF16)
    both = jnp.concatenate([high, low], axis=0)
    return jnp.dot(sums_table, both, preferred_element_type=F32)


def powers(log_decay, frames, mid, sign):
    groups = frames // 8
    coarse = (8 * lax.broadcasted_iota(jnp.int32, (groups, LANES), 0) - mid).astype(F32) * sign
    fine = lax.broadcasted_iota(jnp.int32, (8, LANES), 0).astype(F32) * sign
    coarse = jnp.exp(coarse * log_decay)
    fine = jnp.exp(fine * log_decay)
    return (coarse[:, None, :] * fine[None, :, :]).reshape(frames, LANES)


def chunk(field, c):
    own, rim = field
    inner = own.shape[0]
    if c < RIM:
        return rim.at[c]
    if c >= RIM + inner:
        return rim.at[c - inner]
    return own.at[c - RIM]


def chunk_count(field):
    return field[0].shape[0] + field[1].shape[0]


def prep_chunk(c, rate, field, gains, s3, p3, pinv3, z3, rows, pay):
    frames = field.shape[1]
    middle, prefix_col, inverse_col, sums_table = gains
    mid = frames // 2 - 1
    rate = jnp.where(rate > 0.0, rate, 1.0)
    log_rate = jnp.log(rate)
    gain = jnp.sqrt(1.0 - rate * rate)
    p = powers(log_rate, frames, mid, 1.0) * prefix_col
    pinv = powers(log_rate, frames, mid, -1.0) * inverse_col
    field = field.T
    z = summed(sums_table, field * gain * pinv)
    last = p[frames - 1 : frames, :]
    s3[...] = field
    p3[...] = p
    pinv3[...] = pinv
    z3[...] = z
    half = rate
    for _ in range(frames.bit_length() - 2):
        half = half * half
    rows[0, c : c + 1, :] = gain
    rows[1, c : c + 1, :] = half * middle
    rows[2, c : c + 1, :] = half * half
    pay[0, c : c + 1, :] = last * z[frames - 1 : frames, :]
    scale = last * gain
    pay[1, c : c + 1, :] = scale * scale * jnp.sum(pinv * pinv, axis=0, keepdims=True)


def gain_columns(gains):
    frames = gains.shape[1]
    mid = frames // 2 - 1
    lane = lax.broadcasted_iota(jnp.int32, (8, frames), 1)
    prefix = jnp.broadcast_to(gains, (8, frames))
    step = 1
    while step < frames:
        prefix = prefix * jnp.where(lane >= step, pltpu.roll(prefix, step, 1), 1.0)
        step *= 2
    middle = jnp.broadcast_to(prefix[0:1, mid : mid + 1], (1, LANES))
    whole = jnp.broadcast_to(prefix[0:1, frames - 1 : frames], (1, LANES))
    prefix_col = jnp.broadcast_to(prefix[0:1] / middle, (LANES, frames)).T
    inverse_col = jnp.broadcast_to(middle / prefix[0:1], (LANES, frames)).T
    return middle, whole, prefix_col, inverse_col


def rims_kernel(spikes, decay, first, second, rates_here, sems):
    edge = RIM * LANES
    neurons = spikes.shape[0]
    own = decay.shape[0]
    even = lax.axis_index("tile") % 2 == 0
    top = jnp.where(even, neurons - edge, 0)
    bottom = jnp.where(even, 0, neurons - edge)
    copies = [
        pltpu.make_async_copy(decay, rates_here, sems.at[0]),
        pltpu.make_async_copy(
            spikes.at[pl.ds(pl.multiple_of(top, LANES), edge)], first.at[pl.ds(0, edge)], sems.at[1]
        ),
        pltpu.make_async_copy(
            spikes.at[pl.ds(pl.multiple_of(bottom, LANES), edge)],
            second.at[pl.ds(0, edge)],
            sems.at[2],
        ),
    ]
    for copy in copies:
        copy.start()
    first[edge:, :] = jnp.zeros_like(first[edge:, :])
    second[edge:, :] = jnp.zeros_like(second[edge:, :])
    copies[0].wait()
    lower, upper = rates_here[0:RIM, :], rates_here[own - RIM : own, :]
    first[edge : edge + RIM, :] = jnp.where(even, upper, lower)
    second[edge : edge + RIM, :] = jnp.where(even, lower, upper)
    for copy in copies[1:]:
        copy.wait()


def after_start(compute):
    pl.when(lax.axis_index("tm") >= 0)(compute)


def prep_own_kernel(
    spikes, decay, gains, feet, s3, p3, pinv3, z3, rows, pay, columns, feet_ends, sems
):
    own = s3.shape[0]
    chunks = own + 2 * RIM
    size = feet_ends.shape[0] // 2
    fetches = [
        pltpu.make_async_copy(
            feet.at[pl.ds(start, size)], feet_ends.at[pl.ds(i * size, size)], sems.at[i]
        )
        for i, start in enumerate((0, feet.shape[0] - size))
    ]
    for fetch in fetches:
        fetch.start()

    @after_start
    def _():
        middle, whole, prefix_col, inverse_col = gain_columns(gains[...])
        columns[0] = prefix_col
        columns[1] = inverse_col
        rows[...] = jnp.ones_like(rows)
        rows[0, chunks : chunks + 1, :] = middle
        pay[...] = jnp.zeros_like(pay)
        pay[0, chunks : chunks + 1, :] = whole
        shared = middle, prefix_col, inverse_col, table(spikes.shape[1], False)
        for i in range(own):
            field = spikes[i * LANES : (i + 1) * LANES, :]
            at = [ref.at[i] for ref in (s3, p3, pinv3, z3)]
            prep_chunk(i + RIM, decay[i : i + 1, :], field, shared, *at, rows, pay)

    for fetch in fetches:
        fetch.wait()


def sides(even, first, second):
    return jnp.where(even, second, first), jnp.where(even, first, second)


def prep_rim_kernel(first, second, columns, rows_own, pay_own, s3, p3, pinv3, z3, rows, pay):
    rims, frames = s3.shape[0], s3.shape[1]
    own = rows_own.shape[1] - padded8(1)
    chunks = own + 2 * RIM
    middle = rows_own[0, chunks : chunks + 1, :]
    shared = middle, columns[0], columns[1], table(frames, False)
    rows[...] = rows_own[...]
    pay[...] = pay_own[...]
    even = lax.axis_index("tile") % 2 == 0
    below, above = sides(even, first[...], second[...])
    for i in range(rims):
        message = below if i < RIM else above
        j = i % RIM
        c = i if i < RIM else own + i
        at = [ref.at[i] for ref in (s3, p3, pinv3, z3)]
        field = message[j * LANES : (j + 1) * LANES, :]
        rate = message[RIM * LANES + j : RIM * LANES + j + 1, :]
        prep_chunk(c, rate, field, shared, *at, rows, pay)


def distances(size):
    found = [0]
    bit = size // 2
    while bit:
        found += [other ^ bit for other in found]
        bit //= 2
    return found


def by_block(parts, me, index):
    values = [part[index] for part in parts]
    ordered = []
    for m in range(len(values)):
        value = values[0]
        for distance, other in zip(distances(len(values))[1:], values[1:]):
            value = jnp.where(me == m ^ distance, other, value)
        ordered.append(value)
    return ordered


def block_totals(pay, me, chunks, rows):
    return [rows[2] * whole for whole in by_block(pay, me, (0, slice(chunks, chunks + 1)))]


def step_size(stats):
    both = jnp.sum(jnp.sum(stats[...], axis=0), axis=1, keepdims=True)
    return jnp.broadcast_to(both[0:1] / (both[1:2] + 1e-06), (1, LANES))


def update_kernel(s3, g3, stats, p3, pinv3, rows, new3, z3, pay):
    chunks = chunk_count(s3)
    frames = g3.shape[1]
    sums_table = table(frames, False)
    size = step_size(stats)
    pay[...] = jnp.zeros_like(pay)
    for c in range(chunks):
        field = jnp.maximum(chunk(s3, c)[...] - size * g3[c], 0.0)
        z = summed(sums_table, field * rows[0, c : c + 1, :] * chunk(pinv3, c)[...])
        if len(new3) == 2:
            chunk(new3, c)[...] = field
        elif RIM <= c < chunks - RIM:
            new3[0][c - RIM] = field
        chunk(z3, c)[...] = z
        last = chunk(p3, c)[frames - 1 : frames, :]
        pay[0, c : c + 1, :] = last * z[frames - 1 : frames, :]


def final_kernel(s3, g3, stats, out, here, sems):
    size = step_size(stats)
    part = s3.shape[0] // PARTS
    copies = [
        pltpu.make_async_copy(
            here.at[pl.ds(i * part * LANES, part * LANES)],
            out.at[pl.ds(i * part * LANES, part * LANES)],
            sems.at[i],
        )
        for i in range(PARTS)
    ]
    for i in range(PARTS):

        @after_start
        def _():
            for c in range(i * part, (i + 1) * part):
                field = jnp.maximum(s3[c] - size * g3[c + RIM], 0.0)
                here[c * LANES : (c + 1) * LANES, :] = field.T
            copies[i].start()

    for copy in copies:
        copy.wait()


def picked(ext, pattern, q, first=0):
    parts = [
        ext[pl.ds(pl.multiple_of((pattern[k, q] - first) * NEU_BLOCK, NEU_BLOCK), NEU_BLOCK), :]
        for k in range(K)
    ]
    return jnp.concatenate(parts, axis=0)


def block_of(field, q):
    return field[q * PIX_BLOCK : (q + 1) * PIX_BLOCK, :]


def foot_of(feet, q, stripe):
    count = feet.shape[0] // PIX_BLOCK
    return block_of(feet, q if q < count // 2 else q - stripe + count)


def note_places(pattern, place, start, stop):
    for q in range(start, stop):
        for v in range(2 * HB + 1):
            place[q, v] = -1
        for k in range(K):
            place[q, pattern[k, q] - q] = k


def pull_back(pattern, ext, feet, record, contrib, q):
    foot = foot_of(feet, q, pattern.shape[1])
    fitted = jnp.dot(foot, picked(ext, pattern, q), preferred_element_type=F32)
    residual = (fitted - block_of(record, q).astype(F32)).astype(BF16)
    contrib[q * K * NEU_BLOCK : (q + 1) * K * NEU_BLOCK, :] = lax.dot_general(
        foot, residual, (((0,), (0,)), ((), ())), preferred_element_type=F32
    )


def gathered(contrib, place, c, ranges):
    frames = contrib.shape[1]
    per_chunk = LANES // NEU_BLOCK
    halves = []
    for b in range(c * per_chunk, (c + 1) * per_chunk):
        total = jnp.zeros((NEU_BLOCK, frames), F32)
        for v in range(2 * HB + 1):
            q = b - v
            if any(start <= q < stop for start, stop in ranges):
                k = place[q, v]
                at = pl.multiple_of((q * K + jnp.maximum(k, 0)) * NEU_BLOCK, NEU_BLOCK)
                value = contrib[pl.ds(at, NEU_BLOCK), :]
                if v % 2:
                    value = jnp.where(k >= 0, value, 0.0)
                total = total + value
        halves.append(total)
    return jnp.concatenate(halves, axis=0).T


def edge_kernel(
    pattern_far, z3, p3, rows, pay, pays, feet, record, ext, zones, spill, send_a, send_b, *rest
):
    *traces, contrib, place, pattern, sem = rest
    fetch = pltpu.make_async_copy(pattern_far, pattern, sem)
    fetch.start()
    chunks = chunk_count(z3)
    stripe = pattern.shape[1]
    edge = 2 * HB
    ranges = ((0, edge), (stripe - edge, stripe))

    @after_start
    def _():
        me = lax.axis_index("tm")
        totals = block_totals(pay, me, chunks, rows)
        ends = by_block(pays, me, 0)
        carry = jnp.zeros_like(totals[0])
        for m, end in enumerate(ends):
            carry = jnp.where(m < me, end + totals[m] * carry, carry)
        carry = carry * rows[1]
        for c in range(chunks):
            field = chunk(p3, c)[...] * (chunk(z3, c)[...] + carry[c : c + 1, :])
            at = slice(c * LANES, (c + 1) * LANES)
            if traces and RIM <= c < chunks - RIM:
                field = field.T
                traces[0][(c - RIM) * LANES : (c - RIM + 1) * LANES, :] = field
                ext[at, :] = field.astype(BF16)
            else:
                ext[at, :] = field.astype(BF16).T

    fetch.wait()
    for start, stop in ranges:
        note_places(pattern, place, start, stop)
    for start, stop in ranges:
        for q in range(start, stop):
            pull_back(pattern, ext, feet, record, contrib, q)
    even = lax.axis_index("tile") % 2 == 0
    for i in range(2 * RIM):
        below = gathered(contrib, place, i, ranges)
        above = gathered(contrib, place, chunks - 2 * RIM + i, ranges)
        zones[i] = below
        zones[2 * RIM + i] = above
        send_a[i] = jnp.where(even, above, below).astype(BF16)
        send_b[i] = jnp.where(even, below, above).astype(BF16)
        spill[i] = gathered(contrib, place, 2 * RIM + i, ranges)
        spill[2 * RIM + i] = gathered(contrib, place, chunks - 4 * RIM + i, ranges)

def adjoint_chunk(sums_table, field, p, pinv, rows, c, r3, pay):
    frames = field.shape[0]
    r = summed(sums_table, field * p)
    r3[...] = r
    gain = rows[0, c : c + 1, :]
    pay[0, c : c + 1, :] = rows[1, c : c + 1, :] * r[0:1, :]
    ends = p[frames - 1 : frames, :] * gain * gain
    pay[1, c : c + 1, :] = ends * jnp.sum(pinv * pinv * r, axis=0, keepdims=True)


def inner_kernel(pattern_far, p3, pinv3, rows, ext, spill, feet, record, traces, r3, pay, *rest):
    *out, contrib, place, pattern, sem = rest[: 4 + len(traces)]
    fetch = pltpu.make_async_copy(pattern_far, pattern, sem)
    fetch.start()
    if traces:
        copy = pltpu.make_async_copy(traces[0], out[0], rest[-1])
        copy.start()
    fetch.wait()

    def compute():
        chunks = chunk_count(p3)
        frames = spill.shape[1]
        stripe = pattern.shape[1]
        edge = 2 * HB
        note_places(pattern, place, edge, stripe - edge)
        sums_table = table(frames, True)
        pay[...] = jnp.zeros_like(pay)
        inner = chunks - 4 * RIM
        for q in range(edge, stripe - edge):
            pull_back(pattern, ext, feet, record, contrib, q)
        for i in range(inner):
            c = i + 2 * RIM
            field = gathered(contrib, place, c, ((edge, stripe - edge),))
            if i < 2 * RIM:
                field = field + spill[i]
            if i >= inner - 2 * RIM:
                field = field + spill[i - inner + 4 * RIM]
            p, pinv = chunk(p3, c)[...], chunk(pinv3, c)[...]
            adjoint_chunk(sums_table, field, p, pinv, rows, c, r3.at[i], pay)

    if traces:
        after_start(compute)
        copy.wait()
    else:
        compute()


def border_kernel(zones, got_a, got_b, p3, pinv3, rows, pay_inner, r3, pay):
    chunks = chunk_count(p3)
    frames = zones.shape[1]
    sums_table = table(frames, True)
    pay[...] = pay_inner[...]
    even = lax.axis_index("tile") % 2 == 0
    for i in range(2 * RIM):
        both = sides(even, got_a[i].astype(F32), got_b[i].astype(F32))
        for side, c in ((0, i), (1, chunks - 2 * RIM + i)):
            at = side * 2 * RIM + i
            field = zones[at] + both[side]
            p, pinv = chunk(p3, c)[...], chunk(pinv3, c)[...]
            adjoint_chunk(sums_table, field, p, pinv, rows, c, r3.at[at], pay)


def direction_kernel(
    pattern_far, r_inner, r_border, p3, pinv3, rows, pay, pays, feet, g3, stats, low, high, *rest
):
    pattern, sem, grad_sums = rest
    fetch = pltpu.make_async_copy(pattern_far, pattern, sem)
    fetch.start()
    chunks, frames = g3.shape[0], g3.shape[1]
    own = chunks - 2 * RIM
    stripe = pattern.shape[1]
    per_chunk = LANES // NEU_BLOCK
    low_chunks = low.shape[0] // LANES
    first_high = chunks - high.shape[0] // LANES

    @after_start
    def _():
        me = lax.axis_index("tm")
        totals = block_totals(pay, me, chunks, rows)
        gains = by_block(pay, me, 1)
        starts = by_block(pays, me, 0)
        ends = by_block(pays, me, 1)
        blocks = len(pays)
        entering = [None] * blocks
        state = jnp.zeros_like(totals[0])
        for m in reversed(range(blocks)):
            entering[m] = state
            state = starts[m] + totals[m] * state
        carry = jnp.zeros_like(totals[0])
        adjoint = jnp.zeros_like(totals[0])
        for m in range(blocks):
            end = ends[m] + gains[m] * entering[m]
            carry = jnp.where(m < me, end + totals[m] * carry, carry)
            adjoint = jnp.where(m == me, entering[m], adjoint)
        carry = carry * rows[1]
        sums_table = table(frames, False)
        grad_sq = jnp.zeros((8, LANES), F32)
        for c in range(chunks):
            p = chunk(p3, c)[...]
            if c < 2 * RIM:
                r = r_border[c]
            elif c >= chunks - 2 * RIM:
                r = r_border[c - chunks + 4 * RIM]
            else:
                r = r_inner[c - 2 * RIM]
            scale = rows[0, c : c + 1, :] * chunk(pinv3, c)[...]
            gradient = scale * (r + p[frames - 1 : frames, :] * adjoint[c : c + 1, :])
            g3[c] = gradient
            if RIM <= c < RIM + own:
                grad_sq += jnp.sum((gradient * gradient).reshape(frames // 8, 8, LANES), axis=0)
            z = summed(sums_table, scale * gradient)
            field = (p * (z + carry[c : c + 1, :])).astype(BF16).T
            if c < low_chunks:
                low[c * LANES : (c + 1) * LANES, :] = field
            if c >= first_high:
                high[(c - first_high) * LANES : (c - first_high + 1) * LANES, :] = field
        grad_sums[...] = grad_sq

    fetch.wait()
    image_sq = jnp.zeros((8, frames), F32)
    for q in range(stripe):
        if q + 2 * HB < low_chunks * per_chunk:
            named = picked(low, pattern, q, 0)
        else:
            named = picked(high, pattern, q, first_high * per_chunk)
        image = jnp.dot(foot_of(feet, q, stripe), named, preferred_element_type=F32)
        image_sq += jnp.sum((image * image).reshape(PIX_BLOCK // 8, 8, frames), axis=0)
    both = jnp.concatenate(
        [
            jnp.sum(grad_sums[...], axis=0, keepdims=True),
            jnp.sum(image_sq, axis=0, keepdims=True),
        ],
        axis=0,
    )
    stats[...] = jnp.broadcast_to(both[None], stats.shape)


def f32(*shape):
    return jax.ShapeDtypeStruct(shape, F32)


def bf16(*shape):
    return jax.ShapeDtypeStruct(shape, BF16)


def call(
    kernel, name, micros, outs, args, scratch=(), far=(), far_out=(), keep=(), limit=16
):
    def spec(arg):
        if any(arg is other for other in far):
            return HBM
        return pl.BlockSpec(memory_space=pl.ANY) if arg.dtype == jnp.int32 else VMEM

    in_specs = [jax.tree.map(spec, arg) for arg in args]
    in_specs.append(jax.tree.map(lambda _: VMEM, keep))

    def body(*refs):
        kernel(*refs[: len(args)], *refs[len(args) + 1 :])

    return pl.pallas_call(
        body,
        name=name,
        out_shape=outs,
        in_specs=in_specs,
        out_specs=tuple(
            jax.tree.map(lambda _: HBM if place in far_out else VMEM, out)
            for place, out in enumerate(outs)
        ),
        scratch_shapes=scratch,
        compiler_params=pltpu.CompilerParams(vmem_limit_bytes=int(limit * 2**20)),
        cost_estimate=pl.CostEstimate(
            flops=int(micros * 1e8), bytes_accessed=int(micros * 3e6), transcendentals=0
        ),
    )(*args, keep)


def swapped(first, second):
    size = lax.axis_size("tile")

    def pairs(start):
        both = [(i, i + 1) for i in range(start, size - 1, 2)]
        return both + [(j, i) for i, j in both]

    return lax.ppermute(first, "tile", pairs(0)), lax.ppermute(second, "tile", pairs(1))


def shared_blocks(value):
    size = lax.axis_size("tm")
    known = [value]
    bit = size // 2
    while bit:
        known += [lax.ppermute(x, "tm", [(i, i ^ bit) for i in range(size)]) for x in known]
        bit //= 2
    return tuple(known)


def per_device(recording, footprints, pattern, decay, frame_gain, spikes):
    neurons, frames = spikes.shape
    stripe = pattern.shape[0]
    pattern = pattern.T
    own = neurons // LANES
    chunks = own + 2 * RIM
    lines = own + padded8(1)
    devices = lax.axis_size("tile") * lax.axis_size("tm")
    split = (f32(own, frames, LANES), f32(2 * RIM, frames, LANES))
    message = f32(RIM * LANES + padded8(RIM), frames)
    gains = frame_gain.reshape(1, frames)
    rates = decay.reshape(own, LANES)
    first, second, rates = call(
        rims_kernel,
        "rims",
        1.0,
        (message, message, f32(own, LANES)),
        (spikes, rates),
        [pltpu.SemaphoreType.DMA((3,))],
        far=(spikes, rates),
        limit=53,
    )
    first, second = swapped(first, second)
    ends_size = 4 * HB * PIX_BLOCK
    *owns, rows, pay, columns, feet_ends = call(
        prep_own_kernel,
        "prep_own",
        1.6,
        (split[0],) * 4
        + (f32(3, lines, LANES), f32(2, lines, LANES), f32(2, frames, LANES))
        + (bf16(ends_size, K * NEU_BLOCK),),
        (spikes, rates, gains, footprints),
        [pltpu.SemaphoreType.DMA((2,))],
        far=(footprints,),
        limit=44,
    )
    *rims, rows, pay = call(
        prep_rim_kernel,
        "prep_rim",
        0.3,
        (split[1],) * 4 + (f32(3, lines, LANES), f32(2, lines, LANES)),
        (first, second, columns, rows, pay),
    )
    s3, p3, pinv3, z3 = zip(owns, rims)
    constants = pays = shared_blocks(pay)
    scratch = [
        pltpu.VMEM((stripe * K * NEU_BLOCK, frames), F32),
        pltpu.SMEM((stripe, 2 * HB + 1), jnp.int32),
        pltpu.SMEM(pattern.shape, jnp.int32),
        pltpu.SemaphoreType.DMA,
    ]
    staged = [pltpu.VMEM((neurons, frames), F32), pltpu.SemaphoreType.DMA((PARTS,))]
    middle = stripe * NEU_BLOCK // LANES // 2
    halves = (middle + 2 * RIM, chunks - middle)
    zone = (2 * RIM, frames, LANES)
    border = (4 * RIM, frames, LANES)
    for iteration in range(ITERS):
        ends = iteration == ITERS - 1
        ext, zones, spill, send_a, send_b, *traces = call(
            edge_kernel,
            "edge",
            2.5,
            (
                bf16(chunks * LANES, frames),
                f32(*border),
                f32(*border),
                bf16(*zone),
                bf16(*zone),
            )
            + ((f32(neurons, frames),) if ends else ()),
            (pattern, z3, p3, rows, constants, pays, feet_ends, recording),
            scratch,
            keep=(s3[0],) if ends else (),
        )
        got_a, got_b = swapped(send_a, send_b)
        held = (s3[0],) if ends else ()
        r_inner, pay, *traces = call(
            inner_kernel,
            "inner",
            4.0,
            (f32(chunks - 4 * RIM, frames, LANES), f32(2, lines, LANES))
            + ((f32(neurons, frames),) if ends else ()),
            (pattern, p3, pinv3, rows, ext, spill, footprints, recording, traces),
            scratch + ([pltpu.SemaphoreType.DMA] if ends else []),
            far_out=(2,),
            keep=held,
        )
        r_border, pay = call(
            border_kernel,
            "border",
            0.3,
            (f32(*border), f32(2, lines, LANES)),
            (zones, got_a, got_b, p3, pinv3, rows, pay),
            keep=held,
        )
        pays = shared_blocks(pay)
        g3, stats = call(
            direction_kernel,
            "direction",
            4.0,
            (f32(chunks, frames, LANES), f32(devices, 2, LANES)),
            (pattern, r_inner, r_border, p3, pinv3, rows, constants, pays, footprints),
            [
                pltpu.VMEM((halves[0] * LANES, frames), BF16),
                pltpu.VMEM((halves[1] * LANES, frames), BF16),
                *scratch[2:],
                pltpu.VMEM((8, LANES), F32),
            ],
            keep=held,
        )
        stats = lax.all_to_all(stats, ("tile", "tm"), 0, 0)
        if ends:
            (out,) = call(
                final_kernel,
                "final",
                1.4,
                (f32(neurons, frames),),
                (s3[0], g3, stats),
                staged,
                far_out=(0,),
            )
            return out, traces[0]
        s3, z3, pay = call(
            update_kernel,
            "update",
            0.6,
            (split if iteration < ITERS - 2 else split[:1], split, f32(1, lines, LANES)),
            (s3, g3, stats, p3, pinv3, rows),
        )
        pays = shared_blocks(pay)


def solution(mesh):
    return jax.shard_map(
        per_device,
        mesh=mesh,
        in_specs=(
            P("tile", "tm"),
            P("tile", None),
            P("tile", None),
            P("tile"),
            P("tm"),
            P("tile", "tm"),
        ),
        out_specs=(P("tile", "tm"), P("tile", "tm")),
        check_vma=False,
    )
```

```python
import jax
import jax.numpy as jnp
from jax import lax
from jax.experimental import pallas as pl
from jax.experimental.pallas import tpu as pltpu
from jax.sharding import PartitionSpec as P

NEU_BLOCK = 64
PIX_BLOCK = 256
PARTS = 8
K = 4
HB = 2
ITERS = 2
LANES = 128
RIM = HB * NEU_BLOCK // LANES
F32 = jnp.float32
BF16 = jnp.bfloat16
VMEM = pl.BlockSpec(memory_space=pltpu.VMEM)
HBM = pl.BlockSpec(memory_space=pltpu.HBM)


def padded8(rows):
    return -(-rows // 8) * 8


def table(frames, reverse):
    row = lax.broadcasted_iota(jnp.int32, (frames, 2 * frames), 0)
    col = lax.broadcasted_iota(jnp.int32, (frames, 2 * frames), 1)
    col = jnp.where(col >= frames, col - frames, col)
    keep = col >= row if reverse else col <= row
    return jnp.where(keep, 1.0, 0.0).astype(BF16)


def summed(sums_table, values):
    high = values.astype(BF16)
    low = (values - high.astype(F32)).astype(BF16)
    both = jnp.concatenate([high, low], axis=0)
    return jnp.dot(sums_table, both, preferred_element_type=F32)


def powers(log_decay, frames, mid, sign):
    groups = frames // 8
    coarse = (8 * lax.broadcasted_iota(jnp.int32, (groups, LANES), 0) - mid).astype(F32) * sign
    fine = lax.broadcasted_iota(jnp.int32, (8, LANES), 0).astype(F32) * sign
    coarse = jnp.exp(coarse * log_decay)
    fine = jnp.exp(fine * log_decay)
    return (coarse[:, None, :] * fine[None, :, :]).reshape(frames, LANES)


def chunk(field, c):
    own, rim = field
    inner = own.shape[0]
    if c < RIM:
        return rim.at[c]
    if c >= RIM + inner:
        return rim.at[c - inner]
    return own.at[c - RIM]


def chunk_count(field):
    return field[0].shape[0] + field[1].shape[0]


def prep_chunk(c, rate, field, gains, s3, p3, pinv3, z3, rows, pay):
    frames = field.shape[1]
    middle, prefix_col, inverse_col, sums_table = gains
    mid = frames // 2 - 1
    rate = jnp.where(rate > 0.0, rate, 1.0)
    log_rate = jnp.log(rate)
    gain = jnp.sqrt(1.0 - rate * rate)
    p = powers(log_rate, frames, mid, 1.0) * prefix_col
    pinv = powers(log_rate, frames, mid, -1.0) * inverse_col
    field = field.T
    z = summed(sums_table, field * gain * pinv)
    last = p[frames - 1 : frames, :]
    s3[...] = field
    p3[...] = p
    pinv3[...] = pinv
    z3[...] = z
    half = rate
    for _ in range(frames.bit_length() - 2):
        half = half * half
    rows[0, c : c + 1, :] = gain
    rows[1, c : c + 1, :] = half * middle
    rows[2, c : c + 1, :] = half * half
    pay[0, c : c + 1, :] = last * z[frames - 1 : frames, :]
    scale = last * gain
    pay[1, c : c + 1, :] = scale * scale * jnp.sum(pinv * pinv, axis=0, keepdims=True)


def gain_columns(gains):
    frames = gains.shape[1]
    mid = frames // 2 - 1
    lane = lax.broadcasted_iota(jnp.int32, (8, frames), 1)
    prefix = jnp.broadcast_to(gains, (8, frames))
    step = 1
    while step < frames:
        prefix = prefix * jnp.where(lane >= step, pltpu.roll(prefix, step, 1), 1.0)
        step *= 2
    middle = jnp.broadcast_to(prefix[0:1, mid : mid + 1], (1, LANES))
    whole = jnp.broadcast_to(prefix[0:1, frames - 1 : frames], (1, LANES))
    prefix_col = jnp.broadcast_to(prefix[0:1] / middle, (LANES, frames)).T
    inverse_col = jnp.broadcast_to(middle / prefix[0:1], (LANES, frames)).T
    return middle, whole, prefix_col, inverse_col


def rims_kernel(spikes, decay, first, second, rates_here, sems):
    edge = RIM * LANES
    neurons = spikes.shape[0]
    own = decay.shape[0]
    even = lax.axis_index("tile") % 2 == 0
    top = jnp.where(even, neurons - edge, 0)
    bottom = jnp.where(even, 0, neurons - edge)
    copies = [
        pltpu.make_async_copy(decay, rates_here, sems.at[0]),
        pltpu.make_async_copy(
            spikes.at[pl.ds(pl.multiple_of(top, LANES), edge)], first.at[pl.ds(0, edge)], sems.at[1]
        ),
        pltpu.make_async_copy(
            spikes.at[pl.ds(pl.multiple_of(bottom, LANES), edge)],
            second.at[pl.ds(0, edge)],
            sems.at[2],
        ),
    ]
    for copy in copies:
        copy.start()
    first[edge:, :] = jnp.zeros_like(first[edge:, :])
    second[edge:, :] = jnp.zeros_like(second[edge:, :])
    copies[0].wait()
    lower, upper = rates_here[0:RIM, :], rates_here[own - RIM : own, :]
    first[edge : edge + RIM, :] = jnp.where(even, upper, lower)
    second[edge : edge + RIM, :] = jnp.where(even, lower, upper)
    for copy in copies[1:]:
        copy.wait()


def after_start(compute):
    pl.when(lax.axis_index("tm") >= 0)(compute)


def prep_own_kernel(
    spikes, decay, gains, feet, s3, p3, pinv3, z3, rows, pay, columns, feet_ends, sems
):
    own = s3.shape[0]
    chunks = own + 2 * RIM
    size = feet_ends.shape[0] // 2
    fetches = [
        pltpu.make_async_copy(
            feet.at[pl.ds(start, size)], feet_ends.at[pl.ds(i * size, size)], sems.at[i]
        )
        for i, start in enumerate((0, feet.shape[0] - size))
    ]
    for fetch in fetches:
        fetch.start()

    @after_start
    def _():
        middle, whole, prefix_col, inverse_col = gain_columns(gains[...])
        columns[0] = prefix_col
        columns[1] = inverse_col
        rows[...] = jnp.ones_like(rows)
        rows[0, chunks : chunks + 1, :] = middle
        pay[...] = jnp.zeros_like(pay)
        pay[0, chunks : chunks + 1, :] = whole
        shared = middle, prefix_col, inverse_col, table(spikes.shape[1], False)
        for i in range(own):
            field = spikes[i * LANES : (i + 1) * LANES, :]
            at = [ref.at[i] for ref in (s3, p3, pinv3, z3)]
            prep_chunk(i + RIM, decay[i : i + 1, :], field, shared, *at, rows, pay)

    for fetch in fetches:
        fetch.wait()


def sides(even, first, second):
    return jnp.where(even, second, first), jnp.where(even, first, second)


def prep_rim_kernel(first, second, columns, rows_own, pay_own, s3, p3, pinv3, z3, rows, pay):
    rims, frames = s3.shape[0], s3.shape[1]
    own = rows_own.shape[1] - padded8(1)
    chunks = own + 2 * RIM
    middle = rows_own[0, chunks : chunks + 1, :]
    shared = middle, columns[0], columns[1], table(frames, False)
    rows[...] = rows_own[...]
    pay[...] = pay_own[...]
    even = lax.axis_index("tile") % 2 == 0
    below, above = sides(even, first[...], second[...])
    for i in range(rims):
        message = below if i < RIM else above
        j = i % RIM
        c = i if i < RIM else own + i
        at = [ref.at[i] for ref in (s3, p3, pinv3, z3)]
        field = message[j * LANES : (j + 1) * LANES, :]
        rate = message[RIM * LANES + j : RIM * LANES + j + 1, :]
        prep_chunk(c, rate, field, shared, *at, rows, pay)


def distances(size):
    found = [0]
    bit = size // 2
    while bit:
        found += [other ^ bit for other in found]
        bit //= 2
    return found


def by_block(parts, me, index):
    values = [part[index] for part in parts]
    ordered = []
    for m in range(len(values)):
        value = values[0]
        for distance, other in zip(distances(len(values))[1:], values[1:]):
            value = jnp.where(me == m ^ distance, other, value)
        ordered.append(value)
    return ordered


def block_totals(pay, me, chunks, rows):
    return [rows[2] * whole for whole in by_block(pay, me, (0, slice(chunks, chunks + 1)))]


def step_size(stats):
    both = jnp.sum(jnp.sum(stats[...], axis=0), axis=1, keepdims=True)
    return jnp.broadcast_to(both[0:1] / (both[1:2] + 1e-06), (1, LANES))


def update_kernel(s3, g3, stats, p3, pinv3, rows, new3, z3, pay):
    chunks = chunk_count(s3)
    frames = g3.shape[1]
    sums_table = table(frames, False)
    size = step_size(stats)
    pay[...] = jnp.zeros_like(pay)
    for c in range(chunks):
        field = jnp.maximum(chunk(s3, c)[...] - size * g3[c], 0.0)
        z = summed(sums_table, field * rows[0, c : c + 1, :] * chunk(pinv3, c)[...])
        if len(new3) == 2:
            chunk(new3, c)[...] = field
        elif RIM <= c < chunks - RIM:
            new3[0][c - RIM] = field
        chunk(z3, c)[...] = z
        last = chunk(p3, c)[frames - 1 : frames, :]
        pay[0, c : c + 1, :] = last * z[frames - 1 : frames, :]


def final_kernel(s3, g3, stats, out, here, sems):
    size = step_size(stats)
    part = s3.shape[0] // PARTS
    copies = [
        pltpu.make_async_copy(
            here.at[pl.ds(i * part * LANES, part * LANES)],
            out.at[pl.ds(i * part * LANES, part * LANES)],
            sems.at[i],
        )
        for i in range(PARTS)
    ]
    for i in range(PARTS):

        @after_start
        def _():
            for c in range(i * part, (i + 1) * part):
                field = jnp.maximum(s3[c] - size * g3[c + RIM], 0.0)
                here[c * LANES : (c + 1) * LANES, :] = field.T
            copies[i].start()

    for copy in copies:
        copy.wait()


def picked(ext, pattern, q, first=0):
    parts = [
        ext[pl.ds(pl.multiple_of((pattern[k, q] - first) * NEU_BLOCK, NEU_BLOCK), NEU_BLOCK), :]
        for k in range(K)
    ]
    return jnp.concatenate(parts, axis=0)


def block_of(field, q):
    return field[q * PIX_BLOCK : (q + 1) * PIX_BLOCK, :]


def foot_of(feet, q, stripe):
    count = feet.shape[0] // PIX_BLOCK
    return block_of(feet, q if q < count // 2 else q - stripe + count)


def note_places(pattern, place, start, stop):
    for q in range(start, stop):
        for v in range(2 * HB + 1):
            place[q, v] = -1
        for k in range(K):
            place[q, pattern[k, q] - q] = k


def pull_back(pattern, ext, feet, record, contrib, q, first=0):
    foot = foot_of(feet, q, pattern.shape[1])
    fitted = jnp.dot(foot, picked(ext, pattern, q, first), preferred_element_type=F32)
    residual = (fitted - block_of(record, q).astype(F32)).astype(BF16)
    contrib[q * K * NEU_BLOCK : (q + 1) * K * NEU_BLOCK, :] = lax.dot_general(
        foot, residual, (((0,), (0,)), ((), ())), preferred_element_type=F32
    )


def gathered(contrib, place, c, ranges):
    frames = contrib.shape[1]
    per_chunk = LANES // NEU_BLOCK
    halves = []
    for b in range(c * per_chunk, (c + 1) * per_chunk):
        total = jnp.zeros((NEU_BLOCK, frames), F32)
        for v in range(2 * HB + 1):
            q = b - v
            if any(start <= q < stop for start, stop in ranges):
                k = place[q, v]
                at = pl.multiple_of((q * K + jnp.maximum(k, 0)) * NEU_BLOCK, NEU_BLOCK)
                value = contrib[pl.ds(at, NEU_BLOCK), :]
                if v % 2:
                    value = jnp.where(k >= 0, value, 0.0)
                total = total + value
        halves.append(total)
    return jnp.concatenate(halves, axis=0).T


def edge_kernel(
    pattern_far, z3, p3, rows, pay, pays, feet, record, ext, zones, spill, send_a, send_b, *rest
):
    *traces, contrib, place, pattern, sem, near, state = rest
    fetch = pltpu.make_async_copy(pattern_far, pattern, sem)
    fetch.start()
    chunks = chunk_count(z3)
    stripe = pattern.shape[1]
    edge = 2 * HB
    ranges = ((0, edge), (stripe - edge, stripe))
    near_chunks = near.shape[0] // LANES // 2
    inner = range(near_chunks, chunks - near_chunks)

    def trace(c):
        field = chunk(p3, c)[...] * (chunk(z3, c)[...] + state[c : c + 1, :])
        if traces and RIM <= c < chunks - RIM:
            field = field.T
            traces[0][(c - RIM) * LANES : (c - RIM + 1) * LANES, :] = field
            field = field.astype(BF16)
        else:
            field = field.astype(BF16).T
        ext[c * LANES : (c + 1) * LANES, :] = field
        return field

    @after_start
    def _():
        me = lax.axis_index("tm")
        totals = block_totals(pay, me, chunks, rows)
        ends = by_block(pays, me, 0)
        carry = jnp.zeros_like(totals[0])
        for m, end in enumerate(ends):
            carry = jnp.where(m < me, end + totals[m] * carry, carry)
        state[...] = carry * rows[1]
        for c in range(chunks):
            if c not in inner:
                at = c if c < near_chunks else c - len(inner)
                near[at * LANES : (at + 1) * LANES, :] = trace(c)

    fetch.wait()
    for start, stop in ranges:
        note_places(pattern, place, start, stop)
    for start, stop in ranges:
        first = 0 if start == 0 else len(inner) * LANES // NEU_BLOCK
        for q in range(start, stop):
            pull_back(pattern, near, feet, record, contrib, q, first)
    for c in inner:
        trace(c)
    even = lax.axis_index("tile") % 2 == 0
    for i in range(2 * RIM):
        below = gathered(contrib, place, i, ranges)
        above = gathered(contrib, place, chunks - 2 * RIM + i, ranges)
        zones[i] = below
        zones[2 * RIM + i] = above
        send_a[i] = jnp.where(even, above, below).astype(BF16)
        send_b[i] = jnp.where(even, below, above).astype(BF16)
        spill[i] = gathered(contrib, place, 2 * RIM + i, ranges)
        spill[2 * RIM + i] = gathered(contrib, place, chunks - 4 * RIM + i, ranges)

def adjoint_chunk(sums_table, field, p, pinv, rows, c, r3, pay):
    frames = field.shape[0]
    r = summed(sums_table, field * p)
    r3[...] = r
    gain = rows[0, c : c + 1, :]
    pay[0, c : c + 1, :] = rows[1, c : c + 1, :] * r[0:1, :]
    ends = p[frames - 1 : frames, :] * gain * gain
    pay[1, c : c + 1, :] = ends * jnp.sum(pinv * pinv * r, axis=0, keepdims=True)


def inner_kernel(pattern_far, p3, pinv3, rows, ext, spill, feet, record, traces, r3, pay, *rest):
    *out, contrib, place, pattern, sem = rest[: 4 + len(traces)]
    fetch = pltpu.make_async_copy(pattern_far, pattern, sem)
    fetch.start()
    if traces:
        copy = pltpu.make_async_copy(traces[0], out[0], rest[-1])
        copy.start()
    fetch.wait()

    def compute():
        chunks = chunk_count(p3)
        frames = spill.shape[1]
        stripe = pattern.shape[1]
        edge = 2 * HB
        note_places(pattern, place, edge, stripe - edge)
        sums_table = table(frames, True)
        pay[...] = jnp.zeros_like(pay)
        inner = chunks - 4 * RIM
        for q in range(edge, stripe - edge):
            pull_back(pattern, ext, feet, record, contrib, q)
        for i in range(inner):
            c = i + 2 * RIM
            field = gathered(contrib, place, c, ((edge, stripe - edge),))
            if i < 2 * RIM:
                field = field + spill[i]
            if i >= inner - 2 * RIM:
                field = field + spill[i - inner + 4 * RIM]
            p, pinv = chunk(p3, c)[...], chunk(pinv3, c)[...]
            adjoint_chunk(sums_table, field, p, pinv, rows, c, r3.at[i], pay)

    if traces:
        after_start(compute)
        copy.wait()
    else:
        compute()


def border_kernel(zones, got_a, got_b, p3, pinv3, rows, pay_inner, r3, pay):
    chunks = chunk_count(p3)
    frames = zones.shape[1]
    sums_table = table(frames, True)
    pay[...] = pay_inner[...]
    even = lax.axis_index("tile") % 2 == 0
    for i in range(2 * RIM):
        both = sides(even, got_a[i].astype(F32), got_b[i].astype(F32))
        for side, c in ((0, i), (1, chunks - 2 * RIM + i)):
            at = side * 2 * RIM + i
            field = zones[at] + both[side]
            p, pinv = chunk(p3, c)[...], chunk(pinv3, c)[...]
            adjoint_chunk(sums_table, field, p, pinv, rows, c, r3.at[at], pay)


def direction_kernel(
    pattern_far, r_inner, r_border, p3, pinv3, rows, pay, pays, feet, g3, stats, low, high, *rest
):
    pattern, sem, grad_sums, image_sums, states = rest
    fetch = pltpu.make_async_copy(pattern_far, pattern, sem)
    fetch.start()
    chunks, frames = g3.shape[0], g3.shape[1]
    own = chunks - 2 * RIM
    stripe = pattern.shape[1]
    per_chunk = LANES // NEU_BLOCK
    low_chunks = low.shape[0] // LANES
    first_high = chunks - high.shape[0] // LANES

    sums_table = table(frames, False)

    def work(c):
        p = chunk(p3, c)[...]
        if c < 2 * RIM:
            r = r_border[c]
        elif c >= chunks - 2 * RIM:
            r = r_border[c - chunks + 4 * RIM]
        else:
            r = r_inner[c - 2 * RIM]
        scale = rows[0, c : c + 1, :] * chunk(pinv3, c)[...]
        gradient = scale * (r + p[frames - 1 : frames, :] * states[1, c : c + 1, :])
        g3[c] = gradient
        z = summed(sums_table, scale * gradient)
        field = (p * (z + states[0, c : c + 1, :])).astype(BF16).T
        if c < low_chunks:
            low[c * LANES : (c + 1) * LANES, :] = field
        if c >= first_high:
            high[(c - first_high) * LANES : (c - first_high + 1) * LANES, :] = field
        if RIM <= c < RIM + own:
            return jnp.sum((gradient * gradient).reshape(frames // 8, 8, LANES), axis=0)
        return jnp.zeros((8, LANES), F32)

    def image(q):
        if q + 2 * HB < low_chunks * per_chunk:
            named = picked(low, pattern, q, 0)
        else:
            named = picked(high, pattern, q, first_high * per_chunk)
        value = jnp.dot(foot_of(feet, q, stripe), named, preferred_element_type=F32)
        return jnp.sum((value * value).reshape(PIX_BLOCK // 8, 8, frames), axis=0)

    @after_start
    def _():
        me = lax.axis_index("tm")
        totals = block_totals(pay, me, chunks, rows)
        gains = by_block(pay, me, 1)
        starts = by_block(pays, me, 0)
        ends = by_block(pays, me, 1)
        blocks = len(pays)
        entering = [None] * blocks
        state = jnp.zeros_like(totals[0])
        for m in reversed(range(blocks)):
            entering[m] = state
            state = starts[m] + totals[m] * state
        carry = jnp.zeros_like(totals[0])
        adjoint = jnp.zeros_like(totals[0])
        for m in range(blocks):
            end = ends[m] + gains[m] * entering[m]
            carry = jnp.where(m < me, end + totals[m] * carry, carry)
            adjoint = jnp.where(m == me, entering[m], adjoint)
        states[0] = carry * rows[1]
        states[1] = adjoint
        grad_sums[...] = sum(work(c) for c in range(low_chunks))

    fetch.wait()

    @after_start
    def _():
        grad_sq = grad_sums[...]
        image_sq = jnp.zeros((8, frames), F32)
        q = 0
        rest_chunks = chunks - low_chunks
        low_blocks = (low_chunks * per_chunk) - 2 * HB
        for i in range(rest_chunks):
            grad_sq += work(low_chunks + i)
            while q < low_blocks * (i + 1) // rest_chunks:
                image_sq += image(q)
                q += 1
        grad_sums[...] = grad_sq
        image_sums[...] = image_sq

    image_sq = image_sums[...]
    for q in range(low_chunks * per_chunk - 2 * HB, stripe):
        image_sq += image(q)
    both = jnp.concatenate(
        [
            jnp.sum(grad_sums[...], axis=0, keepdims=True),
            jnp.sum(image_sq, axis=0, keepdims=True),
        ],
        axis=0,
    )
    stats[...] = jnp.broadcast_to(both[None], stats.shape)


def f32(*shape):
    return jax.ShapeDtypeStruct(shape, F32)


def bf16(*shape):
    return jax.ShapeDtypeStruct(shape, BF16)


def call(
    kernel, name, micros, outs, args, scratch=(), far=(), far_out=(), keep=(), limit=16
):
    def spec(arg):
        if any(arg is other for other in far):
            return HBM
        return pl.BlockSpec(memory_space=pl.ANY) if arg.dtype == jnp.int32 else VMEM

    in_specs = [jax.tree.map(spec, arg) for arg in args]
    in_specs.append(jax.tree.map(lambda _: VMEM, keep))

    def body(*refs):
        kernel(*refs[: len(args)], *refs[len(args) + 1 :])

    return pl.pallas_call(
        body,
        name=name,
        out_shape=outs,
        in_specs=in_specs,
        out_specs=tuple(
            jax.tree.map(lambda _: HBM if place in far_out else VMEM, out)
            for place, out in enumerate(outs)
        ),
        scratch_shapes=scratch,
        compiler_params=pltpu.CompilerParams(vmem_limit_bytes=int(limit * 2**20)),
        cost_estimate=pl.CostEstimate(
            flops=int(micros * 1e8), bytes_accessed=int(micros * 3e6), transcendentals=0
        ),
    )(*args, keep)


def swapped(first, second):
    size = lax.axis_size("tile")

    def pairs(start):
        both = [(i, i + 1) for i in range(start, size - 1, 2)]
        return both + [(j, i) for i, j in both]

    return lax.ppermute(first, "tile", pairs(0)), lax.ppermute(second, "tile", pairs(1))


def shared_blocks(value):
    size = lax.axis_size("tm")
    known = [value]
    bit = size // 2
    while bit:
        known += [lax.ppermute(x, "tm", [(i, i ^ bit) for i in range(size)]) for x in known]
        bit //= 2
    return tuple(known)


def per_device(recording, footprints, pattern, decay, frame_gain, spikes):
    neurons, frames = spikes.shape
    stripe = pattern.shape[0]
    pattern = pattern.T
    own = neurons // LANES
    chunks = own + 2 * RIM
    lines = own + padded8(1)
    devices = lax.axis_size("tile") * lax.axis_size("tm")
    split = (f32(own, frames, LANES), f32(2 * RIM, frames, LANES))
    message = f32(RIM * LANES + padded8(RIM), frames)
    gains = frame_gain.reshape(1, frames)
    rates = decay.reshape(own, LANES)
    first, second, rates = call(
        rims_kernel,
        "rims",
        1.0,
        (message, message, f32(own, LANES)),
        (spikes, rates),
        [pltpu.SemaphoreType.DMA((3,))],
        far=(spikes, rates),
        limit=53,
    )
    first, second = swapped(first, second)
    ends_size = 4 * HB * PIX_BLOCK
    *owns, rows, pay, columns, feet_ends = call(
        prep_own_kernel,
        "prep_own",
        1.6,
        (split[0],) * 4
        + (f32(3, lines, LANES), f32(2, lines, LANES), f32(2, frames, LANES))
        + (bf16(ends_size, K * NEU_BLOCK),),
        (spikes, rates, gains, footprints),
        [pltpu.SemaphoreType.DMA((2,))],
        far=(footprints,),
        limit=44,
    )
    *rims, rows, pay = call(
        prep_rim_kernel,
        "prep_rim",
        0.3,
        (split[1],) * 4 + (f32(3, lines, LANES), f32(2, lines, LANES)),
        (first, second, columns, rows, pay),
    )
    s3, p3, pinv3, z3 = zip(owns, rims)
    constants = pays = shared_blocks(pay)
    scratch = [
        pltpu.VMEM((stripe * K * NEU_BLOCK, frames), F32),
        pltpu.SMEM((stripe, 2 * HB + 1), jnp.int32),
        pltpu.SMEM(pattern.shape, jnp.int32),
        pltpu.SemaphoreType.DMA,
    ]
    staged = [pltpu.VMEM((neurons, frames), F32), pltpu.SemaphoreType.DMA((PARTS,))]
    middle = stripe * NEU_BLOCK // LANES // 2
    halves = (middle + 2 * RIM, chunks - middle)
    zone = (2 * RIM, frames, LANES)
    border = (4 * RIM, frames, LANES)
    for iteration in range(ITERS):
        ends = iteration == ITERS - 1
        ext, zones, spill, send_a, send_b, *traces = call(
            edge_kernel,
            "edge",
            2.5,
            (
                bf16(chunks * LANES, frames),
                f32(*border),
                f32(*border),
                bf16(*zone),
                bf16(*zone),
            )
            + ((f32(neurons, frames),) if ends else ()),
            (pattern, z3, p3, rows, constants, pays, feet_ends, recording),
            [
                *scratch,
                pltpu.VMEM((8 * RIM * LANES, frames), BF16),
                pltpu.VMEM((lines, LANES), F32),
            ],
            keep=(s3[0],) if ends else (),
        )
        got_a, got_b = swapped(send_a, send_b)
        held = (s3[0],) if ends else ()
        r_inner, pay, *traces = call(
            inner_kernel,
            "inner",
            4.0,
            (f32(chunks - 4 * RIM, frames, LANES), f32(2, lines, LANES))
            + ((f32(neurons, frames),) if ends else ()),
            (pattern, p3, pinv3, rows, ext, spill, footprints, recording, traces),
            scratch + ([pltpu.SemaphoreType.DMA] if ends else []),
            far_out=(2,),
            keep=held,
        )
        r_border, pay = call(
            border_kernel,
            "border",
            0.3,
            (f32(*border), f32(2, lines, LANES)),
            (zones, got_a, got_b, p3, pinv3, rows, pay),
            keep=held,
        )
        pays = shared_blocks(pay)
        g3, stats = call(
            direction_kernel,
            "direction",
            4.0,
            (f32(chunks, frames, LANES), f32(devices, 2, LANES)),
            (pattern, r_inner, r_border, p3, pinv3, rows, constants, pays, footprints),
            [
                pltpu.VMEM((halves[0] * LANES, frames), BF16),
                pltpu.VMEM((halves[1] * LANES, frames), BF16),
                *scratch[2:],
                pltpu.VMEM((8, LANES), F32),
                pltpu.VMEM((8, frames), F32),
                pltpu.VMEM((2, lines, LANES), F32),
            ],
            keep=held,
        )
        stats = lax.all_to_all(stats, ("tile", "tm"), 0, 0)
        if ends:
            (out,) = call(
                final_kernel,
                "final",
                1.4,
                (f32(neurons, frames),),
                (s3[0], g3, stats),
                staged,
                far_out=(0,),
            )
            return out, traces[0]
        s3, z3, pay = call(
            update_kernel,
            "update",
            0.6,
            (split if iteration < ITERS - 2 else split[:1], split, f32(1, lines, LANES)),
            (s3, g3, stats, p3, pinv3, rows),
        )
        pays = shared_blocks(pay)


def solution(mesh):
    return jax.shard_map(
        per_device,
        mesh=mesh,
        in_specs=(
            P("tile", "tm"),
            P("tile", None),
            P("tile", None),
            P("tile"),
            P("tm"),
            P("tile", "tm"),
        ),
        out_specs=(P("tile", "tm"), P("tile", "tm")),
        check_vma=False,
    )
```

```python
import jax
import jax.numpy as jnp
from jax import lax
from jax.experimental import pallas as pl
from jax.experimental.pallas import tpu as pltpu
from jax.sharding import PartitionSpec as P

NEU_BLOCK = 64
PIX_BLOCK = 256
PARTS = 8
K = 4
HB = 2
ITERS = 2
LANES = 128
RIM = HB * NEU_BLOCK // LANES
F32 = jnp.float32
BF16 = jnp.bfloat16
VMEM = pl.BlockSpec(memory_space=pltpu.VMEM)
HBM = pl.BlockSpec(memory_space=pltpu.HBM)


def padded8(rows):
    return -(-rows // 8) * 8


def table(frames, reverse):
    row = lax.broadcasted_iota(jnp.int32, (frames, 2 * frames), 0)
    col = lax.broadcasted_iota(jnp.int32, (frames, 2 * frames), 1)
    col = jnp.where(col >= frames, col - frames, col)
    keep = col >= row if reverse else col <= row
    return jnp.where(keep, 1.0, 0.0).astype(BF16)


def summed(sums_table, values):
    high = values.astype(BF16)
    low = (values - high.astype(F32)).astype(BF16)
    both = jnp.concatenate([high, low], axis=0)
    return jnp.dot(sums_table, both, preferred_element_type=F32)


def powers(log_decay, frames, mid, sign):
    groups = frames // 8
    coarse = (8 * lax.broadcasted_iota(jnp.int32, (groups, LANES), 0) - mid).astype(F32) * sign
    fine = lax.broadcasted_iota(jnp.int32, (8, LANES), 0).astype(F32) * sign
    coarse = jnp.exp(coarse * log_decay)
    fine = jnp.exp(fine * log_decay)
    return (coarse[:, None, :] * fine[None, :, :]).reshape(frames, LANES)


def chunk(field, c):
    own, rim = field
    inner = own.shape[0]
    if c < RIM:
        return rim.at[c]
    if c >= RIM + inner:
        return rim.at[c - inner]
    return own.at[c - RIM]


def chunk_count(field):
    return field[0].shape[0] + field[1].shape[0]


def prep_chunk(c, rate, field, gains, s3, p3, pinv3, z3, rows, pay):
    frames = field.shape[1]
    middle, prefix_col, inverse_col, sums_table = gains
    mid = frames // 2 - 1
    rate = jnp.where(rate > 0.0, rate, 1.0)
    log_rate = jnp.log(rate)
    gain = jnp.sqrt(1.0 - rate * rate)
    p = powers(log_rate, frames, mid, 1.0) * prefix_col
    pinv = powers(log_rate, frames, mid, -1.0) * inverse_col
    field = field.T
    z = summed(sums_table, field * gain * pinv)
    last = p[frames - 1 : frames, :]
    s3[...] = field
    p3[...] = p
    pinv3[...] = pinv
    z3[...] = z
    half = rate
    for _ in range(frames.bit_length() - 2):
        half = half * half
    rows[0, c : c + 1, :] = gain
    rows[1, c : c + 1, :] = half * middle
    rows[2, c : c + 1, :] = half * half
    pay[0, c : c + 1, :] = last * z[frames - 1 : frames, :]
    scale = last * gain
    pay[1, c : c + 1, :] = scale * scale * jnp.sum(pinv * pinv, axis=0, keepdims=True)


def gain_columns(gains):
    frames = gains.shape[1]
    mid = frames // 2 - 1
    lane = lax.broadcasted_iota(jnp.int32, (8, frames), 1)
    prefix = jnp.broadcast_to(gains, (8, frames))
    step = 1
    while step < frames:
        prefix = prefix * jnp.where(lane >= step, pltpu.roll(prefix, step, 1), 1.0)
        step *= 2
    middle = jnp.broadcast_to(prefix[0:1, mid : mid + 1], (1, LANES))
    whole = jnp.broadcast_to(prefix[0:1, frames - 1 : frames], (1, LANES))
    prefix_col = jnp.broadcast_to(prefix[0:1] / middle, (LANES, frames)).T
    inverse_col = jnp.broadcast_to(middle / prefix[0:1], (LANES, frames)).T
    return middle, whole, prefix_col, inverse_col


def rims_kernel(spikes, decay, first, second, rates_here, sems):
    edge = RIM * LANES
    neurons = spikes.shape[0]
    own = decay.shape[0]
    even = lax.axis_index("tile") % 2 == 0
    top = jnp.where(even, neurons - edge, 0)
    bottom = jnp.where(even, 0, neurons - edge)
    copies = [
        pltpu.make_async_copy(decay, rates_here, sems.at[0]),
        pltpu.make_async_copy(
            spikes.at[pl.ds(pl.multiple_of(top, LANES), edge)], first.at[pl.ds(0, edge)], sems.at[1]
        ),
        *[
            pltpu.make_async_copy(
                spikes.at[pl.ds(pl.multiple_of(bottom, LANES), edge)],
                second.at[i, pl.ds(0, edge)],
                sems.at[2 + i],
            )
            for i in range(2)
        ],
    ]
    for copy in copies:
        copy.start()
    first[edge:, :] = jnp.zeros_like(first[edge:, :])
    second[:, edge:, :] = jnp.zeros_like(second[:, edge:, :])
    copies[0].wait()
    lower, upper = rates_here[0:RIM, :], rates_here[own - RIM : own, :]
    first[edge : edge + RIM, :] = jnp.where(even, upper, lower)
    for i in range(2):
        second[i, edge : edge + RIM, :] = jnp.where(even, lower, upper)
    for copy in copies[1:]:
        copy.wait()


def after_start(compute):
    pl.when(lax.axis_index("tm") >= 0)(compute)


def prep_own_kernel(
    spikes, decay, gains, feet, s3, p3, pinv3, z3, rows, pay, columns, feet_ends, sems
):
    own = s3.shape[0]
    chunks = own + 2 * RIM
    size = feet_ends.shape[0] // 2
    fetches = [
        pltpu.make_async_copy(
            feet.at[pl.ds(start, size)], feet_ends.at[pl.ds(i * size, size)], sems.at[i]
        )
        for i, start in enumerate((0, feet.shape[0] - size))
    ]
    for fetch in fetches:
        fetch.start()

    @after_start
    def _():
        middle, whole, prefix_col, inverse_col = gain_columns(gains[...])
        columns[0] = prefix_col
        columns[1] = inverse_col
        rows[...] = jnp.ones_like(rows)
        rows[0, chunks : chunks + 1, :] = middle
        pay[...] = jnp.zeros_like(pay)
        pay[0, chunks : chunks + 1, :] = whole
        shared = middle, prefix_col, inverse_col, table(spikes.shape[1], False)
        for i in range(own):
            field = spikes[i * LANES : (i + 1) * LANES, :]
            at = [ref.at[i] for ref in (s3, p3, pinv3, z3)]
            prep_chunk(i + RIM, decay[i : i + 1, :], field, shared, *at, rows, pay)

    for fetch in fetches:
        fetch.wait()


def sides(first, second):
    tile = lax.axis_index("tile")
    even = tile % 2 == 0
    inside = jnp.logical_and(tile > 0, tile < lax.axis_size("tile") - 1)
    second = jnp.where(inside, jnp.where(even, second[0], second[1]), 0.0)
    return jnp.where(even, second, first), jnp.where(even, first, second)


def prep_rim_kernel(first, second, columns, rows_own, pay_own, s3, p3, pinv3, z3, rows, pay):
    rims, frames = s3.shape[0], s3.shape[1]
    own = rows_own.shape[1] - padded8(1)
    chunks = own + 2 * RIM
    middle = rows_own[0, chunks : chunks + 1, :]
    shared = middle, columns[0], columns[1], table(frames, False)
    rows[...] = rows_own[...]
    pay[...] = pay_own[...]
    below, above = sides(first[...], (second[0], second[1]))
    for i in range(rims):
        message = below if i < RIM else above
        j = i % RIM
        c = i if i < RIM else own + i
        at = [ref.at[i] for ref in (s3, p3, pinv3, z3)]
        field = message[j * LANES : (j + 1) * LANES, :]
        rate = message[RIM * LANES + j : RIM * LANES + j + 1, :]
        prep_chunk(c, rate, field, shared, *at, rows, pay)


def distances(size):
    found = [0]
    bit = size // 2
    while bit:
        found += [other ^ bit for other in found]
        bit //= 2
    return found


def by_block(parts, me, index):
    values = [part[index] for part in parts]
    ordered = []
    for m in range(len(values)):
        value = values[0]
        for distance, other in zip(distances(len(values))[1:], values[1:]):
            value = jnp.where(me == m ^ distance, other, value)
        ordered.append(value)
    return ordered


def block_totals(pay, me, chunks, rows):
    return [rows[2] * whole for whole in by_block(pay, me, (0, slice(chunks, chunks + 1)))]


def step_size(stats):
    both = jnp.sum(jnp.sum(stats[...], axis=0), axis=1, keepdims=True)
    return jnp.broadcast_to(both[0:1] / (both[1:2] + 1e-06), (1, LANES))


def update_kernel(s3, g3, stats, p3, pinv3, rows, new3, z3, pay):
    chunks = chunk_count(s3)
    frames = g3.shape[1]
    sums_table = table(frames, False)
    size = step_size(stats)
    pay[...] = jnp.zeros_like(pay)
    for c in range(chunks):
        field = jnp.maximum(chunk(s3, c)[...] - size * g3[c], 0.0)
        z = summed(sums_table, field * rows[0, c : c + 1, :] * chunk(pinv3, c)[...])
        if len(new3) == 2:
            chunk(new3, c)[...] = field
        elif RIM <= c < chunks - RIM:
            new3[0][c - RIM] = field
        chunk(z3, c)[...] = z
        last = chunk(p3, c)[frames - 1 : frames, :]
        pay[0, c : c + 1, :] = last * z[frames - 1 : frames, :]


def final_kernel(s3, g3, stats, out, here, sems):
    size = step_size(stats)
    part = s3.shape[0] // PARTS
    copies = [
        pltpu.make_async_copy(
            here.at[pl.ds(i * part * LANES, part * LANES)],
            out.at[pl.ds(i * part * LANES, part * LANES)],
            sems.at[i],
        )
        for i in range(PARTS)
    ]
    for i in range(PARTS):

        @after_start
        def _():
            for c in range(i * part, (i + 1) * part):
                field = jnp.maximum(s3[c] - size * g3[c + RIM], 0.0)
                here[c * LANES : (c + 1) * LANES, :] = field.T
            copies[i].start()

    for copy in copies:
        copy.wait()


def picked(ext, pattern, q, first=0):
    parts = [
        ext[pl.ds(pl.multiple_of((pattern[k, q] - first) * NEU_BLOCK, NEU_BLOCK), NEU_BLOCK), :]
        for k in range(K)
    ]
    return jnp.concatenate(parts, axis=0)


def block_of(field, q):
    return field[q * PIX_BLOCK : (q + 1) * PIX_BLOCK, :]


def foot_of(feet, q, stripe):
    count = feet.shape[0] // PIX_BLOCK
    return block_of(feet, q if q < count // 2 else q - stripe + count)


def note_places(pattern, place, start, stop):
    for q in range(start, stop):
        for v in range(2 * HB + 1):
            place[q, v] = -1
        for k in range(K):
            place[q, pattern[k, q] - q] = k


def pull_back(pattern, ext, feet, record, contrib, q):
    foot = foot_of(feet, q, pattern.shape[1])
    fitted = jnp.dot(foot, picked(ext, pattern, q), preferred_element_type=F32)
    residual = (fitted - block_of(record, q).astype(F32)).astype(BF16)
    contrib[q * K * NEU_BLOCK : (q + 1) * K * NEU_BLOCK, :] = lax.dot_general(
        foot, residual, (((0,), (0,)), ((), ())), preferred_element_type=F32
    )


def gathered(contrib, place, c, ranges):
    frames = contrib.shape[1]
    per_chunk = LANES // NEU_BLOCK
    halves = []
    for b in range(c * per_chunk, (c + 1) * per_chunk):
        total = jnp.zeros((NEU_BLOCK, frames), F32)
        for v in range(2 * HB + 1):
            q = b - v
            if any(start <= q < stop for start, stop in ranges):
                k = place[q, v]
                at = pl.multiple_of((q * K + jnp.maximum(k, 0)) * NEU_BLOCK, NEU_BLOCK)
                value = contrib[pl.ds(at, NEU_BLOCK), :]
                if v % 2:
                    value = jnp.where(k >= 0, value, 0.0)
                total = total + value
        halves.append(total)
    return jnp.concatenate(halves, axis=0).T


def edge_kernel(
    pattern_far, z3, p3, rows, pay, pays, feet, record, ext, zones, spill, send_a, send_b, *rest
):
    *traces, contrib, place, pattern, sem = rest
    fetch = pltpu.make_async_copy(pattern_far, pattern, sem)
    fetch.start()
    chunks = chunk_count(z3)
    stripe = pattern.shape[1]
    edge = 2 * HB
    ranges = ((0, edge), (stripe - edge, stripe))

    @after_start
    def _():
        me = lax.axis_index("tm")
        totals = block_totals(pay, me, chunks, rows)
        ends = by_block(pays, me, 0)
        carry = jnp.zeros_like(totals[0])
        for m, end in enumerate(ends):
            carry = jnp.where(m < me, end + totals[m] * carry, carry)
        carry = carry * rows[1]
        for c in range(chunks):
            field = chunk(p3, c)[...] * (chunk(z3, c)[...] + carry[c : c + 1, :])
            at = slice(c * LANES, (c + 1) * LANES)
            if traces and RIM <= c < chunks - RIM:
                field = field.T
                traces[0][(c - RIM) * LANES : (c - RIM + 1) * LANES, :] = field
                ext[at, :] = field.astype(BF16)
            else:
                ext[at, :] = field.astype(BF16).T

    fetch.wait()
    for start, stop in ranges:
        note_places(pattern, place, start, stop)
    for start, stop in ranges:
        for q in range(start, stop):
            pull_back(pattern, ext, feet, record, contrib, q)
    even = lax.axis_index("tile") % 2 == 0
    for i in range(2 * RIM):
        below = gathered(contrib, place, i, ranges)
        above = gathered(contrib, place, chunks - 2 * RIM + i, ranges)
        zones[i] = below
        zones[2 * RIM + i] = above
        send_a[i] = jnp.where(even, above, below).astype(BF16)
        send_b[0, i] = jnp.where(even, below, above).astype(BF16)
        send_b[1, i] = send_b[0, i]
        spill[i] = gathered(contrib, place, 2 * RIM + i, ranges)
        spill[2 * RIM + i] = gathered(contrib, place, chunks - 4 * RIM + i, ranges)

def adjoint_chunk(sums_table, field, p, pinv, rows, c, r3, pay):
    frames = field.shape[0]
    r = summed(sums_table, field * p)
    r3[...] = r
    gain = rows[0, c : c + 1, :]
    pay[0, c : c + 1, :] = rows[1, c : c + 1, :] * r[0:1, :]
    ends = p[frames - 1 : frames, :] * gain * gain
    pay[1, c : c + 1, :] = ends * jnp.sum(pinv * pinv * r, axis=0, keepdims=True)


def inner_kernel(pattern_far, p3, pinv3, rows, ext, spill, feet, record, traces, r3, pay, *rest):
    *out, contrib, place, pattern, sem = rest[: 4 + len(traces)]
    fetch = pltpu.make_async_copy(pattern_far, pattern, sem)
    fetch.start()
    if traces:
        copy = pltpu.make_async_copy(traces[0], out[0], rest[-1])
        copy.start()
    fetch.wait()

    def compute():
        chunks = chunk_count(p3)
        frames = spill.shape[1]
        stripe = pattern.shape[1]
        edge = 2 * HB
        note_places(pattern, place, edge, stripe - edge)
        sums_table = table(frames, True)
        pay[...] = jnp.zeros_like(pay)
        inner = chunks - 4 * RIM
        for q in range(edge, stripe - edge):
            pull_back(pattern, ext, feet, record, contrib, q)
        for i in range(inner):
            c = i + 2 * RIM
            field = gathered(contrib, place, c, ((edge, stripe - edge),))
            if i < 2 * RIM:
                field = field + spill[i]
            if i >= inner - 2 * RIM:
                field = field + spill[i - inner + 4 * RIM]
            p, pinv = chunk(p3, c)[...], chunk(pinv3, c)[...]
            adjoint_chunk(sums_table, field, p, pinv, rows, c, r3.at[i], pay)

    if traces:
        after_start(compute)
        copy.wait()
    else:
        compute()


def border_kernel(zones, got_a, got_b, p3, pinv3, rows, pay_inner, r3, pay):
    chunks = chunk_count(p3)
    frames = zones.shape[1]
    sums_table = table(frames, True)
    pay[...] = pay_inner[...]
    for i in range(2 * RIM):
        both = sides(got_a[i].astype(F32), (got_b[0, i].astype(F32), got_b[1, i].astype(F32)))
        for side, c in ((0, i), (1, chunks - 2 * RIM + i)):
            at = side * 2 * RIM + i
            field = zones[at] + both[side]
            p, pinv = chunk(p3, c)[...], chunk(pinv3, c)[...]
            adjoint_chunk(sums_table, field, p, pinv, rows, c, r3.at[at], pay)


def direction_kernel(
    pattern_far, r_inner, r_border, p3, pinv3, rows, pay, pays, feet, g3, stats, low, high, *rest
):
    pattern, sem, grad_sums = rest
    fetch = pltpu.make_async_copy(pattern_far, pattern, sem)
    fetch.start()
    chunks, frames = g3.shape[0], g3.shape[1]
    own = chunks - 2 * RIM
    stripe = pattern.shape[1]
    per_chunk = LANES // NEU_BLOCK
    low_chunks = low.shape[0] // LANES
    first_high = chunks - high.shape[0] // LANES

    @after_start
    def _():
        me = lax.axis_index("tm")
        totals = block_totals(pay, me, chunks, rows)
        gains = by_block(pay, me, 1)
        starts = by_block(pays, me, 0)
        ends = by_block(pays, me, 1)
        blocks = len(pays)
        entering = [None] * blocks
        state = jnp.zeros_like(totals[0])
        for m in reversed(range(blocks)):
            entering[m] = state
            state = starts[m] + totals[m] * state
        carry = jnp.zeros_like(totals[0])
        adjoint = jnp.zeros_like(totals[0])
        for m in range(blocks):
            end = ends[m] + gains[m] * entering[m]
            carry = jnp.where(m < me, end + totals[m] * carry, carry)
            adjoint = jnp.where(m == me, entering[m], adjoint)
        carry = carry * rows[1]
        sums_table = table(frames, False)
        grad_sq = jnp.zeros((8, LANES), F32)
        for c in range(chunks):
            p = chunk(p3, c)[...]
            if c < 2 * RIM:
                r = r_border[c]
            elif c >= chunks - 2 * RIM:
                r = r_border[c - chunks + 4 * RIM]
            else:
                r = r_inner[c - 2 * RIM]
            scale = rows[0, c : c + 1, :] * chunk(pinv3, c)[...]
            gradient = scale * (r + p[frames - 1 : frames, :] * adjoint[c : c + 1, :])
            g3[c] = gradient
            if RIM <= c < RIM + own:
                grad_sq += jnp.sum((gradient * gradient).reshape(frames // 8, 8, LANES), axis=0)
            z = summed(sums_table, scale * gradient)
            field = (p * (z + carry[c : c + 1, :])).astype(BF16).T
            if c < low_chunks:
                low[c * LANES : (c + 1) * LANES, :] = field
            if c >= first_high:
                high[(c - first_high) * LANES : (c - first_high + 1) * LANES, :] = field
        grad_sums[...] = grad_sq

    fetch.wait()
    image_sq = jnp.zeros((8, frames), F32)
    for q in range(stripe):
        if q + 2 * HB < low_chunks * per_chunk:
            named = picked(low, pattern, q, 0)
        else:
            named = picked(high, pattern, q, first_high * per_chunk)
        image = jnp.dot(foot_of(feet, q, stripe), named, preferred_element_type=F32)
        image_sq += jnp.sum((image * image).reshape(PIX_BLOCK // 8, 8, frames), axis=0)
    both = jnp.concatenate(
        [
            jnp.sum(grad_sums[...], axis=0, keepdims=True),
            jnp.sum(image_sq, axis=0, keepdims=True),
        ],
        axis=0,
    )
    stats[...] = jnp.broadcast_to(both[None], stats.shape)


def f32(*shape):
    return jax.ShapeDtypeStruct(shape, F32)


def bf16(*shape):
    return jax.ShapeDtypeStruct(shape, BF16)


def call(
    kernel, name, micros, outs, args, scratch=(), far=(), far_out=(), keep=(), limit=16
):
    def spec(arg):
        if any(arg is other for other in far):
            return HBM
        return pl.BlockSpec(memory_space=pl.ANY) if arg.dtype == jnp.int32 else VMEM

    in_specs = [jax.tree.map(spec, arg) for arg in args]
    in_specs.append(jax.tree.map(lambda _: VMEM, keep))

    def body(*refs):
        kernel(*refs[: len(args)], *refs[len(args) + 1 :])

    return pl.pallas_call(
        body,
        name=name,
        out_shape=outs,
        in_specs=in_specs,
        out_specs=tuple(
            jax.tree.map(lambda _: HBM if place in far_out else VMEM, out)
            for place, out in enumerate(outs)
        ),
        scratch_shapes=scratch,
        compiler_params=pltpu.CompilerParams(vmem_limit_bytes=int(limit * 2**20)),
        cost_estimate=pl.CostEstimate(
            flops=int(micros * 1e8), bytes_accessed=int(micros * 3e6), transcendentals=0
        ),
    )(*args, keep)


def swapped(first, second):
    size = lax.axis_size("tile")
    both = [(i, i + 1) for i in range(0, size - 1, 2)]
    groups = [[0, size - 1]] + [[i, i + 1] for i in range(1, size - 2, 2)]
    return (
        lax.ppermute(first, "tile", both + [(j, i) for i, j in both]),
        lax.all_to_all(second, "tile", 0, 0, axis_index_groups=groups),
    )


def shared_blocks(value):
    size = lax.axis_size("tm")
    known = [value]
    bit = size // 2
    while bit:
        known += [lax.ppermute(x, "tm", [(i, i ^ bit) for i in range(size)]) for x in known]
        bit //= 2
    return tuple(known)


def per_device(recording, footprints, pattern, decay, frame_gain, spikes):
    neurons, frames = spikes.shape
    stripe = pattern.shape[0]
    pattern = pattern.T
    own = neurons // LANES
    chunks = own + 2 * RIM
    lines = own + padded8(1)
    devices = lax.axis_size("tile") * lax.axis_size("tm")
    split = (f32(own, frames, LANES), f32(2 * RIM, frames, LANES))
    message = f32(RIM * LANES + padded8(RIM), frames)
    gains = frame_gain.reshape(1, frames)
    rates = decay.reshape(own, LANES)
    first, second, rates = call(
        rims_kernel,
        "rims",
        1.0,
        (message, f32(2, *message.shape), f32(own, LANES)),
        (spikes, rates),
        [pltpu.SemaphoreType.DMA((4,))],
        far=(spikes, rates),
        limit=53,
    )
    first, second = swapped(first, second)
    ends_size = 4 * HB * PIX_BLOCK
    *owns, rows, pay, columns, feet_ends = call(
        prep_own_kernel,
        "prep_own",
        1.6,
        (split[0],) * 4
        + (f32(3, lines, LANES), f32(2, lines, LANES), f32(2, frames, LANES))
        + (bf16(ends_size, K * NEU_BLOCK),),
        (spikes, rates, gains, footprints),
        [pltpu.SemaphoreType.DMA((2,))],
        far=(footprints,),
        limit=44,
    )
    *rims, rows, pay = call(
        prep_rim_kernel,
        "prep_rim",
        0.3,
        (split[1],) * 4 + (f32(3, lines, LANES), f32(2, lines, LANES)),
        (first, second, columns, rows, pay),
    )
    s3, p3, pinv3, z3 = zip(owns, rims)
    constants = pays = shared_blocks(pay)
    scratch = [
        pltpu.VMEM((stripe * K * NEU_BLOCK, frames), F32),
        pltpu.SMEM((stripe, 2 * HB + 1), jnp.int32),
        pltpu.SMEM(pattern.shape, jnp.int32),
        pltpu.SemaphoreType.DMA,
    ]
    staged = [pltpu.VMEM((neurons, frames), F32), pltpu.SemaphoreType.DMA((PARTS,))]
    middle = stripe * NEU_BLOCK // LANES // 2
    halves = (middle + 2 * RIM, chunks - middle)
    zone = (2 * RIM, frames, LANES)
    border = (4 * RIM, frames, LANES)
    for iteration in range(ITERS):
        ends = iteration == ITERS - 1
        ext, zones, spill, send_a, send_b, *traces = call(
            edge_kernel,
            "edge",
            2.5,
            (
                bf16(chunks * LANES, frames),
                f32(*border),
                f32(*border),
                bf16(*zone),
                bf16(2, *zone),
            )
            + ((f32(neurons, frames),) if ends else ()),
            (pattern, z3, p3, rows, constants, pays, feet_ends, recording),
            scratch,
            keep=(s3[0],) if ends else (),
        )
        got_a, got_b = swapped(send_a, send_b)
        held = (s3[0],) if ends else ()
        r_inner, pay, *traces = call(
            inner_kernel,
            "inner",
            4.0,
            (f32(chunks - 4 * RIM, frames, LANES), f32(2, lines, LANES))
            + ((f32(neurons, frames),) if ends else ()),
            (pattern, p3, pinv3, rows, ext, spill, footprints, recording, traces),
            scratch + ([pltpu.SemaphoreType.DMA] if ends else []),
            far_out=(2,),
            keep=held,
        )
        r_border, pay = call(
            border_kernel,
            "border",
            0.3,
            (f32(*border), f32(2, lines, LANES)),
            (zones, got_a, got_b, p3, pinv3, rows, pay),
            keep=held,
        )
        pays = shared_blocks(pay)
        g3, stats = call(
            direction_kernel,
            "direction",
            4.0,
            (f32(chunks, frames, LANES), f32(devices, 2, LANES)),
            (pattern, r_inner, r_border, p3, pinv3, rows, constants, pays, footprints),
            [
                pltpu.VMEM((halves[0] * LANES, frames), BF16),
                pltpu.VMEM((halves[1] * LANES, frames), BF16),
                *scratch[2:],
                pltpu.VMEM((8, LANES), F32),
            ],
            keep=held,
        )
        stats = lax.all_to_all(stats, ("tile", "tm"), 0, 0)
        if ends:
            (out,) = call(
                final_kernel,
                "final",
                1.4,
                (f32(neurons, frames),),
                (s3[0], g3, stats),
                staged,
                far_out=(0,),
            )
            return out, traces[0]
        s3, z3, pay = call(
            update_kernel,
            "update",
            0.6,
            (split if iteration < ITERS - 2 else split[:1], split, f32(1, lines, LANES)),
            (s3, g3, stats, p3, pinv3, rows),
        )
        pays = shared_blocks(pay)


def solution(mesh):
    return jax.shard_map(
        per_device,
        mesh=mesh,
        in_specs=(
            P("tile", "tm"),
            P("tile", None),
            P("tile", None),
            P("tile"),
            P("tm"),
            P("tile", "tm"),
        ),
        out_specs=(P("tile", "tm"), P("tile", "tm")),
        check_vma=False,
    )
```

```python
import jax
import jax.numpy as jnp
from jax import lax
from jax.experimental import pallas as pl
from jax.experimental.pallas import tpu as pltpu
from jax.sharding import PartitionSpec as P

NEU_BLOCK = 64
PIX_BLOCK = 256
PARTS = 8
K = 4
HB = 2
ITERS = 2
LANES = 128
RIM = HB * NEU_BLOCK // LANES
F32 = jnp.float32
BF16 = jnp.bfloat16
VMEM = pl.BlockSpec(memory_space=pltpu.VMEM)
HBM = pl.BlockSpec(memory_space=pltpu.HBM)


def padded8(rows):
    return -(-rows // 8) * 8


def table(frames, reverse):
    row = lax.broadcasted_iota(jnp.int32, (frames, 2 * frames), 0)
    col = lax.broadcasted_iota(jnp.int32, (frames, 2 * frames), 1)
    col = jnp.where(col >= frames, col - frames, col)
    keep = col >= row if reverse else col <= row
    return jnp.where(keep, 1.0, 0.0).astype(BF16)


def summed(sums_table, values):
    high = values.astype(BF16)
    low = (values - high.astype(F32)).astype(BF16)
    both = jnp.concatenate([high, low], axis=0)
    return jnp.dot(sums_table, both, preferred_element_type=F32)


def powers(log_decay, frames, mid, sign):
    groups = frames // 8
    coarse = (8 * lax.broadcasted_iota(jnp.int32, (groups, LANES), 0) - mid).astype(F32) * sign
    fine = lax.broadcasted_iota(jnp.int32, (8, LANES), 0).astype(F32) * sign
    coarse = jnp.exp(coarse * log_decay)
    fine = jnp.exp(fine * log_decay)
    return (coarse[:, None, :] * fine[None, :, :]).reshape(frames, LANES)


def chunk(field, c):
    own, rim = field
    inner = own.shape[0]
    if c < RIM:
        return rim.at[c]
    if c >= RIM + inner:
        return rim.at[c - inner]
    return own.at[c - RIM]


def chunk_count(field):
    return field[0].shape[0] + field[1].shape[0]


def prep_chunk(c, rate, field, gains, s3, p3, pinv3, z3, rows, pay):
    frames = field.shape[1]
    middle, prefix_col, inverse_col, sums_table = gains
    mid = frames // 2 - 1
    rate = jnp.where(rate > 0.0, rate, 1.0)
    log_rate = jnp.log(rate)
    gain = jnp.sqrt(1.0 - rate * rate)
    p = powers(log_rate, frames, mid, 1.0) * prefix_col
    pinv = powers(log_rate, frames, mid, -1.0) * inverse_col
    field = field.T
    z = summed(sums_table, field * gain * pinv)
    last = p[frames - 1 : frames, :]
    s3[...] = field
    p3[...] = p
    pinv3[...] = pinv
    z3[...] = z
    half = rate
    for _ in range(frames.bit_length() - 2):
        half = half * half
    rows[0, c : c + 1, :] = gain
    rows[1, c : c + 1, :] = half * middle
    rows[2, c : c + 1, :] = half * half
    pay[0, c : c + 1, :] = last * z[frames - 1 : frames, :]
    scale = last * gain
    pay[1, c : c + 1, :] = scale * scale * jnp.sum(pinv * pinv, axis=0, keepdims=True)


def gain_columns(gains):
    frames = gains.shape[1]
    mid = frames // 2 - 1
    lane = lax.broadcasted_iota(jnp.int32, (8, frames), 1)
    prefix = jnp.broadcast_to(gains, (8, frames))
    step = 1
    while step < frames:
        prefix = prefix * jnp.where(lane >= step, pltpu.roll(prefix, step, 1), 1.0)
        step *= 2
    middle = jnp.broadcast_to(prefix[0:1, mid : mid + 1], (1, LANES))
    whole = jnp.broadcast_to(prefix[0:1, frames - 1 : frames], (1, LANES))
    prefix_col = jnp.broadcast_to(prefix[0:1] / middle, (LANES, frames)).T
    inverse_col = jnp.broadcast_to(middle / prefix[0:1], (LANES, frames)).T
    return middle, whole, prefix_col, inverse_col


def rims_kernel(spikes, decay, first, second, rates_here, sems):
    edge = RIM * LANES
    neurons = spikes.shape[0]
    own = decay.shape[0]
    even = lax.axis_index("tile") % 2 == 0
    top = jnp.where(even, neurons - edge, 0)
    bottom = jnp.where(even, 0, neurons - edge)
    copies = [
        pltpu.make_async_copy(decay, rates_here, sems.at[0]),
        pltpu.make_async_copy(
            spikes.at[pl.ds(pl.multiple_of(top, LANES), edge)], first.at[pl.ds(0, edge)], sems.at[1]
        ),
        pltpu.make_async_copy(
            spikes.at[pl.ds(pl.multiple_of(bottom, LANES), edge)],
            second.at[pl.ds(0, edge)],
            sems.at[2],
        ),
    ]
    for copy in copies:
        copy.start()
    first[edge:, :] = jnp.zeros_like(first[edge:, :])
    second[edge:, :] = jnp.zeros_like(second[edge:, :])
    copies[0].wait()
    lower, upper = rates_here[0:RIM, :], rates_here[own - RIM : own, :]
    first[edge : edge + RIM, :] = jnp.where(even, upper, lower)
    second[edge : edge + RIM, :] = jnp.where(even, lower, upper)
    for copy in copies[1:]:
        copy.wait()


def after_start(compute):
    pl.when(lax.axis_index("tm") >= 0)(compute)


def prep_own_kernel(
    spikes, decay, gains, feet, s3, p3, pinv3, z3, rows, pay, columns, feet_ends, sems
):
    own = s3.shape[0]
    chunks = own + 2 * RIM
    size = feet_ends.shape[0] // 2
    fetches = [
        pltpu.make_async_copy(
            feet.at[pl.ds(start, size)], feet_ends.at[pl.ds(i * size, size)], sems.at[i]
        )
        for i, start in enumerate((0, feet.shape[0] - size))
    ]
    for fetch in fetches:
        fetch.start()

    @after_start
    def _():
        middle, whole, prefix_col, inverse_col = gain_columns(gains[...])
        columns[0] = prefix_col
        columns[1] = inverse_col
        rows[...] = jnp.ones_like(rows)
        rows[0, chunks : chunks + 1, :] = middle
        pay[...] = jnp.zeros_like(pay)
        pay[0, chunks : chunks + 1, :] = whole
        shared = middle, prefix_col, inverse_col, table(spikes.shape[1], False)
        for i in range(own):
            field = spikes[i * LANES : (i + 1) * LANES, :]
            at = [ref.at[i] for ref in (s3, p3, pinv3, z3)]
            prep_chunk(i + RIM, decay[i : i + 1, :], field, shared, *at, rows, pay)

    for fetch in fetches:
        fetch.wait()


def sides(even, first, second):
    return jnp.where(even, second, first), jnp.where(even, first, second)


def prep_rim_kernel(first, second, columns, rows_own, pay_own, s3, p3, pinv3, z3, rows, pay):
    rims, frames = s3.shape[0], s3.shape[1]
    own = rows_own.shape[1] - padded8(1)
    chunks = own + 2 * RIM
    middle = rows_own[0, chunks : chunks + 1, :]
    shared = middle, columns[0], columns[1], table(frames, False)
    rows[...] = rows_own[...]
    pay[...] = pay_own[...]
    even = lax.axis_index("tile") % 2 == 0
    below, above = sides(even, first[...], second[...])
    for i in range(rims):
        message = below if i < RIM else above
        j = i % RIM
        c = i if i < RIM else own + i
        at = [ref.at[i] for ref in (s3, p3, pinv3, z3)]
        field = message[j * LANES : (j + 1) * LANES, :]
        rate = message[RIM * LANES + j : RIM * LANES + j + 1, :]
        prep_chunk(c, rate, field, shared, *at, rows, pay)


def by_block(parts, me, index):
    values = [part[index] for part in parts]
    ordered = []
    for m in range(len(values)):
        value = values[0]
        for j in range(1, len(values)):
            value = jnp.where(me == m ^ j, values[j], value)
        ordered.append(value)
    return ordered


def block_totals(pay, me, chunks, rows):
    return [rows[2] * whole for whole in by_block(pay, me, (0, slice(chunks, chunks + 1)))]


def step_size(stats):
    both = jnp.sum(jnp.sum(stats[...], axis=0), axis=1, keepdims=True)
    return jnp.broadcast_to(both[0:1] / (both[1:2] + 1e-06), (1, LANES))


def update_kernel(s3, g3, stats, p3, pinv3, rows, new3, z3, pay):
    chunks = chunk_count(s3)
    frames = g3.shape[1]
    sums_table = table(frames, False)
    size = step_size(stats)
    pay[...] = jnp.zeros_like(pay)
    for c in range(chunks):
        field = jnp.maximum(chunk(s3, c)[...] - size * g3[c], 0.0)
        z = summed(sums_table, field * rows[0, c : c + 1, :] * chunk(pinv3, c)[...])
        if len(new3) == 2:
            chunk(new3, c)[...] = field
        elif RIM <= c < chunks - RIM:
            new3[0][c - RIM] = field
        chunk(z3, c)[...] = z
        last = chunk(p3, c)[frames - 1 : frames, :]
        pay[0, c : c + 1, :] = last * z[frames - 1 : frames, :]


def final_kernel(s3, g3, stats, out, here, sems):
    size = step_size(stats)
    part = s3.shape[0] // PARTS
    copies = [
        pltpu.make_async_copy(
            here.at[pl.ds(i * part * LANES, part * LANES)],
            out.at[pl.ds(i * part * LANES, part * LANES)],
            sems.at[i],
        )
        for i in range(PARTS)
    ]
    for i in range(PARTS):

        @after_start
        def _():
            for c in range(i * part, (i + 1) * part):
                field = jnp.maximum(s3[c] - size * g3[c + RIM], 0.0)
                here[c * LANES : (c + 1) * LANES, :] = field.T
            copies[i].start()

    for copy in copies:
        copy.wait()


def picked(ext, pattern, q, first=0):
    parts = [
        ext[pl.ds(pl.multiple_of((pattern[k, q] - first) * NEU_BLOCK, NEU_BLOCK), NEU_BLOCK), :]
        for k in range(K)
    ]
    return jnp.concatenate(parts, axis=0)


def block_of(field, q):
    return field[q * PIX_BLOCK : (q + 1) * PIX_BLOCK, :]


def foot_of(feet, q, stripe):
    count = feet.shape[0] // PIX_BLOCK
    return block_of(feet, q if q < count // 2 else q - stripe + count)


def note_places(pattern, place, start, stop):
    for q in range(start, stop):
        for v in range(2 * HB + 1):
            place[q, v] = -1
        for k in range(K):
            place[q, pattern[k, q] - q] = k


def pull_back(pattern, ext, feet, record, contrib, q):
    foot = foot_of(feet, q, pattern.shape[1])
    fitted = jnp.dot(foot, picked(ext, pattern, q), preferred_element_type=F32)
    residual = (fitted - block_of(record, q).astype(F32)).astype(BF16)
    contrib[q * K * NEU_BLOCK : (q + 1) * K * NEU_BLOCK, :] = lax.dot_general(
        foot, residual, (((0,), (0,)), ((), ())), preferred_element_type=F32
    )


def gathered(contrib, place, c, ranges):
    frames = contrib.shape[1]
    per_chunk = LANES // NEU_BLOCK
    halves = []
    for b in range(c * per_chunk, (c + 1) * per_chunk):
        total = jnp.zeros((NEU_BLOCK, frames), F32)
        for v in range(2 * HB + 1):
            q = b - v
            if any(start <= q < stop for start, stop in ranges):
                k = place[q, v]
                at = pl.multiple_of((q * K + jnp.maximum(k, 0)) * NEU_BLOCK, NEU_BLOCK)
                value = contrib[pl.ds(at, NEU_BLOCK), :]
                if v % 2:
                    value = jnp.where(k >= 0, value, 0.0)
                total = total + value
        halves.append(total)
    return jnp.concatenate(halves, axis=0).T


def edge_kernel(
    pattern_far, z3, p3, rows, pay, pays, feet, record, ext, zones, spill, send_a, send_b, *rest
):
    *traces, contrib, place, pattern, sem = rest
    fetch = pltpu.make_async_copy(pattern_far, pattern, sem)
    fetch.start()
    chunks = chunk_count(z3)
    stripe = pattern.shape[1]
    edge = 2 * HB
    ranges = ((0, edge), (stripe - edge, stripe))

    @after_start
    def _():
        me = lax.axis_index("tm")
        totals = block_totals(pay, me, chunks, rows)
        ends = by_block(pays, me, 0)
        carry = jnp.zeros_like(totals[0])
        for m, end in enumerate(ends):
            carry = jnp.where(m < me, end + totals[m] * carry, carry)
        carry = carry * rows[1]
        for c in range(chunks):
            field = chunk(p3, c)[...] * (chunk(z3, c)[...] + carry[c : c + 1, :])
            at = slice(c * LANES, (c + 1) * LANES)
            if traces and RIM <= c < chunks - RIM:
                field = field.T
                traces[0][(c - RIM) * LANES : (c - RIM + 1) * LANES, :] = field
                ext[at, :] = field.astype(BF16)
            else:
                ext[at, :] = field.astype(BF16).T

    fetch.wait()
    for start, stop in ranges:
        note_places(pattern, place, start, stop)
    for start, stop in ranges:
        for q in range(start, stop):
            pull_back(pattern, ext, feet, record, contrib, q)
    even = lax.axis_index("tile") % 2 == 0
    for i in range(2 * RIM):
        below = gathered(contrib, place, i, ranges)
        above = gathered(contrib, place, chunks - 2 * RIM + i, ranges)
        zones[i] = below
        zones[2 * RIM + i] = above
        send_a[i] = jnp.where(even, above, below).astype(BF16)
        send_b[i] = jnp.where(even, below, above).astype(BF16)
        spill[i] = gathered(contrib, place, 2 * RIM + i, ranges)
        spill[2 * RIM + i] = gathered(contrib, place, chunks - 4 * RIM + i, ranges)

def adjoint_chunk(sums_table, field, p, pinv, rows, c, r3, pay):
    frames = field.shape[0]
    r = summed(sums_table, field * p)
    r3[...] = r
    gain = rows[0, c : c + 1, :]
    pay[0, c : c + 1, :] = rows[1, c : c + 1, :] * r[0:1, :]
    ends = p[frames - 1 : frames, :] * gain * gain
    pay[1, c : c + 1, :] = ends * jnp.sum(pinv * pinv * r, axis=0, keepdims=True)


def inner_kernel(pattern_far, p3, pinv3, rows, ext, spill, feet, record, traces, r3, pay, *rest):
    *out, contrib, place, pattern, sem = rest[: 4 + len(traces)]
    fetch = pltpu.make_async_copy(pattern_far, pattern, sem)
    fetch.start()
    if traces:
        copy = pltpu.make_async_copy(traces[0], out[0], rest[-1])
        copy.start()
    fetch.wait()

    def compute():
        chunks = chunk_count(p3)
        frames = spill.shape[1]
        stripe = pattern.shape[1]
        edge = 2 * HB
        note_places(pattern, place, edge, stripe - edge)
        sums_table = table(frames, True)
        pay[...] = jnp.zeros_like(pay)
        inner = chunks - 4 * RIM
        for q in range(edge, stripe - edge):
            pull_back(pattern, ext, feet, record, contrib, q)
        for i in range(inner):
            c = i + 2 * RIM
            field = gathered(contrib, place, c, ((edge, stripe - edge),))
            if i < 2 * RIM:
                field = field + spill[i]
            if i >= inner - 2 * RIM:
                field = field + spill[i - inner + 4 * RIM]
            p, pinv = chunk(p3, c)[...], chunk(pinv3, c)[...]
            adjoint_chunk(sums_table, field, p, pinv, rows, c, r3.at[i], pay)

    if traces:
        after_start(compute)
        copy.wait()
    else:
        compute()


def border_kernel(zones, got_a, got_b, p3, pinv3, rows, pay_inner, r3, pay):
    chunks = chunk_count(p3)
    frames = zones.shape[1]
    sums_table = table(frames, True)
    pay[...] = pay_inner[...]
    even = lax.axis_index("tile") % 2 == 0
    for i in range(2 * RIM):
        both = sides(even, got_a[i].astype(F32), got_b[i].astype(F32))
        for side, c in ((0, i), (1, chunks - 2 * RIM + i)):
            at = side * 2 * RIM + i
            field = zones[at] + both[side]
            p, pinv = chunk(p3, c)[...], chunk(pinv3, c)[...]
            adjoint_chunk(sums_table, field, p, pinv, rows, c, r3.at[at], pay)


def direction_kernel(
    pattern_far, r_inner, r_border, p3, pinv3, rows, pay, pays, feet, g3, stats, low, high, *rest
):
    pattern, sem, grad_sums = rest
    fetch = pltpu.make_async_copy(pattern_far, pattern, sem)
    fetch.start()
    chunks, frames = g3.shape[0], g3.shape[1]
    own = chunks - 2 * RIM
    stripe = pattern.shape[1]
    per_chunk = LANES // NEU_BLOCK
    low_chunks = low.shape[0] // LANES
    first_high = chunks - high.shape[0] // LANES

    @after_start
    def _():
        me = lax.axis_index("tm")
        totals = block_totals(pay, me, chunks, rows)
        gains = by_block(pay, me, 1)
        starts = by_block(pays, me, 0)
        ends = by_block(pays, me, 1)
        blocks = len(pays)
        entering = [None] * blocks
        state = jnp.zeros_like(totals[0])
        for m in reversed(range(blocks)):
            entering[m] = state
            state = starts[m] + totals[m] * state
        carry = jnp.zeros_like(totals[0])
        adjoint = jnp.zeros_like(totals[0])
        for m in range(blocks):
            end = ends[m] + gains[m] * entering[m]
            carry = jnp.where(m < me, end + totals[m] * carry, carry)
            adjoint = jnp.where(m == me, entering[m], adjoint)
        carry = carry * rows[1]
        sums_table = table(frames, False)
        grad_sq = jnp.zeros((8, LANES), F32)
        for c in range(chunks):
            p = chunk(p3, c)[...]
            if c < 2 * RIM:
                r = r_border[c]
            elif c >= chunks - 2 * RIM:
                r = r_border[c - chunks + 4 * RIM]
            else:
                r = r_inner[c - 2 * RIM]
            scale = rows[0, c : c + 1, :] * chunk(pinv3, c)[...]
            gradient = scale * (r + p[frames - 1 : frames, :] * adjoint[c : c + 1, :])
            g3[c] = gradient
            if RIM <= c < RIM + own:
                grad_sq += jnp.sum((gradient * gradient).reshape(frames // 8, 8, LANES), axis=0)
            z = summed(sums_table, scale * gradient)
            field = (p * (z + carry[c : c + 1, :])).astype(BF16).T
            if c < low_chunks:
                low[c * LANES : (c + 1) * LANES, :] = field
            if c >= first_high:
                high[(c - first_high) * LANES : (c - first_high + 1) * LANES, :] = field
        grad_sums[...] = grad_sq

    fetch.wait()
    image_sq = jnp.zeros((8, frames), F32)
    for q in range(stripe):
        if q + 2 * HB < low_chunks * per_chunk:
            named = picked(low, pattern, q, 0)
        else:
            named = picked(high, pattern, q, first_high * per_chunk)
        image = jnp.dot(foot_of(feet, q, stripe), named, preferred_element_type=F32)
        image_sq += jnp.sum((image * image).reshape(PIX_BLOCK // 8, 8, frames), axis=0)
    both = jnp.concatenate(
        [
            jnp.sum(grad_sums[...], axis=0, keepdims=True),
            jnp.sum(image_sq, axis=0, keepdims=True),
        ],
        axis=0,
    )
    stats[...] = jnp.broadcast_to(both[None], stats.shape)


def f32(*shape):
    return jax.ShapeDtypeStruct(shape, F32)


def bf16(*shape):
    return jax.ShapeDtypeStruct(shape, BF16)


def call(
    kernel, name, micros, outs, args, scratch=(), far=(), far_out=(), keep=(), limit=16
):
    def spec(arg):
        if any(arg is other for other in far):
            return HBM
        return pl.BlockSpec(memory_space=pl.ANY) if arg.dtype == jnp.int32 else VMEM

    in_specs = [jax.tree.map(spec, arg) for arg in args]
    in_specs.append(jax.tree.map(lambda _: VMEM, keep))

    def body(*refs):
        kernel(*refs[: len(args)], *refs[len(args) + 1 :])

    return pl.pallas_call(
        body,
        name=name,
        out_shape=outs,
        in_specs=in_specs,
        out_specs=tuple(
            jax.tree.map(lambda _: HBM if place in far_out else VMEM, out)
            for place, out in enumerate(outs)
        ),
        scratch_shapes=scratch,
        compiler_params=pltpu.CompilerParams(vmem_limit_bytes=int(limit * 2**20)),
        cost_estimate=pl.CostEstimate(
            flops=int(micros * 1e8), bytes_accessed=int(micros * 3e6), transcendentals=0
        ),
    )(*args, keep)


def swapped(first, second):
    size = lax.axis_size("tile")

    def pairs(start):
        both = [(i, i + 1) for i in range(start, size - 1, 2)]
        return both + [(j, i) for i, j in both]

    return lax.ppermute(first, "tile", pairs(0)), lax.ppermute(second, "tile", pairs(1))


def shared_blocks(value):
    size = lax.axis_size("tm")
    others = [
        lax.ppermute(value, "tm", [(i, i ^ j) for i in range(size)])
        for j in reversed(range(1, size))
    ]
    return (value, *reversed(others))


def per_device(recording, footprints, pattern, decay, frame_gain, spikes):
    neurons, frames = spikes.shape
    stripe = pattern.shape[0]
    pattern = pattern.T
    own = neurons // LANES
    chunks = own + 2 * RIM
    lines = own + padded8(1)
    devices = lax.axis_size("tile") * lax.axis_size("tm")
    split = (f32(own, frames, LANES), f32(2 * RIM, frames, LANES))
    message = f32(RIM * LANES + padded8(RIM), frames)
    gains = frame_gain.reshape(1, frames)
    rates = decay.reshape(own, LANES)
    first, second, rates = call(
        rims_kernel,
        "rims",
        1.0,
        (message, message, f32(own, LANES)),
        (spikes, rates),
        [pltpu.SemaphoreType.DMA((3,))],
        far=(spikes, rates),
        limit=53,
    )
    first, second = swapped(first, second)
    ends_size = 4 * HB * PIX_BLOCK
    *owns, rows, pay, columns, feet_ends = call(
        prep_own_kernel,
        "prep_own",
        1.6,
        (split[0],) * 4
        + (f32(3, lines, LANES), f32(2, lines, LANES), f32(2, frames, LANES))
        + (bf16(ends_size, K * NEU_BLOCK),),
        (spikes, rates, gains, footprints),
        [pltpu.SemaphoreType.DMA((2,))],
        far=(footprints,),
        limit=44,
    )
    *rims, rows, pay = call(
        prep_rim_kernel,
        "prep_rim",
        0.3,
        (split[1],) * 4 + (f32(3, lines, LANES), f32(2, lines, LANES)),
        (first, second, columns, rows, pay),
    )
    s3, p3, pinv3, z3 = zip(owns, rims)
    constants = pays = shared_blocks(pay)
    scratch = [
        pltpu.VMEM((stripe * K * NEU_BLOCK, frames), F32),
        pltpu.SMEM((stripe, 2 * HB + 1), jnp.int32),
        pltpu.SMEM(pattern.shape, jnp.int32),
        pltpu.SemaphoreType.DMA,
    ]
    staged = [pltpu.VMEM((neurons, frames), F32), pltpu.SemaphoreType.DMA((PARTS,))]
    middle = stripe * NEU_BLOCK // LANES // 2
    halves = (middle + 2 * RIM, chunks - middle)
    zone = (2 * RIM, frames, LANES)
    border = (4 * RIM, frames, LANES)
    for iteration in range(ITERS):
        ends = iteration == ITERS - 1
        ext, zones, spill, send_a, send_b, *traces = call(
            edge_kernel,
            "edge",
            2.5,
            (
                bf16(chunks * LANES, frames),
                f32(*border),
                f32(*border),
                bf16(*zone),
                bf16(*zone),
            )
            + ((f32(neurons, frames),) if ends else ()),
            (pattern, z3, p3, rows, constants, pays, feet_ends, recording),
            scratch,
            keep=(s3[0],) if ends else (),
        )
        got_a, got_b = swapped(send_a, send_b)
        held = (s3[0],) if ends else ()
        r_inner, pay, *traces = call(
            inner_kernel,
            "inner",
            4.0,
            (f32(chunks - 4 * RIM, frames, LANES), f32(2, lines, LANES))
            + ((f32(neurons, frames),) if ends else ()),
            (pattern, p3, pinv3, rows, ext, spill, footprints, recording, traces),
            scratch + ([pltpu.SemaphoreType.DMA] if ends else []),
            far_out=(2,),
            keep=held,
        )
        r_border, pay = call(
            border_kernel,
            "border",
            0.3,
            (f32(*border), f32(2, lines, LANES)),
            (zones, got_a, got_b, p3, pinv3, rows, pay),
            keep=held,
        )
        pays = shared_blocks(pay)
        g3, stats = call(
            direction_kernel,
            "direction",
            4.0,
            (f32(chunks, frames, LANES), f32(devices, 2, LANES)),
            (pattern, r_inner, r_border, p3, pinv3, rows, constants, pays, footprints),
            [
                pltpu.VMEM((halves[0] * LANES, frames), BF16),
                pltpu.VMEM((halves[1] * LANES, frames), BF16),
                *scratch[2:],
                pltpu.VMEM((8, LANES), F32),
            ],
            keep=held,
        )
        stats = lax.all_to_all(stats, ("tile", "tm"), 0, 0)
        if ends:
            (out,) = call(
                final_kernel,
                "final",
                1.4,
                (f32(neurons, frames),),
                (s3[0], g3, stats),
                staged,
                far_out=(0,),
            )
            return out, traces[0]
        s3, z3, pay = call(
            update_kernel,
            "update",
            0.6,
            (split if iteration < ITERS - 2 else split[:1], split, f32(1, lines, LANES)),
            (s3, g3, stats, p3, pinv3, rows),
        )
        pays = shared_blocks(pay)


def solution(mesh):
    return jax.shard_map(
        per_device,
        mesh=mesh,
        in_specs=(
            P("tile", "tm"),
            P("tile", None),
            P("tile", None),
            P("tile"),
            P("tm"),
            P("tile", "tm"),
        ),
        out_specs=(P("tile", "tm"), P("tile", "tm")),
        check_vma=False,
    )
```

```python
import jax
import jax.numpy as jnp
from jax import lax
from jax.experimental import pallas as pl
from jax.experimental.pallas import tpu as pltpu
from jax.sharding import PartitionSpec as P

NEU_BLOCK = 64
PIX_BLOCK = 256
PARTS = 8
K = 4
HB = 2
ITERS = 2
LANES = 128
RIM = HB * NEU_BLOCK // LANES
F32 = jnp.float32
BF16 = jnp.bfloat16
VMEM = pl.BlockSpec(memory_space=pltpu.VMEM)
HBM = pl.BlockSpec(memory_space=pltpu.HBM)


def padded8(rows):
    return -(-rows // 8) * 8


def table(frames, reverse):
    row = lax.broadcasted_iota(jnp.int32, (frames, 2 * frames), 0)
    col = lax.broadcasted_iota(jnp.int32, (frames, 2 * frames), 1)
    col = jnp.where(col >= frames, col - frames, col)
    keep = col >= row if reverse else col <= row
    return jnp.where(keep, 1.0, 0.0).astype(BF16)


def summed(sums_table, values):
    high = values.astype(BF16)
    low = (values - high.astype(F32)).astype(BF16)
    both = jnp.concatenate([high, low], axis=0)
    return jnp.dot(sums_table, both, preferred_element_type=F32)


def powers(log_decay, frames, mid, sign):
    groups = frames // 8
    coarse = (8 * lax.broadcasted_iota(jnp.int32, (groups, LANES), 0) - mid).astype(F32) * sign
    fine = lax.broadcasted_iota(jnp.int32, (8, LANES), 0).astype(F32) * sign
    coarse = jnp.exp(coarse * log_decay)
    fine = jnp.exp(fine * log_decay)
    return (coarse[:, None, :] * fine[None, :, :]).reshape(frames, LANES)


def chunk(field, c):
    own, rim = field
    inner = own.shape[0]
    if c < RIM:
        return rim.at[c]
    if c >= RIM + inner:
        return rim.at[c - inner]
    return own.at[c - RIM]


def chunk_count(field):
    return field[0].shape[0] + field[1].shape[0]


def prep_chunk(c, chunks, rate, field, gains, s3, p3, pinv3, z3, rows, pay):
    frames = field.shape[1]
    middle, prefix_col, inverse_col, sums_table = gains
    mid = frames // 2 - 1
    rate = jnp.where(rate > 0.0, rate, 1.0)
    log_rate = jnp.log(rate)
    gain = jnp.sqrt(1.0 - rate * rate)
    p = powers(log_rate, frames, mid, 1.0) * prefix_col
    pinv = powers(log_rate, frames, mid, -1.0) * inverse_col
    field = field.T
    z = summed(sums_table, field * gain * pinv)
    last = p[frames - 1 : frames, :]
    s3[...] = field
    p3[...] = p
    pinv3[...] = pinv
    z3[...] = z
    half = rate
    for _ in range(frames.bit_length() - 2):
        half = half * half
    rows[0, c : c + 1, :] = gain
    rows[1, c : c + 1, :] = half * middle
    rows[2, c : c + 1, :] = half * half
    pay[c : c + 1, :] = last * z[frames - 1 : frames, :]
    scale = last * gain
    squares = scale * scale * jnp.sum(pinv * pinv, axis=0, keepdims=True)
    pay[chunks + c : chunks + c + 1, :] = squares


def gain_columns(gains):
    frames = gains.shape[1]
    mid = frames // 2 - 1
    lane = lax.broadcasted_iota(jnp.int32, (8, frames), 1)
    prefix = jnp.broadcast_to(gains, (8, frames))
    step = 1
    while step < frames:
        prefix = prefix * jnp.where(lane >= step, pltpu.roll(prefix, step, 1), 1.0)
        step *= 2
    middle = jnp.broadcast_to(prefix[0:1, mid : mid + 1], (1, LANES))
    whole = jnp.broadcast_to(prefix[0:1, frames - 1 : frames], (1, LANES))
    prefix_col = jnp.broadcast_to(prefix[0:1] / middle, (LANES, frames)).T
    inverse_col = jnp.broadcast_to(middle / prefix[0:1], (LANES, frames)).T
    return middle, whole, prefix_col, inverse_col


def rims_kernel(spikes, decay, first, second, rates_here, sems):
    edge = RIM * LANES
    neurons = spikes.shape[0]
    own = decay.shape[0]
    even = lax.axis_index("tile") % 2 == 0
    top = jnp.where(even, neurons - edge, 0)
    bottom = jnp.where(even, 0, neurons - edge)
    copies = [
        pltpu.make_async_copy(decay, rates_here, sems.at[0]),
        pltpu.make_async_copy(
            spikes.at[pl.ds(pl.multiple_of(top, LANES), edge)], first.at[pl.ds(0, edge)], sems.at[1]
        ),
        pltpu.make_async_copy(
            spikes.at[pl.ds(pl.multiple_of(bottom, LANES), edge)],
            second.at[pl.ds(0, edge)],
            sems.at[2],
        ),
    ]
    for copy in copies:
        copy.start()
    first[edge:, :] = jnp.zeros_like(first[edge:, :])
    second[edge:, :] = jnp.zeros_like(second[edge:, :])
    copies[0].wait()
    lower, upper = rates_here[0:RIM, :], rates_here[own - RIM : own, :]
    first[edge : edge + RIM, :] = jnp.where(even, upper, lower)
    second[edge : edge + RIM, :] = jnp.where(even, lower, upper)
    for copy in copies[1:]:
        copy.wait()


def after_start(compute):
    pl.when(lax.axis_index("tm") >= 0)(compute)


def prep_own_kernel(
    spikes, decay, gains, feet, s3, p3, pinv3, z3, rows, pay, columns, feet_ends, sems
):
    own = s3.shape[0]
    chunks = own + 2 * RIM
    size = feet_ends.shape[0] // 2
    fetches = [
        pltpu.make_async_copy(
            feet.at[pl.ds(start, size)], feet_ends.at[pl.ds(i * size, size)], sems.at[i]
        )
        for i, start in enumerate((0, feet.shape[0] - size))
    ]
    for fetch in fetches:
        fetch.start()

    @after_start
    def _():
        middle, whole, prefix_col, inverse_col = gain_columns(gains[...])
        columns[0] = prefix_col
        columns[1] = inverse_col
        rows[...] = jnp.ones_like(rows)
        rows[0, chunks : chunks + 1, :] = middle
        pay[...] = jnp.zeros_like(pay)
        pay[2 * chunks : 2 * chunks + 1, :] = whole
        shared = middle, prefix_col, inverse_col, table(spikes.shape[1], False)
        for i in range(own):
            field = spikes[i * LANES : (i + 1) * LANES, :]
            at = [ref.at[i] for ref in (s3, p3, pinv3, z3)]
            rate = decay[i : i + 1, :]
            prep_chunk(i + RIM, chunks, rate, field, shared, *at, rows, pay)

    for fetch in fetches:
        fetch.wait()


def sides(even, first, second):
    return jnp.where(even, second, first), jnp.where(even, first, second)


def prep_rim_kernel(first, second, columns, rows_own, pay_own, s3, p3, pinv3, z3, rows, pay):
    rims, frames = s3.shape[0], s3.shape[1]
    own = rows_own.shape[1] - padded8(1)
    chunks = own + 2 * RIM
    middle = rows_own[0, chunks : chunks + 1, :]
    shared = middle, columns[0], columns[1], table(frames, False)
    rows[...] = rows_own[...]
    pay[...] = pay_own[...]
    even = lax.axis_index("tile") % 2 == 0
    below, above = sides(even, first[...], second[...])
    for i in range(rims):
        message = below if i < RIM else above
        j = i % RIM
        c = i if i < RIM else own + i
        at = [ref.at[i] for ref in (s3, p3, pinv3, z3)]
        field = message[j * LANES : (j + 1) * LANES, :]
        rate = message[RIM * LANES + j : RIM * LANES + j + 1, :]
        prep_chunk(c, chunks, rate, field, shared, *at, rows, pay)


def by_block(parts, me, index):
    values = [part[index] for part in parts]
    ordered = []
    for m in range(len(values)):
        value = values[0]
        for j in range(1, len(values)):
            value = jnp.where(me == m ^ j, values[j], value)
        ordered.append(value)
    return ordered


def block_totals(pay, me, chunks, rows):
    wholes = by_block(pay, me, slice(2 * chunks, 2 * chunks + 1))
    return [rows[2, 0:chunks] * whole for whole in wholes]


def step_size(stats):
    both = jnp.sum(jnp.sum(stats[...], axis=0), axis=1, keepdims=True)
    return jnp.broadcast_to(both[0:1] / (both[1:2] + 1e-06), (1, LANES))


def update_kernel(s3, g3, stats, p3, pinv3, rows, new3, z3, pay):
    chunks = chunk_count(s3)
    frames = g3.shape[1]
    sums_table = table(frames, False)
    size = step_size(stats)
    pay[...] = jnp.zeros_like(pay)
    for c in range(chunks):
        field = jnp.maximum(chunk(s3, c)[...] - size * g3[c], 0.0)
        z = summed(sums_table, field * rows[0, c : c + 1, :] * chunk(pinv3, c)[...])
        if len(new3) == 2:
            chunk(new3, c)[...] = field
        elif RIM <= c < chunks - RIM:
            new3[0][c - RIM] = field
        chunk(z3, c)[...] = z
        last = chunk(p3, c)[frames - 1 : frames, :]
        pay[c : c + 1, :] = last * z[frames - 1 : frames, :]


def final_kernel(s3, g3, stats, out, here, sems):
    size = step_size(stats)
    part = s3.shape[0] // PARTS
    copies = [
        pltpu.make_async_copy(
            here.at[pl.ds(i * part * LANES, part * LANES)],
            out.at[pl.ds(i * part * LANES, part * LANES)],
            sems.at[i],
        )
        for i in range(PARTS)
    ]
    for i in range(PARTS):

        @after_start
        def _():
            for c in range(i * part, (i + 1) * part):
                field = jnp.maximum(s3[c] - size * g3[c + RIM], 0.0)
                here[c * LANES : (c + 1) * LANES, :] = field.T
            copies[i].start()

    for copy in copies:
        copy.wait()


def picked(ext, pattern, q, first=0):
    parts = [
        ext[pl.ds(pl.multiple_of((pattern[k, q] - first) * NEU_BLOCK, NEU_BLOCK), NEU_BLOCK), :]
        for k in range(K)
    ]
    return jnp.concatenate(parts, axis=0)


def block_of(field, q):
    return field[q * PIX_BLOCK : (q + 1) * PIX_BLOCK, :]


def foot_of(feet, q, stripe):
    count = feet.shape[0] // PIX_BLOCK
    return block_of(feet, q if q < count // 2 else q - stripe + count)


def note_places(pattern, place, start, stop):
    for q in range(start, stop):
        for v in range(2 * HB + 1):
            place[q, v] = -1
        for k in range(K):
            place[q, pattern[k, q] - q] = k


def pull_back(pattern, ext, feet, record, contrib, q):
    foot = foot_of(feet, q, pattern.shape[1])
    fitted = jnp.dot(foot, picked(ext, pattern, q), preferred_element_type=F32)
    residual = (fitted - block_of(record, q).astype(F32)).astype(BF16)
    contrib[q * K * NEU_BLOCK : (q + 1) * K * NEU_BLOCK, :] = lax.dot_general(
        foot, residual, (((0,), (0,)), ((), ())), preferred_element_type=F32
    )


def gathered(contrib, place, c, ranges):
    frames = contrib.shape[1]
    per_chunk = LANES // NEU_BLOCK
    halves = []
    for b in range(c * per_chunk, (c + 1) * per_chunk):
        total = jnp.zeros((NEU_BLOCK, frames), F32)
        for v in range(2 * HB + 1):
            q = b - v
            if any(start <= q < stop for start, stop in ranges):
                k = place[q, v]
                at = pl.multiple_of((q * K + jnp.maximum(k, 0)) * NEU_BLOCK, NEU_BLOCK)
                value = contrib[pl.ds(at, NEU_BLOCK), :]
                if v % 2:
                    value = jnp.where(k >= 0, value, 0.0)
                total = total + value
        halves.append(total)
    return jnp.concatenate(halves, axis=0).T


def edge_kernel(
    pattern_far, z3, p3, rows, pay, pays, feet, record, ext, zones, spill, send_a, send_b, *rest
):
    *traces, contrib, place, pattern, sem = rest
    fetch = pltpu.make_async_copy(pattern_far, pattern, sem)
    fetch.start()
    chunks = chunk_count(z3)
    stripe = pattern.shape[1]
    edge = 2 * HB
    ranges = ((0, edge), (stripe - edge, stripe))

    @after_start
    def _():
        me = lax.axis_index("tm")
        totals = block_totals(pay, me, chunks, rows)
        ends = by_block(pays, me, slice(0, chunks))
        carry = jnp.zeros_like(totals[0])
        for m, end in enumerate(ends):
            carry = jnp.where(m < me, end + totals[m] * carry, carry)
        carry = carry * rows[1, 0:chunks]
        for c in range(chunks):
            field = chunk(p3, c)[...] * (chunk(z3, c)[...] + carry[c : c + 1, :])
            at = slice(c * LANES, (c + 1) * LANES)
            if traces and RIM <= c < chunks - RIM:
                field = field.T
                traces[0][(c - RIM) * LANES : (c - RIM + 1) * LANES, :] = field
                ext[at, :] = field.astype(BF16)
            else:
                ext[at, :] = field.astype(BF16).T

    fetch.wait()
    for start, stop in ranges:
        note_places(pattern, place, start, stop)
    for start, stop in ranges:
        for q in range(start, stop):
            pull_back(pattern, ext, feet, record, contrib, q)
    even = lax.axis_index("tile") % 2 == 0
    for i in range(2 * RIM):
        below = gathered(contrib, place, i, ranges)
        above = gathered(contrib, place, chunks - 2 * RIM + i, ranges)
        zones[i] = below
        zones[2 * RIM + i] = above
        send_a[i] = jnp.where(even, above, below).astype(BF16)
        send_b[i] = jnp.where(even, below, above).astype(BF16)
        spill[i] = gathered(contrib, place, 2 * RIM + i, ranges)
        spill[2 * RIM + i] = gathered(contrib, place, chunks - 4 * RIM + i, ranges)

def adjoint_chunk(sums_table, field, p, pinv, rows, c, chunks, r3, pay):
    frames = field.shape[0]
    r = summed(sums_table, field * p)
    r3[...] = r
    gain = rows[0, c : c + 1, :]
    pay[c : c + 1, :] = rows[1, c : c + 1, :] * r[0:1, :]
    ends = p[frames - 1 : frames, :] * gain * gain
    ends = ends * jnp.sum(pinv * pinv * r, axis=0, keepdims=True)
    pay[chunks + c : chunks + c + 1, :] = ends


def inner_kernel(pattern_far, p3, pinv3, rows, ext, spill, feet, record, traces, r3, pay, *rest):
    *out, contrib, place, pattern, sem = rest[: 4 + len(traces)]
    fetch = pltpu.make_async_copy(pattern_far, pattern, sem)
    fetch.start()
    if traces:
        copy = pltpu.make_async_copy(traces[0], out[0], rest[-1])
        copy.start()
    fetch.wait()

    def compute():
        chunks = chunk_count(p3)
        frames = spill.shape[1]
        stripe = pattern.shape[1]
        edge = 2 * HB
        note_places(pattern, place, edge, stripe - edge)
        sums_table = table(frames, True)
        pay[...] = jnp.zeros_like(pay)
        inner = chunks - 4 * RIM
        for q in range(edge, stripe - edge):
            pull_back(pattern, ext, feet, record, contrib, q)
        for i in range(inner):
            c = i + 2 * RIM
            field = gathered(contrib, place, c, ((edge, stripe - edge),))
            if i < 2 * RIM:
                field = field + spill[i]
            if i >= inner - 2 * RIM:
                field = field + spill[i - inner + 4 * RIM]
            p, pinv = chunk(p3, c)[...], chunk(pinv3, c)[...]
            adjoint_chunk(sums_table, field, p, pinv, rows, c, chunks, r3.at[i], pay)

    if traces:
        after_start(compute)
        copy.wait()
    else:
        compute()


def border_kernel(zones, got_a, got_b, p3, pinv3, rows, pay_inner, r3, pay):
    chunks = chunk_count(p3)
    frames = zones.shape[1]
    sums_table = table(frames, True)
    pay[...] = pay_inner[...]
    even = lax.axis_index("tile") % 2 == 0
    for i in range(2 * RIM):
        both = sides(even, got_a[i].astype(F32), got_b[i].astype(F32))
        for side, c in ((0, i), (1, chunks - 2 * RIM + i)):
            at = side * 2 * RIM + i
            field = zones[at] + both[side]
            p, pinv = chunk(p3, c)[...], chunk(pinv3, c)[...]
            adjoint_chunk(sums_table, field, p, pinv, rows, c, chunks, r3.at[at], pay)


def direction_kernel(
    pattern_far, r_inner, r_border, p3, pinv3, rows, pay, pays, feet, g3, stats, low, high, *rest
):
    pattern, sem, grad_sums = rest
    fetch = pltpu.make_async_copy(pattern_far, pattern, sem)
    fetch.start()
    chunks, frames = g3.shape[0], g3.shape[1]
    own = chunks - 2 * RIM
    stripe = pattern.shape[1]
    per_chunk = LANES // NEU_BLOCK
    low_chunks = low.shape[0] // LANES
    first_high = chunks - high.shape[0] // LANES

    @after_start
    def _():
        me = lax.axis_index("tm")
        totals = block_totals(pay, me, chunks, rows)
        gains = by_block(pay, me, slice(chunks, 2 * chunks))
        starts = by_block(pays, me, slice(0, chunks))
        ends = by_block(pays, me, slice(chunks, 2 * chunks))
        blocks = len(pays)
        entering = [None] * blocks
        state = jnp.zeros_like(totals[0])
        for m in reversed(range(blocks)):
            entering[m] = state
            state = starts[m] + totals[m] * state
        carry = jnp.zeros_like(totals[0])
        adjoint = jnp.zeros_like(totals[0])
        for m in range(blocks):
            end = ends[m] + gains[m] * entering[m]
            carry = jnp.where(m < me, end + totals[m] * carry, carry)
            adjoint = jnp.where(m == me, entering[m], adjoint)
        carry = carry * rows[1, 0:chunks]
        sums_table = table(frames, False)
        grad_sq = jnp.zeros((8, LANES), F32)
        for c in range(chunks):
            p = chunk(p3, c)[...]
            if c < 2 * RIM:
                r = r_border[c]
            elif c >= chunks - 2 * RIM:
                r = r_border[c - chunks + 4 * RIM]
            else:
                r = r_inner[c - 2 * RIM]
            scale = rows[0, c : c + 1, :] * chunk(pinv3, c)[...]
            gradient = scale * (r + p[frames - 1 : frames, :] * adjoint[c : c + 1, :])
            g3[c] = gradient
            if RIM <= c < RIM + own:
                grad_sq += jnp.sum((gradient * gradient).reshape(frames // 8, 8, LANES), axis=0)
            z = summed(sums_table, scale * gradient)
            field = (p * (z + carry[c : c + 1, :])).astype(BF16).T
            if c < low_chunks:
                low[c * LANES : (c + 1) * LANES, :] = field
            if c >= first_high:
                high[(c - first_high) * LANES : (c - first_high + 1) * LANES, :] = field
        grad_sums[...] = grad_sq

    fetch.wait()
    image_sq = jnp.zeros((8, frames), F32)
    for q in range(stripe):
        if q + 2 * HB < low_chunks * per_chunk:
            named = picked(low, pattern, q, 0)
        else:
            named = picked(high, pattern, q, first_high * per_chunk)
        image = jnp.dot(foot_of(feet, q, stripe), named, preferred_element_type=F32)
        image_sq += jnp.sum((image * image).reshape(PIX_BLOCK // 8, 8, frames), axis=0)
    both = jnp.concatenate(
        [
            jnp.sum(grad_sums[...], axis=0, keepdims=True),
            jnp.sum(image_sq, axis=0, keepdims=True),
        ],
        axis=0,
    )
    stats[...] = jnp.broadcast_to(both[None], stats.shape)


def f32(*shape):
    return jax.ShapeDtypeStruct(shape, F32)


def bf16(*shape):
    return jax.ShapeDtypeStruct(shape, BF16)


def call(
    kernel, name, micros, outs, args, scratch=(), far=(), far_out=(), keep=(), limit=16
):
    def spec(arg):
        if any(arg is other for other in far):
            return HBM
        return pl.BlockSpec(memory_space=pl.ANY) if arg.dtype == jnp.int32 else VMEM

    in_specs = [jax.tree.map(spec, arg) for arg in args]
    in_specs.append(jax.tree.map(lambda _: VMEM, keep))

    def body(*refs):
        kernel(*refs[: len(args)], *refs[len(args) + 1 :])

    return pl.pallas_call(
        body,
        name=name,
        out_shape=outs,
        in_specs=in_specs,
        out_specs=tuple(
            jax.tree.map(lambda _: HBM if place in far_out else VMEM, out)
            for place, out in enumerate(outs)
        ),
        scratch_shapes=scratch,
        compiler_params=pltpu.CompilerParams(vmem_limit_bytes=int(limit * 2**20)),
        cost_estimate=pl.CostEstimate(
            flops=int(micros * 1e8), bytes_accessed=int(micros * 3e6), transcendentals=0
        ),
    )(*args, keep)


def swapped(first, second):
    size = lax.axis_size("tile")

    def pairs(start):
        both = [(i, i + 1) for i in range(start, size - 1, 2)]
        return both + [(j, i) for i, j in both]

    return lax.ppermute(first, "tile", pairs(0)), lax.ppermute(second, "tile", pairs(1))


def shared_blocks(value):
    size = lax.axis_size("tm")
    others = [
        lax.ppermute(value, "tm", [(i, i ^ j) for i in range(size)])
        for j in reversed(range(1, size))
    ]
    return (value, *reversed(others))


def per_device(recording, footprints, pattern, decay, frame_gain, spikes):
    neurons, frames = spikes.shape
    stripe = pattern.shape[0]
    pattern = pattern.T
    own = neurons // LANES
    chunks = own + 2 * RIM
    lines = own + padded8(1)
    pay_lines = padded8(2 * chunks + 1)
    devices = lax.axis_size("tile") * lax.axis_size("tm")
    split = (f32(own, frames, LANES), f32(2 * RIM, frames, LANES))
    message = f32(RIM * LANES + padded8(RIM), frames)
    gains = frame_gain.reshape(1, frames)
    rates = decay.reshape(own, LANES)
    first, second, rates = call(
        rims_kernel,
        "rims",
        1.0,
        (message, message, f32(own, LANES)),
        (spikes, rates),
        [pltpu.SemaphoreType.DMA((3,))],
        far=(spikes, rates),
        limit=53,
    )
    first, second = swapped(first, second)
    ends_size = 4 * HB * PIX_BLOCK
    *owns, rows, pay, columns, feet_ends = call(
        prep_own_kernel,
        "prep_own",
        1.6,
        (split[0],) * 4
        + (f32(3, lines, LANES), f32(pay_lines, LANES), f32(2, frames, LANES))
        + (bf16(ends_size, K * NEU_BLOCK),),
        (spikes, rates, gains, footprints),
        [pltpu.SemaphoreType.DMA((2,))],
        far=(footprints,),
        limit=44,
    )
    *rims, rows, pay = call(
        prep_rim_kernel,
        "prep_rim",
        0.3,
        (split[1],) * 4 + (f32(3, lines, LANES), f32(pay_lines, LANES)),
        (first, second, columns, rows, pay),
    )
    s3, p3, pinv3, z3 = zip(owns, rims)
    constants = pays = shared_blocks(pay)
    scratch = [
        pltpu.VMEM((stripe * K * NEU_BLOCK, frames), F32),
        pltpu.SMEM((stripe, 2 * HB + 1), jnp.int32),
        pltpu.SMEM(pattern.shape, jnp.int32),
        pltpu.SemaphoreType.DMA,
    ]
    staged = [pltpu.VMEM((neurons, frames), F32), pltpu.SemaphoreType.DMA((PARTS,))]
    middle = stripe * NEU_BLOCK // LANES // 2
    halves = (middle + 2 * RIM, chunks - middle)
    zone = (2 * RIM, frames, LANES)
    border = (4 * RIM, frames, LANES)
    for iteration in range(ITERS):
        ends = iteration == ITERS - 1
        ext, zones, spill, send_a, send_b, *traces = call(
            edge_kernel,
            "edge",
            2.5,
            (
                bf16(chunks * LANES, frames),
                f32(*border),
                f32(*border),
                bf16(*zone),
                bf16(*zone),
            )
            + ((f32(neurons, frames),) if ends else ()),
            (pattern, z3, p3, rows, constants, pays, feet_ends, recording),
            scratch,
            keep=(s3[0],) if ends else (),
        )
        got_a, got_b = swapped(send_a, send_b)
        held = (s3[0],) if ends else ()
        r_inner, pay, *traces = call(
            inner_kernel,
            "inner",
            4.0,
            (f32(chunks - 4 * RIM, frames, LANES), f32(pay_lines, LANES))
            + ((f32(neurons, frames),) if ends else ()),
            (pattern, p3, pinv3, rows, ext, spill, footprints, recording, traces),
            scratch + ([pltpu.SemaphoreType.DMA] if ends else []),
            far_out=(2,),
            keep=held,
        )
        r_border, pay = call(
            border_kernel,
            "border",
            0.3,
            (f32(*border), f32(pay_lines, LANES)),
            (zones, got_a, got_b, p3, pinv3, rows, pay),
            keep=held,
        )
        pays = shared_blocks(pay)
        g3, stats = call(
            direction_kernel,
            "direction",
            4.0,
            (f32(chunks, frames, LANES), f32(devices, 2, LANES)),
            (pattern, r_inner, r_border, p3, pinv3, rows, constants, pays, footprints),
            [
                pltpu.VMEM((halves[0] * LANES, frames), BF16),
                pltpu.VMEM((halves[1] * LANES, frames), BF16),
                *scratch[2:],
                pltpu.VMEM((8, LANES), F32),
            ],
            keep=held,
        )
        stats = lax.all_to_all(stats, ("tile", "tm"), 0, 0)
        if ends:
            (out,) = call(
                final_kernel,
                "final",
                1.4,
                (f32(neurons, frames),),
                (s3[0], g3, stats),
                staged,
                far_out=(0,),
            )
            return out, traces[0]
        s3, z3, pay = call(
            update_kernel,
            "update",
            0.6,
            (split if iteration < ITERS - 2 else split[:1], split, f32(lines, LANES)),
            (s3, g3, stats, p3, pinv3, rows),
        )
        pays = shared_blocks(pay)


def solution(mesh):
    return jax.shard_map(
        per_device,
        mesh=mesh,
        in_specs=(
            P("tile", "tm"),
            P("tile", None),
            P("tile", None),
            P("tile"),
            P("tm"),
            P("tile", "tm"),
        ),
        out_specs=(P("tile", "tm"), P("tile", "tm")),
        check_vma=False,
    )
```

```python
import jax
import jax.numpy as jnp
from jax import lax
from jax.experimental import pallas as pl
from jax.experimental.pallas import tpu as pltpu
from jax.sharding import PartitionSpec as P

NEU_BLOCK = 64
PIX_BLOCK = 256
PARTS = 8
K = 4
HB = 2
ITERS = 2
LANES = 128
RIM = HB * NEU_BLOCK // LANES
F32 = jnp.float32
BF16 = jnp.bfloat16
VMEM = pl.BlockSpec(memory_space=pltpu.VMEM)
HBM = pl.BlockSpec(memory_space=pltpu.HBM)


def padded8(rows):
    return -(-rows // 8) * 8


def table(frames, reverse):
    row = lax.broadcasted_iota(jnp.int32, (frames, 2 * frames), 0)
    col = lax.broadcasted_iota(jnp.int32, (frames, 2 * frames), 1)
    col = jnp.where(col >= frames, col - frames, col)
    keep = col >= row if reverse else col <= row
    return jnp.where(keep, 1.0, 0.0).astype(BF16)


def summed(sums_table, values):
    high = values.astype(BF16)
    low = (values - high.astype(F32)).astype(BF16)
    both = jnp.concatenate([high, low], axis=0)
    return jnp.dot(sums_table, both, preferred_element_type=F32)


def powers(log_decay, frames, mid, sign):
    groups = frames // 8
    coarse = (8 * lax.broadcasted_iota(jnp.int32, (groups, LANES), 0) - mid).astype(F32) * sign
    fine = lax.broadcasted_iota(jnp.int32, (8, LANES), 0).astype(F32) * sign
    coarse = jnp.exp(coarse * log_decay)
    fine = jnp.exp(fine * log_decay)
    return (coarse[:, None, :] * fine[None, :, :]).reshape(frames, LANES)


def chunk(field, c):
    own, rim = field
    inner = own.shape[0]
    if c < RIM:
        return rim.at[c]
    if c >= RIM + inner:
        return rim.at[c - inner]
    return own.at[c - RIM]


def chunk_count(field):
    return field[0].shape[0] + field[1].shape[0]


def prep_chunk(c, rate, field, gains, s3, p3, pinv3, z3, rows, pay):
    frames = field.shape[1]
    middle, prefix_col, inverse_col, sums_table = gains
    mid = frames // 2 - 1
    rate = jnp.where(rate > 0.0, rate, 1.0)
    log_rate = jnp.log(rate)
    gain = jnp.sqrt(1.0 - rate * rate)
    p = powers(log_rate, frames, mid, 1.0) * prefix_col
    pinv = powers(log_rate, frames, mid, -1.0) * inverse_col
    field = field.T
    z = summed(sums_table, field * gain * pinv)
    last = p[frames - 1 : frames, :]
    s3[...] = field
    p3[...] = p
    pinv3[...] = pinv
    z3[...] = z
    half = rate
    for _ in range(frames.bit_length() - 2):
        half = half * half
    rows[0, c : c + 1, :] = gain
    rows[1, c : c + 1, :] = half * middle
    rows[2, c : c + 1, :] = half * half
    pay[0, c : c + 1, :] = last * z[frames - 1 : frames, :]
    scale = last * gain
    pay[1, c : c + 1, :] = scale * scale * jnp.sum(pinv * pinv, axis=0, keepdims=True)


def gain_columns(gains):
    frames = gains.shape[1]
    mid = frames // 2 - 1
    lane = lax.broadcasted_iota(jnp.int32, (8, frames), 1)
    prefix = jnp.broadcast_to(gains, (8, frames))
    step = 1
    while step < frames:
        prefix = prefix * jnp.where(lane >= step, pltpu.roll(prefix, step, 1), 1.0)
        step *= 2
    middle = jnp.broadcast_to(prefix[0:1, mid : mid + 1], (1, LANES))
    whole = jnp.broadcast_to(prefix[0:1, frames - 1 : frames], (1, LANES))
    prefix_col = jnp.broadcast_to(prefix[0:1] / middle, (LANES, frames)).T
    inverse_col = jnp.broadcast_to(middle / prefix[0:1], (LANES, frames)).T
    return middle, whole, prefix_col, inverse_col


def rims_kernel(spikes, decay, first, second, rates_here, sems):
    edge = RIM * LANES
    neurons = spikes.shape[0]
    own = decay.shape[0]
    even = lax.axis_index("tile") % 2 == 0
    top = jnp.where(even, neurons - edge, 0)
    bottom = jnp.where(even, 0, neurons - edge)
    copies = [
        pltpu.make_async_copy(decay, rates_here, sems.at[0]),
        pltpu.make_async_copy(
            spikes.at[pl.ds(pl.multiple_of(top, LANES), edge)], first.at[pl.ds(0, edge)], sems.at[1]
        ),
        pltpu.make_async_copy(
            spikes.at[pl.ds(pl.multiple_of(bottom, LANES), edge)],
            second.at[pl.ds(0, edge)],
            sems.at[2],
        ),
    ]
    for copy in copies:
        copy.start()
    first[edge:, :] = jnp.zeros_like(first[edge:, :])
    second[edge:, :] = jnp.zeros_like(second[edge:, :])
    copies[0].wait()
    lower, upper = rates_here[0:RIM, :], rates_here[own - RIM : own, :]
    first[edge : edge + RIM, :] = jnp.where(even, upper, lower)
    second[edge : edge + RIM, :] = jnp.where(even, lower, upper)
    for copy in copies[1:]:
        copy.wait()


def after_start(compute):
    pl.when(lax.axis_index("tm") >= 0)(compute)


def prep_own_kernel(
    spikes, decay, gains, feet, s3, p3, pinv3, z3, rows, pay, columns, feet_ends, sems
):
    own = s3.shape[0]
    chunks = own + 2 * RIM
    size = feet_ends.shape[0] // 2
    fetches = [
        pltpu.make_async_copy(
            feet.at[pl.ds(start, size)], feet_ends.at[pl.ds(i * size, size)], sems.at[i]
        )
        for i, start in enumerate((0, feet.shape[0] - size))
    ]
    for fetch in fetches:
        fetch.start()

    @after_start
    def _():
        middle, whole, prefix_col, inverse_col = gain_columns(gains[...])
        columns[0] = prefix_col
        columns[1] = inverse_col
        rows[...] = jnp.ones_like(rows)
        rows[0, chunks : chunks + 1, :] = middle
        pay[...] = jnp.zeros_like(pay)
        pay[0, chunks : chunks + 1, :] = whole
        shared = middle, prefix_col, inverse_col, table(spikes.shape[1], False)
        for i in range(own):
            field = spikes[i * LANES : (i + 1) * LANES, :]
            at = [ref.at[i] for ref in (s3, p3, pinv3, z3)]
            prep_chunk(i + RIM, decay[i : i + 1, :], field, shared, *at, rows, pay)

    for fetch in fetches:
        fetch.wait()


def sides(even, first, second):
    return jnp.where(even, second, first), jnp.where(even, first, second)


def prep_rim_kernel(second, first, columns, rows_own, pay_own, s3, p3, pinv3, z3, rows, pay):
    rims, frames = s3.shape[0], s3.shape[1]
    own = rows_own.shape[1] - padded8(1)
    chunks = own + 2 * RIM
    middle = rows_own[0, chunks : chunks + 1, :]
    shared = middle, columns[0], columns[1], table(frames, False)
    rows[...] = rows_own[...]
    pay[...] = pay_own[...]
    even = lax.axis_index("tile") % 2 == 0
    below, above = sides(even, first[...], second[...])
    for i in range(rims):
        message = below if i < RIM else above
        j = i % RIM
        c = i if i < RIM else own + i
        at = [ref.at[i] for ref in (s3, p3, pinv3, z3)]
        field = message[j * LANES : (j + 1) * LANES, :]
        rate = message[RIM * LANES + j : RIM * LANES + j + 1, :]
        prep_chunk(c, rate, field, shared, *at, rows, pay)


def by_block(parts, me, index):
    values = [part[index] for part in parts]
    ordered = []
    for m in range(len(values)):
        value = values[0]
        for j in range(1, len(values)):
            value = jnp.where(me == m ^ j, values[j], value)
        ordered.append(value)
    return ordered


def block_totals(pay, me, chunks, rows):
    return [rows[2] * whole for whole in by_block(pay, me, (0, slice(chunks, chunks + 1)))]


def step_size(stats):
    both = jnp.sum(jnp.sum(stats[...], axis=0), axis=1, keepdims=True)
    return jnp.broadcast_to(both[0:1] / (both[1:2] + 1e-06), (1, LANES))


def update_kernel(s3, g3, stats, p3, pinv3, rows, new3, z3, pay):
    chunks = chunk_count(s3)
    frames = g3.shape[1]
    sums_table = table(frames, False)
    size = step_size(stats)
    pay[...] = jnp.zeros_like(pay)
    for c in range(chunks):
        field = jnp.maximum(chunk(s3, c)[...] - size * g3[c], 0.0)
        z = summed(sums_table, field * rows[0, c : c + 1, :] * chunk(pinv3, c)[...])
        if len(new3) == 2:
            chunk(new3, c)[...] = field
        elif RIM <= c < chunks - RIM:
            new3[0][c - RIM] = field
        chunk(z3, c)[...] = z
        last = chunk(p3, c)[frames - 1 : frames, :]
        pay[0, c : c + 1, :] = last * z[frames - 1 : frames, :]


def final_kernel(s3, g3, stats, out, here, sems):
    size = step_size(stats)
    part = s3.shape[0] // PARTS
    copies = [
        pltpu.make_async_copy(
            here.at[pl.ds(i * part * LANES, part * LANES)],
            out.at[pl.ds(i * part * LANES, part * LANES)],
            sems.at[i],
        )
        for i in range(PARTS)
    ]
    for i in range(PARTS):

        @after_start
        def _():
            for c in range(i * part, (i + 1) * part):
                field = jnp.maximum(s3[c] - size * g3[c + RIM], 0.0)
                here[c * LANES : (c + 1) * LANES, :] = field.T
            copies[i].start()

    for copy in copies:
        copy.wait()


def picked(ext, pattern, q, first=0):
    parts = [
        ext[pl.ds(pl.multiple_of((pattern[k, q] - first) * NEU_BLOCK, NEU_BLOCK), NEU_BLOCK), :]
        for k in range(K)
    ]
    return jnp.concatenate(parts, axis=0)


def block_of(field, q):
    return field[q * PIX_BLOCK : (q + 1) * PIX_BLOCK, :]


def foot_of(feet, q, stripe):
    count = feet.shape[0] // PIX_BLOCK
    return block_of(feet, q if q < count // 2 else q - stripe + count)


def note_places(pattern, place, start, stop):
    for q in range(start, stop):
        for v in range(2 * HB + 1):
            place[q, v] = -1
        for k in range(K):
            place[q, pattern[k, q] - q] = k


def pull_back(pattern, ext, feet, record, contrib, q):
    foot = foot_of(feet, q, pattern.shape[1])
    fitted = jnp.dot(foot, picked(ext, pattern, q), preferred_element_type=F32)
    residual = (fitted - block_of(record, q).astype(F32)).astype(BF16)
    contrib[q * K * NEU_BLOCK : (q + 1) * K * NEU_BLOCK, :] = lax.dot_general(
        foot, residual, (((0,), (0,)), ((), ())), preferred_element_type=F32
    )


def gathered(contrib, place, c, ranges):
    frames = contrib.shape[1]
    per_chunk = LANES // NEU_BLOCK
    halves = []
    for b in range(c * per_chunk, (c + 1) * per_chunk):
        total = jnp.zeros((NEU_BLOCK, frames), F32)
        for v in range(2 * HB + 1):
            q = b - v
            if any(start <= q < stop for start, stop in ranges):
                k = place[q, v]
                at = pl.multiple_of((q * K + jnp.maximum(k, 0)) * NEU_BLOCK, NEU_BLOCK)
                value = contrib[pl.ds(at, NEU_BLOCK), :]
                if v % 2:
                    value = jnp.where(k >= 0, value, 0.0)
                total = total + value
        halves.append(total)
    return jnp.concatenate(halves, axis=0).T


def edge_kernel(
    pattern_far, z3, p3, rows, pay, pays, feet, record, ext, zones, spill, send_a, send_b, *rest
):
    *traces, contrib, place, pattern, sem = rest
    fetch = pltpu.make_async_copy(pattern_far, pattern, sem)
    fetch.start()
    chunks = chunk_count(z3)
    stripe = pattern.shape[1]
    edge = 2 * HB
    ranges = ((0, edge), (stripe - edge, stripe))

    @after_start
    def _():
        me = lax.axis_index("tm")
        totals = block_totals(pay, me, chunks, rows)
        ends = by_block(pays, me, 0)
        carry = jnp.zeros_like(totals[0])
        for m, end in enumerate(ends):
            carry = jnp.where(m < me, end + totals[m] * carry, carry)
        carry = carry * rows[1]
        for c in range(chunks):
            field = chunk(p3, c)[...] * (chunk(z3, c)[...] + carry[c : c + 1, :])
            at = slice(c * LANES, (c + 1) * LANES)
            if traces and RIM <= c < chunks - RIM:
                field = field.T
                traces[0][(c - RIM) * LANES : (c - RIM + 1) * LANES, :] = field
                ext[at, :] = field.astype(BF16)
            else:
                ext[at, :] = field.astype(BF16).T

    fetch.wait()
    for start, stop in ranges:
        note_places(pattern, place, start, stop)
    for start, stop in ranges:
        for q in range(start, stop):
            pull_back(pattern, ext, feet, record, contrib, q)
    even = lax.axis_index("tile") % 2 == 0
    for i in range(2 * RIM):
        below = gathered(contrib, place, i, ranges)
        above = gathered(contrib, place, chunks - 2 * RIM + i, ranges)
        zones[i] = below
        zones[2 * RIM + i] = above
        send_a[i] = jnp.where(even, above, below).astype(BF16)
        send_b[i] = jnp.where(even, below, above).astype(BF16)
        spill[i] = gathered(contrib, place, 2 * RIM + i, ranges)
        spill[2 * RIM + i] = gathered(contrib, place, chunks - 4 * RIM + i, ranges)

def adjoint_chunk(sums_table, field, p, pinv, rows, c, r3, pay):
    frames = field.shape[0]
    r = summed(sums_table, field * p)
    r3[...] = r
    gain = rows[0, c : c + 1, :]
    pay[0, c : c + 1, :] = rows[1, c : c + 1, :] * r[0:1, :]
    ends = p[frames - 1 : frames, :] * gain * gain
    pay[1, c : c + 1, :] = ends * jnp.sum(pinv * pinv * r, axis=0, keepdims=True)


def inner_kernel(pattern_far, p3, pinv3, rows, ext, spill, feet, record, traces, r3, pay, *rest):
    *out, contrib, place, pattern, sem = rest[: 4 + len(traces)]
    fetch = pltpu.make_async_copy(pattern_far, pattern, sem)
    fetch.start()
    if traces:
        copy = pltpu.make_async_copy(traces[0], out[0], rest[-1])
        copy.start()
    fetch.wait()

    def compute():
        chunks = chunk_count(p3)
        frames = spill.shape[1]
        stripe = pattern.shape[1]
        edge = 2 * HB
        note_places(pattern, place, edge, stripe - edge)
        sums_table = table(frames, True)
        pay[...] = jnp.zeros_like(pay)
        inner = chunks - 4 * RIM
        for q in range(edge, stripe - edge):
            pull_back(pattern, ext, feet, record, contrib, q)
        for i in range(inner):
            c = i + 2 * RIM
            field = gathered(contrib, place, c, ((edge, stripe - edge),))
            if i < 2 * RIM:
                field = field + spill[i]
            if i >= inner - 2 * RIM:
                field = field + spill[i - inner + 4 * RIM]
            p, pinv = chunk(p3, c)[...], chunk(pinv3, c)[...]
            adjoint_chunk(sums_table, field, p, pinv, rows, c, r3.at[i], pay)

    if traces:
        after_start(compute)
        copy.wait()
    else:
        compute()


def border_kernel(zones, got_b, got_a, p3, pinv3, rows, pay_inner, r3, pay):
    chunks = chunk_count(p3)
    frames = zones.shape[1]
    sums_table = table(frames, True)
    pay[...] = pay_inner[...]
    even = lax.axis_index("tile") % 2 == 0
    for i in range(2 * RIM):
        both = sides(even, got_a[i].astype(F32), got_b[i].astype(F32))
        for side, c in ((0, i), (1, chunks - 2 * RIM + i)):
            at = side * 2 * RIM + i
            field = zones[at] + both[side]
            p, pinv = chunk(p3, c)[...], chunk(pinv3, c)[...]
            adjoint_chunk(sums_table, field, p, pinv, rows, c, r3.at[at], pay)


def direction_kernel(
    pattern_far, r_inner, r_border, p3, pinv3, rows, pay, pays, feet, g3, stats, low, high, *rest
):
    pattern, sem, grad_sums = rest
    fetch = pltpu.make_async_copy(pattern_far, pattern, sem)
    fetch.start()
    chunks, frames = g3.shape[0], g3.shape[1]
    own = chunks - 2 * RIM
    stripe = pattern.shape[1]
    per_chunk = LANES // NEU_BLOCK
    low_chunks = low.shape[0] // LANES
    first_high = chunks - high.shape[0] // LANES

    @after_start
    def _():
        me = lax.axis_index("tm")
        totals = block_totals(pay, me, chunks, rows)
        gains = by_block(pay, me, 1)
        starts = by_block(pays, me, 0)
        ends = by_block(pays, me, 1)
        blocks = len(pays)
        entering = [None] * blocks
        state = jnp.zeros_like(totals[0])
        for m in reversed(range(blocks)):
            entering[m] = state
            state = starts[m] + totals[m] * state
        carry = jnp.zeros_like(totals[0])
        adjoint = jnp.zeros_like(totals[0])
        for m in range(blocks):
            end = ends[m] + gains[m] * entering[m]
            carry = jnp.where(m < me, end + totals[m] * carry, carry)
            adjoint = jnp.where(m == me, entering[m], adjoint)
        carry = carry * rows[1]
        sums_table = table(frames, False)
        grad_sq = jnp.zeros((8, LANES), F32)
        for c in range(chunks):
            p = chunk(p3, c)[...]
            if c < 2 * RIM:
                r = r_border[c]
            elif c >= chunks - 2 * RIM:
                r = r_border[c - chunks + 4 * RIM]
            else:
                r = r_inner[c - 2 * RIM]
            scale = rows[0, c : c + 1, :] * chunk(pinv3, c)[...]
            gradient = scale * (r + p[frames - 1 : frames, :] * adjoint[c : c + 1, :])
            g3[c] = gradient
            if RIM <= c < RIM + own:
                grad_sq += jnp.sum((gradient * gradient).reshape(frames // 8, 8, LANES), axis=0)
            z = summed(sums_table, scale * gradient)
            field = (p * (z + carry[c : c + 1, :])).astype(BF16).T
            if c < low_chunks:
                low[c * LANES : (c + 1) * LANES, :] = field
            if c >= first_high:
                high[(c - first_high) * LANES : (c - first_high + 1) * LANES, :] = field
        grad_sums[...] = grad_sq

    fetch.wait()
    image_sq = jnp.zeros((8, frames), F32)
    for q in range(stripe):
        if q + 2 * HB < low_chunks * per_chunk:
            named = picked(low, pattern, q, 0)
        else:
            named = picked(high, pattern, q, first_high * per_chunk)
        image = jnp.dot(foot_of(feet, q, stripe), named, preferred_element_type=F32)
        image_sq += jnp.sum((image * image).reshape(PIX_BLOCK // 8, 8, frames), axis=0)
    both = jnp.concatenate(
        [
            jnp.sum(grad_sums[...], axis=0, keepdims=True),
            jnp.sum(image_sq, axis=0, keepdims=True),
        ],
        axis=0,
    )
    stats[...] = jnp.broadcast_to(both[None], stats.shape)


def f32(*shape):
    return jax.ShapeDtypeStruct(shape, F32)


def bf16(*shape):
    return jax.ShapeDtypeStruct(shape, BF16)


def call(
    kernel, name, micros, outs, args, scratch=(), far=(), far_out=(), keep=(), limit=16
):
    def spec(arg):
        if any(arg is other for other in far):
            return HBM
        return pl.BlockSpec(memory_space=pl.ANY) if arg.dtype == jnp.int32 else VMEM

    in_specs = [jax.tree.map(spec, arg) for arg in args]
    in_specs.append(jax.tree.map(lambda _: VMEM, keep))

    def body(*refs):
        kernel(*refs[: len(args)], *refs[len(args) + 1 :])

    return pl.pallas_call(
        body,
        name=name,
        out_shape=outs,
        in_specs=in_specs,
        out_specs=tuple(
            jax.tree.map(lambda _: HBM if place in far_out else VMEM, out)
            for place, out in enumerate(outs)
        ),
        scratch_shapes=scratch,
        compiler_params=pltpu.CompilerParams(vmem_limit_bytes=int(limit * 2**20)),
        cost_estimate=pl.CostEstimate(
            flops=int(micros * 1e8), bytes_accessed=int(micros * 3e6), transcendentals=0
        ),
    )(*args, keep)


def swapped(first, second):
    size = lax.axis_size("tile")

    def pairs(start):
        both = [(i, i + 1) for i in range(start, size - 1, 2)]
        return both + [(j, i) for i, j in both]

    second = lax.ppermute(second, "tile", pairs(1))
    return lax.ppermute(first, "tile", pairs(0)), second


def shared_blocks(value):
    size = lax.axis_size("tm")
    others = [
        lax.ppermute(value, "tm", [(i, i ^ j) for i in range(size)])
        for j in reversed(range(1, size))
    ]
    return (value, *reversed(others))


def per_device(recording, footprints, pattern, decay, frame_gain, spikes):
    neurons, frames = spikes.shape
    stripe = pattern.shape[0]
    pattern = pattern.T
    own = neurons // LANES
    chunks = own + 2 * RIM
    lines = own + padded8(1)
    devices = lax.axis_size("tile") * lax.axis_size("tm")
    split = (f32(own, frames, LANES), f32(2 * RIM, frames, LANES))
    message = f32(RIM * LANES + padded8(RIM), frames)
    gains = frame_gain.reshape(1, frames)
    rates = decay.reshape(own, LANES)
    first, second, rates = call(
        rims_kernel,
        "rims",
        1.0,
        (message, message, f32(own, LANES)),
        (spikes, rates),
        [pltpu.SemaphoreType.DMA((3,))],
        far=(spikes, rates),
        limit=53,
    )
    first, second = swapped(first, second)
    ends_size = 4 * HB * PIX_BLOCK
    *owns, rows, pay, columns, feet_ends = call(
        prep_own_kernel,
        "prep_own",
        1.6,
        (split[0],) * 4
        + (f32(3, lines, LANES), f32(2, lines, LANES), f32(2, frames, LANES))
        + (bf16(ends_size, K * NEU_BLOCK),),
        (spikes, rates, gains, footprints),
        [pltpu.SemaphoreType.DMA((2,))],
        far=(footprints,),
        limit=44,
    )
    *rims, rows, pay = call(
        prep_rim_kernel,
        "prep_rim",
        0.3,
        (split[1],) * 4 + (f32(3, lines, LANES), f32(2, lines, LANES)),
        (second, first, columns, rows, pay),
    )
    s3, p3, pinv3, z3 = zip(owns, rims)
    constants = pays = shared_blocks(pay)
    scratch = [
        pltpu.VMEM((stripe * K * NEU_BLOCK, frames), F32),
        pltpu.SMEM((stripe, 2 * HB + 1), jnp.int32),
        pltpu.SMEM(pattern.shape, jnp.int32),
        pltpu.SemaphoreType.DMA,
    ]
    staged = [pltpu.VMEM((neurons, frames), F32), pltpu.SemaphoreType.DMA((PARTS,))]
    middle = stripe * NEU_BLOCK // LANES // 2
    halves = (middle + 2 * RIM, chunks - middle)
    zone = (2 * RIM, frames, LANES)
    border = (4 * RIM, frames, LANES)
    for iteration in range(ITERS):
        ends = iteration == ITERS - 1
        ext, zones, spill, send_a, send_b, *traces = call(
            edge_kernel,
            "edge",
            2.5,
            (
                bf16(chunks * LANES, frames),
                f32(*border),
                f32(*border),
                bf16(*zone),
                bf16(*zone),
            )
            + ((f32(neurons, frames),) if ends else ()),
            (pattern, z3, p3, rows, constants, pays, feet_ends, recording),
            scratch,
            keep=(s3[0],) if ends else (),
        )
        got_a, got_b = swapped(send_a, send_b)
        held = (s3[0],) if ends else ()
        r_inner, pay, *traces = call(
            inner_kernel,
            "inner",
            4.0,
            (f32(chunks - 4 * RIM, frames, LANES), f32(2, lines, LANES))
            + ((f32(neurons, frames),) if ends else ()),
            (pattern, p3, pinv3, rows, ext, spill, footprints, recording, traces),
            scratch + ([pltpu.SemaphoreType.DMA] if ends else []),
            far_out=(2,),
            keep=held,
        )
        r_border, pay = call(
            border_kernel,
            "border",
            0.3,
            (f32(*border), f32(2, lines, LANES)),
            (zones, got_b, got_a, p3, pinv3, rows, pay),
            keep=held,
        )
        pays = shared_blocks(pay)
        g3, stats = call(
            direction_kernel,
            "direction",
            4.0,
            (f32(chunks, frames, LANES), f32(devices, 2, LANES)),
            (pattern, r_inner, r_border, p3, pinv3, rows, constants, pays, footprints),
            [
                pltpu.VMEM((halves[0] * LANES, frames), BF16),
                pltpu.VMEM((halves[1] * LANES, frames), BF16),
                *scratch[2:],
                pltpu.VMEM((8, LANES), F32),
            ],
            keep=held,
        )
        stats = lax.all_to_all(stats, ("tile", "tm"), 0, 0)
        if ends:
            (out,) = call(
                final_kernel,
                "final",
                1.4,
                (f32(neurons, frames),),
                (s3[0], g3, stats),
                staged,
                far_out=(0,),
            )
            return out, traces[0]
        s3, z3, pay = call(
            update_kernel,
            "update",
            0.6,
            (split if iteration < ITERS - 2 else split[:1], split, f32(1, lines, LANES)),
            (s3, g3, stats, p3, pinv3, rows),
        )
        pays = shared_blocks(pay)


def solution(mesh):
    return jax.shard_map(
        per_device,
        mesh=mesh,
        in_specs=(
            P("tile", "tm"),
            P("tile", None),
            P("tile", None),
            P("tile"),
            P("tm"),
            P("tile", "tm"),
        ),
        out_specs=(P("tile", "tm"), P("tile", "tm")),
        check_vma=False,
    )
```

```python
import jax
import jax.numpy as jnp
from jax import lax
from jax.experimental import pallas as pl
from jax.experimental.pallas import tpu as pltpu
from jax.sharding import PartitionSpec as P

NEU_BLOCK = 64
PIX_BLOCK = 256
PARTS = 8
K = 4
HB = 2
ITERS = 2
LANES = 128
RIM = HB * NEU_BLOCK // LANES
F32 = jnp.float32
BF16 = jnp.bfloat16
VMEM = pl.BlockSpec(memory_space=pltpu.VMEM)
HBM = pl.BlockSpec(memory_space=pltpu.HBM)


def padded8(rows):
    return -(-rows // 8) * 8


def table(frames, reverse):
    row = lax.broadcasted_iota(jnp.int32, (frames, 2 * frames), 0)
    col = lax.broadcasted_iota(jnp.int32, (frames, 2 * frames), 1)
    col = jnp.where(col >= frames, col - frames, col)
    keep = col >= row if reverse else col <= row
    return jnp.where(keep, 1.0, 0.0).astype(BF16)


def summed(sums_table, values):
    high = values.astype(BF16)
    low = (values - high.astype(F32)).astype(BF16)
    both = jnp.concatenate([high, low], axis=0)
    return jnp.dot(sums_table, both, preferred_element_type=F32)


def powers(log_decay, frames, mid, sign):
    groups = frames // 8
    coarse = (8 * lax.broadcasted_iota(jnp.int32, (groups, LANES), 0) - mid).astype(F32) * sign
    fine = lax.broadcasted_iota(jnp.int32, (8, LANES), 0).astype(F32) * sign
    coarse = jnp.exp(coarse * log_decay)
    fine = jnp.exp(fine * log_decay)
    return (coarse[:, None, :] * fine[None, :, :]).reshape(frames, LANES)


def chunk(field, c):
    own, rim = field
    inner = own.shape[0]
    if c < RIM:
        return rim.at[c]
    if c >= RIM + inner:
        return rim.at[c - inner]
    return own.at[c - RIM]


def chunk_count(field):
    return field[0].shape[0] + field[1].shape[0]


def prep_chunk(c, rate, field, gains, s3, p3, pinv3, z3, rows, pay):
    frames = field.shape[1]
    middle, prefix_col, inverse_col, sums_table = gains
    mid = frames // 2 - 1
    rate = jnp.where(rate > 0.0, rate, 1.0)
    log_rate = jnp.log(rate)
    gain = jnp.sqrt(1.0 - rate * rate)
    p = powers(log_rate, frames, mid, 1.0) * prefix_col
    pinv = powers(log_rate, frames, mid, -1.0) * inverse_col
    field = field.T
    z = summed(sums_table, field * gain * pinv)
    last = p[frames - 1 : frames, :]
    s3[...] = field
    p3[...] = p
    pinv3[...] = pinv
    z3[...] = z
    half = rate
    for _ in range(frames.bit_length() - 2):
        half = half * half
    rows[0, c : c + 1, :] = gain
    rows[1, c : c + 1, :] = half * middle
    rows[2, c : c + 1, :] = half * half
    pay[0, c : c + 1, :] = last * z[frames - 1 : frames, :]
    scale = last * gain
    pay[1, c : c + 1, :] = scale * scale * jnp.sum(pinv * pinv, axis=0, keepdims=True)


def gain_columns(gains):
    frames = gains.shape[1]
    mid = frames // 2 - 1
    lane = lax.broadcasted_iota(jnp.int32, (8, frames), 1)
    prefix = jnp.broadcast_to(gains, (8, frames))
    step = 1
    while step < frames:
        prefix = prefix * jnp.where(lane >= step, pltpu.roll(prefix, step, 1), 1.0)
        step *= 2
    middle = jnp.broadcast_to(prefix[0:1, mid : mid + 1], (1, LANES))
    whole = jnp.broadcast_to(prefix[0:1, frames - 1 : frames], (1, LANES))
    prefix_col = jnp.broadcast_to(prefix[0:1] / middle, (LANES, frames)).T
    inverse_col = jnp.broadcast_to(middle / prefix[0:1], (LANES, frames)).T
    return middle, whole, prefix_col, inverse_col


def rims_kernel(spikes, decay, first, second, rates_here, sems):
    edge = RIM * LANES
    neurons = spikes.shape[0]
    own = decay.shape[0]
    even = lax.axis_index("tile") % 2 == 0
    top = jnp.where(even, neurons - edge, 0)
    bottom = jnp.where(even, 0, neurons - edge)
    copies = [
        pltpu.make_async_copy(decay, rates_here, sems.at[0]),
        pltpu.make_async_copy(
            spikes.at[pl.ds(pl.multiple_of(top, LANES), edge)], first.at[pl.ds(0, edge)], sems.at[1]
        ),
        pltpu.make_async_copy(
            spikes.at[pl.ds(pl.multiple_of(bottom, LANES), edge)],
            second.at[pl.ds(0, edge)],
            sems.at[2],
        ),
    ]
    for copy in copies:
        copy.start()
    first[edge:, :] = jnp.zeros_like(first[edge:, :])
    second[edge:, :] = jnp.zeros_like(second[edge:, :])
    copies[0].wait()
    lower, upper = rates_here[0:RIM, :], rates_here[own - RIM : own, :]
    first[edge : edge + RIM, :] = jnp.where(even, upper, lower)
    second[edge : edge + RIM, :] = jnp.where(even, lower, upper)
    for copy in copies[1:]:
        copy.wait()


def after_start(compute):
    pl.when(lax.axis_index("tm") >= 0)(compute)


def prep_own_kernel(
    spikes, decay, gains, feet, s3, p3, pinv3, z3, rows, pay, columns, feet_ends, sems
):
    own = s3.shape[0]
    chunks = own + 2 * RIM
    size = feet_ends.shape[0] // 2
    fetches = [
        pltpu.make_async_copy(
            feet.at[pl.ds(start, size)], feet_ends.at[pl.ds(i * size, size)], sems.at[i]
        )
        for i, start in enumerate((0, feet.shape[0] - size))
    ]
    for fetch in fetches:
        fetch.start()

    @after_start
    def _():
        middle, whole, prefix_col, inverse_col = gain_columns(gains[...])
        columns[0] = prefix_col
        columns[1] = inverse_col
        rows[...] = jnp.ones_like(rows)
        rows[0, chunks : chunks + 1, :] = middle
        pay[...] = jnp.zeros_like(pay)
        pay[0, chunks : chunks + 1, :] = whole
        shared = middle, prefix_col, inverse_col, table(spikes.shape[1], False)
        for i in range(own):
            field = spikes[i * LANES : (i + 1) * LANES, :]
            at = [ref.at[i] for ref in (s3, p3, pinv3, z3)]
            prep_chunk(i + RIM, decay[i : i + 1, :], field, shared, *at, rows, pay)

    for fetch in fetches:
        fetch.wait()


def sides(even, first, second):
    return jnp.where(even, second, first), jnp.where(even, first, second)


def prep_rim_kernel(first, second, columns, rows_own, pay_own, s3, p3, pinv3, z3, rows, pay):
    rims, frames = s3.shape[0], s3.shape[1]
    own = rows_own.shape[1] - padded8(1)
    chunks = own + 2 * RIM
    middle = rows_own[0, chunks : chunks + 1, :]
    shared = middle, columns[0], columns[1], table(frames, False)
    rows[...] = rows_own[...]
    pay[...] = pay_own[...]
    even = lax.axis_index("tile") % 2 == 0
    below, above = sides(even, first[...], second[...])
    for i in range(rims):
        message = below if i < RIM else above
        j = i % RIM
        c = i if i < RIM else own + i
        at = [ref.at[i] for ref in (s3, p3, pinv3, z3)]
        field = message[j * LANES : (j + 1) * LANES, :]
        rate = message[RIM * LANES + j : RIM * LANES + j + 1, :]
        prep_chunk(c, rate, field, shared, *at, rows, pay)


def by_block(parts, me, index):
    values = [part[index] for part in parts]
    ordered = []
    for m in range(len(values)):
        value = values[0]
        for j in range(1, len(values)):
            value = jnp.where(me == m ^ j, values[j], value)
        ordered.append(value)
    return ordered


def block_totals(pay, me, chunks, rows):
    return [rows[2] * whole for whole in by_block(pay, me, (0, slice(chunks, chunks + 1)))]


def step_size(stats):
    both = jnp.sum(jnp.sum(stats[...], axis=0), axis=1, keepdims=True)
    return jnp.broadcast_to(both[0:1] / (both[1:2] + 1e-06), (1, LANES))


def update_kernel(s3, g3, stats, p3, pinv3, rows, new3, z3, pay):
    chunks = chunk_count(s3)
    frames = g3.shape[1]
    sums_table = table(frames, False)
    size = step_size(stats)
    pay[...] = jnp.zeros_like(pay)
    for c in range(chunks):
        field = jnp.maximum(chunk(s3, c)[...] - size * g3[c], 0.0)
        z = summed(sums_table, field * rows[0, c : c + 1, :] * chunk(pinv3, c)[...])
        if len(new3) == 2:
            chunk(new3, c)[...] = field
        elif RIM <= c < chunks - RIM:
            new3[0][c - RIM] = field
        chunk(z3, c)[...] = z
        last = chunk(p3, c)[frames - 1 : frames, :]
        pay[0, c : c + 1, :] = last * z[frames - 1 : frames, :]


def final_kernel(s3, g3, stats, out, here, sems):
    size = step_size(stats)
    part = s3.shape[0] // PARTS
    copies = [
        pltpu.make_async_copy(
            here.at[pl.ds(i * part * LANES, part * LANES)],
            out.at[pl.ds(i * part * LANES, part * LANES)],
            sems.at[i],
        )
        for i in range(PARTS)
    ]
    for i in range(PARTS):

        @after_start
        def _():
            for c in range(i * part, (i + 1) * part):
                field = jnp.maximum(s3[c] - size * g3[c + RIM], 0.0)
                here[c * LANES : (c + 1) * LANES, :] = field.T
            copies[i].start()

    for copy in copies:
        copy.wait()


def picked(ext, pattern, q, first=0):
    parts = [
        ext[pl.ds(pl.multiple_of((pattern[k, q] - first) * NEU_BLOCK, NEU_BLOCK), NEU_BLOCK), :]
        for k in range(K)
    ]
    return jnp.concatenate(parts, axis=0)


def block_of(field, q):
    return field[q * PIX_BLOCK : (q + 1) * PIX_BLOCK, :]


def foot_of(feet, q, stripe):
    count = feet.shape[0] // PIX_BLOCK
    return block_of(feet, q if q < count // 2 else q - stripe + count)


def note_places(pattern, place, start, stop):
    for q in range(start, stop):
        for v in range(2 * HB + 1):
            place[q, v] = -1
        for k in range(K):
            place[q, pattern[k, q] - q] = k


def pull_back(pattern, ext, feet, record, contrib, q):
    foot = foot_of(feet, q, pattern.shape[1])
    fitted = jnp.dot(foot, picked(ext, pattern, q), preferred_element_type=F32)
    residual = (fitted - block_of(record, q).astype(F32)).astype(BF16)
    contrib[q * K * NEU_BLOCK : (q + 1) * K * NEU_BLOCK, :] = lax.dot_general(
        foot, residual, (((0,), (0,)), ((), ())), preferred_element_type=F32
    )


def gathered(contrib, place, c, ranges):
    frames = contrib.shape[1]
    per_chunk = LANES // NEU_BLOCK
    halves = []
    for b in range(c * per_chunk, (c + 1) * per_chunk):
        total = jnp.zeros((NEU_BLOCK, frames), F32)
        for v in range(2 * HB + 1):
            q = b - v
            if any(start <= q < stop for start, stop in ranges):
                k = place[q, v]
                at = pl.multiple_of((q * K + jnp.maximum(k, 0)) * NEU_BLOCK, NEU_BLOCK)
                value = contrib[pl.ds(at, NEU_BLOCK), :]
                if v % 2:
                    value = jnp.where(k >= 0, value, 0.0)
                total = total + value
        halves.append(total)
    return jnp.concatenate(halves, axis=0).T


def edge_kernel(
    pattern_far, z3, p3, rows, pay, pays, feet, record, ext, zones, spill, send_a, send_b, *rest
):
    *traces, contrib, place, pattern, sem = rest
    fetch = pltpu.make_async_copy(pattern_far, pattern, sem)
    fetch.start()
    chunks = chunk_count(z3)
    stripe = pattern.shape[1]
    edge = 2 * HB
    ranges = ((0, edge), (stripe - edge, stripe))

    @after_start
    def _():
        me = lax.axis_index("tm")
        totals = block_totals(pay, me, chunks, rows)
        ends = by_block(pays, me, 0)
        carry = jnp.zeros_like(totals[0])
        for m, end in enumerate(ends):
            carry = jnp.where(m < me, end + totals[m] * carry, carry)
        carry = carry * rows[1]
        for c in range(chunks):
            field = chunk(p3, c)[...] * (chunk(z3, c)[...] + carry[c : c + 1, :])
            at = slice(c * LANES, (c + 1) * LANES)
            if traces and RIM <= c < chunks - RIM:
                field = field.T
                traces[0][(c - RIM) * LANES : (c - RIM + 1) * LANES, :] = field
                ext[at, :] = field.astype(BF16)
            else:
                ext[at, :] = field.astype(BF16).T

    fetch.wait()
    for start, stop in ranges:
        note_places(pattern, place, start, stop)
    for start, stop in ranges:
        for q in range(start, stop):
            pull_back(pattern, ext, feet, record, contrib, q)
    even = lax.axis_index("tile") % 2 == 0
    for i in range(2 * RIM):
        below = gathered(contrib, place, i, ranges)
        above = gathered(contrib, place, chunks - 2 * RIM + i, ranges)
        zones[i] = below
        zones[2 * RIM + i] = above
        for to, other, held in ((send_a, above, below), (send_b, below, above)):
            to[i] = jnp.where(even, other, held).astype(BF16)
        lows = [value - value.astype(BF16).astype(F32) for value in (below, above)]
        at = 2 * RIM + i % RIM
        for to, takes in ((send_a, jnp.logical_not(even)), (send_b, even)):
            if i < RIM:

                @pl.when(takes)
                def _():
                    to[at] = lows[0].astype(BF16)

            else:

                @pl.when(jnp.logical_not(takes))
                def _():
                    to[at] = lows[1].astype(BF16)

        spill[i] = gathered(contrib, place, 2 * RIM + i, ranges)
        spill[2 * RIM + i] = gathered(contrib, place, chunks - 4 * RIM + i, ranges)

def adjoint_chunk(sums_table, field, p, pinv, rows, c, r3, pay):
    frames = field.shape[0]
    r = summed(sums_table, field * p)
    r3[...] = r
    gain = rows[0, c : c + 1, :]
    pay[0, c : c + 1, :] = rows[1, c : c + 1, :] * r[0:1, :]
    ends = p[frames - 1 : frames, :] * gain * gain
    pay[1, c : c + 1, :] = ends * jnp.sum(pinv * pinv * r, axis=0, keepdims=True)


def inner_kernel(pattern_far, p3, pinv3, rows, ext, spill, feet, record, traces, r3, pay, *rest):
    *out, contrib, place, pattern, sem = rest[: 4 + len(traces)]
    fetch = pltpu.make_async_copy(pattern_far, pattern, sem)
    fetch.start()
    if traces:
        copy = pltpu.make_async_copy(traces[0], out[0], rest[-1])
        copy.start()
    fetch.wait()

    def compute():
        chunks = chunk_count(p3)
        frames = spill.shape[1]
        stripe = pattern.shape[1]
        edge = 2 * HB
        note_places(pattern, place, edge, stripe - edge)
        sums_table = table(frames, True)
        pay[...] = jnp.zeros_like(pay)
        inner = chunks - 4 * RIM
        for q in range(edge, stripe - edge):
            pull_back(pattern, ext, feet, record, contrib, q)
        for i in range(inner):
            c = i + 2 * RIM
            field = gathered(contrib, place, c, ((edge, stripe - edge),))
            if i < 2 * RIM:
                field = field + spill[i]
            if i >= inner - 2 * RIM:
                field = field + spill[i - inner + 4 * RIM]
            p, pinv = chunk(p3, c)[...], chunk(pinv3, c)[...]
            adjoint_chunk(sums_table, field, p, pinv, rows, c, r3.at[i], pay)

    if traces:
        after_start(compute)
        copy.wait()
    else:
        compute()


def border_kernel(zones, got_a, got_b, p3, pinv3, rows, pay_inner, r3, pay):
    chunks = chunk_count(p3)
    frames = zones.shape[1]
    sums_table = table(frames, True)
    pay[...] = pay_inner[...]
    even = lax.axis_index("tile") % 2 == 0
    for i in range(2 * RIM):
        both = sides(even, got_a[i].astype(F32), got_b[i].astype(F32))
        at = 2 * RIM + i % RIM
        lows = sides(even, got_a[at].astype(F32), got_b[at].astype(F32))
        for side, c in ((0, i), (1, chunks - 2 * RIM + i)):
            at = side * 2 * RIM + i
            field = zones[at] + both[side]
            if (i >= RIM) == (side == 0):
                field = field + lows[side]
            p, pinv = chunk(p3, c)[...], chunk(pinv3, c)[...]
            adjoint_chunk(sums_table, field, p, pinv, rows, c, r3.at[at], pay)


def direction_kernel(
    pattern_far, r_inner, r_border, p3, pinv3, rows, pay, pays, feet, g3, stats, low, high, *rest
):
    pattern, sem, grad_sums = rest
    fetch = pltpu.make_async_copy(pattern_far, pattern, sem)
    fetch.start()
    chunks, frames = g3.shape[0], g3.shape[1]
    own = chunks - 2 * RIM
    stripe = pattern.shape[1]
    per_chunk = LANES // NEU_BLOCK
    low_chunks = low.shape[0] // LANES
    first_high = chunks - high.shape[0] // LANES

    @after_start
    def _():
        me = lax.axis_index("tm")
        totals = block_totals(pay, me, chunks, rows)
        gains = by_block(pay, me, 1)
        starts = by_block(pays, me, 0)
        ends = by_block(pays, me, 1)
        blocks = len(pays)
        entering = [None] * blocks
        state = jnp.zeros_like(totals[0])
        for m in reversed(range(blocks)):
            entering[m] = state
            state = starts[m] + totals[m] * state
        carry = jnp.zeros_like(totals[0])
        adjoint = jnp.zeros_like(totals[0])
        for m in range(blocks):
            end = ends[m] + gains[m] * entering[m]
            carry = jnp.where(m < me, end + totals[m] * carry, carry)
            adjoint = jnp.where(m == me, entering[m], adjoint)
        carry = carry * rows[1]
        sums_table = table(frames, False)
        grad_sq = jnp.zeros((8, LANES), F32)
        for c in range(chunks):
            p = chunk(p3, c)[...]
            if c < 2 * RIM:
                r = r_border[c]
            elif c >= chunks - 2 * RIM:
                r = r_border[c - chunks + 4 * RIM]
            else:
                r = r_inner[c - 2 * RIM]
            scale = rows[0, c : c + 1, :] * chunk(pinv3, c)[...]
            gradient = scale * (r + p[frames - 1 : frames, :] * adjoint[c : c + 1, :])
            g3[c] = gradient
            if RIM <= c < RIM + own:
                grad_sq += jnp.sum((gradient * gradient).reshape(frames // 8, 8, LANES), axis=0)
            z = summed(sums_table, scale * gradient)
            field = (p * (z + carry[c : c + 1, :])).astype(BF16).T
            if c < low_chunks:
                low[c * LANES : (c + 1) * LANES, :] = field
            if c >= first_high:
                high[(c - first_high) * LANES : (c - first_high + 1) * LANES, :] = field
        grad_sums[...] = grad_sq

    fetch.wait()
    image_sq = jnp.zeros((8, frames), F32)
    for q in range(stripe):
        if q + 2 * HB < low_chunks * per_chunk:
            named = picked(low, pattern, q, 0)
        else:
            named = picked(high, pattern, q, first_high * per_chunk)
        image = jnp.dot(foot_of(feet, q, stripe), named, preferred_element_type=F32)
        image_sq += jnp.sum((image * image).reshape(PIX_BLOCK // 8, 8, frames), axis=0)
    both = jnp.concatenate(
        [
            jnp.sum(grad_sums[...], axis=0, keepdims=True),
            jnp.sum(image_sq, axis=0, keepdims=True),
        ],
        axis=0,
    )
    stats[...] = jnp.broadcast_to(both[None], stats.shape)


def f32(*shape):
    return jax.ShapeDtypeStruct(shape, F32)


def bf16(*shape):
    return jax.ShapeDtypeStruct(shape, BF16)


def call(
    kernel, name, micros, outs, args, scratch=(), far=(), far_out=(), keep=(), limit=16
):
    def spec(arg):
        if any(arg is other for other in far):
            return HBM
        return pl.BlockSpec(memory_space=pl.ANY) if arg.dtype == jnp.int32 else VMEM

    in_specs = [jax.tree.map(spec, arg) for arg in args]
    in_specs.append(jax.tree.map(lambda _: VMEM, keep))

    def body(*refs):
        kernel(*refs[: len(args)], *refs[len(args) + 1 :])

    return pl.pallas_call(
        body,
        name=name,
        out_shape=outs,
        in_specs=in_specs,
        out_specs=tuple(
            jax.tree.map(lambda _: HBM if place in far_out else VMEM, out)
            for place, out in enumerate(outs)
        ),
        scratch_shapes=scratch,
        compiler_params=pltpu.CompilerParams(vmem_limit_bytes=int(limit * 2**20)),
        cost_estimate=pl.CostEstimate(
            flops=int(micros * 1e8), bytes_accessed=int(micros * 3e6), transcendentals=0
        ),
    )(*args, keep)


def swapped(first, second):
    size = lax.axis_size("tile")

    def pairs(start):
        both = [(i, i + 1) for i in range(start, size - 1, 2)]
        return both + [(j, i) for i, j in both]

    return lax.ppermute(first, "tile", pairs(0)), lax.ppermute(second, "tile", pairs(1))


def shared_blocks(value):
    size = lax.axis_size("tm")
    others = [
        lax.ppermute(value, "tm", [(i, i ^ j) for i in range(size)])
        for j in reversed(range(1, size))
    ]
    return (value, *reversed(others))


def per_device(recording, footprints, pattern, decay, frame_gain, spikes):
    neurons, frames = spikes.shape
    stripe = pattern.shape[0]
    pattern = pattern.T
    own = neurons // LANES
    chunks = own + 2 * RIM
    lines = own + padded8(1)
    devices = lax.axis_size("tile") * lax.axis_size("tm")
    split = (f32(own, frames, LANES), f32(2 * RIM, frames, LANES))
    message = f32(RIM * LANES + padded8(RIM), frames)
    gains = frame_gain.reshape(1, frames)
    rates = decay.reshape(own, LANES)
    first, second, rates = call(
        rims_kernel,
        "rims",
        1.0,
        (message, message, f32(own, LANES)),
        (spikes, rates),
        [pltpu.SemaphoreType.DMA((3,))],
        far=(spikes, rates),
        limit=53,
    )
    first, second = swapped(first, second)
    ends_size = 4 * HB * PIX_BLOCK
    *owns, rows, pay, columns, feet_ends = call(
        prep_own_kernel,
        "prep_own",
        1.6,
        (split[0],) * 4
        + (f32(3, lines, LANES), f32(2, lines, LANES), f32(2, frames, LANES))
        + (bf16(ends_size, K * NEU_BLOCK),),
        (spikes, rates, gains, footprints),
        [pltpu.SemaphoreType.DMA((2,))],
        far=(footprints,),
        limit=44,
    )
    *rims, rows, pay = call(
        prep_rim_kernel,
        "prep_rim",
        0.3,
        (split[1],) * 4 + (f32(3, lines, LANES), f32(2, lines, LANES)),
        (first, second, columns, rows, pay),
    )
    s3, p3, pinv3, z3 = zip(owns, rims)
    constants = pays = shared_blocks(pay)
    scratch = [
        pltpu.VMEM((stripe * K * NEU_BLOCK, frames), F32),
        pltpu.SMEM((stripe, 2 * HB + 1), jnp.int32),
        pltpu.SMEM(pattern.shape, jnp.int32),
        pltpu.SemaphoreType.DMA,
    ]
    staged = [pltpu.VMEM((neurons, frames), F32), pltpu.SemaphoreType.DMA((PARTS,))]
    middle = stripe * NEU_BLOCK // LANES // 2
    halves = (middle + 2 * RIM, chunks - middle)
    border = (4 * RIM, frames, LANES)
    for iteration in range(ITERS):
        ends = iteration == ITERS - 1
        ext, zones, spill, send_a, send_b, *traces = call(
            edge_kernel,
            "edge",
            2.5,
            (
                bf16(chunks * LANES, frames),
                f32(*border),
                f32(*border),
                bf16(3 * RIM, frames, LANES),
                bf16(3 * RIM, frames, LANES),
            )
            + ((f32(neurons, frames),) if ends else ()),
            (pattern, z3, p3, rows, constants, pays, feet_ends, recording),
            scratch,
            keep=(s3[0],) if ends else (),
        )
        got_a, got_b = swapped(send_a, send_b)
        held = (s3[0],) if ends else ()
        r_inner, pay, *traces = call(
            inner_kernel,
            "inner",
            4.0,
            (f32(chunks - 4 * RIM, frames, LANES), f32(2, lines, LANES))
            + ((f32(neurons, frames),) if ends else ()),
            (pattern, p3, pinv3, rows, ext, spill, footprints, recording, traces),
            scratch + ([pltpu.SemaphoreType.DMA] if ends else []),
            far_out=(2,),
            keep=held,
        )
        r_border, pay = call(
            border_kernel,
            "border",
            0.3,
            (f32(*border), f32(2, lines, LANES)),
            (zones, got_a, got_b, p3, pinv3, rows, pay),
            keep=held,
        )
        pays = shared_blocks(pay)
        g3, stats = call(
            direction_kernel,
            "direction",
            4.0,
            (f32(chunks, frames, LANES), f32(devices, 2, LANES)),
            (pattern, r_inner, r_border, p3, pinv3, rows, constants, pays, footprints),
            [
                pltpu.VMEM((halves[0] * LANES, frames), BF16),
                pltpu.VMEM((halves[1] * LANES, frames), BF16),
                *scratch[2:],
                pltpu.VMEM((8, LANES), F32),
            ],
            keep=held,
        )
        stats = lax.all_to_all(stats, ("tile", "tm"), 0, 0)
        if ends:
            (out,) = call(
                final_kernel,
                "final",
                1.4,
                (f32(neurons, frames),),
                (s3[0], g3, stats),
                staged,
                far_out=(0,),
            )
            return out, traces[0]
        s3, z3, pay = call(
            update_kernel,
            "update",
            0.6,
            (split if iteration < ITERS - 2 else split[:1], split, f32(1, lines, LANES)),
            (s3, g3, stats, p3, pinv3, rows),
        )
        pays = shared_blocks(pay)


def solution(mesh):
    return jax.shard_map(
        per_device,
        mesh=mesh,
        in_specs=(
            P("tile", "tm"),
            P("tile", None),
            P("tile", None),
            P("tile"),
            P("tm"),
            P("tile", "tm"),
        ),
        out_specs=(P("tile", "tm"), P("tile", "tm")),
        check_vma=False,
    )
```

```python
import jax
import jax.numpy as jnp
from jax import lax
from jax.experimental import pallas as pl
from jax.experimental.pallas import tpu as pltpu
from jax.sharding import PartitionSpec as P

NEU_BLOCK = 64
PIX_BLOCK = 256
PARTS = 8
K = 4
HB = 2
ITERS = 2
LANES = 128
RIM = HB * NEU_BLOCK // LANES
F32 = jnp.float32
BF16 = jnp.bfloat16
VMEM = pl.BlockSpec(memory_space=pltpu.VMEM)
HBM = pl.BlockSpec(memory_space=pltpu.HBM)


def padded8(rows):
    return -(-rows // 8) * 8


def table(frames, reverse):
    row = lax.broadcasted_iota(jnp.int32, (frames, 2 * frames), 0)
    col = lax.broadcasted_iota(jnp.int32, (frames, 2 * frames), 1)
    col = jnp.where(col >= frames, col - frames, col)
    keep = col >= row if reverse else col <= row
    return jnp.where(keep, 1.0, 0.0).astype(BF16)


def summed(sums_table, values):
    high = values.astype(BF16)
    low = (values - high.astype(F32)).astype(BF16)
    both = jnp.concatenate([high, low], axis=0)
    return jnp.dot(sums_table, both, preferred_element_type=F32)


def powers(log_decay, frames, mid, sign):
    groups = frames // 8
    coarse = (8 * lax.broadcasted_iota(jnp.int32, (groups, LANES), 0) - mid).astype(F32) * sign
    fine = lax.broadcasted_iota(jnp.int32, (8, LANES), 0).astype(F32) * sign
    coarse = jnp.exp(coarse * log_decay)
    fine = jnp.exp(fine * log_decay)
    return (coarse[:, None, :] * fine[None, :, :]).reshape(frames, LANES)


def chunk(field, c):
    own, rim = field
    inner = own.shape[0]
    if c < RIM:
        return rim.at[c]
    if c >= RIM + inner:
        return rim.at[c - inner]
    return own.at[c - RIM]


def chunk_count(field):
    return field[0].shape[0] + field[1].shape[0]


def prep_chunk(c, rate, field, gains, s3, p3, pinv3, z3, rows, pay):
    frames = field.shape[1]
    middle, prefix_col, inverse_col, sums_table = gains
    mid = frames // 2 - 1
    rate = jnp.where(rate > 0.0, rate, 1.0)
    log_rate = jnp.log(rate)
    gain = jnp.sqrt(1.0 - rate * rate)
    p = powers(log_rate, frames, mid, 1.0) * prefix_col
    pinv = powers(log_rate, frames, mid, -1.0) * inverse_col
    field = field.T
    z = summed(sums_table, field * gain * pinv)
    last = p[frames - 1 : frames, :]
    s3[...] = field
    p3[...] = p
    pinv3[...] = pinv
    z3[...] = z
    half = rate
    for _ in range(frames.bit_length() - 2):
        half = half * half
    rows[0, c : c + 1, :] = gain
    rows[1, c : c + 1, :] = half * middle
    rows[2, c : c + 1, :] = half * half
    pay[0, c : c + 1, :] = last * z[frames - 1 : frames, :]
    scale = last * gain
    pay[1, c : c + 1, :] = scale * scale * jnp.sum(pinv * pinv, axis=0, keepdims=True)


def gain_columns(gains):
    frames = gains.shape[1]
    mid = frames // 2 - 1
    lane = lax.broadcasted_iota(jnp.int32, (8, frames), 1)
    prefix = jnp.broadcast_to(gains, (8, frames))
    step = 1
    while step < frames:
        prefix = prefix * jnp.where(lane >= step, pltpu.roll(prefix, step, 1), 1.0)
        step *= 2
    middle = jnp.broadcast_to(prefix[0:1, mid : mid + 1], (1, LANES))
    whole = jnp.broadcast_to(prefix[0:1, frames - 1 : frames], (1, LANES))
    prefix_col = jnp.broadcast_to(prefix[0:1] / middle, (LANES, frames)).T
    inverse_col = jnp.broadcast_to(middle / prefix[0:1], (LANES, frames)).T
    return middle, whole, prefix_col, inverse_col


def rims_kernel(spikes, decay, first, second, rates_here, sems):
    edge = RIM * LANES
    neurons = spikes.shape[0]
    own = decay.shape[0]
    even = lax.axis_index("tile") % 2 == 0
    top = jnp.where(even, neurons - edge, 0)
    bottom = jnp.where(even, 0, neurons - edge)
    copies = [
        pltpu.make_async_copy(decay, rates_here, sems.at[0]),
        pltpu.make_async_copy(
            spikes.at[pl.ds(pl.multiple_of(top, LANES), edge)], first.at[pl.ds(0, edge)], sems.at[1]
        ),
        pltpu.make_async_copy(
            spikes.at[pl.ds(pl.multiple_of(bottom, LANES), edge)],
            second.at[pl.ds(0, edge)],
            sems.at[2],
        ),
    ]
    for copy in copies:
        copy.start()
    first[edge:, :] = jnp.zeros_like(first[edge:, :])
    second[edge:, :] = jnp.zeros_like(second[edge:, :])
    copies[0].wait()
    lower, upper = rates_here[0:RIM, :], rates_here[own - RIM : own, :]
    first[edge : edge + RIM, :] = jnp.where(even, upper, lower)
    second[edge : edge + RIM, :] = jnp.where(even, lower, upper)
    for copy in copies[1:]:
        copy.wait()


def after_start(compute):
    pl.when(lax.axis_index("tm") >= 0)(compute)


def prep_own_kernel(
    spikes, decay, gains, feet, s3, p3, pinv3, z3, rows, pay, columns, feet_ends, sems
):
    own = s3.shape[0]
    chunks = own + 2 * RIM
    size = feet_ends.shape[0] // 2
    fetches = [
        pltpu.make_async_copy(
            feet.at[pl.ds(start, size)], feet_ends.at[pl.ds(i * size, size)], sems.at[i]
        )
        for i, start in enumerate((0, feet.shape[0] - size))
    ]
    for fetch in fetches:
        fetch.start()

    @after_start
    def _():
        middle, whole, prefix_col, inverse_col = gain_columns(gains[...])
        columns[0] = prefix_col
        columns[1] = inverse_col
        rows[...] = jnp.ones_like(rows)
        rows[0, chunks : chunks + 1, :] = middle
        pay[...] = jnp.zeros_like(pay)
        pay[0, chunks : chunks + 1, :] = whole
        shared = middle, prefix_col, inverse_col, table(spikes.shape[1], False)
        for i in range(own):
            field = spikes[i * LANES : (i + 1) * LANES, :]
            at = [ref.at[i] for ref in (s3, p3, pinv3, z3)]
            prep_chunk(i + RIM, decay[i : i + 1, :], field, shared, *at, rows, pay)

    for fetch in fetches:
        fetch.wait()


def sides(even, first, second):
    return jnp.where(even, second, first), jnp.where(even, first, second)


def prep_rim_kernel(first, second, columns, rows_own, pay_own, s3, p3, pinv3, z3, rows, pay):
    rims, frames = s3.shape[0], s3.shape[1]
    own = rows_own.shape[1] - padded8(1)
    chunks = own + 2 * RIM
    middle = rows_own[0, chunks : chunks + 1, :]
    shared = middle, columns[0], columns[1], table(frames, False)
    rows[...] = rows_own[...]
    pay[...] = pay_own[...]
    even = lax.axis_index("tile") % 2 == 0
    below, above = sides(even, first[...], second[...])
    for i in range(rims):
        message = below if i < RIM else above
        j = i % RIM
        c = i if i < RIM else own + i
        at = [ref.at[i] for ref in (s3, p3, pinv3, z3)]
        field = message[j * LANES : (j + 1) * LANES, :]
        rate = message[RIM * LANES + j : RIM * LANES + j + 1, :]
        prep_chunk(c, rate, field, shared, *at, rows, pay)


def by_block(parts, me, index):
    values = [part[index] for part in parts]
    ordered = []
    for m in range(len(values)):
        value = values[0]
        for j in range(1, len(values)):
            value = jnp.where(me == m ^ j, values[j], value)
        ordered.append(value)
    return ordered


def block_totals(pay, me, chunks, rows):
    return [rows[2] * whole for whole in by_block(pay, me, (0, slice(chunks, chunks + 1)))]


def step_size(stats):
    both = jnp.sum(jnp.sum(stats[...], axis=0), axis=1, keepdims=True)
    return jnp.broadcast_to(both[0:1] / (both[1:2] + 1e-06), (1, LANES))


def update_kernel(s3, g3, stats, p3, pinv3, rows, new3, z3, pay):
    chunks = chunk_count(s3)
    frames = g3.shape[1]
    sums_table = table(frames, False)
    size = step_size(stats)
    pay[...] = jnp.zeros_like(pay)
    for c in range(chunks):
        field = jnp.maximum(chunk(s3, c)[...] - size * g3[c], 0.0)
        z = summed(sums_table, field * rows[0, c : c + 1, :] * chunk(pinv3, c)[...])
        if len(new3) == 2:
            chunk(new3, c)[...] = field
        elif RIM <= c < chunks - RIM:
            new3[0][c - RIM] = field
        chunk(z3, c)[...] = z
        last = chunk(p3, c)[frames - 1 : frames, :]
        pay[0, c : c + 1, :] = last * z[frames - 1 : frames, :]


def final_kernel(s3, g3, stats, out, here, sems):
    size = step_size(stats)
    part = s3.shape[0] // PARTS
    copies = [
        pltpu.make_async_copy(
            here.at[pl.ds(i * part * LANES, part * LANES)],
            out.at[pl.ds(i * part * LANES, part * LANES)],
            sems.at[i],
        )
        for i in range(PARTS)
    ]
    for i in range(PARTS):

        @after_start
        def _():
            for c in range(i * part, (i + 1) * part):
                field = jnp.maximum(s3[c] - size * g3[c + RIM], 0.0)
                here[c * LANES : (c + 1) * LANES, :] = field.T
            copies[i].start()

    for copy in copies:
        copy.wait()


def picked(ext, pattern, q, first=0):
    parts = [
        ext[pl.ds(pl.multiple_of((pattern[k, q] - first) * NEU_BLOCK, NEU_BLOCK), NEU_BLOCK), :]
        for k in range(K)
    ]
    return jnp.concatenate(parts, axis=0)


def block_of(field, q):
    return field[q * PIX_BLOCK : (q + 1) * PIX_BLOCK, :]


def foot_of(feet, q, stripe):
    count = feet.shape[0] // PIX_BLOCK
    return block_of(feet, q if q < count // 2 else q - stripe + count)


def note_places(pattern, place, start, stop):
    for q in range(start, stop):
        for v in range(2 * HB + 1):
            place[q, v] = -1
        for k in range(K):
            place[q, pattern[k, q] - q] = k


def pull_back(pattern, ext, feet, record, contrib, q):
    foot = foot_of(feet, q, pattern.shape[1])
    fitted = jnp.dot(foot, picked(ext, pattern, q), preferred_element_type=F32)
    residual = (fitted - block_of(record, q).astype(F32)).astype(BF16)
    contrib[q * K * NEU_BLOCK : (q + 1) * K * NEU_BLOCK, :] = lax.dot_general(
        foot, residual, (((0,), (0,)), ((), ())), preferred_element_type=F32
    )


def gathered(contrib, place, c, ranges):
    frames = contrib.shape[1]
    per_chunk = LANES // NEU_BLOCK
    halves = []
    for b in range(c * per_chunk, (c + 1) * per_chunk):
        total = jnp.zeros((NEU_BLOCK, frames), F32)
        for v in range(2 * HB + 1):
            q = b - v
            if any(start <= q < stop for start, stop in ranges):
                k = place[q, v]
                at = pl.multiple_of((q * K + jnp.maximum(k, 0)) * NEU_BLOCK, NEU_BLOCK)
                value = contrib[pl.ds(at, NEU_BLOCK), :]
                if v % 2:
                    value = jnp.where(k >= 0, value, 0.0)
                total = total + value
        halves.append(total)
    return jnp.concatenate(halves, axis=0).T


def edge_kernel(
    pattern_far, z3, p3, rows, pay, pays, feet, record, ext, zones, spill, send_a, send_b, *rest
):
    *traces, contrib, place, pattern, sem = rest
    fetch = pltpu.make_async_copy(pattern_far, pattern, sem)
    fetch.start()
    chunks = chunk_count(z3)
    stripe = pattern.shape[1]
    edge = 2 * HB
    ranges = ((0, edge), (stripe - edge, stripe))

    @after_start
    def _():
        me = lax.axis_index("tm")
        totals = block_totals(pay, me, chunks, rows)
        ends = by_block(pays, me, 0)
        carry = jnp.zeros_like(totals[0])
        for m, end in enumerate(ends):
            carry = jnp.where(m < me, end + totals[m] * carry, carry)
        carry = carry * rows[1]
        for c in range(chunks):
            field = chunk(p3, c)[...] * (chunk(z3, c)[...] + carry[c : c + 1, :])
            at = slice(c * LANES, (c + 1) * LANES)
            if traces and RIM <= c < chunks - RIM:
                field = field.T
                traces[0][(c - RIM) * LANES : (c - RIM + 1) * LANES, :] = field
                ext[at, :] = field.astype(BF16)
            else:
                ext[at, :] = field.astype(BF16).T

    fetch.wait()
    for start, stop in ranges:
        note_places(pattern, place, start, stop)
    for start, stop in ranges:
        for q in range(start, stop):
            pull_back(pattern, ext, feet, record, contrib, q)
    even = lax.axis_index("tile") % 2 == 0
    for i in range(2 * RIM):
        below = gathered(contrib, place, i, ranges)
        above = gathered(contrib, place, chunks - 2 * RIM + i, ranges)
        zones[i] = below
        zones[2 * RIM + i] = above
        for to, other, held in ((send_a, above, below), (send_b, below, above)):
            to[i] = jnp.where(even, other, held).astype(BF16)
        spill[i] = gathered(contrib, place, 2 * RIM + i, ranges)
        spill[2 * RIM + i] = gathered(contrib, place, chunks - 4 * RIM + i, ranges)
    for i in range(RIM):
        lows = [
            zones[at] - zones[at].astype(BF16).astype(F32)
            for at in (i, 3 * RIM + i)
        ]
        send_a[2 * RIM + i] = jnp.where(even, lows[1], lows[0]).astype(BF16)
        send_b[2 * RIM + i] = jnp.where(even, lows[0], lows[1]).astype(BF16)

def adjoint_chunk(sums_table, field, p, pinv, rows, c, r3, pay):
    frames = field.shape[0]
    r = summed(sums_table, field * p)
    r3[...] = r
    gain = rows[0, c : c + 1, :]
    pay[0, c : c + 1, :] = rows[1, c : c + 1, :] * r[0:1, :]
    ends = p[frames - 1 : frames, :] * gain * gain
    pay[1, c : c + 1, :] = ends * jnp.sum(pinv * pinv * r, axis=0, keepdims=True)


def inner_kernel(pattern_far, p3, pinv3, rows, ext, spill, feet, record, traces, r3, pay, *rest):
    *out, contrib, place, pattern, sem = rest[: 4 + len(traces)]
    fetch = pltpu.make_async_copy(pattern_far, pattern, sem)
    fetch.start()
    if traces:
        copy = pltpu.make_async_copy(traces[0], out[0], rest[-1])
        copy.start()
    fetch.wait()

    def compute():
        chunks = chunk_count(p3)
        frames = spill.shape[1]
        stripe = pattern.shape[1]
        edge = 2 * HB
        note_places(pattern, place, edge, stripe - edge)
        sums_table = table(frames, True)
        pay[...] = jnp.zeros_like(pay)
        inner = chunks - 4 * RIM
        for q in range(edge, stripe - edge):
            pull_back(pattern, ext, feet, record, contrib, q)
        for i in range(inner):
            c = i + 2 * RIM
            field = gathered(contrib, place, c, ((edge, stripe - edge),))
            if i < 2 * RIM:
                field = field + spill[i]
            if i >= inner - 2 * RIM:
                field = field + spill[i - inner + 4 * RIM]
            p, pinv = chunk(p3, c)[...], chunk(pinv3, c)[...]
            adjoint_chunk(sums_table, field, p, pinv, rows, c, r3.at[i], pay)

    if traces:
        after_start(compute)
        copy.wait()
    else:
        compute()


def border_kernel(zones, got_a, got_b, p3, pinv3, rows, pay_inner, r3, pay):
    chunks = chunk_count(p3)
    frames = zones.shape[1]
    sums_table = table(frames, True)
    pay[...] = pay_inner[...]
    even = lax.axis_index("tile") % 2 == 0
    for i in range(2 * RIM):
        both = sides(even, got_a[i].astype(F32), got_b[i].astype(F32))
        at = 2 * RIM + i % RIM
        lows = sides(even, got_a[at].astype(F32), got_b[at].astype(F32))
        for side, c in ((0, i), (1, chunks - 2 * RIM + i)):
            at = side * 2 * RIM + i
            field = zones[at] + both[side]
            if (i >= RIM) == (side == 0):
                field = field + lows[side]
            p, pinv = chunk(p3, c)[...], chunk(pinv3, c)[...]
            adjoint_chunk(sums_table, field, p, pinv, rows, c, r3.at[at], pay)


def direction_kernel(
    pattern_far, r_inner, r_border, p3, pinv3, rows, pay, pays, feet, g3, stats, low, high, *rest
):
    pattern, sem, grad_sums = rest
    fetch = pltpu.make_async_copy(pattern_far, pattern, sem)
    fetch.start()
    chunks, frames = g3.shape[0], g3.shape[1]
    own = chunks - 2 * RIM
    stripe = pattern.shape[1]
    per_chunk = LANES // NEU_BLOCK
    low_chunks = low.shape[0] // LANES
    first_high = chunks - high.shape[0] // LANES

    @after_start
    def _():
        me = lax.axis_index("tm")
        totals = block_totals(pay, me, chunks, rows)
        gains = by_block(pay, me, 1)
        starts = by_block(pays, me, 0)
        ends = by_block(pays, me, 1)
        blocks = len(pays)
        entering = [None] * blocks
        state = jnp.zeros_like(totals[0])
        for m in reversed(range(blocks)):
            entering[m] = state
            state = starts[m] + totals[m] * state
        carry = jnp.zeros_like(totals[0])
        adjoint = jnp.zeros_like(totals[0])
        for m in range(blocks):
            end = ends[m] + gains[m] * entering[m]
            carry = jnp.where(m < me, end + totals[m] * carry, carry)
            adjoint = jnp.where(m == me, entering[m], adjoint)
        carry = carry * rows[1]
        sums_table = table(frames, False)
        grad_sq = jnp.zeros((8, LANES), F32)
        for c in range(chunks):
            p = chunk(p3, c)[...]
            if c < 2 * RIM:
                r = r_border[c]
            elif c >= chunks - 2 * RIM:
                r = r_border[c - chunks + 4 * RIM]
            else:
                r = r_inner[c - 2 * RIM]
            scale = rows[0, c : c + 1, :] * chunk(pinv3, c)[...]
            gradient = scale * (r + p[frames - 1 : frames, :] * adjoint[c : c + 1, :])
            g3[c] = gradient
            if RIM <= c < RIM + own:
                grad_sq += jnp.sum((gradient * gradient).reshape(frames // 8, 8, LANES), axis=0)
            z = summed(sums_table, scale * gradient)
            field = (p * (z + carry[c : c + 1, :])).astype(BF16).T
            if c < low_chunks:
                low[c * LANES : (c + 1) * LANES, :] = field
            if c >= first_high:
                high[(c - first_high) * LANES : (c - first_high + 1) * LANES, :] = field
        grad_sums[...] = grad_sq

    fetch.wait()
    image_sq = jnp.zeros((8, frames), F32)
    for q in range(stripe):
        if q + 2 * HB < low_chunks * per_chunk:
            named = picked(low, pattern, q, 0)
        else:
            named = picked(high, pattern, q, first_high * per_chunk)
        image = jnp.dot(foot_of(feet, q, stripe), named, preferred_element_type=F32)
        image_sq += jnp.sum((image * image).reshape(PIX_BLOCK // 8, 8, frames), axis=0)
    both = jnp.concatenate(
        [
            jnp.sum(grad_sums[...], axis=0, keepdims=True),
            jnp.sum(image_sq, axis=0, keepdims=True),
        ],
        axis=0,
    )
    stats[...] = jnp.broadcast_to(both[None], stats.shape)


def f32(*shape):
    return jax.ShapeDtypeStruct(shape, F32)


def bf16(*shape):
    return jax.ShapeDtypeStruct(shape, BF16)


def call(
    kernel, name, micros, outs, args, scratch=(), far=(), far_out=(), keep=(), limit=16
):
    def spec(arg):
        if any(arg is other for other in far):
            return HBM
        return pl.BlockSpec(memory_space=pl.ANY) if arg.dtype == jnp.int32 else VMEM

    in_specs = [jax.tree.map(spec, arg) for arg in args]
    in_specs.append(jax.tree.map(lambda _: VMEM, keep))

    def body(*refs):
        kernel(*refs[: len(args)], *refs[len(args) + 1 :])

    return pl.pallas_call(
        body,
        name=name,
        out_shape=outs,
        in_specs=in_specs,
        out_specs=tuple(
            jax.tree.map(lambda _: HBM if place in far_out else VMEM, out)
            for place, out in enumerate(outs)
        ),
        scratch_shapes=scratch,
        compiler_params=pltpu.CompilerParams(vmem_limit_bytes=int(limit * 2**20)),
        cost_estimate=pl.CostEstimate(
            flops=int(micros * 1e8), bytes_accessed=int(micros * 3e6), transcendentals=0
        ),
    )(*args, keep)


def swapped(first, second):
    size = lax.axis_size("tile")

    def pairs(start):
        both = [(i, i + 1) for i in range(start, size - 1, 2)]
        return both + [(j, i) for i, j in both]

    return lax.ppermute(first, "tile", pairs(0)), lax.ppermute(second, "tile", pairs(1))


def shared_blocks(value):
    size = lax.axis_size("tm")
    others = [
        lax.ppermute(value, "tm", [(i, i ^ j) for i in range(size)])
        for j in reversed(range(1, size))
    ]
    return (value, *reversed(others))


def per_device(recording, footprints, pattern, decay, frame_gain, spikes):
    neurons, frames = spikes.shape
    stripe = pattern.shape[0]
    pattern = pattern.T
    own = neurons // LANES
    chunks = own + 2 * RIM
    lines = own + padded8(1)
    devices = lax.axis_size("tile") * lax.axis_size("tm")
    split = (f32(own, frames, LANES), f32(2 * RIM, frames, LANES))
    message = f32(RIM * LANES + padded8(RIM), frames)
    gains = frame_gain.reshape(1, frames)
    rates = decay.reshape(own, LANES)
    first, second, rates = call(
        rims_kernel,
        "rims",
        1.0,
        (message, message, f32(own, LANES)),
        (spikes, rates),
        [pltpu.SemaphoreType.DMA((3,))],
        far=(spikes, rates),
        limit=53,
    )
    first, second = swapped(first, second)
    ends_size = 4 * HB * PIX_BLOCK
    *owns, rows, pay, columns, feet_ends = call(
        prep_own_kernel,
        "prep_own",
        1.6,
        (split[0],) * 4
        + (f32(3, lines, LANES), f32(2, lines, LANES), f32(2, frames, LANES))
        + (bf16(ends_size, K * NEU_BLOCK),),
        (spikes, rates, gains, footprints),
        [pltpu.SemaphoreType.DMA((2,))],
        far=(footprints,),
        limit=44,
    )
    *rims, rows, pay = call(
        prep_rim_kernel,
        "prep_rim",
        0.3,
        (split[1],) * 4 + (f32(3, lines, LANES), f32(2, lines, LANES)),
        (first, second, columns, rows, pay),
    )
    s3, p3, pinv3, z3 = zip(owns, rims)
    constants = pays = shared_blocks(pay)
    scratch = [
        pltpu.VMEM((stripe * K * NEU_BLOCK, frames), F32),
        pltpu.SMEM((stripe, 2 * HB + 1), jnp.int32),
        pltpu.SMEM(pattern.shape, jnp.int32),
        pltpu.SemaphoreType.DMA,
    ]
    staged = [pltpu.VMEM((neurons, frames), F32), pltpu.SemaphoreType.DMA((PARTS,))]
    middle = stripe * NEU_BLOCK // LANES // 2
    halves = (middle + 2 * RIM, chunks - middle)
    border = (4 * RIM, frames, LANES)
    for iteration in range(ITERS):
        ends = iteration == ITERS - 1
        ext, zones, spill, send_a, send_b, *traces = call(
            edge_kernel,
            "edge",
            2.5,
            (
                bf16(chunks * LANES, frames),
                f32(*border),
                f32(*border),
                bf16(3 * RIM, frames, LANES),
                bf16(3 * RIM, frames, LANES),
            )
            + ((f32(neurons, frames),) if ends else ()),
            (pattern, z3, p3, rows, constants, pays, feet_ends, recording),
            scratch,
            keep=(s3[0],) if ends else (),
        )
        got_a, got_b = swapped(send_a, send_b)
        held = (s3[0],) if ends else ()
        r_inner, pay, *traces = call(
            inner_kernel,
            "inner",
            4.0,
            (f32(chunks - 4 * RIM, frames, LANES), f32(2, lines, LANES))
            + ((f32(neurons, frames),) if ends else ()),
            (pattern, p3, pinv3, rows, ext, spill, footprints, recording, traces),
            scratch + ([pltpu.SemaphoreType.DMA] if ends else []),
            far_out=(2,),
            keep=held,
        )
        r_border, pay = call(
            border_kernel,
            "border",
            0.3,
            (f32(*border), f32(2, lines, LANES)),
            (zones, got_a, got_b, p3, pinv3, rows, pay),
            keep=held,
        )
        pays = shared_blocks(pay)
        g3, stats = call(
            direction_kernel,
            "direction",
            4.0,
            (f32(chunks, frames, LANES), f32(devices, 2, LANES)),
            (pattern, r_inner, r_border, p3, pinv3, rows, constants, pays, footprints),
            [
                pltpu.VMEM((halves[0] * LANES, frames), BF16),
                pltpu.VMEM((halves[1] * LANES, frames), BF16),
                *scratch[2:],
                pltpu.VMEM((8, LANES), F32),
            ],
            keep=held,
        )
        stats = lax.all_to_all(stats, ("tile", "tm"), 0, 0)
        if ends:
            (out,) = call(
                final_kernel,
                "final",
                1.4,
                (f32(neurons, frames),),
                (s3[0], g3, stats),
                staged,
                far_out=(0,),
            )
            return out, traces[0]
        s3, z3, pay = call(
            update_kernel,
            "update",
            0.6,
            (split if iteration < ITERS - 2 else split[:1], split, f32(1, lines, LANES)),
            (s3, g3, stats, p3, pinv3, rows),
        )
        pays = shared_blocks(pay)


def solution(mesh):
    return jax.shard_map(
        per_device,
        mesh=mesh,
        in_specs=(
            P("tile", "tm"),
            P("tile", None),
            P("tile", None),
            P("tile"),
            P("tm"),
            P("tile", "tm"),
        ),
        out_specs=(P("tile", "tm"), P("tile", "tm")),
        check_vma=False,
    )
```
